32 devices in a mesh: gx: 4 (over x, core), gy: 4 (over z), gz: 2 (over y).
Axes of the slice: x: 2, y: 2, z: 4, core: 2. Of those that a mesh axis runs over, the one named last changes fastest.
Arguments:
- charges: float32 [64, 128, 512], P('gz', 'gy', 'gx'), may hold values from -8 to 8
- kernel_taps: float32 [3, 2, 17], replicated, may hold values from 0 to 2
Outputs:
- potential: float32 [64, 128, 512], P('gz', 'gy', 'gx')
The draws below stay inside these ranges and needn't reach their ends.
All inputs are finite; a program needn't handle non-finite values.
Results may differ from the reference program's by a relative error of at most 0.0001.
Values sent between devices are 32-bit elements; how exact they have to be, the bound alone decides.
No kernel may reach another device: no remote copies, remote signals or barrier semaphores. Data moves between devices by JAX's collectives and lax.ppermute only.
A program may use at most 128 MiB of HBM per device.

```python
import jax
import jax.numpy as jnp
from jax import lax

RADIUS = 8
TERMS = 2
LEVELS = 3
TAPS = 17
NZ = 64
NY = 128
NX = 512


def draw_kernel_taps(key, part):
    key_width = jax.random.fold_in(key, 11)
    key_scale = jax.random.fold_in(key, 23)
    fraction = jax.random.uniform(key_width, (LEVELS, TERMS), jnp.float32)
    base_width = 1.5 * 3.3 ** jnp.arange(TERMS).astype(jnp.float32)
    widths = base_width[None, :] * 2.0 ** fraction
    magnitude = jax.random.uniform(key_scale, (LEVELS, TERMS), jnp.float32, 0.5, 1.5)
    distance = (jnp.arange(TAPS) - RADIUS).astype(jnp.float32)
    profile = jnp.exp(-(distance[None, None, :] / widths[:, :, None]) ** 2)
    profile = profile / jnp.sqrt(jnp.sum(profile * profile, axis=2, keepdims=True))
    level_factor = 2.0 ** (-0.5 * jnp.arange(LEVELS).astype(jnp.float32))
    scaling = magnitude ** (1.0 / 3.0) * level_factor[:, None]
    return profile * scaling[:, :, None]


def levels(own_key, shape, cuts, smallest, high):
    loudness = 1.0
    for position, parts in cuts:
        heights = jax.random.uniform(jax.random.fold_in(jax.random.fold_in(own_key, 6), position), (parts,), jnp.float32, smallest / len(cuts), high / len(cuts))
        loudness = loudness * jnp.repeat(jnp.exp(heights), shape[position] // parts).reshape((-1,) + (1,) * (len(shape) - 1 - position))
    return loudness


def noise(stream_key, shape, width, reach, cuts=(), dtype=jnp.bfloat16):
    gain = levels(stream_key, shape, cuts, -0.22, 0.18) if cuts else 1.0
    array = jax.random.normal(stream_key, shape, jnp.float32) * width * gain
    return jnp.minimum(jnp.maximum(array, -reach), reach).astype(dtype)


def setup_inputs(seed: int = 0) -> dict:
    arg_keys = jax.random.split(jax.random.key(seed), 3)
    charges = noise(arg_keys[0], (NZ, NY, NX), 1.0, 8.0, ((0, 2), (1, 4), (2, 4)), jnp.float32)
    kernel_taps = draw_kernel_taps(jax.random.fold_in(arg_keys[2], 71), 0)
    return {"charges": charges, "kernel_taps": kernel_taps}


RESTRICT_WEIGHTS = ((-3, -0.0625), (-1, 0.5625), (0, 1.0), (1, 0.5625), (3, -0.0625))


def convolve_axis(padded, kernel_row, axis_dim, length):
    summed = kernel_row[0] * lax.slice_in_dim(padded, 0, length, axis=axis_dim)
    for offset in range(1, TAPS):
        summed = summed + kernel_row[offset] * lax.slice_in_dim(padded, offset, offset + length, axis=axis_dim)
    return summed


def level_field(grid_charges, kernel_rows):
    extent_z, extent_y, extent_x = grid_charges.shape
    padded = jnp.pad(grid_charges, RADIUS)
    result_field = jnp.zeros(grid_charges.shape, jnp.float32)
    for term_index in range(TERMS):
        smoothed = convolve_axis(padded, kernel_rows[term_index], 0, extent_z)
        smoothed = convolve_axis(smoothed, kernel_rows[term_index], 1, extent_y)
        smoothed = convolve_axis(smoothed, kernel_rows[term_index], 2, extent_x)
        result_field = result_field + smoothed
    return result_field


def restrict_axis(padded, axis_dim, margin, count):
    summed = None
    for offset, weight in RESTRICT_WEIGHTS:
        first = margin + offset
        piece = lax.slice_in_dim(padded, first, first + 2 * count - 1, stride=2, axis=axis_dim)
        summed = weight * piece if summed is None else summed + weight * piece
    return summed


def restrict_padded(padded, margin, counts):
    result_field = restrict_axis(padded, 0, margin, counts[0])
    result_field = restrict_axis(result_field, 1, margin, counts[1])
    return restrict_axis(result_field, 2, margin, counts[2])


def prolong_axis(padded, axis_dim, margin, count):
    def take(shift):
        return lax.slice_in_dim(padded, margin + shift, margin + shift + count, axis=axis_dim)
    centre = take(0)
    odd_cells = 0.5625 * (centre + take(1)) - 0.0625 * (take(-1) + take(2))
    stacked = jnp.stack([centre, odd_cells], axis=axis_dim + 1)
    new_shape = list(centre.shape)
    new_shape[axis_dim] = 2 * count
    return stacked.reshape(new_shape)


def prolong_padded(padded, margin, counts):
    result_field = prolong_axis(padded, 0, margin, counts[0])
    result_field = prolong_axis(result_field, 1, margin, counts[1])
    return prolong_axis(result_field, 2, margin, counts[2])


def restrict_grid(grid_charges):
    extent_z, extent_y, extent_x = grid_charges.shape
    return restrict_padded(jnp.pad(grid_charges, 3), 3, (extent_z // 2, extent_y // 2, extent_x // 2))


def prolong_grid(coarse_field):
    return prolong_padded(jnp.pad(coarse_field, 2), 2, coarse_field.shape)


def reference(charges, kernel_taps):
    mid_charges = restrict_grid(charges)
    coarse_charges = restrict_grid(mid_charges)
    fine_potential = level_field(charges, kernel_taps[0])
    mid_potential = level_field(mid_charges, kernel_taps[1])
    coarse_potential = level_field(coarse_charges, kernel_taps[2])
    mid_total = mid_potential + prolong_grid(coarse_potential)
    return fine_potential + prolong_grid(mid_total)
```

```python
import jax
import jax.numpy as jnp
from jax import lax
from jax.sharding import PartitionSpec as P

RADIUS = 8
TAPS = 17
WEIGHTS = ((-3, -0.0625), (-1, 0.5625), (0, 1.0), (1, 0.5625), (3, -0.0625))
EXACT = lax.Precision.HIGHEST


def interpolation(difference):
    out = jnp.zeros(difference.shape, jnp.float32)
    for offset, weight in WEIGHTS:
        out = jnp.where(difference == offset, weight, out)
    return out


def banded(taps, rows, columns, valid):
    offset = columns[None, :] - rows[:, None] + RADIUS
    out = jnp.zeros((taps.shape[0],) + offset.shape, jnp.float32)
    for tap in range(TAPS):
        out = jnp.where((offset == tap)[None], taps[:, tap, None, None], out)
    return jnp.where(valid[None, None, :], out, 0.0)


class Axis:
    def __init__(self, name, length):
        self.name, self.length = name, length
        self.count, self.index = lax.axis_size(name), lax.axis_index(name)
        mid, coarse = length // 2, length // 4
        self.first = (0, -1, -2)
        self.extent = (length, mid + 3, coarse + 5)
        self.brick = (length, mid, coarse)
        fine_rows = jnp.arange(length)
        mid_rows = jnp.arange(mid + 3) - 1
        coarse_rows = jnp.arange(coarse + 5) - 2
        self.rows = (fine_rows, mid_rows, coarse_rows)

        def inside(rows, brick):
            place = rows + self.index * brick
            return (place >= 0) & (place < brick * self.count)

        to_mid = interpolation(fine_rows[None, :] - 2 * mid_rows[:, None])
        self.to_mid = jnp.where(inside(mid_rows, mid)[:, None], to_mid, 0.0)
        to_coarse = interpolation(mid_rows[None, :] - 2 * coarse_rows[:, None])
        self.to_coarse = jnp.where(inside(coarse_rows, coarse)[:, None], to_coarse, 0.0)
        self.own = [(self.rows[level], jnp.full((self.extent[level],), True)) for level in range(3)]

    def from_brick(self, level, steps, low, size):
        places = self.first[level] + low + jnp.arange(size) + steps * self.brick[level]
        other = self.index + steps
        valid = (other >= 0) & (other < self.count)
        return places, jnp.broadcast_to(valid, (size,))

    def operators(self, taps, places):
        columns = [
            (jnp.concatenate([p for p, _ in level]), jnp.concatenate([v for _, v in level]))
            for level in places
        ]
        bands = [banded(taps[level], self.rows[level], *columns[level]) for level in range(3)]
        mid = jnp.einsum("ko,tkj->toj", self.to_mid, bands[1], precision=EXACT)
        widen = jnp.dot(self.to_coarse, self.to_mid, precision=EXACT)
        coarse = jnp.einsum("ko,tkj->toj", widen, bands[2], precision=EXACT)
        return bands[0], mid, coarse


def edge(x, dim, width, last):
    length = x.shape[dim]
    return lax.slice_in_dim(x, length - width, length, axis=dim) if last else lax.slice_in_dim(x, 0, width, axis=dim)


def hop(arrays, axis, dim, widths, steps, routes):
    gathered = [[] for _ in arrays]
    places = [[] for _ in arrays]
    below = None
    for names, pairs, up, below in routes:
        for level, (x, width) in enumerate(zip(arrays, widths)):
            if not width:
                continue
            size = x.shape[dim]
            message = jnp.where(up, edge(x, dim, width, True), edge(x, dim, width, False))
            gathered[level].append(lax.ppermute(message, names, pairs))
            lower = axis.from_brick(level, -steps, size - width, width)
            higher = axis.from_brick(level, steps, 0, width)
            places[level].append(tuple(jnp.where(below, a, b) for a, b in zip(lower, higher)))
    if len(routes) == 2 and not isinstance(below, bool):
        for level in range(3):
            a, b = gathered[level]
            gathered[level] = [jnp.where(below, b, a), jnp.where(below, a, b)]
            a, b = places[level]
            places[level] = [tuple(jnp.where(below, q, p) for p, q in zip(a, b)), tuple(jnp.where(below, p, q) for p, q in zip(a, b))]
    return gathered, places


def ring(axis):
    n = axis.count
    up = [(i, (i + 1) % n) for i in range(n)]
    return [((axis.name,), up, True, True), ((axis.name,), [(b, a) for a, b in up], False, False)]


def folded(axis, beside):
    n, m = axis.count, lax.axis_size(beside)
    pairs = []
    for c in range(0, m, 2):
        cycle = [c * n + i for i in range(n)] + [(c + 1) * n + i for i in reversed(range(n))]
        pairs += list(zip(cycle, cycle[1:] + cycle[:1]))
    even = lax.axis_index(beside) % 2 == 0
    names = (beside, axis.name)
    return [(names, pairs, even, even), (names, [(b, a) for a, b in pairs], ~even, ~even)]


def swap(axis, steps):
    n = axis.count
    pairs = [(i, i + steps) for i in range(n - steps)]
    up = axis.index + steps < n
    return [((axis.name,), pairs + [(b, a) for a, b in pairs], up, ~up)]


def line(axis, steps):
    n = axis.count
    pairs = [(i, i + steps) for i in range(n - steps)]
    return [((axis.name,), pairs, True, True), ((axis.name,), [(b, a) for a, b in pairs], False, False)]


def near(axis, beside):
    if axis.count <= 2:
        return swap(axis, 1)
    if beside is not None and lax.axis_size(beside) % 2 == 0:
        return folded(axis, beside)
    return ring(axis)


def gather(arrays, axis, dim, beside):
    coarse = axis.brick[2]
    spill = axis.extent[2] - coarse
    widths = (RADIUS, RADIUS + 3, min(axis.extent[2], RADIUS + spill))
    pieces = [[x] for x in arrays]
    places = [[own] for own in axis.own]
    if axis.count > 1:
        got, where = hop(arrays, axis, dim, widths, 1, near(axis, beside))
        for level in range(3):
            pieces[level] += got[level]
            places[level] += where[level]
    steps = 2
    while steps < axis.count and (steps - 1) * coarse <= RADIUS + 4:
        width = min(axis.extent[2], RADIUS + 4 + 1 - (steps - 1) * coarse)
        routes = swap(axis, steps) if axis.count <= 2 * steps else line(axis, steps)
        got, where = hop(arrays, axis, dim, (0, 0, width), steps, routes)
        pieces[2] += got[2]
        places[2] += where[2]
        steps += 1
    return [jnp.concatenate(p, axis=dim) for p in pieces], places


def local(charges, kernel_taps):
    az, ay, ax = (Axis(name, size) for name, size in zip(("gz", "gy", "gx"), charges.shape))

    def shrink(x, z, y, w):
        x = jnp.einsum("zyx,kx->zyk", x, w, precision=EXACT)
        x = jnp.einsum("zyx,ky->zkx", x, y, precision=EXACT)
        return jnp.einsum("zyx,kz->kyx", x, z, precision=EXACT)

    mid = shrink(charges, az.to_mid, ay.to_mid, ax.to_mid)
    coarse = shrink(mid, az.to_coarse, ay.to_coarse, ax.to_coarse)
    grids = [charges, mid, coarse]
    grids, places = gather(grids, az, 0, None)
    oz = az.operators(kernel_taps, places)
    grids, places = gather(grids, ay, 1, "gx")
    oy = ay.operators(kernel_taps, places)
    grids, places = gather(grids, ax, 2, None)
    ox = ax.operators(kernel_taps, places)
    total = 0.0
    for level in range(3):
        x = jnp.einsum("zyx,tkx->tzyk", grids[level], ox[level], precision=EXACT)
        x = jnp.einsum("tzyx,tky->tzkx", x, oy[level], precision=EXACT)
        total = total + jnp.einsum("tzyx,tkz->kyx", x, oz[level], precision=EXACT)
    return total


def solution(mesh):
    return jax.shard_map(
        local,
        mesh=mesh,
        in_specs=(P("gz", "gy", "gx"), P()),
        out_specs=P("gz", "gy", "gx"),
        check_vma=False,
    )
```

```python
import jax
import jax.numpy as jnp
from jax import lax
from jax.experimental import pallas as pl
from jax.experimental.pallas import tpu as pltpu
from jax.sharding import PartitionSpec as P

RADIUS = 8
TAPS = 17
TERMS = 2
WEIGHTS = ((-3, -0.0625), (-1, 0.5625), (0, 1.0), (1, 0.5625), (3, -0.0625))
EXACT = lax.Precision.HIGHEST
SPAN = RADIUS + 5
EDGE = RADIUS + 3
F32, BF16 = jnp.float32, jnp.bfloat16
PARAMS = pltpu.CompilerParams(vmem_limit_bytes=48 * 1024 * 1024)
VMEM = pl.BlockSpec(memory_space=pltpu.VMEM)
SMEM = pl.BlockSpec(memory_space=pltpu.SMEM)


def up8(n):
    return -(-n // 8) * 8


def iota(shape, dim):
    return lax.broadcasted_iota(jnp.int32, shape, dim)


def weight_of(difference):
    size = jnp.abs(difference)
    out = jnp.where(size == 1, 0.5625, jnp.where(size == 3, -0.0625, 0.0))
    return jnp.where(size == 0, 1.0, out)


def choose(condition, a, b):
    return jnp.where(condition, jnp.where(a, 1, 0), jnp.where(b, 1, 0)) != 0


class Cut:
    def __init__(self, name, length):
        self.name, self.fine = name, length
        self.count = lax.axis_size(name)
        self.mid, self.coarse = length // 2, length // 4
        self.mid_all, self.coarse_all = self.mid + 3, self.coarse + 5
        self.second = max(SPAN - self.coarse, 0)

    def index(self):
        return lax.axis_index(self.name)

    def holds_mid(self, k):
        k = k + self.index() * self.mid
        return (k >= 0) & (k < self.mid * self.count)

    def holds_coarse(self, k):
        k = k + self.index() * self.coarse
        return (k >= 0) & (k < self.coarse * self.count)


class Route:
    def __init__(self, names, pairs, up, below):
        self.names, self.pairs, self.up, self.below = names, pairs, up, below

    def __call__(self, x):
        return lax.ppermute(x, self.names, self.pairs)


def flip(pairs):
    return [(b, a) for a, b in pairs]


def swap(cut, steps):
    pairs = [(i, i + steps) for i in range(cut.count - steps)]

    def up():
        return cut.index() + steps < cut.count

    return [Route(cut.name, pairs + flip(pairs), up, lambda: ~up())]


def both_ways(cut, steps):
    pairs = [(i, i + steps) for i in range(cut.count - steps)]
    yes, no = (lambda: cut.index() >= 0), (lambda: cut.index() < 0)
    return [Route(cut.name, pairs, yes, yes), Route(cut.name, flip(pairs), no, no)]


def folded(cut, beside, names):
    n, m = cut.count, lax.axis_size(beside)

    def place(c, i):
        return c * n + i if names[0] == beside else i * m + c

    pairs = []
    for c in range(0, m, 2):
        cycle = [place(c, i) for i in range(n)] + [place(c + 1, i) for i in reversed(range(n))]
        pairs += list(zip(cycle, cycle[1:] + cycle[:1]))

    def even():
        return lax.axis_index(beside) % 2 == 0

    def odd():
        return lax.axis_index(beside) % 2 == 1

    return [Route(names, pairs, even, even), Route(names, flip(pairs), odd, odd)]


def split(x):
    high = x.astype(BF16)
    return high, (x - high.astype(F32)).astype(BF16)


def pick(selector, x):
    nt = (((1,), (1,)), ((), ()))
    a = x.astype(BF16)
    rest = x - a.astype(F32)
    b = rest.astype(BF16)
    c = (rest - b.astype(F32)).astype(BF16)
    out = lax.dot_general(selector, c, nt, preferred_element_type=F32)
    out = out + lax.dot_general(selector, b, nt, preferred_element_type=F32)
    return out + lax.dot_general(selector, a, nt, preferred_element_type=F32)


class Sizes:
    def __init__(self, z, y, x):
        self.z, self.y, self.x = z, y, x
        self.z_routes = swap(z, 1) if z.count <= 2 else both_ways(z, 1)
        self.z2_routes = [] if z.count <= 2 else swap(z, 2) if z.count <= 4 else both_ways(z, 2)
        self.y_routes = folded(y, x.name, (x.name, y.name))
        self.y2_routes = swap(y, 2)
        self.x_routes = folded(x, z.name, (x.name, z.name))
        self.z_fine = RADIUS * y.fine
        self.z_rows = up8(self.z_fine + SPAN * y.mid_all)
        self.z2_rows = up8(z.second * y.mid_all)
        self.fine_planes = z.fine + RADIUS * len(self.z_routes)
        self.sum_planes = z.mid_all + SPAN * len(self.z_routes) + z.second * len(self.z2_routes)
        self.y_fine = RADIUS * self.fine_planes
        self.y_rows = up8(self.y_fine + SPAN * self.sum_planes)
        self.y2_rows = up8(y.second * self.sum_planes)
        self.fine_rows = y.fine + 2 * RADIUS
        self.low = up8(y.mid_all)
        self.high = self.low + up8(SPAN)
        self.far = self.high + up8(SPAN)
        self.sum_rows = -(-(self.far + y.second) // 16) * 16
        self.x_sends = RADIUS + EDGE + SPAN
        cells = max(self.fine_planes * self.fine_rows, self.sum_planes * self.sum_rows)
        self.x_cells = -(-cells // 128) * 128
        assert x.mid_all + x.coarse_all <= x.fine and self.x_sends <= 32
        assert z.coarse >= RADIUS and y.coarse >= RADIUS and y.count == 4


def restrict_kernel(s, nz, charges, own, *rest):
    messages, (wide, mid, high, coarse) = rest[:-4], rest[-4:]
    z, y, x = s.z, s.y, s.x
    lanes = (x.fine, x.fine)
    cell, lane = iota(lanes, 0), iota(lanes, 1)
    k = lane - 1
    to_mid = jnp.where((lane < x.mid_all) & x.holds_mid(k), weight_of(cell - 2 * k), 0.0)
    c = lane - x.mid_all - 2
    inside = (lane >= x.mid_all) & (lane < x.mid_all + x.coarse_all) & x.holds_coarse(c)
    to_coarse = jnp.where(inside, weight_of(cell - 1 - 2 * c), 0.0)
    narrow = to_mid + jnp.dot(to_mid, to_coarse, precision=EXACT, preferred_element_type=F32)
    grid = charges[...]
    reduced = jnp.dot(grid.reshape(z.fine * y.fine, x.fine), narrow, precision=EXACT, preferred_element_type=F32)
    wide[...] = jnp.zeros(wide.shape, F32)
    wide[:, 8 : 8 + y.fine, :] = reduced.reshape(z.fine, y.fine, x.fine)
    rows = 0.0
    for offset, weight in WEIGHTS:
        rows = rows + weight * wide[:, pl.ds(6 + offset, y.mid_all, stride=2), :]
    keep = y.holds_mid(iota((y.mid_all, x.fine), 0) - 1)
    mid[...] = jnp.zeros(mid.shape, F32)
    coarse[...] = jnp.zeros(coarse.shape, F32)
    high[...] = jnp.zeros(high.shape, F32)
    for p in range(z.mid_all):
        total = 0.0
        for offset, weight in WEIGHTS:
            at = 2 * (p - 1) + offset
            if 0 <= at < z.fine:
                total = total + weight * rows[at]
        total = jnp.where(keep & z.holds_mid(p - 1), total, 0.0)
        mid[p, : y.mid_all] = total
        high[p, 8 : 8 + y.mid_all] = total
    rows = 0.0
    for offset, weight in WEIGHTS:
        rows = rows + weight * high[:, pl.ds(5 + offset, y.coarse_all, stride=2), :]
    keep = y.holds_coarse(iota((y.coarse_all, x.fine), 0) - 2)
    for p in range(z.coarse_all):
        total = 0.0
        for offset, weight in WEIGHTS:
            at = 2 * (p - 2) + offset + 1
            if 0 <= at < z.mid_all:
                total = total + weight * rows[at]
        coarse[p, : y.coarse_all] = jnp.where(keep & z.holds_coarse(p - 2), total, 0.0)
    is_mid = iota(mid.shape[1:], 1) < x.mid_all
    for p in range(z.mid_all):
        own[p] = jnp.where(is_mid, mid[p], coarse[p]) if p < z.coarse_all else jnp.where(is_mid, mid[p], 0.0)
    for message, route in zip(messages, s.z_routes):
        up = route.up().astype(jnp.int32)
        message[: s.z_fine] = charges[pl.ds(up * (z.fine - RADIUS), RADIUS)].reshape(s.z_fine, x.fine)
        for p in range(SPAN):
            plane = jnp.where(is_mid, mid[up * (z.mid_all - SPAN) + p], coarse[up * (z.coarse_all - SPAN) + p])
            at = s.z_fine + p * y.mid_all
            message[at : at + y.mid_all] = plane[: y.mid_all]
        filled = s.z_fine + SPAN * y.mid_all
        if filled < s.z_rows:
            message[filled:] = jnp.zeros((s.z_rows - filled, x.fine), F32)
    for message, route in zip(messages[nz:], s.z2_routes):
        up = route.up().astype(jnp.int32)
        message[...] = jnp.zeros(message.shape, F32)
        for p in range(z.second):
            plane = jnp.where(is_mid, 0.0, coarse[up * (z.coarse_all - z.second) + p])
            message[p * y.mid_all : (p + 1) * y.mid_all] = plane[: y.mid_all]


def slabs(s, z_messages, z2_messages):
    out = []
    for message in z_messages:
        out += [(message, s.z_fine + p * s.y.mid_all) for p in range(SPAN)]
    for message in z2_messages:
        out += [(message, p * s.y.mid_all) for p in range(s.z.second)]
    return out


def spread_kernel(s, nz, nz2, charges, own, *rest):
    z_messages, z2_messages = rest[:nz], rest[nz : nz + nz2]
    messages = rest[nz + nz2 : -1]
    far = rest[-1]
    z, y, x = s.z, s.y, s.x
    is_mid = iota((SPAN, x.fine), 1) < x.mid_all
    planes = slabs(s, z_messages, z2_messages)

    def rows_of(p, first, count):
        if p < z.mid_all:
            return own[p, first : first + count]
        message, at = planes[p - z.mid_all]
        return message[at + first : at + first + count]

    for message, route in zip(messages, s.y_routes):
        up = route.up()
        message[: RADIUS * z.fine] = jnp.where(
            up, charges[:, y.fine - RADIUS :, :], charges[:, :RADIUS, :]
        ).reshape(RADIUS * z.fine, x.fine)
        at = RADIUS * z.fine
        for z_message in z_messages:
            slab = z_message[: s.z_fine].reshape(RADIUS, y.fine, x.fine)
            edge = jnp.where(up, slab[:, y.fine - RADIUS :], slab[:, :RADIUS])
            message[at : at + RADIUS * RADIUS] = edge.reshape(RADIUS * RADIUS, x.fine)
            at += RADIUS * RADIUS
        for p in range(s.sum_planes):
            last = jnp.where(
                is_mid, rows_of(p, y.mid_all - SPAN, SPAN), rows_of(p, y.coarse_all - SPAN, SPAN)
            )
            message[at : at + SPAN] = jnp.where(up, last, rows_of(p, 0, SPAN))
            at += SPAN
        if at < s.y_rows:
            message[at:] = jnp.zeros((s.y_rows - at, x.fine), F32)
    up = s.y2_routes[0].up()
    count = y.second
    for p in range(s.sum_planes):
        far[p * count : (p + 1) * count] = jnp.where(up, rows_of(p, y.coarse_all - count, count), rows_of(p, 0, count))
    if s.sum_planes * count < s.y2_rows:
        far[s.sum_planes * count :] = jnp.zeros((s.y2_rows - s.sum_planes * count, x.fine), F32)


def collect_kernel(s, nz, nz2, charges, own, *rest):
    z_messages, z2_messages = rest[:nz], rest[nz : nz + nz2]
    ahead, behind, far, fine, sums, first, second = rest[nz + nz2 :]
    z, y, x = s.z, s.y, s.x
    below = s.y_routes[0].below()
    planes = slabs(s, z_messages, z2_messages)

    def sides(start, count):
        a, b = ahead[start : start + count], behind[start : start + count]
        return jnp.where(below, a, b), jnp.where(below, b, a)

    def fine_planes(at, count, body, row):
        low, high = sides(row, RADIUS * count)
        fine[at : at + count, : y.fine] = body
        fine[at : at + count, y.fine : y.fine + RADIUS] = low.reshape(count, RADIUS, x.fine)
        fine[at : at + count, y.fine + RADIUS :] = high.reshape(count, RADIUS, x.fine)

    fine_planes(0, z.fine, charges[...], 0)
    at = z.fine
    for z_message in z_messages:
        fine_planes(at, RADIUS, z_message[: s.z_fine].reshape(RADIUS, y.fine, x.fine), RADIUS * at)
        at += RADIUS
    sums[...] = jnp.zeros(sums.shape, F32)
    for p in range(s.sum_planes):
        if p < z.mid_all:
            sums[p, : s.low] = own[p]
        else:
            message, at = planes[p - z.mid_all]
            sums[p, : y.mid_all] = message[at : at + y.mid_all]
        low, high = sides(s.y_fine + p * SPAN, SPAN)
        sums[p, s.low : s.low + SPAN] = low
        sums[p, s.high : s.high + SPAN] = high
        sums[p, s.far : s.far + y.second] = far[p * y.second : (p + 1) * y.second]
    row, lane = iota((2 * RADIUS, x.fine), 0), iota((2 * RADIUS, x.fine), 1)
    up = s.x_routes[0].up()
    is_first = row < RADIUS
    goes_up = choose(up, is_first, ~is_first)
    slot = jnp.where(is_first, row, row - RADIUS)
    wanted = jnp.where(goes_up, x.fine - RADIUS + slot, slot)
    picked = pick((lane == wanted).astype(BF16), fine[...].reshape(s.fine_planes * s.fine_rows, x.fine))
    width = EDGE + SPAN
    row, lane = iota((2 * width, x.fine), 0), iota((2 * width, x.fine), 1)
    is_first = row < width
    goes_up = choose(up, is_first, ~is_first)
    slot = jnp.where(is_first, row, row - width)
    from_mid = jnp.where(goes_up, x.mid_all - EDGE + slot, slot)
    from_coarse = slot - EDGE + jnp.where(goes_up, x.mid_all + x.coarse_all - SPAN, x.mid_all)
    wanted = jnp.where(slot < EDGE, from_mid, from_coarse)
    picked_sums = pick((lane == wanted).astype(BF16), sums[...].reshape(s.sum_planes * s.sum_rows, x.fine))
    for n, message in enumerate((first, second)):
        cells = s.fine_planes * s.fine_rows
        message[:RADIUS, :cells] = picked[n * RADIUS : (n + 1) * RADIUS]
        if cells < s.x_cells:
            message[:RADIUS, cells:] = jnp.zeros((RADIUS, s.x_cells - cells), F32)
        cells = s.sum_planes * s.sum_rows
        message[RADIUS:, :cells] = picked_sums[n * width : (n + 1) * width]
        if cells < s.x_cells:
            message[RADIUS:, cells:] = jnp.zeros((width, s.x_cells - cells), F32)


def band(taps, level, offset, valid):
    at = jnp.where(valid, offset + RADIUS, -1)
    out = [jnp.zeros(at.shape, F32) for _ in range(TERMS)]
    for tap in range(TAPS):
        here = at == tap
        out = [jnp.where(here, taps[level, term, tap], total) for term, total in enumerate(out)]
    return out


def dot(a, b):
    return jnp.dot(a, b, precision=EXACT, preferred_element_type=F32)


def operator_kernel(s, taps, x_fine, x_sums, y_fine, y_mid, y_coarse):
    y, x = s.y, s.x
    own, edge = x.fine, 2 * 32
    shape = (own + edge, x.fine)
    row, lane = iota(shape, 0), iota(shape, 1)
    t = row - own
    lower, higher = x.index() > 0, x.index() < x.count - 1
    is_own = row < own
    is_low = ~is_own & (t < 32)
    q = jnp.where(is_low, t, t - 32)
    side = choose(is_low, lower, higher)

    def place(own_place, own_valid, first, count, low_place, high_place):
        r = q - first
        there = (r >= 0) & (r < count) & side
        valid = choose(is_own, own_valid, there)
        return jnp.where(is_own, own_place, jnp.where(is_low, low_place + r, high_place + r)), valid

    where, valid = place(row, row >= 0, 0, RADIUS, -RADIUS, x.fine)
    fine = band(taps, 0, where - lane, valid)
    where, valid = place(row - 1, row < x.mid_all, RADIUS, EDGE, 2 - EDGE, x.mid - 1)
    mid = band(taps, 1, where - (lane - 1), valid & (lane < x.mid_all))
    first = x.mid_all
    where, valid = place(
        row - first - 2, (row >= first) & (row < first + x.coarse_all), RADIUS + EDGE, SPAN, 3 - SPAN, x.coarse - 2
    )
    coarse = band(taps, 2, where - (lane - 2), valid & (lane < x.coarse_all))
    a, b = iota((x.fine, x.fine), 0), iota((x.fine, x.fine), 1)
    from_mid = jnp.where((a < x.mid_all) & x.holds_mid(a - 1), weight_of(b - 2 * (a - 1)), 0.0)
    from_coarse = jnp.where((a < x.coarse_all) & x.holds_coarse(a - 2), weight_of(b - 1 - 2 * (a - 2)), 0.0)
    from_coarse = dot(from_coarse, from_mid)
    columns = [(x_fine, 0, fine)]
    columns += [(x_sums, 0, [dot(m, from_mid) for m in mid])]
    columns += [(x_sums, TERMS * x.fine, [dot(c, from_coarse) for c in coarse])]
    for out, at, terms in columns:
        for term, matrix in enumerate(terms):
            high, low = split(matrix)
            cols = slice(at + term * x.fine, at + (term + 1) * x.fine)
            out[0:own, cols] = high[:own]
            out[own : 2 * own, cols] = high[:own]
            out[2 * own : 3 * own, cols] = low[:own]
            out[3 * own : 3 * own + edge, cols] = high[own:]
            out[3 * own + edge : 3 * own + 2 * edge, cols] = high[own:]
            out[3 * own + 2 * edge : 3 * own + 3 * edge, cols] = low[own:]
            out[3 * own + 3 * edge :, cols] = jnp.zeros((edge, x.fine), BF16)

    lower, higher = y.index() > 0, y.index() < y.count - 1
    far_below = s.y2_routes[0].below()
    n = up8(y.mid_all)

    def write(out, size, terms):
        part = iota((y.fine, 3 * size), 1) >= 2 * size
        for term, matrix in enumerate(terms):
            high, low = split(matrix)
            out[term * y.fine : (term + 1) * y.fine] = jnp.where(part, low.astype(F32), high.astype(F32)).astype(BF16)

    def columns_of(rows, size):
        lane = iota((rows, 3 * size), 1)
        return jnp.where(lane >= 2 * size, lane - 2 * size, jnp.where(lane >= size, lane - size, lane))

    c = columns_of(y.fine, s.fine_rows)
    is_low = (c >= y.fine) & (c < y.fine + RADIUS)
    is_high = c >= y.fine + RADIUS
    where = jnp.where(is_low, c - y.fine - RADIUS, jnp.where(is_high, c - RADIUS, c))
    valid = choose(is_low, lower, choose(is_high, higher, c >= 0))
    write(y_fine, s.fine_rows, band(taps, 0, where - iota(c.shape, 0), valid))

    c = columns_of(n, s.sum_rows)
    r = iota(c.shape, 0)
    is_low = (c >= s.low) & (c < s.low + SPAN)
    is_high = (c >= s.high) & (c < s.high + SPAN)
    is_far = (c >= s.far) & (c < s.far + y.second)
    where = jnp.where(is_low, c - s.low + 2 - SPAN, jnp.where(is_high, c - s.high + y.mid - 1, c - 1))
    valid = choose(is_low, lower, choose(is_high, higher, c < y.mid_all))
    mid = band(taps, 1, where - (r - 1), valid & (r < y.mid_all))
    far = jnp.where(far_below, -2 - y.coarse, 2 * y.coarse - 2)
    where = jnp.where(is_low, c - s.low + 3 - SPAN, jnp.where(is_high, c - s.high + y.coarse - 2, c - 2))
    where = jnp.where(is_far, c - s.far + far, where)
    valid = choose(is_low, lower, choose(is_high, higher, (c < y.coarse_all) | is_far))
    coarse = band(taps, 2, where - (r - 2), valid & (r < y.coarse_all))
    o, k = iota((y.fine, n), 0), iota((y.fine, n), 1)
    from_mid = jnp.where((k < y.mid_all) & y.holds_mid(k - 1), weight_of(o - 2 * (k - 1)), 0.0)
    o, k = iota((n, n), 0), iota((n, n), 1)
    from_coarse = jnp.where((k < y.coarse_all) & y.holds_coarse(k - 2), weight_of(o - 1 - 2 * (k - 2)), 0.0)
    from_coarse = dot(from_mid, from_coarse)
    write(y_mid, s.sum_rows, [dot(from_mid, m) for m in mid])
    write(y_coarse, s.sum_rows, [dot(from_coarse, m) for m in coarse])


def sum_kernel(s, taps, fine, sums, first, second, x_fine, x_sums, y_fine, y_mid, y_coarse, out, *scratch):
    turned, t_fine, t_mid, t_coarse, p_mid, p_coarse = scratch
    z, y, x = s.z, s.y, s.x
    below = s.x_routes[0].below()
    low = jnp.where(below, first[...], second[...])
    high = jnp.where(below, second[...], first[...])
    turned[...] = jnp.concatenate([low, high, low, high], axis=0).T

    def along_x(grid, start, rows, weights):
        edge = turned[start : start + rows]
        edge_high, edge_low = split(edge)
        lane = iota(edge.shape, 1) < 64
        packed = jnp.where(lane, edge_high.astype(F32), edge_low.astype(F32)).astype(BF16)
        grid_high, grid_low = split(grid)
        joined = jnp.concatenate([grid_high, grid_low, grid_high, packed, edge_high], axis=1)
        return split(jnp.dot(joined, weights[...], preferred_element_type=F32))

    def along_y(high, low, weights):
        joined = jnp.concatenate([high, low, high], axis=0)
        result = jnp.dot(weights[...], joined, preferred_element_type=F32)
        return [result[t * y.fine : (t + 1) * y.fine, t * x.fine : (t + 1) * x.fine] for t in range(TERMS)]

    def starts(routes, below_at, above_at, cut, steps):
        result = []
        for route in routes:
            lower = route.below()
            i = cut.index()
            valid = choose(lower, i - steps >= 0, i + steps < cut.count)
            result.append((jnp.where(lower, below_at, above_at), valid))
        return result

    t_fine[...] = jnp.zeros(t_fine.shape, F32)
    t_mid[...] = jnp.zeros(t_mid.shape, F32)
    t_coarse[...] = jnp.zeros(t_coarse.shape, F32)
    group = 8
    fine_at = [(RADIUS + p, None) for p in range(z.fine)]
    for start, valid in starts(s.z_routes, 0, z.fine + RADIUS, z, 1):
        fine_at += [(start + p, valid) for p in range(RADIUS)]
    for g in range(0, s.fine_planes, group):
        n = s.fine_rows
        grid = fine[g : g + group].reshape(group * n, x.fine)
        a, b = along_x(grid, g * n, group * n, x_fine)
        for p in range(group):
            at, valid = fine_at[g + p]
            for t, part in enumerate(along_y(a[p * n : (p + 1) * n], b[p * n : (p + 1) * n], y_fine)):
                t_fine[at, t] = part if valid is None else jnp.where(valid, part, 0.0)

    mid_at = [(SPAN - 3 + p, None) for p in range(z.mid_all)]
    coarse_at = [(SPAN - 5 + p if p < z.coarse_all else None, None) for p in range(z.mid_all)]
    for start, valid in starts(s.z_routes, 0, z.mid + SPAN - 3, z, 1):
        mid_at += [(start + p, valid) for p in range(SPAN)]
    for start, valid in starts(s.z_routes, 0, z.coarse + SPAN - 5, z, 1):
        coarse_at += [(start + p, valid) for p in range(SPAN)]
    for start, valid in starts(s.z2_routes, SPAN - 5 - z.coarse, 2 * z.coarse + SPAN - 5, z, 2):
        mid_at += [(None, None)] * z.second
        coarse_at += [(start + p, valid) for p in range(z.second)]
    group = 4
    for g in range(0, s.sum_planes, group):
        n = s.sum_rows
        count = min(group, s.sum_planes - g)
        grid = sums[g : g + count].reshape(count * n, x.fine)
        a, b = along_x(grid, g * n, count * n, x_sums)
        for p in range(count):
            rows = slice(p * n, (p + 1) * n)
            for which, (held, weights) in enumerate(((t_mid, y_mid), (t_coarse, y_coarse))):
                at, valid = (mid_at, coarse_at)[which][g + p]
                if at is None:
                    continue
                cols = slice(which * TERMS * x.fine, (which + 1) * TERMS * x.fine)
                for t, part in enumerate(along_y(a[rows, cols], b[rows, cols], weights)):
                    if valid is None:
                        held[at, t] = part
                    else:
                        held[at, t] = held[at, t] + jnp.where(valid, part, 0.0)

    def along_z(held, level, base, count):
        totals = [None] * count
        for t in range(TERMS):
            for j in range(count + TAPS - 1):
                plane = held[base + j, t]
                for i in range(max(0, j - TAPS + 1), min(count, j + 1)):
                    term = taps[level, t, j - i] * plane
                    totals[i] = term if totals[i] is None else totals[i] + term
        return totals

    block = 4
    for k in range(0, z.coarse_all, block):
        count = min(block, z.coarse_all - k)
        for i, total in enumerate(along_z(t_coarse, 2, k, count)):
            p_coarse[k + i] = jnp.where(z.holds_coarse(k + i - 2), total, 0.0)
    for k in range(0, z.mid_all, block):
        count = min(block, z.mid_all - k)
        for i, total in enumerate(along_z(t_mid, 1, k + SPAN - 11, count)):
            m = k + i - 1
            for offset, weight in WEIGHTS:
                if (m - offset) % 2 == 0 and 0 <= (m - offset) // 2 + 2 < z.coarse_all:
                    total = total + weight * p_coarse[(m - offset) // 2 + 2]
            p_mid[k + i] = jnp.where(z.holds_mid(m), total, 0.0)

    def step(b, carry):
        for i, total in enumerate(along_z(t_fine, 0, b * block, block)):
            for offset, weight in WEIGHTS:
                if (i - offset) % 2 == 0:
                    total = total + weight * p_mid[b * (block // 2) + (i - offset) // 2 + 1]
            out[b * block + i] = total
        return carry

    lax.fori_loop(0, z.fine // block, step, 0)


def call(kernel, outs, ins, scratch=(), flops=10**7):
    specs = [SMEM if a.ndim == 3 and a.shape[-1] == TAPS else VMEM for a in ins]
    size = sum(a.size * a.dtype.itemsize for a in ins) + sum(o.size * o.dtype.itemsize for o in outs)
    return pl.pallas_call(
        kernel,
        out_shape=tuple(outs),
        in_specs=specs,
        out_specs=tuple(VMEM for _ in outs),
        scratch_shapes=list(scratch),
        compiler_params=PARAMS,
        cost_estimate=pl.CostEstimate(flops=flops, bytes_accessed=size, transcendentals=0),
    )(*ins)


def array(*shape, dtype=F32):
    return jax.ShapeDtypeStruct(shape, dtype)


def local(charges, kernel_taps):
    z, y, x = (Cut(name, size) for name, size in zip(("gz", "gy", "gx"), charges.shape))
    s = Sizes(z, y, x)
    n = x.fine
    nz, nz2 = len(s.z_routes), len(s.z2_routes)

    def bound(kernel, *static):
        return lambda *refs: kernel(s, *static, *refs)

    rows = up8(y.mid_all)
    own, *messages = call(
        bound(restrict_kernel, nz),
        [array(z.mid_all, rows, n)] + [array(s.z_rows, n)] * nz + [array(s.z2_rows, n)] * nz2,
        [charges],
        [
            pltpu.VMEM((z.fine, y.fine + 16, n), F32),
            pltpu.VMEM((z.mid_all, rows, n), F32),
            pltpu.VMEM((z.mid_all, up8(y.mid + 24), n), F32),
            pltpu.VMEM((z.mid_all, rows, n), F32),
        ],
    )
    z_got = [route(m) for route, m in zip(s.z_routes + s.z2_routes, messages)]
    operators = call(
        bound(operator_kernel),
        [
            array(5 * n, TERMS * n, dtype=BF16),
            array(5 * n, 2 * TERMS * n, dtype=BF16),
            array(TERMS * y.fine, 3 * s.fine_rows, dtype=BF16),
            array(TERMS * y.fine, 3 * s.sum_rows, dtype=BF16),
            array(TERMS * y.fine, 3 * s.sum_rows, dtype=BF16),
        ],
        [kernel_taps],
    )
    ahead, behind, far = call(
        bound(spread_kernel, nz, nz2),
        [array(s.y_rows, n), array(s.y_rows, n), array(s.y2_rows, n)],
        [charges, own, *z_got],
    )
    ahead, behind = s.y_routes[0](ahead), s.y_routes[1](behind)
    far = s.y2_routes[0](far)
    fine, sums, first, second = call(
        bound(collect_kernel, nz, nz2),
        [
            array(s.fine_planes, s.fine_rows, n),
            array(s.sum_planes, s.sum_rows, n),
            array(s.x_sends, s.x_cells),
            array(s.x_sends, s.x_cells),
        ],
        [charges, own, *z_got, ahead, behind, far],
    )
    first, second = s.x_routes[0](first), s.x_routes[1](second)
    (out,) = call(
        bound(sum_kernel),
        [array(z.fine, y.fine, n)],
        [kernel_taps, fine, sums, first, second, *operators],
        [
            pltpu.VMEM((s.x_cells, n), F32),
            pltpu.VMEM((z.fine + 2 * RADIUS, TERMS, y.fine, n), F32),
            pltpu.VMEM((z.mid + 2 * SPAN - 3, TERMS, y.fine, n), F32),
            pltpu.VMEM((2 * z.coarse + SPAN, TERMS, y.fine, n), F32),
            pltpu.VMEM((z.mid_all, y.fine, n), F32),
            pltpu.VMEM((z.coarse_all, y.fine, n), F32),
        ],
    )
    return out


def solution(mesh):
    return jax.shard_map(
        local,
        mesh=mesh,
        in_specs=(P("gz", "gy", "gx"), P()),
        out_specs=P("gz", "gy", "gx"),
        check_vma=False,
    )
```

```python
import jax
import jax.numpy as jnp
from jax import lax
from jax.experimental import pallas as pl
from jax.experimental.pallas import tpu as pltpu
from jax.sharding import PartitionSpec as P

RADIUS = 8
TAPS = 17
TERMS = 2
WEIGHTS = ((-3, -0.0625), (-1, 0.5625), (0, 1.0), (1, 0.5625), (3, -0.0625))
EXACT = lax.Precision.HIGHEST
SPAN = RADIUS + 5
EDGE = RADIUS + 3
F32, BF16 = jnp.float32, jnp.bfloat16
PARAMS = pltpu.CompilerParams(vmem_limit_bytes=32 * 1024 * 1024)
VMEM = pl.BlockSpec(memory_space=pltpu.VMEM)
SMEM = pl.BlockSpec(memory_space=pltpu.SMEM)


def up8(n):
    return -(-n // 8) * 8


def iota(shape, dim):
    return lax.broadcasted_iota(jnp.int32, shape, dim)


def weight_of(difference):
    size = jnp.abs(difference)
    out = jnp.where(size == 1, 0.5625, jnp.where(size == 3, -0.0625, 0.0))
    return jnp.where(size == 0, 1.0, out)


def choose(condition, a, b):
    return jnp.where(condition, jnp.where(a, 1, 0), jnp.where(b, 1, 0)) != 0


class Cut:
    def __init__(self, name, length):
        self.name, self.fine = name, length
        self.count = lax.axis_size(name)
        self.mid, self.coarse = length // 2, length // 4
        self.mid_all, self.coarse_all = self.mid + 3, self.coarse + 5
        self.second = max(SPAN - self.coarse, 0)

    def index(self):
        return lax.axis_index(self.name)

    def holds_mid(self, k):
        k = k + self.index() * self.mid
        return (k >= 0) & (k < self.mid * self.count)

    def holds_coarse(self, k):
        k = k + self.index() * self.coarse
        return (k >= 0) & (k < self.coarse * self.count)


class Route:
    def __init__(self, names, pairs, up, below):
        self.names, self.pairs, self.up, self.below = names, pairs, up, below

    def __call__(self, x):
        return lax.ppermute(x, self.names, self.pairs)


def flip(pairs):
    return [(b, a) for a, b in pairs]


def swap(cut, steps):
    pairs = [(i, i + steps) for i in range(cut.count - steps)]

    def up():
        return cut.index() + steps < cut.count

    return [Route(cut.name, pairs + flip(pairs), up, lambda: ~up())]


def both_ways(cut, steps):
    pairs = [(i, i + steps) for i in range(cut.count - steps)]
    yes, no = (lambda: cut.index() >= 0), (lambda: cut.index() < 0)
    return [Route(cut.name, pairs, yes, yes), Route(cut.name, flip(pairs), no, no)]


def folded(cut, beside, names):
    n, m = cut.count, lax.axis_size(beside)

    def place(c, i):
        return c * n + i if names[0] == beside else i * m + c

    pairs = []
    for c in range(0, m, 2):
        cycle = [place(c, i) for i in range(n)] + [place(c + 1, i) for i in reversed(range(n))]
        pairs += list(zip(cycle, cycle[1:] + cycle[:1]))

    def even():
        return lax.axis_index(beside) % 2 == 0

    def odd():
        return lax.axis_index(beside) % 2 == 1

    return [Route(names, pairs, even, even), Route(names, flip(pairs), odd, odd)]


def split(x):
    high = x.astype(BF16)
    return high, (x - high.astype(F32)).astype(BF16)


def pick(selector, x):
    nt = (((1,), (1,)), ((), ()))
    a = x.astype(BF16)
    rest = x - a.astype(F32)
    b = rest.astype(BF16)
    c = (rest - b.astype(F32)).astype(BF16)
    out = lax.dot_general(selector, c, nt, preferred_element_type=F32)
    out = out + lax.dot_general(selector, b, nt, preferred_element_type=F32)
    return out + lax.dot_general(selector, a, nt, preferred_element_type=F32)


class Sizes:
    def __init__(self, z, y, x):
        self.z, self.y, self.x = z, y, x
        self.z_routes = swap(z, 1) if z.count <= 2 else both_ways(z, 1)
        self.z2_routes = [] if z.count <= 2 else swap(z, 2) if z.count <= 4 else both_ways(z, 2)
        self.y_routes = folded(y, x.name, (x.name, y.name))
        self.y2_routes = swap(y, 2)
        self.x_routes = folded(x, z.name, (x.name, z.name))
        self.z_fine = RADIUS * y.fine
        self.z_rows = up8(self.z_fine + SPAN * y.mid_all)
        self.z2_rows = up8(z.second * y.mid_all)
        self.slab_planes = SPAN * len(self.z_routes) + z.second * len(self.z2_routes)
        self.fine_planes = z.fine + RADIUS * len(self.z_routes)
        self.sum_planes = z.mid_all + RADIUS * len(self.z_routes)
        self.y_fine = RADIUS * z.fine
        self.y_rows = up8(self.y_fine + SPAN * z.mid_all)
        self.slab_fine = RADIUS * RADIUS * len(self.z_routes)
        self.slab_rows = up8(self.slab_fine + SPAN * self.slab_planes)
        self.far_rows = up8(y.second * (z.coarse_all + self.slab_planes))
        self.fine_rows = y.fine + 2 * RADIUS
        self.far = y.coarse_all
        self.low = y.mid_all
        self.high = self.low + SPAN
        self.sum_rows = -(-(self.high + SPAN) // 16) * 16
        self.x_sends = RADIUS + EDGE + SPAN
        cells = max(self.fine_planes * self.fine_rows, self.sum_planes * self.sum_rows)
        self.x_cells = -(-cells // 128) * 128
        assert x.mid_all + x.coarse_all <= x.fine and self.x_sends <= 32
        assert self.far + y.second <= self.low
        assert z.coarse >= RADIUS and y.coarse >= RADIUS and y.count == 4


def restrict_kernel(s, nz, charges, held, own, ahead, behind, *rest):
    messages, (wide, mid, high, coarse) = rest[:-4], rest[-4:]
    z, y, x = s.z, s.y, s.x
    lanes = (x.fine, x.fine)
    cell, lane = iota(lanes, 0), iota(lanes, 1)
    k = lane - 1
    to_mid = jnp.where((lane < x.mid_all) & x.holds_mid(k), weight_of(cell - 2 * k), 0.0)
    c = lane - x.mid_all - 2
    inside = (lane >= x.mid_all) & (lane < x.mid_all + x.coarse_all) & x.holds_coarse(c)
    to_coarse = jnp.where(inside, weight_of(cell - 1 - 2 * c), 0.0)
    narrow = to_mid + jnp.dot(to_mid, to_coarse, precision=EXACT, preferred_element_type=F32)
    grid = charges[...]
    held[...] = grid
    reduced = jnp.dot(grid.reshape(z.fine * y.fine, x.fine), narrow, precision=EXACT, preferred_element_type=F32)
    wide[...] = jnp.zeros(wide.shape, F32)
    wide[:, 8 : 8 + y.fine, :] = reduced.reshape(z.fine, y.fine, x.fine)
    rows = 0.0
    for offset, weight in WEIGHTS:
        rows = rows + weight * wide[:, pl.ds(6 + offset, y.mid_all, stride=2), :]
    keep = y.holds_mid(iota((y.mid_all, x.fine), 0) - 1)
    mid[...] = jnp.zeros(mid.shape, F32)
    coarse[...] = jnp.zeros(coarse.shape, F32)
    high[...] = jnp.zeros(high.shape, F32)
    for p in range(z.mid_all):
        total = 0.0
        for offset, weight in WEIGHTS:
            at = 2 * (p - 1) + offset
            if 0 <= at < z.fine:
                total = total + weight * rows[at]
        total = jnp.where(keep & z.holds_mid(p - 1), total, 0.0)
        mid[p, : y.mid_all] = total
        high[p, 8 : 8 + y.mid_all] = total
    rows = 0.0
    for offset, weight in WEIGHTS:
        rows = rows + weight * high[:, pl.ds(5 + offset, y.coarse_all, stride=2), :]
    keep = y.holds_coarse(iota((y.coarse_all, x.fine), 0) - 2)
    for p in range(z.coarse_all):
        total = 0.0
        for offset, weight in WEIGHTS:
            at = 2 * (p - 2) + offset + 1
            if 0 <= at < z.mid_all:
                total = total + weight * rows[at]
        coarse[p, : y.coarse_all] = jnp.where(keep & z.holds_coarse(p - 2), total, 0.0)
    is_mid = iota(mid.shape[1:], 1) < x.mid_all
    for p in range(z.mid_all):
        own[p] = jnp.where(is_mid, mid[p], coarse[p]) if p < z.coarse_all else jnp.where(is_mid, mid[p], 0.0)
    is_side = iota((SPAN, x.fine), 1) < x.mid_all
    for message, route in zip((ahead, behind), s.y_routes):
        up = route.up()
        edge = jnp.where(up, charges[:, y.fine - RADIUS :, :], charges[:, :RADIUS, :])
        message[: s.y_fine] = edge.reshape(s.y_fine, x.fine)
        for p in range(z.mid_all):
            last = jnp.where(is_side, own[p, y.mid_all - SPAN : y.mid_all], own[p, y.coarse_all - SPAN : y.coarse_all])
            at = s.y_fine + p * SPAN
            message[at : at + SPAN] = jnp.where(up, last, own[p, :SPAN])
        filled = s.y_fine + SPAN * z.mid_all
        if filled < s.y_rows:
            message[filled:] = jnp.zeros((s.y_rows - filled, x.fine), F32)
    for message, route in zip(messages, s.z_routes):
        up = route.up().astype(jnp.int32)
        message[: s.z_fine] = charges[pl.ds(up * (z.fine - RADIUS), RADIUS)].reshape(s.z_fine, x.fine)
        for p in range(SPAN):
            plane = jnp.where(is_mid, mid[up * (z.mid_all - SPAN) + p], coarse[up * (z.coarse_all - SPAN) + p])
            at = s.z_fine + p * y.mid_all
            message[at : at + y.mid_all] = plane[: y.mid_all]
        filled = s.z_fine + SPAN * y.mid_all
        if filled < s.z_rows:
            message[filled:] = jnp.zeros((s.z_rows - filled, x.fine), F32)
    for message, route in zip(messages[nz:], s.z2_routes):
        up = route.up().astype(jnp.int32)
        message[...] = jnp.zeros(message.shape, F32)
        for p in range(z.second):
            plane = jnp.where(is_mid, 0.0, coarse[up * (z.coarse_all - z.second) + p])
            message[p * y.mid_all : (p + 1) * y.mid_all] = plane[: y.mid_all]


def slabs(s, z_messages, z2_messages):
    out = []
    for message in z_messages:
        out += [(message, s.z_fine + p * s.y.mid_all) for p in range(SPAN)]
    for message in z2_messages:
        out += [(message, p * s.y.mid_all) for p in range(s.z.second)]
    return out


def spread_kernel(s, nz, nz2, _, own, *rest):
    z_messages, z2_messages = rest[:nz], rest[nz : nz + nz2]
    ahead, behind, far = rest[-3:]
    z, y, x = s.z, s.y, s.x
    is_mid = iota((SPAN, x.fine), 1) < x.mid_all
    planes = slabs(s, z_messages, z2_messages)
    for message, route in zip((ahead, behind), s.y_routes):
        up = route.up()
        at = 0
        for z_message in z_messages:
            slab = z_message[: s.z_fine].reshape(RADIUS, y.fine, x.fine)
            edge = jnp.where(up, slab[:, y.fine - RADIUS :], slab[:, :RADIUS])
            message[at : at + RADIUS * RADIUS] = edge.reshape(RADIUS * RADIUS, x.fine)
            at += RADIUS * RADIUS
        for held, first in planes:
            top, end = held[first + y.mid_all - SPAN : first + y.mid_all], first + y.coarse_all
            last = jnp.where(is_mid, top, held[end - SPAN : end])
            message[at : at + SPAN] = jnp.where(up, last, held[first : first + SPAN])
            at += SPAN
        if at < s.slab_rows:
            message[at:] = jnp.zeros((s.slab_rows - at, x.fine), F32)
    up = s.y2_routes[0].up()
    count, end = y.second, y.coarse_all
    at = 0
    for p in range(z.coarse_all):
        far[at : at + count] = jnp.where(up, own[p, end - count : end], own[p, :count])
        at += count
    for held, first in planes:
        far[at : at + count] = jnp.where(up, held[first + end - count : first + end], held[first : first + count])
        at += count
    if at < s.far_rows:
        far[at:] = jnp.zeros((s.far_rows - at, x.fine), F32)


def collect_kernel(s, nz, nz2, charges, own, *rest):
    z_messages, z2_messages = rest[:nz], rest[nz : nz + nz2]
    pairs = rest[nz + nz2 : nz + nz2 + 4]
    far, fine, sums, first, second, raw = rest[nz + nz2 + 4 :]
    z, y, x = s.z, s.y, s.x
    below = s.y_routes[0].below()
    planes = slabs(s, z_messages, z2_messages)

    def sides(which, start, count):
        a, b = (message[start : start + count] for message in pairs[2 * which : 2 * which + 2])
        return jnp.where(below, a, b), jnp.where(below, b, a)

    def fine_planes(at, count, body, which, row):
        low, high = sides(which, row, RADIUS * count)
        fine[at : at + count, : y.fine] = body
        fine[at : at + count, y.fine : y.fine + RADIUS] = low.reshape(count, RADIUS, x.fine)
        fine[at : at + count, y.fine + RADIUS :] = high.reshape(count, RADIUS, x.fine)

    fine_planes(0, z.fine, charges[...], 0, 0)
    at = z.fine
    for n, z_message in enumerate(z_messages):
        slab = z_message[: s.z_fine].reshape(RADIUS, y.fine, x.fine)
        fine_planes(at, RADIUS, slab, 1, n * RADIUS * RADIUS)
        at += RADIUS
    sums[...] = jnp.zeros(sums.shape, F32)
    raw[...] = jnp.zeros(raw.shape, F32)
    is_mid = iota((y.second, x.fine), 1) < x.mid_all

    def rows_of_plane(out, p, body, which, row, far_row):
        low, high = sides(which, row, SPAN)
        out[p, : y.mid_all] = body
        out[p, s.low : s.low + SPAN] = low
        out[p, s.high : s.high + SPAN] = high
        if far_row is not None:
            at = slice(s.far, s.far + y.second)
            out[p, at] = jnp.where(is_mid, out[p, at], far[far_row : far_row + y.second])

    for p in range(z.mid_all):
        far_row = p * y.second if p < z.coarse_all else None
        rows_of_plane(sums, p, own[p, : y.mid_all], 0, s.y_fine + p * SPAN, far_row)
    for p, (held, at) in enumerate(planes):
        far_row = (z.coarse_all + p) * y.second
        rows_of_plane(raw, p, held[at : at + y.mid_all], 1, s.slab_fine + p * SPAN, far_row)
    is_mid = iota((s.sum_rows, x.fine), 1) < x.mid_all

    def number(condition, a, b):
        return jnp.where(condition, a, b)

    for n, route in enumerate(s.z_routes):
        lower, base = route.below(), n * SPAN
        for j in range(RADIUS):
            a = raw[base + number(lower, SPAN - 3 - RADIUS, 3) + j]
            b = raw[base + number(lower, SPAN - 5 - RADIUS, 5) + j]
            sums[z.mid_all + n * RADIUS + j] = jnp.where(is_mid, a, b)
        for i in range(3):
            at = number(lower, 0, z.mid) + i
            sums[at] = sums[at] + jnp.where(is_mid, raw[base + number(lower, SPAN - 3, 0) + i], 0.0)
        for i in range(5):
            at = number(lower, 0, z.coarse) + i
            sums[at] = sums[at] + jnp.where(is_mid, 0.0, raw[base + number(lower, SPAN - 5, 0) + i])
    for n, route in enumerate(s.z2_routes):
        base = len(s.z_routes) * SPAN + n * z.second
        start = z.mid_all + number(route.below(), RADIUS - z.coarse, RADIUS + z.coarse - 5)
        for p in range(z.second):
            sums[start + p] = sums[start + p] + jnp.where(is_mid, 0.0, raw[base + p])

    row, lane = iota((2 * RADIUS, x.fine), 0), iota((2 * RADIUS, x.fine), 1)
    up = s.x_routes[0].up()
    is_first = row < RADIUS
    goes_up = choose(up, is_first, ~is_first)
    slot = jnp.where(is_first, row, row - RADIUS)
    wanted = jnp.where(goes_up, x.fine - RADIUS + slot, slot)
    picked = pick((lane == wanted).astype(BF16), fine[...].reshape(s.fine_planes * s.fine_rows, x.fine))
    width = EDGE + SPAN
    row, lane = iota((2 * width, x.fine), 0), iota((2 * width, x.fine), 1)
    is_first = row < width
    goes_up = choose(up, is_first, ~is_first)
    slot = jnp.where(is_first, row, row - width)
    from_mid = jnp.where(goes_up, x.mid_all - EDGE + slot, slot)
    from_coarse = slot - EDGE + jnp.where(goes_up, x.mid_all + x.coarse_all - SPAN, x.mid_all)
    wanted = jnp.where(slot < EDGE, from_mid, from_coarse)
    picked_sums = pick((lane == wanted).astype(BF16), sums[...].reshape(s.sum_planes * s.sum_rows, x.fine))
    for n, message in enumerate((first, second)):
        cells = s.fine_planes * s.fine_rows
        message[:RADIUS, :cells] = picked[n * RADIUS : (n + 1) * RADIUS]
        if cells < s.x_cells:
            message[:RADIUS, cells:] = jnp.zeros((RADIUS, s.x_cells - cells), F32)
        cells = s.sum_planes * s.sum_rows
        message[RADIUS:, :cells] = picked_sums[n * width : (n + 1) * width]
        if cells < s.x_cells:
            message[RADIUS:, cells:] = jnp.zeros((width, s.x_cells - cells), F32)


def band(taps, level, offset, valid):
    at = jnp.where(valid, offset + RADIUS, -1)
    out = [jnp.zeros(at.shape, F32) for _ in range(TERMS)]
    for tap in range(TAPS):
        here = at == tap
        out = [jnp.where(here, taps[level, term, tap], total) for term, total in enumerate(out)]
    return out


def dot(a, b):
    return jnp.dot(a, b, precision=EXACT, preferred_element_type=F32)


def operator_kernel(s, taps, x_fine, x_sums, y_fine, y_mid, y_coarse):
    y, x = s.y, s.x
    own, edge = x.fine, 2 * 32
    shape = (own + edge, x.fine)
    row, lane = iota(shape, 0), iota(shape, 1)
    t = row - own
    lower, higher = x.index() > 0, x.index() < x.count - 1
    is_own = row < own
    is_low = ~is_own & (t < 32)
    q = jnp.where(is_low, t, t - 32)
    side = choose(is_low, lower, higher)

    def place(own_place, own_valid, first, count, low_place, high_place):
        r = q - first
        there = (r >= 0) & (r < count) & side
        valid = choose(is_own, own_valid, there)
        return jnp.where(is_own, own_place, jnp.where(is_low, low_place + r, high_place + r)), valid

    where, valid = place(row, row >= 0, 0, RADIUS, -RADIUS, x.fine)
    fine = band(taps, 0, where - lane, valid)
    where, valid = place(row - 1, row < x.mid_all, RADIUS, EDGE, 2 - EDGE, x.mid - 1)
    mid = band(taps, 1, where - (lane - 1), valid & (lane < x.mid_all))
    first = x.mid_all
    where, valid = place(
        row - first - 2, (row >= first) & (row < first + x.coarse_all), RADIUS + EDGE, SPAN, 3 - SPAN, x.coarse - 2
    )
    coarse = band(taps, 2, where - (lane - 2), valid & (lane < x.coarse_all))
    a, b = iota((x.fine, x.fine), 0), iota((x.fine, x.fine), 1)
    from_mid = jnp.where((a < x.mid_all) & x.holds_mid(a - 1), weight_of(b - 2 * (a - 1)), 0.0)
    from_coarse = jnp.where((a < x.coarse_all) & x.holds_coarse(a - 2), weight_of(b - 1 - 2 * (a - 2)), 0.0)
    from_coarse = dot(from_coarse, from_mid)
    columns = [(x_fine, 0, fine)]
    columns += [(x_sums, 0, [dot(m, from_mid) for m in mid])]
    columns += [(x_sums, TERMS * x.fine, [dot(c, from_coarse) for c in coarse])]
    for out, at, terms in columns:
        for term, matrix in enumerate(terms):
            high, low = split(matrix)
            cols = slice(at + term * x.fine, at + (term + 1) * x.fine)
            out[0:own, cols] = high[:own]
            out[own : 2 * own, cols] = high[:own]
            out[2 * own : 3 * own, cols] = low[:own]
            out[3 * own : 3 * own + edge, cols] = high[own:]
            out[3 * own + edge : 3 * own + 2 * edge, cols] = high[own:]
            out[3 * own + 2 * edge : 3 * own + 3 * edge, cols] = low[own:]
            out[3 * own + 3 * edge :, cols] = jnp.zeros((edge, x.fine), BF16)

    lower, higher = y.index() > 0, y.index() < y.count - 1
    far_below = s.y2_routes[0].below()
    n = up8(y.mid_all)

    def write(out, size, terms):
        part = iota((y.fine, 3 * size), 1) >= 2 * size
        for term, matrix in enumerate(terms):
            high, low = split(matrix)
            out[term * y.fine : (term + 1) * y.fine] = jnp.where(part, low.astype(F32), high.astype(F32)).astype(BF16)

    def columns_of(rows, size):
        lane = iota((rows, 3 * size), 1)
        return jnp.where(lane >= 2 * size, lane - 2 * size, jnp.where(lane >= size, lane - size, lane))

    c = columns_of(y.fine, s.fine_rows)
    is_low = (c >= y.fine) & (c < y.fine + RADIUS)
    is_high = c >= y.fine + RADIUS
    where = jnp.where(is_low, c - y.fine - RADIUS, jnp.where(is_high, c - RADIUS, c))
    valid = choose(is_low, lower, choose(is_high, higher, c >= 0))
    write(y_fine, s.fine_rows, band(taps, 0, where - iota(c.shape, 0), valid))

    c = columns_of(n, s.sum_rows)
    r = iota(c.shape, 0)
    is_low = (c >= s.low) & (c < s.low + SPAN)
    is_high = (c >= s.high) & (c < s.high + SPAN)
    is_far = (c >= s.far) & (c < s.far + y.second)
    where = jnp.where(is_low, c - s.low + 2 - SPAN, jnp.where(is_high, c - s.high + y.mid - 1, c - 1))
    valid = choose(is_low, lower, choose(is_high, higher, c < y.mid_all))
    mid = band(taps, 1, where - (r - 1), valid & (r < y.mid_all))
    far = jnp.where(far_below, -2 - y.coarse, 2 * y.coarse - 2)
    where = jnp.where(is_low, c - s.low + 3 - SPAN, jnp.where(is_high, c - s.high + y.coarse - 2, c - 2))
    where = jnp.where(is_far, c - s.far + far, where)
    valid = choose(is_low, lower, choose(is_high, higher, (c < y.coarse_all) | is_far))
    coarse = band(taps, 2, where - (r - 2), valid & (r < y.coarse_all))
    o, k = iota((y.fine, n), 0), iota((y.fine, n), 1)
    from_mid = jnp.where((k < y.mid_all) & y.holds_mid(k - 1), weight_of(o - 2 * (k - 1)), 0.0)
    o, k = iota((n, n), 0), iota((n, n), 1)
    from_coarse = jnp.where((k < y.coarse_all) & y.holds_coarse(k - 2), weight_of(o - 1 - 2 * (k - 2)), 0.0)
    from_coarse = dot(from_mid, from_coarse)
    write(y_mid, s.sum_rows, [dot(from_mid, m) for m in mid])
    write(y_coarse, s.sum_rows, [dot(from_coarse, m) for m in coarse])


def own_kernel(s, fine, sums, x_fine, x_sums, fine_part, sums_part):
    def along_x(grid, weights):
        high, low = split(grid)
        joined = jnp.concatenate([high, low, high], axis=1)
        return jnp.dot(joined, weights[: 3 * s.x.fine], preferred_element_type=F32)

    cells = s.fine_planes * s.fine_rows
    fine_part[...] = along_x(fine[...].reshape(cells, s.x.fine), x_fine)
    cells = s.sum_planes * s.sum_rows
    sums_part[...] = along_x(sums[...].reshape(cells, s.x.fine), x_sums)


def sum_kernel(s, taps, fine, sums, first, second, x_fine, x_sums, y_fine, y_mid, y_coarse, out, *scratch):
    turned, t_fine, t_mid, t_coarse, p_mid, p_coarse = scratch
    z, y, x = s.z, s.y, s.x
    below = s.x_routes[0].below()
    low = jnp.where(below, first[...], second[...])
    high = jnp.where(below, second[...], first[...])
    turned[...] = jnp.concatenate([low, high, low, high], axis=0).T

    def along_x(held, start, rows, weights):
        edge = turned[start : start + rows]
        edge_high, edge_low = split(edge)
        lane = iota(edge.shape, 1) < 64
        packed = jnp.where(lane, edge_high.astype(F32), edge_low.astype(F32)).astype(BF16)
        joined = jnp.concatenate([packed, edge_high], axis=1)
        part = jnp.dot(joined, weights[3 * x.fine :], preferred_element_type=F32)
        return split(held[start : start + rows] + part)

    def along_y(high, low, weights):
        joined = jnp.concatenate([high, low, high], axis=0)
        result = jnp.dot(weights[...], joined, preferred_element_type=F32)
        return [result[t * y.fine : (t + 1) * y.fine, t * x.fine : (t + 1) * x.fine] for t in range(TERMS)]

    def starts(below_at, above_at):
        result = []
        for route in s.z_routes:
            lower, i = route.below(), z.index()
            valid = choose(lower, i >= 1, i + 1 < z.count)
            result.append((jnp.where(lower, below_at, above_at), valid))
        return result

    t_fine[...] = jnp.zeros(t_fine.shape, F32)
    t_mid[...] = jnp.zeros(t_mid.shape, F32)
    t_coarse[...] = jnp.zeros(t_coarse.shape, F32)

    def store(held, at, valid, parts):
        for t, part in enumerate(parts):
            held[at, t] = part if valid is None else jnp.where(valid, part, 0.0)

    mid_at = [(RADIUS + p, None) for p in range(z.mid_all)]
    coarse_at = [(RADIUS + p if p < z.coarse_all else None, None) for p in range(z.mid_all)]
    for start, valid in starts(0, z.mid + 3 + RADIUS):
        mid_at += [(start + p, valid) for p in range(RADIUS)]
    for start, valid in starts(0, z.coarse + 5 + RADIUS):
        coarse_at += [(start + p, valid) for p in range(RADIUS)]
    group = 4
    for g in range(0, s.sum_planes, group):
        n = s.sum_rows
        count = min(group, s.sum_planes - g)
        a, b = along_x(sums, g * n, count * n, x_sums)
        for p in range(count):
            rows = slice(p * n, (p + 1) * n)
            for which, (held, weights) in enumerate(((t_mid, y_mid), (t_coarse, y_coarse))):
                at, valid = (mid_at, coarse_at)[which][g + p]
                if at is not None:
                    cols = slice(which * TERMS * x.fine, (which + 1) * TERMS * x.fine)
                    store(held, at, valid, along_y(a[rows, cols], b[rows, cols], weights))

    group = 8
    fine_at = [(RADIUS + p, None) for p in range(z.fine)]
    for start, valid in starts(0, z.fine + RADIUS):
        fine_at += [(start + p, valid) for p in range(RADIUS)]
    for g in range(0, s.fine_planes, group):
        n = s.fine_rows
        a, b = along_x(fine, g * n, group * n, x_fine)
        for p in range(group):
            rows = slice(p * n, (p + 1) * n)
            store(t_fine, *fine_at[g + p], along_y(a[rows], b[rows], y_fine))

    def along_z(held, level, base, count):
        totals = [None] * count
        for t in range(TERMS):
            for j in range(count + TAPS - 1):
                plane = held[base + j, t]
                for i in range(max(0, j - TAPS + 1), min(count, j + 1)):
                    term = taps[level, t, j - i] * plane
                    totals[i] = term if totals[i] is None else totals[i] + term
        return totals

    block = 4
    for k in range(0, z.coarse_all, block):
        count = min(block, z.coarse_all - k)
        for i, total in enumerate(along_z(t_coarse, 2, k, count)):
            p_coarse[k + i] = jnp.where(z.holds_coarse(k + i - 2), total, 0.0)
    for k in range(0, z.mid_all, block):
        count = min(block, z.mid_all - k)
        for i, total in enumerate(along_z(t_mid, 1, k, count)):
            m = k + i - 1
            for offset, weight in WEIGHTS:
                if (m - offset) % 2 == 0 and 0 <= (m - offset) // 2 + 2 < z.coarse_all:
                    total = total + weight * p_coarse[(m - offset) // 2 + 2]
            p_mid[k + i] = jnp.where(z.holds_mid(m), total, 0.0)

    def step(b, carry):
        for i, total in enumerate(along_z(t_fine, 0, b * block, block)):
            for offset, weight in WEIGHTS:
                if (i - offset) % 2 == 0:
                    total = total + weight * p_mid[b * (block // 2) + (i - offset) // 2 + 1]
            out[b * block + i] = total
        return carry

    lax.fori_loop(0, z.fine // block, step, 0)


def call(kernel, outs, ins, scratch=(), flops=10**7):
    specs = [SMEM if a.ndim == 3 and a.shape[-1] == TAPS else VMEM for a in ins]
    size = sum(a.size * a.dtype.itemsize for a in ins) + sum(o.size * o.dtype.itemsize for o in outs)
    return pl.pallas_call(
        kernel,
        out_shape=tuple(outs),
        in_specs=specs,
        out_specs=tuple(VMEM for _ in outs),
        scratch_shapes=list(scratch),
        compiler_params=PARAMS,
        cost_estimate=pl.CostEstimate(flops=flops, bytes_accessed=size, transcendentals=0),
    )(*ins)


def array(*shape, dtype=F32):
    return jax.ShapeDtypeStruct(shape, dtype)


def local(charges, kernel_taps):
    z, y, x = (Cut(name, size) for name, size in zip(("gz", "gy", "gx"), charges.shape))
    s = Sizes(z, y, x)
    n = x.fine
    nz, nz2 = len(s.z_routes), len(s.z2_routes)

    def bound(kernel, *static):
        return lambda *refs: kernel(s, *static, *refs)

    rows = up8(y.mid_all)
    held, own, ahead, behind, *messages = call(
        bound(restrict_kernel, nz),
        [array(*charges.shape), array(z.mid_all, rows, n)] + [array(s.y_rows, n)] * 2 + [array(s.z_rows, n)] * nz + [array(s.z2_rows, n)] * nz2,
        [charges],
        [
            pltpu.VMEM((z.fine, y.fine + 16, n), F32),
            pltpu.VMEM((z.mid_all, rows, n), F32),
            pltpu.VMEM((z.mid_all, up8(y.mid + 24), n), F32),
            pltpu.VMEM((z.mid_all, rows, n), F32),
        ],
    )
    z_got = [route(m) for route, m in zip(s.z_routes + s.z2_routes, messages)]
    sides = [s.y_routes[0](ahead), s.y_routes[1](behind)]
    operators = call(
        bound(operator_kernel),
        [
            array(5 * n, TERMS * n, dtype=BF16),
            array(5 * n, 2 * TERMS * n, dtype=BF16),
            array(TERMS * y.fine, 3 * s.fine_rows, dtype=BF16),
            array(TERMS * y.fine, 3 * s.sum_rows, dtype=BF16),
            array(TERMS * y.fine, 3 * s.sum_rows, dtype=BF16),
        ],
        [kernel_taps],
    )
    ahead, behind, far = call(
        bound(spread_kernel, nz, nz2),
        [array(s.slab_rows, n), array(s.slab_rows, n), array(s.far_rows, n)],
        [operators[-1], own, *z_got],
    )
    sides += [s.y_routes[0](ahead), s.y_routes[1](behind)]
    far = s.y2_routes[0](far)
    fine, sums, first, second = call(
        bound(collect_kernel, nz, nz2),
        [
            array(s.fine_planes, s.fine_rows, n),
            array(s.sum_planes, s.sum_rows, n),
            array(s.x_sends, s.x_cells),
            array(s.x_sends, s.x_cells),
        ],
        [held, own, *z_got, *sides, far],
        [pltpu.VMEM((s.slab_planes, s.sum_rows, n), F32)],
    )
    first, second = s.x_routes[0](first), s.x_routes[1](second)
    fine, sums = call(
        bound(own_kernel),
        [array(s.fine_planes * s.fine_rows, TERMS * n), array(s.sum_planes * s.sum_rows, 2 * TERMS * n)],
        [fine, sums, *operators[:2]],
    )
    (out,) = call(
        bound(sum_kernel),
        [array(z.fine, y.fine, n)],
        [kernel_taps, fine, sums, first, second, *operators],
        [
            pltpu.VMEM((s.x_cells, n), F32),
            pltpu.VMEM((z.fine + 2 * RADIUS, TERMS, y.fine, n), F32),
            pltpu.VMEM((z.mid + 2 * RADIUS + 3, TERMS, y.fine, n), F32),
            pltpu.VMEM((z.coarse + 2 * RADIUS + 5, TERMS, y.fine, n), F32),
            pltpu.VMEM((z.mid_all, y.fine, n), F32),
            pltpu.VMEM((z.coarse_all, y.fine, n), F32),
        ],
    )
    return out


def solution(mesh):
    return jax.shard_map(
        local,
        mesh=mesh,
        in_specs=(P("gz", "gy", "gx"), P()),
        out_specs=P("gz", "gy", "gx"),
        check_vma=False,
    )
```

```python
import jax
import jax.numpy as jnp
from jax import lax
from jax.experimental import pallas as pl
from jax.experimental.pallas import tpu as pltpu
from jax.sharding import PartitionSpec as P

RADIUS = 8
TAPS = 17
TERMS = 2
WEIGHTS = ((-3, -0.0625), (-1, 0.5625), (0, 1.0), (1, 0.5625), (3, -0.0625))
EXACT = lax.Precision.HIGHEST
SPAN = RADIUS + 5
EDGE = RADIUS + 3
F32, BF16 = jnp.float32, jnp.bfloat16
PARAMS = pltpu.CompilerParams(vmem_limit_bytes=32 * 1024 * 1024)
VMEM = pl.BlockSpec(memory_space=pltpu.VMEM)
SMEM = pl.BlockSpec(memory_space=pltpu.SMEM)


def up8(n):
    return -(-n // 8) * 8


def iota(shape, dim):
    return lax.broadcasted_iota(jnp.int32, shape, dim)


def weight_of(difference):
    size = jnp.abs(difference)
    out = jnp.where(size == 1, 0.5625, jnp.where(size == 3, -0.0625, 0.0))
    return jnp.where(size == 0, 1.0, out)


def choose(condition, a, b):
    return jnp.where(condition, jnp.where(a, 1, 0), jnp.where(b, 1, 0)) != 0


class Cut:
    def __init__(self, name, length):
        self.name, self.fine = name, length
        self.count = lax.axis_size(name)
        self.mid, self.coarse = length // 2, length // 4
        self.mid_all, self.coarse_all = self.mid + 3, self.coarse + 5
        self.second = max(SPAN - self.coarse, 0)

    def index(self):
        return lax.axis_index(self.name)

    def holds_mid(self, k):
        k = k + self.index() * self.mid
        return (k >= 0) & (k < self.mid * self.count)

    def holds_coarse(self, k):
        k = k + self.index() * self.coarse
        return (k >= 0) & (k < self.coarse * self.count)


class Route:
    def __init__(self, names, pairs, up, below):
        self.names, self.pairs, self.up, self.below = names, pairs, up, below

    def __call__(self, x):
        return lax.ppermute(x, self.names, self.pairs)


def flip(pairs):
    return [(b, a) for a, b in pairs]


def swap(cut, steps):
    pairs = [(i, i + steps) for i in range(cut.count - steps)]

    def up():
        return cut.index() + steps < cut.count

    return [Route(cut.name, pairs + flip(pairs), up, lambda: ~up())]


def both_ways(cut, steps):
    pairs = [(i, i + steps) for i in range(cut.count - steps)]
    yes, no = (lambda: cut.index() >= 0), (lambda: cut.index() < 0)
    return [Route(cut.name, pairs, yes, yes), Route(cut.name, flip(pairs), no, no)]


def folded(cut, beside, names):
    n, m = cut.count, lax.axis_size(beside)

    def place(c, i):
        return c * n + i if names[0] == beside else i * m + c

    pairs = []
    for c in range(0, m, 2):
        cycle = [place(c, i) for i in range(n)] + [place(c + 1, i) for i in reversed(range(n))]
        pairs += list(zip(cycle, cycle[1:] + cycle[:1]))

    def even():
        return lax.axis_index(beside) % 2 == 0

    def odd():
        return lax.axis_index(beside) % 2 == 1

    return [Route(names, pairs, even, even), Route(names, flip(pairs), odd, odd)]


def split(x):
    high = x.astype(BF16)
    return high, (x - high.astype(F32)).astype(BF16)


def pick(selector, x):
    nt = (((1,), (1,)), ((), ()))
    a = x.astype(BF16)
    rest = x - a.astype(F32)
    b = rest.astype(BF16)
    c = (rest - b.astype(F32)).astype(BF16)
    out = lax.dot_general(selector, c, nt, preferred_element_type=F32)
    out = out + lax.dot_general(selector, b, nt, preferred_element_type=F32)
    return out + lax.dot_general(selector, a, nt, preferred_element_type=F32)


class Sizes:
    def __init__(self, z, y, x):
        self.z, self.y, self.x = z, y, x
        self.z_routes = swap(z, 1) if z.count <= 2 else both_ways(z, 1)
        self.z2_routes = [] if z.count <= 2 else swap(z, 2) if z.count <= 4 else both_ways(z, 2)
        self.y_routes = folded(y, x.name, (x.name, y.name))
        self.y2_routes = swap(y, 2)
        self.x_routes = folded(x, z.name, (x.name, z.name))
        self.z_fine = RADIUS * y.fine
        self.z_rows = up8(self.z_fine + SPAN * y.mid_all)
        self.z2_rows = up8(z.second * y.mid_all)
        self.slab_planes = SPAN * len(self.z_routes) + z.second * len(self.z2_routes)
        self.fine_planes = z.fine + RADIUS * len(self.z_routes)
        self.sum_planes = z.mid_all + RADIUS * len(self.z_routes)
        self.y_fine = RADIUS * z.fine
        self.y_rows = up8(self.y_fine + SPAN * z.mid_all)
        self.slab_fine = RADIUS * RADIUS * len(self.z_routes)
        self.slab_rows = up8(self.slab_fine + SPAN * self.slab_planes)
        self.far_groups = x.fine // x.coarse_all
        self.far_planes = -(-(z.coarse_all + self.slab_planes) // self.far_groups)
        self.far_rows = up8(y.second * self.far_planes)
        self.fine_rows = y.fine + 2 * RADIUS
        self.far = y.coarse_all
        self.low = y.mid_all
        self.high = self.low + SPAN
        self.sum_rows = -(-(self.high + SPAN) // 16) * 16
        self.edge_sums = EDGE + SPAN
        self.fine_blocks = -(-self.fine_planes * self.fine_rows // 128)
        self.sum_blocks = -(-self.sum_planes * self.sum_rows // 128)
        self.x_rows = self.fine_blocks * RADIUS + self.sum_blocks * self.edge_sums
        assert x.mid_all + x.coarse_all <= x.fine
        assert self.far + y.second <= self.low
        assert z.coarse >= RADIUS and y.coarse >= RADIUS and y.count == 4


def restrict_kernel(s, nz, source, charges, own, ahead, behind, *rest):
    messages, (wide, mid, high, coarse) = rest[:-4], rest[-4:]
    z, y, x = s.z, s.y, s.x
    lanes = (x.fine, x.fine)
    cell, lane = iota(lanes, 0), iota(lanes, 1)
    k = lane - 1
    to_mid = jnp.where((lane < x.mid_all) & x.holds_mid(k), weight_of(cell - 2 * k), 0.0)
    c = lane - x.mid_all - 2
    inside = (lane >= x.mid_all) & (lane < x.mid_all + x.coarse_all) & x.holds_coarse(c)
    to_coarse = jnp.where(inside, weight_of(cell - 1 - 2 * c), 0.0)
    narrow = to_mid + jnp.dot(to_mid, to_coarse, precision=EXACT, preferred_element_type=F32)
    wide[...] = jnp.zeros(wide.shape, F32)
    charges[...] = source[...]
    cells = source[...].reshape(z.fine * y.fine, x.fine)
    reduced = jnp.dot(cells, narrow, precision=EXACT, preferred_element_type=F32)
    wide[:, 8 : 8 + y.fine, :] = reduced.reshape(z.fine, y.fine, x.fine)
    rows = 0.0
    for offset, weight in WEIGHTS:
        rows = rows + weight * wide[:, pl.ds(6 + offset, y.mid_all, stride=2), :]
    keep = y.holds_mid(iota((y.mid_all, x.fine), 0) - 1)
    mid[...] = jnp.zeros(mid.shape, F32)
    coarse[...] = jnp.zeros(coarse.shape, F32)
    high[...] = jnp.zeros(high.shape, F32)
    for p in range(z.mid_all):
        total = 0.0
        for offset, weight in WEIGHTS:
            at = 2 * (p - 1) + offset
            if 0 <= at < z.fine:
                total = total + weight * rows[at]
        total = jnp.where(keep & z.holds_mid(p - 1), total, 0.0)
        mid[p, : y.mid_all] = total
        high[p, 8 : 8 + y.mid_all] = total
    rows = 0.0
    for offset, weight in WEIGHTS:
        rows = rows + weight * high[:, pl.ds(5 + offset, y.coarse_all, stride=2), :]
    keep = y.holds_coarse(iota((y.coarse_all, x.fine), 0) - 2)
    for p in range(z.coarse_all):
        total = 0.0
        for offset, weight in WEIGHTS:
            at = 2 * (p - 2) + offset + 1
            if 0 <= at < z.mid_all:
                total = total + weight * rows[at]
        coarse[p, : y.coarse_all] = jnp.where(keep & z.holds_coarse(p - 2), total, 0.0)
    is_mid = iota(mid.shape[1:], 1) < x.mid_all
    for p in range(z.mid_all):
        own[p] = jnp.where(is_mid, mid[p], coarse[p]) if p < z.coarse_all else jnp.where(is_mid, mid[p], 0.0)
    is_side = iota((SPAN, x.fine), 1) < x.mid_all
    for message, route in zip((ahead, behind), s.y_routes):
        up = route.up()
        edge = jnp.where(up, charges[:, y.fine - RADIUS :, :], charges[:, :RADIUS, :])
        message[: s.y_fine] = edge.reshape(s.y_fine, x.fine)
        for p in range(z.mid_all):
            last = jnp.where(is_side, own[p, y.mid_all - SPAN : y.mid_all], own[p, y.coarse_all - SPAN : y.coarse_all])
            at = s.y_fine + p * SPAN
            message[at : at + SPAN] = jnp.where(up, last, own[p, :SPAN])
        filled = s.y_fine + SPAN * z.mid_all
        if filled < s.y_rows:
            message[filled:] = jnp.zeros((s.y_rows - filled, x.fine), F32)
    for message, route in zip(messages, s.z_routes):
        up = route.up().astype(jnp.int32)
        message[: s.z_fine] = charges[pl.ds(up * (z.fine - RADIUS), RADIUS)].reshape(s.z_fine, x.fine)
        for p in range(SPAN):
            plane = jnp.where(is_mid, mid[up * (z.mid_all - SPAN) + p], coarse[up * (z.coarse_all - SPAN) + p])
            at = s.z_fine + p * y.mid_all
            message[at : at + y.mid_all] = plane[: y.mid_all]
        filled = s.z_fine + SPAN * y.mid_all
        if filled < s.z_rows:
            message[filled:] = jnp.zeros((s.z_rows - filled, x.fine), F32)
    for message, route in zip(messages[nz:], s.z2_routes):
        up = route.up().astype(jnp.int32)
        message[...] = jnp.zeros(message.shape, F32)
        for p in range(z.second):
            plane = jnp.where(is_mid, 0.0, coarse[up * (z.coarse_all - z.second) + p])
            message[p * y.mid_all : (p + 1) * y.mid_all] = plane[: y.mid_all]


def slabs(s, z_messages, z2_messages):
    out = []
    for message in z_messages:
        out += [(message, s.z_fine + p * s.y.mid_all) for p in range(SPAN)]
    for message in z2_messages:
        out += [(message, p * s.y.mid_all) for p in range(s.z.second)]
    return out


def spread_kernel(s, nz, nz2, _, own, *rest):
    z_messages, z2_messages = rest[:nz], rest[nz : nz + nz2]
    ahead, behind, far, rows = rest[-4:]
    z, y, x = s.z, s.y, s.x
    is_mid = iota((SPAN, x.fine), 1) < x.mid_all
    planes = slabs(s, z_messages, z2_messages)
    for message, route in zip((ahead, behind), s.y_routes):
        up = route.up()
        at = 0
        for z_message in z_messages:
            slab = z_message[: s.z_fine].reshape(RADIUS, y.fine, x.fine)
            edge = jnp.where(up, slab[:, y.fine - RADIUS :], slab[:, :RADIUS])
            message[at : at + RADIUS * RADIUS] = edge.reshape(RADIUS * RADIUS, x.fine)
            at += RADIUS * RADIUS
        for held, first in planes:
            top, end = held[first + y.mid_all - SPAN : first + y.mid_all], first + y.coarse_all
            last = jnp.where(is_mid, top, held[end - SPAN : end])
            message[at : at + SPAN] = jnp.where(up, last, held[first : first + SPAN])
            at += SPAN
        if at < s.slab_rows:
            message[at:] = jnp.zeros((s.slab_rows - at, x.fine), F32)
    up = s.y2_routes[0].up()
    count, end = y.second, y.coarse_all
    rows[...] = jnp.zeros(rows.shape, F32)
    sources = [(own.at[p], 0) for p in range(z.coarse_all)] + planes
    for p, (held, first) in enumerate(sources):
        g, at = p // s.far_planes, p % s.far_planes * count
        last = held[first + end - count : first + end]
        rows[g, at : at + count] = jnp.where(up, last, held[first : first + count])
    lane = iota(far.shape, 1)
    total = jnp.zeros(far.shape, F32)
    for g in range(s.far_groups):
        start = g * x.coarse_all
        turned = pltpu.roll(rows[g], (start - x.mid_all) % x.fine, 1)
        total = jnp.where((lane >= start) & (lane < start + x.coarse_all), turned, total)
    far[...] = total


def collect_kernel(s, nz, nz2, charges, own, *rest):
    z_messages, z2_messages = rest[:nz], rest[nz : nz + nz2]
    pairs = rest[nz + nz2 : nz + nz2 + 4]
    far, fine, sums, first, second, raw, rows = rest[nz + nz2 + 4 :]
    z, y, x = s.z, s.y, s.x
    below = s.y_routes[0].below()
    planes = slabs(s, z_messages, z2_messages)

    def sides(which, start, count):
        a, b = (message[start : start + count] for message in pairs[2 * which : 2 * which + 2])
        return jnp.where(below, a, b), jnp.where(below, b, a)

    def fine_planes(at, count, body, which, row):
        low, high = sides(which, row, RADIUS * count)
        fine[at : at + count, : y.fine] = body
        fine[at : at + count, y.fine : y.fine + RADIUS] = low.reshape(count, RADIUS, x.fine)
        fine[at : at + count, y.fine + RADIUS :] = high.reshape(count, RADIUS, x.fine)

    fine_planes(0, z.fine, charges[...], 0, 0)
    at = z.fine
    for n, z_message in enumerate(z_messages):
        slab = z_message[: s.z_fine].reshape(RADIUS, y.fine, x.fine)
        fine_planes(at, RADIUS, slab, 1, n * RADIUS * RADIUS)
        at += RADIUS
    sums[...] = jnp.zeros(sums.shape, F32)
    raw[...] = jnp.zeros(raw.shape, F32)
    for g in range(s.far_groups):
        rows[g] = pltpu.roll(far[...], (x.mid_all - g * x.coarse_all) % x.fine, 1)
    is_mid = iota((y.second, x.fine), 1) < x.mid_all

    def rows_of_plane(out, p, body, which, row, far_plane):
        low, high = sides(which, row, SPAN)
        out[p, : y.mid_all] = body
        out[p, s.low : s.low + SPAN] = low
        out[p, s.high : s.high + SPAN] = high
        if far_plane is not None:
            at = slice(s.far, s.far + y.second)
            start = far_plane % s.far_planes * y.second
            out[p, at] = jnp.where(is_mid, out[p, at], rows[far_plane // s.far_planes, start : start + y.second])

    for p in range(z.mid_all):
        far_plane = p if p < z.coarse_all else None
        rows_of_plane(sums, p, own[p, : y.mid_all], 0, s.y_fine + p * SPAN, far_plane)
    for p, (held, at) in enumerate(planes):
        rows_of_plane(raw, p, held[at : at + y.mid_all], 1, s.slab_fine + p * SPAN, z.coarse_all + p)
    is_mid = iota((s.sum_rows, x.fine), 1) < x.mid_all

    def number(condition, a, b):
        return jnp.where(condition, a, b)

    for n, route in enumerate(s.z_routes):
        lower, base = route.below(), n * SPAN
        for j in range(RADIUS):
            a = raw[base + number(lower, SPAN - 3 - RADIUS, 3) + j]
            b = raw[base + number(lower, SPAN - 5 - RADIUS, 5) + j]
            sums[z.mid_all + n * RADIUS + j] = jnp.where(is_mid, a, b)
        for i in range(3):
            at = number(lower, 0, z.mid) + i
            sums[at] = sums[at] + jnp.where(is_mid, raw[base + number(lower, SPAN - 3, 0) + i], 0.0)
        for i in range(5):
            at = number(lower, 0, z.coarse) + i
            sums[at] = sums[at] + jnp.where(is_mid, 0.0, raw[base + number(lower, SPAN - 5, 0) + i])
    for n, route in enumerate(s.z2_routes):
        base = len(s.z_routes) * SPAN + n * z.second
        start = z.mid_all + number(route.below(), RADIUS - z.coarse, RADIUS + z.coarse - 5)
        for p in range(z.second):
            sums[start + p] = sums[start + p] + jnp.where(is_mid, 0.0, raw[base + p])

    row, lane = iota((2 * RADIUS, x.fine), 0), iota((2 * RADIUS, x.fine), 1)
    up = s.x_routes[0].up()
    is_first = row < RADIUS
    goes_up = choose(up, is_first, ~is_first)
    slot = jnp.where(is_first, row, row - RADIUS)
    wanted = jnp.where(goes_up, x.fine - RADIUS + slot, slot)
    picked = pick((lane == wanted).astype(BF16), fine[...].reshape(s.fine_planes * s.fine_rows, x.fine))
    width = EDGE + SPAN
    row, lane = iota((2 * width, x.fine), 0), iota((2 * width, x.fine), 1)
    is_first = row < width
    goes_up = choose(up, is_first, ~is_first)
    slot = jnp.where(is_first, row, row - width)
    from_mid = jnp.where(goes_up, x.mid_all - EDGE + slot, slot)
    from_coarse = slot - EDGE + jnp.where(goes_up, x.mid_all + x.coarse_all - SPAN, x.mid_all)
    wanted = jnp.where(slot < EDGE, from_mid, from_coarse)
    picked_sums = pick((lane == wanted).astype(BF16), sums[...].reshape(s.sum_planes * s.sum_rows, x.fine))
    spare = s.sum_blocks * 128 - picked_sums.shape[1]
    if spare:
        picked_sums = jnp.concatenate([picked_sums, jnp.zeros((2 * width, spare), F32)], axis=1)
    spare = s.fine_blocks * 128 - picked.shape[1]
    if spare:
        picked = jnp.concatenate([picked, jnp.zeros((2 * RADIUS, spare), F32)], axis=1)
    for n, message in enumerate((first, second)):
        for b in range(s.fine_blocks):
            message[b * RADIUS : (b + 1) * RADIUS] = picked[n * RADIUS : (n + 1) * RADIUS, b * 128 : (b + 1) * 128]
        for b in range(s.sum_blocks):
            at = s.fine_blocks * RADIUS + b * width
            message[at : at + width] = picked_sums[n * width : (n + 1) * width, b * 128 : (b + 1) * 128]


def band(taps, level, offset, valid):
    at = jnp.where(valid, offset + RADIUS, -1)
    out = [jnp.zeros(at.shape, F32) for _ in range(TERMS)]
    for tap in range(TAPS):
        here = at == tap
        out = [jnp.where(here, taps[level, term, tap], total) for term, total in enumerate(out)]
    return out


def dot(a, b):
    return jnp.dot(a, b, precision=EXACT, preferred_element_type=F32)


def operator_kernel(s, taps, x_fine, x_sums, y_fine, y_mid, y_coarse):
    y, x = s.y, s.x
    own, edge = x.fine, 64
    shape = (own + edge, x.fine)
    row, lane = iota(shape, 0), iota(shape, 1)
    t = row - own
    lower, higher = x.index() > 0, x.index() < x.count - 1
    is_own = row < own

    def place(half, own_place, own_valid, first, count, low_place, high_place):
        is_low = t < half
        r = jnp.where(is_low, t, t - half) - first
        there = (r >= 0) & (r < count) & (t < 2 * half) & choose(is_low, lower, higher)
        valid = choose(is_own, own_valid, there)
        return jnp.where(is_own, own_place, jnp.where(is_low, low_place + r, high_place + r)), valid

    half = s.edge_sums
    where, valid = place(RADIUS, row, row >= 0, 0, RADIUS, -RADIUS, x.fine)
    fine = band(taps, 0, where - lane, valid)
    where, valid = place(half, row - 1, row < x.mid_all, 0, EDGE, 2 - EDGE, x.mid - 1)
    mid = band(taps, 1, where - (lane - 1), valid & (lane < x.mid_all))
    first = x.mid_all
    inside = (row >= first) & (row < first + x.coarse_all)
    where, valid = place(half, row - first - 2, inside, EDGE, SPAN, 3 - SPAN, x.coarse - 2)
    coarse = band(taps, 2, where - (lane - 2), valid & (lane < x.coarse_all))
    a, b = iota((x.fine, x.fine), 0), iota((x.fine, x.fine), 1)
    from_mid = jnp.where((a < x.mid_all) & x.holds_mid(a - 1), weight_of(b - 2 * (a - 1)), 0.0)
    from_coarse = jnp.where((a < x.coarse_all) & x.holds_coarse(a - 2), weight_of(b - 1 - 2 * (a - 2)), 0.0)
    from_coarse = dot(from_coarse, from_mid)
    columns = [(x_fine, RADIUS, 0, fine)]
    columns += [(x_sums, half, 0, [dot(m, from_mid) for m in mid])]
    columns += [(x_sums, half, TERMS * x.fine, [dot(c, from_coarse) for c in coarse])]
    for out, half, at, terms in columns:
        for term, matrix in enumerate(terms):
            high, low = split(matrix)
            cols = slice(at + term * x.fine, at + (term + 1) * x.fine)
            n = 2 * half
            ends = high[own : own + n]
            out[0:own, cols] = high[:own]
            out[own : 2 * own, cols] = high[:own]
            out[2 * own : 3 * own, cols] = low[:own]
            out[3 * own :, cols] = jnp.zeros((out.shape[0] - 3 * own, x.fine), BF16)
            last = 2 * n if 3 * n <= 128 else 128
            out[3 * own : 3 * own + n, cols] = ends
            out[3 * own + n : 3 * own + 2 * n, cols] = ends
            out[3 * own + last : 3 * own + last + n, cols] = low[own : own + n]

    lower, higher = y.index() > 0, y.index() < y.count - 1
    far_below = s.y2_routes[0].below()
    n = up8(y.mid_all)

    def write(out, size, terms):
        part = iota((y.fine, 3 * size), 1) >= 2 * size
        for term, matrix in enumerate(terms):
            high, low = split(matrix)
            out[term * y.fine : (term + 1) * y.fine] = jnp.where(part, low.astype(F32), high.astype(F32)).astype(BF16)

    def columns_of(rows, size):
        lane = iota((rows, 3 * size), 1)
        return jnp.where(lane >= 2 * size, lane - 2 * size, jnp.where(lane >= size, lane - size, lane))

    c = columns_of(y.fine, s.fine_rows)
    is_low = (c >= y.fine) & (c < y.fine + RADIUS)
    is_high = c >= y.fine + RADIUS
    where = jnp.where(is_low, c - y.fine - RADIUS, jnp.where(is_high, c - RADIUS, c))
    valid = choose(is_low, lower, choose(is_high, higher, c >= 0))
    write(y_fine, s.fine_rows, band(taps, 0, where - iota(c.shape, 0), valid))

    c = columns_of(n, s.sum_rows)
    r = iota(c.shape, 0)
    is_low = (c >= s.low) & (c < s.low + SPAN)
    is_high = (c >= s.high) & (c < s.high + SPAN)
    is_far = (c >= s.far) & (c < s.far + y.second)
    where = jnp.where(is_low, c - s.low + 2 - SPAN, jnp.where(is_high, c - s.high + y.mid - 1, c - 1))
    valid = choose(is_low, lower, choose(is_high, higher, c < y.mid_all))
    mid = band(taps, 1, where - (r - 1), valid & (r < y.mid_all))
    far = jnp.where(far_below, -2 - y.coarse, 2 * y.coarse - 2)
    where = jnp.where(is_low, c - s.low + 3 - SPAN, jnp.where(is_high, c - s.high + y.coarse - 2, c - 2))
    where = jnp.where(is_far, c - s.far + far, where)
    valid = choose(is_low, lower, choose(is_high, higher, (c < y.coarse_all) | is_far))
    coarse = band(taps, 2, where - (r - 2), valid & (r < y.coarse_all))
    o, k = iota((y.fine, n), 0), iota((y.fine, n), 1)
    from_mid = jnp.where((k < y.mid_all) & y.holds_mid(k - 1), weight_of(o - 2 * (k - 1)), 0.0)
    o, k = iota((n, n), 0), iota((n, n), 1)
    from_coarse = jnp.where((k < y.coarse_all) & y.holds_coarse(k - 2), weight_of(o - 1 - 2 * (k - 2)), 0.0)
    from_coarse = dot(from_mid, from_coarse)
    write(y_mid, s.sum_rows, [dot(from_mid, m) for m in mid])
    write(y_coarse, s.sum_rows, [dot(from_coarse, m) for m in coarse])


def own_kernel(s, fine, sums, x_fine, x_sums, fine_part, sums_part):
    def along_x(grid, weights):
        high, low = split(grid)
        joined = jnp.concatenate([high, low, high], axis=1)
        return jnp.dot(joined, weights[: 3 * s.x.fine], preferred_element_type=F32)

    cells = s.fine_planes * s.fine_rows
    fine_part[...] = along_x(fine[...].reshape(cells, s.x.fine), x_fine)
    cells = s.sum_planes * s.sum_rows
    sums_part[...] = along_x(sums[...].reshape(cells, s.x.fine), x_sums)


def sum_kernel(s, taps, fine, sums, first, second, x_fine, x_sums, y_fine, y_mid, y_coarse, out, *scratch):
    fine_ends, sums_ends, t_fine, t_mid, t_coarse, p_mid, p_coarse = scratch
    z, y, x = s.z, s.y, s.x
    below = s.x_routes[0].below()
    for out_ends, blocks, start, half in (
        (fine_ends, s.fine_blocks, 0, RADIUS),
        (sums_ends, s.sum_blocks, s.fine_blocks * RADIUS, s.edge_sums),
    ):
        copies = 128 // (2 * half)
        copies = min(copies, 3)
        for b in range(blocks):
            at = slice(start + b * half, start + (b + 1) * half)
            one, two = first[at], second[at]
            rows = [jnp.where(below, one, two), jnp.where(below, two, one)] * copies
            rows.append(jnp.zeros((128 - 2 * half * copies, 128), F32))
            out_ends[b * 128 : (b + 1) * 128] = jnp.concatenate(rows, axis=0).T

    def along_x(held, ends, half, start, rows, weights):
        edge = ends[start : start + rows]
        edge_high, edge_low = split(edge)
        lane = iota(edge.shape, 1)
        is_low = (lane >= 2 * half) & (lane < 4 * half)
        joined = jnp.where(is_low, edge_low.astype(F32), edge_high.astype(F32)).astype(BF16)
        if 6 * half > 128:
            joined = jnp.concatenate([joined, edge_high], axis=1)
        part = jnp.dot(joined, weights[3 * x.fine :], preferred_element_type=F32)
        return split(held[start : start + rows] + part)

    def along_y(high, low, weights):
        joined = jnp.concatenate([high, low, high], axis=0)
        result = jnp.dot(weights[...], joined, preferred_element_type=F32)
        return [result[t * y.fine : (t + 1) * y.fine, t * x.fine : (t + 1) * x.fine] for t in range(TERMS)]

    def starts(below_at, above_at):
        result = []
        for route in s.z_routes:
            lower, i = route.below(), z.index()
            valid = choose(lower, i >= 1, i + 1 < z.count)
            result.append((jnp.where(lower, below_at, above_at), valid))
        return result

    t_fine[...] = jnp.zeros(t_fine.shape, F32)
    t_mid[...] = jnp.zeros(t_mid.shape, F32)
    t_coarse[...] = jnp.zeros(t_coarse.shape, F32)

    def store(held, at, valid, parts):
        for t, part in enumerate(parts):
            held[at, t] = part if valid is None else jnp.where(valid, part, 0.0)

    mid_at = [(RADIUS + p, None) for p in range(z.mid_all)]
    coarse_at = [(RADIUS + p if p < z.coarse_all else None, None) for p in range(z.mid_all)]
    for start, valid in starts(0, z.mid + 3 + RADIUS):
        mid_at += [(start + p, valid) for p in range(RADIUS)]
    for start, valid in starts(0, z.coarse + 5 + RADIUS):
        coarse_at += [(start + p, valid) for p in range(RADIUS)]
    def sum_group(g, count):
        n = s.sum_rows
        a, b = along_x(sums, sums_ends, s.edge_sums, g * n, count * n, x_sums)
        for p in range(count):
            rows = slice(p * n, (p + 1) * n)
            for which, (held, weights) in enumerate(((t_mid, y_mid), (t_coarse, y_coarse))):
                at, valid = (mid_at, coarse_at)[which][g + p]
                if at is not None:
                    cols = slice(which * TERMS * x.fine, (which + 1) * TERMS * x.fine)
                    store(held, at, valid, along_y(a[rows, cols], b[rows, cols], weights))

    fine_at = [(RADIUS + p, None) for p in range(z.fine)]
    for start, valid in starts(0, z.fine + RADIUS):
        fine_at += [(start + p, valid) for p in range(RADIUS)]

    def fine_group(g, count):
        n = s.fine_rows
        a, b = along_x(fine, fine_ends, RADIUS, g * n, count * n, x_fine)
        for p in range(count):
            rows = slice(p * n, (p + 1) * n)
            store(t_fine, *fine_at[g + p], along_y(a[rows], b[rows], y_fine))

    def along_z(held, level, base, count):
        totals = [None] * count
        for t in range(TERMS):
            for j in range(count + TAPS - 1):
                plane = held[base + j, t]
                for i in range(max(0, j - TAPS + 1), min(count, j + 1)):
                    term = taps[level, t, j - i] * plane
                    totals[i] = term if totals[i] is None else totals[i] + term
        return totals

    block = 4

    def coarse_block(k):
        count = min(block, z.coarse_all - k)
        for i, total in enumerate(along_z(t_coarse, 2, k, count)):
            p_coarse[k + i] = jnp.where(z.holds_coarse(k + i - 2), total, 0.0)

    def mid_block(k):
        count = min(block, z.mid_all - k)
        for i, total in enumerate(along_z(t_mid, 1, k, count)):
            m = k + i - 1
            for offset, weight in WEIGHTS:
                if (m - offset) % 2 == 0 and 0 <= (m - offset) // 2 + 2 < z.coarse_all:
                    total = total + weight * p_coarse[(m - offset) // 2 + 2]
            p_mid[k + i] = jnp.where(z.holds_mid(m), total, 0.0)

    def fine_block(k):
        for i, total in enumerate(along_z(t_fine, 0, k, block)):
            for offset, weight in WEIGHTS:
                if (i - offset) % 2 == 0:
                    total = total + weight * p_mid[k // 2 + (i - offset) // 2 + 1]
            out[k + i] = total

    for g in range(0, s.sum_planes, 4):
        sum_group(g, min(4, s.sum_planes - g))
    later = [lambda k=k: coarse_block(k) for k in range(0, z.coarse_all, block)]
    later += [lambda k=k: mid_block(k) for k in range(0, z.mid_all, block)]
    groups = list(range(z.fine, s.fine_planes, 8)) + list(range(0, z.fine, 8))
    done = 0
    for n, g in enumerate(groups):
        fine_group(g, 8)
        for _ in range(3):
            if later:
                later.pop(0)()
        if g < z.fine:
            ready = g if g + 8 < z.fine else z.fine
            later += [lambda k=k: fine_block(k) for k in range(done, ready, block)]
            done = max(done, ready)
    while later:
        later.pop(0)()


def call(kernel, outs, ins, scratch=(), flops=10**7):
    specs = [SMEM if a.ndim == 3 and a.shape[-1] == TAPS else VMEM for a in ins]
    size = sum(a.size * a.dtype.itemsize for a in ins) + sum(o.size * o.dtype.itemsize for o in outs)
    return pl.pallas_call(
        kernel,
        out_shape=tuple(outs),
        in_specs=specs,
        out_specs=tuple(VMEM for _ in outs),
        scratch_shapes=list(scratch),
        compiler_params=PARAMS,
        cost_estimate=pl.CostEstimate(flops=flops, bytes_accessed=size, transcendentals=0),
    )(*ins)


def array(*shape, dtype=F32):
    return jax.ShapeDtypeStruct(shape, dtype)


def local(charges, kernel_taps):
    z, y, x = (Cut(name, size) for name, size in zip(("gz", "gy", "gx"), charges.shape))
    s = Sizes(z, y, x)
    n = x.fine
    nz, nz2 = len(s.z_routes), len(s.z2_routes)

    def bound(kernel, *static):
        return lambda *refs: kernel(s, *static, *refs)

    rows = up8(y.mid_all)
    held, own, ahead, behind, *messages = call(
        bound(restrict_kernel, nz),
        [array(*charges.shape), array(z.mid_all, rows, n)] + [array(s.y_rows, n)] * 2 + [array(s.z_rows, n)] * nz + [array(s.z2_rows, n)] * nz2,
        [charges],
        [
            pltpu.VMEM((z.fine, y.fine + 16, n), F32),
            pltpu.VMEM((z.mid_all, rows, n), F32),
            pltpu.VMEM((z.mid_all, up8(y.mid + 24), n), F32),
            pltpu.VMEM((z.mid_all, rows, n), F32),
        ],
    )
    z_got = [route(m) for route, m in zip(s.z_routes + s.z2_routes, messages)]
    sides = [s.y_routes[0](ahead), s.y_routes[1](behind)]
    operators = call(
        bound(operator_kernel),
        [
            array(3 * n + 128, TERMS * n, dtype=BF16),
            array(3 * n + 256, 2 * TERMS * n, dtype=BF16),
            array(TERMS * y.fine, 3 * s.fine_rows, dtype=BF16),
            array(TERMS * y.fine, 3 * s.sum_rows, dtype=BF16),
            array(TERMS * y.fine, 3 * s.sum_rows, dtype=BF16),
        ],
        [kernel_taps],
    )
    ahead, behind, far = call(
        bound(spread_kernel, nz, nz2),
        [array(s.slab_rows, n), array(s.slab_rows, n), array(s.far_rows, n)],
        [operators[-1], own, *z_got],
        [pltpu.VMEM((s.far_groups, s.far_rows, n), F32)],
    )
    sides += [s.y_routes[0](ahead), s.y_routes[1](behind)]
    far = s.y2_routes[0](far)
    fine, sums, first, second = call(
        bound(collect_kernel, nz, nz2),
        [
            array(s.fine_planes, s.fine_rows, n),
            array(s.sum_planes, s.sum_rows, n),
            array(s.x_rows, n),
            array(s.x_rows, n),
        ],
        [held, own, *z_got, *sides, far],
        [pltpu.VMEM((s.slab_planes, s.sum_rows, n), F32), pltpu.VMEM((s.far_groups, s.far_rows, n), F32)],
    )
    first, second = s.x_routes[0](first), s.x_routes[1](second)
    fine, sums = call(
        bound(own_kernel),
        [array(s.fine_planes * s.fine_rows, TERMS * n), array(s.sum_planes * s.sum_rows, 2 * TERMS * n)],
        [fine, sums, *operators[:2]],
    )
    (out,) = call(
        bound(sum_kernel),
        [array(z.fine, y.fine, n)],
        [kernel_taps, fine, sums, first, second, *operators],
        [
            pltpu.VMEM((s.fine_blocks * 128, n), F32),
            pltpu.VMEM((s.sum_blocks * 128, n), F32),
            pltpu.VMEM((z.fine + 2 * RADIUS, TERMS, y.fine, n), F32),
            pltpu.VMEM((z.mid + 2 * RADIUS + 3, TERMS, y.fine, n), F32),
            pltpu.VMEM((z.coarse + 2 * RADIUS + 5, TERMS, y.fine, n), F32),
            pltpu.VMEM((z.mid_all, y.fine, n), F32),
            pltpu.VMEM((z.coarse_all, y.fine, n), F32),
        ],
    )
    return out


def solution(mesh):
    return jax.shard_map(
        local,
        mesh=mesh,
        in_specs=(P("gz", "gy", "gx"), P()),
        out_specs=P("gz", "gy", "gx"),
        check_vma=False,
    )
```

```python
import jax
import jax.numpy as jnp
from jax import lax
from jax.experimental import pallas as pl
from jax.experimental.pallas import tpu as pltpu
from jax.sharding import PartitionSpec as P

RADIUS = 8
TAPS = 17
TERMS = 2
WEIGHTS = ((-3, -0.0625), (-1, 0.5625), (0, 1.0), (1, 0.5625), (3, -0.0625))
EXACT = lax.Precision.HIGHEST
SPAN = RADIUS + 5
EDGE = RADIUS + 3
F32, BF16 = jnp.float32, jnp.bfloat16
PARAMS = pltpu.CompilerParams(vmem_limit_bytes=32 * 1024 * 1024)
VMEM = pl.BlockSpec(memory_space=pltpu.VMEM)
SMEM = pl.BlockSpec(memory_space=pltpu.SMEM)


def up8(n):
    return -(-n // 8) * 8


def iota(shape, dim):
    return lax.broadcasted_iota(jnp.int32, shape, dim)


def weight_of(difference):
    size = jnp.abs(difference)
    out = jnp.where(size == 1, 0.5625, jnp.where(size == 3, -0.0625, 0.0))
    return jnp.where(size == 0, 1.0, out)


def choose(condition, a, b):
    return jnp.where(condition, jnp.where(a, 1, 0), jnp.where(b, 1, 0)) != 0


class Cut:
    def __init__(self, name, length):
        self.name, self.fine = name, length
        self.count = lax.axis_size(name)
        self.mid, self.coarse = length // 2, length // 4
        self.mid_all, self.coarse_all = self.mid + 3, self.coarse + 5
        self.second = max(SPAN - self.coarse, 0)

    def index(self):
        return lax.axis_index(self.name)

    def holds_mid(self, k):
        k = k + self.index() * self.mid
        return (k >= 0) & (k < self.mid * self.count)

    def holds_coarse(self, k):
        k = k + self.index() * self.coarse
        return (k >= 0) & (k < self.coarse * self.count)


class Route:
    def __init__(self, names, pairs, up, below):
        self.names, self.pairs, self.up, self.below = names, pairs, up, below

    def __call__(self, x):
        return lax.ppermute(x, self.names, self.pairs)


def flip(pairs):
    return [(b, a) for a, b in pairs]


def swap(cut, steps):
    pairs = [(i, i + steps) for i in range(cut.count - steps)]

    def up():
        return cut.index() + steps < cut.count

    return [Route(cut.name, pairs + flip(pairs), up, lambda: ~up())]


def both_ways(cut, steps):
    pairs = [(i, i + steps) for i in range(cut.count - steps)]
    yes, no = (lambda: cut.index() >= 0), (lambda: cut.index() < 0)
    return [Route(cut.name, pairs, yes, yes), Route(cut.name, flip(pairs), no, no)]


def folded(cut, beside, names):
    n, m = cut.count, lax.axis_size(beside)

    def place(c, i):
        return c * n + i if names[0] == beside else i * m + c

    pairs = []
    for c in range(0, m, 2):
        cycle = [place(c, i) for i in range(n)] + [place(c + 1, i) for i in reversed(range(n))]
        pairs += list(zip(cycle, cycle[1:] + cycle[:1]))

    def even():
        return lax.axis_index(beside) % 2 == 0

    def odd():
        return lax.axis_index(beside) % 2 == 1

    return [Route(names, pairs, even, even), Route(names, flip(pairs), odd, odd)]


def split(x):
    high = x.astype(BF16)
    return high, (x - high.astype(F32)).astype(BF16)


def pick(selector, x):
    nt = (((1,), (1,)), ((), ()))
    a = x.astype(BF16)
    rest = x - a.astype(F32)
    b = rest.astype(BF16)
    c = (rest - b.astype(F32)).astype(BF16)
    out = lax.dot_general(selector, c, nt, preferred_element_type=F32)
    out = out + lax.dot_general(selector, b, nt, preferred_element_type=F32)
    return out + lax.dot_general(selector, a, nt, preferred_element_type=F32)


class Sizes:
    def __init__(self, z, y, x):
        self.z, self.y, self.x = z, y, x
        self.z_routes = swap(z, 1) if z.count <= 2 else both_ways(z, 1)
        self.z2_routes = [] if z.count <= 2 else swap(z, 2) if z.count <= 4 else both_ways(z, 2)
        self.y_routes = folded(y, x.name, (x.name, y.name))
        self.y2_routes = swap(y, 2)
        self.x_routes = folded(x, z.name, (x.name, z.name))
        self.z_fine = RADIUS * y.fine
        self.z_rows = up8(self.z_fine + SPAN * y.mid_all)
        self.z2_rows = up8(z.second * y.mid_all)
        self.slab_planes = SPAN * len(self.z_routes) + z.second * len(self.z2_routes)
        self.fine_planes = z.fine + RADIUS * len(self.z_routes)
        self.sum_planes = z.mid_all + RADIUS * len(self.z_routes)
        self.y_fine = RADIUS * z.fine
        self.y_rows = up8(self.y_fine + SPAN * z.mid_all)
        self.slab_fine = RADIUS * RADIUS * len(self.z_routes)
        self.slab_rows = up8(self.slab_fine + SPAN * self.slab_planes)
        self.far_groups = x.fine // x.coarse_all
        self.far_planes = -(-(z.coarse_all + self.slab_planes) // self.far_groups)
        self.far_rows = up8(y.second * self.far_planes)
        self.fine_rows = y.fine + 2 * RADIUS
        self.far = y.coarse_all
        self.low = y.mid_all
        self.high = self.low + SPAN
        self.sum_rows = -(-(self.high + SPAN) // 16) * 16
        self.edge_sums = EDGE + SPAN
        self.side = x.fine // RADIUS
        self.fine_groups = -(-self.fine_planes // self.side)
        self.fine_ends = self.fine_groups * self.fine_rows
        self.sum_blocks = -(-self.sum_planes * self.sum_rows // 128)
        self.x_rows = self.fine_ends + self.sum_blocks * self.edge_sums
        assert x.mid_all + x.coarse_all <= x.fine
        assert self.far + y.second <= self.low
        assert z.coarse >= RADIUS and y.coarse >= RADIUS and y.count == 4


def restrict_kernel(s, nz, source, charges, own, ahead, behind, *rest):
    messages, (wide, mid, high, coarse) = rest[:-4], rest[-4:]
    z, y, x = s.z, s.y, s.x
    lanes = (x.fine, x.fine)
    cell, lane = iota(lanes, 0), iota(lanes, 1)
    k = lane - 1
    to_mid = jnp.where((lane < x.mid_all) & x.holds_mid(k), weight_of(cell - 2 * k), 0.0)
    c = lane - x.mid_all - 2
    inside = (lane >= x.mid_all) & (lane < x.mid_all + x.coarse_all) & x.holds_coarse(c)
    to_coarse = jnp.where(inside, weight_of(cell - 1 - 2 * c), 0.0)
    narrow = to_mid + jnp.dot(to_mid, to_coarse, precision=EXACT, preferred_element_type=F32)
    wide[...] = jnp.zeros(wide.shape, F32)
    charges[...] = source[...]
    cells = source[...].reshape(z.fine * y.fine, x.fine)
    reduced = jnp.dot(cells, narrow, precision=EXACT, preferred_element_type=F32)
    wide[:, 8 : 8 + y.fine, :] = reduced.reshape(z.fine, y.fine, x.fine)
    rows = 0.0
    for offset, weight in WEIGHTS:
        rows = rows + weight * wide[:, pl.ds(6 + offset, y.mid_all, stride=2), :]
    keep = y.holds_mid(iota((y.mid_all, x.fine), 0) - 1)
    mid[...] = jnp.zeros(mid.shape, F32)
    coarse[...] = jnp.zeros(coarse.shape, F32)
    high[...] = jnp.zeros(high.shape, F32)
    for p in range(z.mid_all):
        total = 0.0
        for offset, weight in WEIGHTS:
            at = 2 * (p - 1) + offset
            if 0 <= at < z.fine:
                total = total + weight * rows[at]
        total = jnp.where(keep & z.holds_mid(p - 1), total, 0.0)
        mid[p, : y.mid_all] = total
        high[p, 8 : 8 + y.mid_all] = total
    rows = 0.0
    for offset, weight in WEIGHTS:
        rows = rows + weight * high[:, pl.ds(5 + offset, y.coarse_all, stride=2), :]
    keep = y.holds_coarse(iota((y.coarse_all, x.fine), 0) - 2)
    for p in range(z.coarse_all):
        total = 0.0
        for offset, weight in WEIGHTS:
            at = 2 * (p - 2) + offset + 1
            if 0 <= at < z.mid_all:
                total = total + weight * rows[at]
        coarse[p, : y.coarse_all] = jnp.where(keep & z.holds_coarse(p - 2), total, 0.0)
    is_mid = iota(mid.shape[1:], 1) < x.mid_all
    for p in range(z.mid_all):
        own[p] = jnp.where(is_mid, mid[p], coarse[p]) if p < z.coarse_all else jnp.where(is_mid, mid[p], 0.0)
    is_side = iota((SPAN, x.fine), 1) < x.mid_all
    for message, route in zip((ahead, behind), s.y_routes):
        up = route.up()
        edge = jnp.where(up, charges[:, y.fine - RADIUS :, :], charges[:, :RADIUS, :])
        message[: s.y_fine] = edge.reshape(s.y_fine, x.fine)
        for p in range(z.mid_all):
            last = jnp.where(is_side, own[p, y.mid_all - SPAN : y.mid_all], own[p, y.coarse_all - SPAN : y.coarse_all])
            at = s.y_fine + p * SPAN
            message[at : at + SPAN] = jnp.where(up, last, own[p, :SPAN])
        filled = s.y_fine + SPAN * z.mid_all
        if filled < s.y_rows:
            message[filled:] = jnp.zeros((s.y_rows - filled, x.fine), F32)
    for message, route in zip(messages, s.z_routes):
        up = route.up().astype(jnp.int32)
        message[: s.z_fine] = charges[pl.ds(up * (z.fine - RADIUS), RADIUS)].reshape(s.z_fine, x.fine)
        for p in range(SPAN):
            plane = jnp.where(is_mid, mid[up * (z.mid_all - SPAN) + p], coarse[up * (z.coarse_all - SPAN) + p])
            at = s.z_fine + p * y.mid_all
            message[at : at + y.mid_all] = plane[: y.mid_all]
        filled = s.z_fine + SPAN * y.mid_all
        if filled < s.z_rows:
            message[filled:] = jnp.zeros((s.z_rows - filled, x.fine), F32)
    for message, route in zip(messages[nz:], s.z2_routes):
        up = route.up().astype(jnp.int32)
        message[...] = jnp.zeros(message.shape, F32)
        for p in range(z.second):
            plane = jnp.where(is_mid, 0.0, coarse[up * (z.coarse_all - z.second) + p])
            message[p * y.mid_all : (p + 1) * y.mid_all] = plane[: y.mid_all]


def slabs(s, z_messages, z2_messages):
    out = []
    for message in z_messages:
        out += [(message, s.z_fine + p * s.y.mid_all) for p in range(SPAN)]
    for message in z2_messages:
        out += [(message, p * s.y.mid_all) for p in range(s.z.second)]
    return out


def spread_kernel(s, nz, nz2, _, own, *rest):
    z_messages, z2_messages = rest[:nz], rest[nz : nz + nz2]
    ahead, behind, far, rows = rest[-4:]
    z, y, x = s.z, s.y, s.x
    is_mid = iota((SPAN, x.fine), 1) < x.mid_all
    planes = slabs(s, z_messages, z2_messages)
    for message, route in zip((ahead, behind), s.y_routes):
        up = route.up()
        at = 0
        for z_message in z_messages:
            slab = z_message[: s.z_fine].reshape(RADIUS, y.fine, x.fine)
            edge = jnp.where(up, slab[:, y.fine - RADIUS :], slab[:, :RADIUS])
            message[at : at + RADIUS * RADIUS] = edge.reshape(RADIUS * RADIUS, x.fine)
            at += RADIUS * RADIUS
        for held, first in planes:
            top, end = held[first + y.mid_all - SPAN : first + y.mid_all], first + y.coarse_all
            last = jnp.where(is_mid, top, held[end - SPAN : end])
            message[at : at + SPAN] = jnp.where(up, last, held[first : first + SPAN])
            at += SPAN
        if at < s.slab_rows:
            message[at:] = jnp.zeros((s.slab_rows - at, x.fine), F32)
    up = s.y2_routes[0].up()
    count, end = y.second, y.coarse_all
    rows[...] = jnp.zeros(rows.shape, F32)
    sources = [(own.at[p], 0) for p in range(z.coarse_all)] + planes
    for p, (held, first) in enumerate(sources):
        g, at = p // s.far_planes, p % s.far_planes * count
        last = held[first + end - count : first + end]
        rows[g, at : at + count] = jnp.where(up, last, held[first : first + count])
    lane = iota(far.shape, 1)
    total = jnp.zeros(far.shape, F32)
    for g in range(s.far_groups):
        start = g * x.coarse_all
        turned = pltpu.roll(rows[g], (start - x.mid_all) % x.fine, 1)
        total = jnp.where((lane >= start) & (lane < start + x.coarse_all), turned, total)
    far[...] = total


def collect_kernel(s, nz, nz2, charges, own, *rest):
    z_messages, z2_messages = rest[:nz], rest[nz : nz + nz2]
    pairs = rest[nz + nz2 : nz + nz2 + 4]
    far, fine, sums, first, second, raw, rows = rest[nz + nz2 + 4 :]
    z, y, x = s.z, s.y, s.x
    below = s.y_routes[0].below()
    planes = slabs(s, z_messages, z2_messages)

    def sides(which, start, count):
        a, b = (message[start : start + count] for message in pairs[2 * which : 2 * which + 2])
        return jnp.where(below, a, b), jnp.where(below, b, a)

    def fine_planes(at, count, body, which, row):
        low, high = sides(which, row, RADIUS * count)
        fine[at : at + count, : y.fine] = body
        fine[at : at + count, y.fine : y.fine + RADIUS] = low.reshape(count, RADIUS, x.fine)
        fine[at : at + count, y.fine + RADIUS :] = high.reshape(count, RADIUS, x.fine)

    fine_planes(0, z.fine, charges[...], 0, 0)
    at = z.fine
    for n, z_message in enumerate(z_messages):
        slab = z_message[: s.z_fine].reshape(RADIUS, y.fine, x.fine)
        fine_planes(at, RADIUS, slab, 1, n * RADIUS * RADIUS)
        at += RADIUS
    sums[...] = jnp.zeros(sums.shape, F32)
    raw[...] = jnp.zeros(raw.shape, F32)
    for g in range(s.far_groups):
        rows[g] = pltpu.roll(far[...], (x.mid_all - g * x.coarse_all) % x.fine, 1)
    is_mid = iota((y.second, x.fine), 1) < x.mid_all

    def rows_of_plane(out, p, body, which, row, far_plane):
        low, high = sides(which, row, SPAN)
        out[p, : y.mid_all] = body
        out[p, s.low : s.low + SPAN] = low
        out[p, s.high : s.high + SPAN] = high
        if far_plane is not None:
            at = slice(s.far, s.far + y.second)
            start = far_plane % s.far_planes * y.second
            out[p, at] = jnp.where(is_mid, out[p, at], rows[far_plane // s.far_planes, start : start + y.second])

    for p in range(z.mid_all):
        far_plane = p if p < z.coarse_all else None
        rows_of_plane(sums, p, own[p, : y.mid_all], 0, s.y_fine + p * SPAN, far_plane)
    for p, (held, at) in enumerate(planes):
        rows_of_plane(raw, p, held[at : at + y.mid_all], 1, s.slab_fine + p * SPAN, z.coarse_all + p)
    is_mid = iota((s.sum_rows, x.fine), 1) < x.mid_all

    def number(condition, a, b):
        return jnp.where(condition, a, b)

    for n, route in enumerate(s.z_routes):
        lower, base = route.below(), n * SPAN
        for j in range(RADIUS):
            a = raw[base + number(lower, SPAN - 3 - RADIUS, 3) + j]
            b = raw[base + number(lower, SPAN - 5 - RADIUS, 5) + j]
            sums[z.mid_all + n * RADIUS + j] = jnp.where(is_mid, a, b)
        for i in range(3):
            at = number(lower, 0, z.mid) + i
            sums[at] = sums[at] + jnp.where(is_mid, raw[base + number(lower, SPAN - 3, 0) + i], 0.0)
        for i in range(5):
            at = number(lower, 0, z.coarse) + i
            sums[at] = sums[at] + jnp.where(is_mid, 0.0, raw[base + number(lower, SPAN - 5, 0) + i])
    for n, route in enumerate(s.z2_routes):
        base = len(s.z_routes) * SPAN + n * z.second
        start = z.mid_all + number(route.below(), RADIUS - z.coarse, RADIUS + z.coarse - 5)
        for p in range(z.second):
            sums[start + p] = sums[start + p] + jnp.where(is_mid, 0.0, raw[base + p])

    up = s.x_routes[0].up()
    lane = iota((s.fine_rows, x.fine), 1)
    for g in range(s.fine_groups):
        ends = [jnp.zeros(lane.shape, F32)] * 2
        for j in range(min(s.side, s.fine_planes - g * s.side)):
            plane = fine[g * s.side + j]
            here = (lane >= RADIUS * j) & (lane < RADIUS * (j + 1))
            for n, start in enumerate((x.fine - RADIUS, 0)):
                shift = (RADIUS * j - start) % x.fine
                ends[n] = jnp.where(here, pltpu.roll(plane, shift, 1) if shift else plane, ends[n])
        rows = slice(g * s.fine_rows, (g + 1) * s.fine_rows)
        first[rows] = jnp.where(up, ends[0], ends[1])
        second[rows] = jnp.where(up, ends[1], ends[0])
    width = EDGE + SPAN
    row, lane = iota((2 * width, x.fine), 0), iota((2 * width, x.fine), 1)
    is_first = row < width
    goes_up = choose(up, is_first, ~is_first)
    slot = jnp.where(is_first, row, row - width)
    from_mid = jnp.where(goes_up, x.mid_all - EDGE + slot, slot)
    from_coarse = slot - EDGE + jnp.where(goes_up, x.mid_all + x.coarse_all - SPAN, x.mid_all)
    wanted = jnp.where(slot < EDGE, from_mid, from_coarse)
    picked_sums = pick((lane == wanted).astype(BF16), sums[...].reshape(s.sum_planes * s.sum_rows, x.fine))
    spare = s.sum_blocks * 128 - picked_sums.shape[1]
    if spare:
        picked_sums = jnp.concatenate([picked_sums, jnp.zeros((2 * width, spare), F32)], axis=1)
    for n, message in enumerate((first, second)):
        for b in range(s.sum_blocks):
            at = s.fine_ends + b * width
            message[at : at + width] = picked_sums[n * width : (n + 1) * width, b * 128 : (b + 1) * 128]


def band(taps, level, offset, valid):
    at = jnp.where(valid, offset + RADIUS, -1)
    out = [jnp.zeros(at.shape, F32) for _ in range(TERMS)]
    for tap in range(TAPS):
        here = at == tap
        out = [jnp.where(here, taps[level, term, tap], total) for term, total in enumerate(out)]
    return out


def dot(a, b):
    return jnp.dot(a, b, precision=EXACT, preferred_element_type=F32)


def z_columns(s):
    return s.z.fine * RADIUS


def lower_x(x):
    return x.index() > 0


def higher_x(x):
    return x.index() < x.count - 1


def operator_kernel(s, taps, x_fine, x_sums, ends, y_fine, y_mid, y_coarse):
    y, x = s.y, s.x
    own, edge = x.fine, 64
    shape = (own + edge, x.fine)
    row, lane = iota(shape, 0), iota(shape, 1)
    t = row - own
    lower, higher = x.index() > 0, x.index() < x.count - 1
    is_own = row < own

    def place(half, own_place, own_valid, first, count, low_place, high_place):
        is_low = t < half
        r = jnp.where(is_low, t, t - half) - first
        there = (r >= 0) & (r < count) & (t < 2 * half) & choose(is_low, lower, higher)
        valid = choose(is_own, own_valid, there)
        return jnp.where(is_own, own_place, jnp.where(is_low, low_place + r, high_place + r)), valid

    half = s.edge_sums
    fine = band(taps, 0, row - lane, is_own)
    where, valid = place(half, row - 1, row < x.mid_all, 0, EDGE, 2 - EDGE, x.mid - 1)
    mid = band(taps, 1, where - (lane - 1), valid & (lane < x.mid_all))
    first = x.mid_all
    inside = (row >= first) & (row < first + x.coarse_all)
    where, valid = place(half, row - first - 2, inside, EDGE, SPAN, 3 - SPAN, x.coarse - 2)
    coarse = band(taps, 2, where - (lane - 2), valid & (lane < x.coarse_all))
    a, b = iota((x.fine, x.fine), 0), iota((x.fine, x.fine), 1)
    from_mid = jnp.where((a < x.mid_all) & x.holds_mid(a - 1), weight_of(b - 2 * (a - 1)), 0.0)
    from_coarse = jnp.where((a < x.coarse_all) & x.holds_coarse(a - 2), weight_of(b - 1 - 2 * (a - 2)), 0.0)
    from_coarse = dot(from_coarse, from_mid)
    columns = [(x_fine, 0, 0, fine)]
    columns += [(x_sums, half, 0, [dot(m, from_mid) for m in mid])]
    columns += [(x_sums, half, TERMS * x.fine, [dot(c, from_coarse) for c in coarse])]
    for out, half, at, terms in columns:
        for term, matrix in enumerate(terms):
            high, low = split(matrix)
            cols = slice(at + term * x.fine, at + (term + 1) * x.fine)
            n = 2 * half
            out[0:own, cols] = high[:own]
            out[own : 2 * own, cols] = high[:own]
            out[2 * own : 3 * own, cols] = low[:own]
            if n:
                out[3 * own :, cols] = jnp.zeros((out.shape[0] - 3 * own, x.fine), BF16)
                out[3 * own : 3 * own + n, cols] = high[own : own + n]
                out[3 * own + n : 3 * own + 2 * n, cols] = high[own : own + n]
                out[3 * own + 128 : 3 * own + 128 + n, cols] = low[own : own + n]

    z, slots, wide = s.z, s.side * s.fine_groups, z_columns(s)
    slot, column = iota((slots, wide), 0), iota((slots, wide), 1)
    where, valid = slot, slot < z.fine
    for n, route in enumerate(s.z_routes):
        lower, i, first = route.below(), z.index(), z.fine + n * RADIUS
        here = (slot >= first) & (slot < first + RADIUS)
        where = jnp.where(here, slot - first + jnp.where(lower, -RADIUS, z.fine), where)
        valid = choose(here, choose(lower, i >= 1, i + 1 < z.count), valid)
    planes = band(taps, 0, where - column // RADIUS, valid)
    r, c = iota((RADIUS, wide), 0), iota((RADIUS, wide), 1) % RADIUS
    cells = (slots, RADIUS, wide)
    for side, (offset, valid) in enumerate(((r - c - RADIUS, lower_x(x)), (r - c + RADIUS, higher_x(x)))):
        columns = band(taps, 0, offset, choose(valid, r >= 0, r < 0))
        for term in range(TERMS):
            joint = jnp.broadcast_to(planes[term][:, None, :], cells) * jnp.broadcast_to(columns[term][None], cells)
            high, low = split(joint.reshape(slots * RADIUS, wide))
            at = 2 * term + side
            ends[at, : slots * RADIUS] = high
            ends[at, slots * RADIUS : 2 * slots * RADIUS] = high
            ends[at, 2 * slots * RADIUS :] = low

    lower, higher = y.index() > 0, y.index() < y.count - 1
    far_below = s.y2_routes[0].below()
    n = up8(y.mid_all)

    def write(out, size, terms):
        part = iota((y.fine, 3 * size), 1) >= 2 * size
        for term, matrix in enumerate(terms):
            high, low = split(matrix)
            out[term * y.fine : (term + 1) * y.fine] = jnp.where(part, low.astype(F32), high.astype(F32)).astype(BF16)

    def columns_of(rows, size):
        lane = iota((rows, 3 * size), 1)
        return jnp.where(lane >= 2 * size, lane - 2 * size, jnp.where(lane >= size, lane - size, lane))

    c = columns_of(y.fine, s.fine_rows)
    is_low = (c >= y.fine) & (c < y.fine + RADIUS)
    is_high = c >= y.fine + RADIUS
    where = jnp.where(is_low, c - y.fine - RADIUS, jnp.where(is_high, c - RADIUS, c))
    valid = choose(is_low, lower, choose(is_high, higher, c >= 0))
    write(y_fine, s.fine_rows, band(taps, 0, where - iota(c.shape, 0), valid))

    c = columns_of(n, s.sum_rows)
    r = iota(c.shape, 0)
    is_low = (c >= s.low) & (c < s.low + SPAN)
    is_high = (c >= s.high) & (c < s.high + SPAN)
    is_far = (c >= s.far) & (c < s.far + y.second)
    where = jnp.where(is_low, c - s.low + 2 - SPAN, jnp.where(is_high, c - s.high + y.mid - 1, c - 1))
    valid = choose(is_low, lower, choose(is_high, higher, c < y.mid_all))
    mid = band(taps, 1, where - (r - 1), valid & (r < y.mid_all))
    far = jnp.where(far_below, -2 - y.coarse, 2 * y.coarse - 2)
    where = jnp.where(is_low, c - s.low + 3 - SPAN, jnp.where(is_high, c - s.high + y.coarse - 2, c - 2))
    where = jnp.where(is_far, c - s.far + far, where)
    valid = choose(is_low, lower, choose(is_high, higher, (c < y.coarse_all) | is_far))
    coarse = band(taps, 2, where - (r - 2), valid & (r < y.coarse_all))
    o, k = iota((y.fine, n), 0), iota((y.fine, n), 1)
    from_mid = jnp.where((k < y.mid_all) & y.holds_mid(k - 1), weight_of(o - 2 * (k - 1)), 0.0)
    o, k = iota((n, n), 0), iota((n, n), 1)
    from_coarse = jnp.where((k < y.coarse_all) & y.holds_coarse(k - 2), weight_of(o - 1 - 2 * (k - 2)), 0.0)
    from_coarse = dot(from_mid, from_coarse)
    write(y_mid, s.sum_rows, [dot(from_mid, m) for m in mid])
    write(y_coarse, s.sum_rows, [dot(from_coarse, m) for m in coarse])


def contract_y(s, weights, high, low):
    joined = jnp.concatenate([high, low, high], axis=0)
    result = jnp.dot(weights[...], joined, preferred_element_type=F32)
    n, m = s.y.fine, s.x.fine
    return [result[t * n : (t + 1) * n, t * m : (t + 1) * m] for t in range(TERMS)]


def contract_z(taps, held, level, base, count):
    totals = [None] * count
    for t in range(TERMS):
        for j in range(count + TAPS - 1):
            plane = held[base + j, t]
            for i in range(max(0, j - TAPS + 1), min(count, j + 1)):
                term = taps[level, t, j - i] * plane
                totals[i] = term if totals[i] is None else totals[i] + term
    return totals


def slab_starts(s, below_at, above_at):
    result = []
    for route in s.z_routes:
        lower, i = route.below(), s.z.index()
        valid = choose(lower, i >= 1, i + 1 < s.z.count)
        result.append((jnp.where(lower, below_at, above_at), valid))
    return result


def store_terms(held, at, valid, parts):
    for t, part in enumerate(parts):
        held[at, t] = part if valid is None else jnp.where(valid, part, 0.0)


BLOCK = 4


def own_kernel(s, taps, fine, sums, x_fine, x_sums, y_fine, fine_part, sums_part, t_fine):
    z, x = s.z, s.x

    def along_x(grid, weights):
        high, low = split(grid)
        joined = jnp.concatenate([high, low, high], axis=1)
        return jnp.dot(joined, weights[: 3 * x.fine], preferred_element_type=F32)

    t_fine[...] = jnp.zeros(t_fine.shape, F32)
    fine_at = [(RADIUS + p, None) for p in range(z.fine)]
    for start, valid in slab_starts(s, 0, z.fine + RADIUS):
        fine_at += [(start + p, valid) for p in range(RADIUS)]

    def fine_group(g, count):
        n = s.fine_rows
        a, b = split(along_x(fine[g : g + count].reshape(count * n, x.fine), x_fine))
        for p in range(count):
            rows = slice(p * n, (p + 1) * n)
            store_terms(t_fine, *fine_at[g + p], contract_y(s, y_fine, a[rows], b[rows]))

    def fine_block(k):
        for i, total in enumerate(contract_z(taps, t_fine, 0, k, BLOCK)):
            fine_part[k + i] = total

    def sum_part(g, count):
        n = s.sum_rows
        grid = sums[g : g + count].reshape(count * n, x.fine)
        sums_part[g * n : (g + count) * n] = along_x(grid, x_sums)

    later = []
    done = 0
    for g in list(range(z.fine, s.fine_planes, 8)) + list(range(0, z.fine, 8)):
        fine_group(g, 8)
        while later:
            later.pop(0)()
        if g < z.fine:
            ready = g if g + 8 < z.fine else z.fine
            later += [lambda k=k: fine_block(k) for k in range(done, ready, BLOCK)]
            done = max(done, ready)
    starts = list(range(0, s.sum_planes, 8))
    while later or starts:
        if starts:
            sum_part(starts[0], min(8, s.sum_planes - starts[0]))
            starts.pop(0)
        if later:
            later.pop(0)()


def sum_kernel(s, taps, fine, sums, first, second, x_sums, ends, y_fine, y_mid, y_coarse, out, *scratch):
    sums_ends, t_mid, t_coarse, p_mid, p_coarse = scratch
    z, y, x = s.z, s.y, s.x
    below = s.x_routes[0].below()
    half = s.edge_sums
    for b in range(s.sum_blocks):
        at = slice(s.fine_ends + b * half, s.fine_ends + (b + 1) * half)
        one, two = first[at], second[at]
        rows = [jnp.where(below, one, two), jnp.where(below, two, one)] * 2
        rows.append(jnp.zeros((128 - 4 * half, 128), F32))
        sums_ends[b * 128 : (b + 1) * 128] = jnp.concatenate(rows, axis=0).T

    def along_x(start, rows):
        edge_high, edge_low = split(sums_ends[start : start + rows])
        is_high = iota(edge_high.shape, 1) < 2 * half
        packed = jnp.where(is_high, edge_high.astype(F32), edge_low.astype(F32)).astype(BF16)
        joined = jnp.concatenate([packed, edge_high], axis=1)
        part = jnp.dot(joined, x_sums[3 * x.fine :], preferred_element_type=F32)
        return split(sums[start : start + rows] + part)

    def fine_edges():
        columns = []
        for flip in range(2):
            for g in range(s.fine_groups):
                at = slice(g * s.fine_rows, (g + 1) * s.fine_rows)
                pair = (first[at], second[at])
                columns.append(jnp.where(below, pair[flip], pair[1 - flip]))
        high, low = split(jnp.concatenate(columns, axis=1))
        joined = jnp.concatenate([high, low, high], axis=0)
        high, low = split(jnp.dot(y_fine[...], joined, preferred_element_type=F32))
        width = s.fine_groups * x.fine
        result = []
        for side in range(2):
            total = 0.0
            for t in range(TERMS):
                rows, cols = slice(t * y.fine, (t + 1) * y.fine), slice(side * width, (side + 1) * width)
                a, b = high[rows, cols], low[rows, cols]
                joined = jnp.concatenate([a, b, a], axis=1)
                total = total + jnp.dot(joined, ends[2 * t + side], preferred_element_type=F32)
            result.append(total)
        return result

    t_mid[...] = jnp.zeros(t_mid.shape, F32)
    t_coarse[...] = jnp.zeros(t_coarse.shape, F32)
    mid_at = [(RADIUS + p, None) for p in range(z.mid_all)]
    coarse_at = [(RADIUS + p if p < z.coarse_all else None, None) for p in range(z.mid_all)]
    for start, valid in slab_starts(s, 0, z.mid + 3 + RADIUS):
        mid_at += [(start + p, valid) for p in range(RADIUS)]
    for start, valid in slab_starts(s, 0, z.coarse + 5 + RADIUS):
        coarse_at += [(start + p, valid) for p in range(RADIUS)]
    def sum_group(g, count):
        n = s.sum_rows
        a, b = along_x(g * n, count * n)
        for p in range(count):
            rows = slice(p * n, (p + 1) * n)
            for which, (held, weights) in enumerate(((t_mid, y_mid), (t_coarse, y_coarse))):
                at, valid = (mid_at, coarse_at)[which][g + p]
                if at is not None:
                    cols = slice(which * TERMS * x.fine, (which + 1) * TERMS * x.fine)
                    store_terms(held, at, valid, contract_y(s, weights, a[rows, cols], b[rows, cols]))

    def coarse_block(k):
        count = min(BLOCK, z.coarse_all - k)
        for i, total in enumerate(contract_z(taps, t_coarse, 2, k, count)):
            p_coarse[k + i] = jnp.where(z.holds_coarse(k + i - 2), total, 0.0)

    def mid_block(k):
        count = min(BLOCK, z.mid_all - k)
        for i, total in enumerate(contract_z(taps, t_mid, 1, k, count)):
            m = k + i - 1
            for offset, weight in WEIGHTS:
                if (m - offset) % 2 == 0 and 0 <= (m - offset) // 2 + 2 < z.coarse_all:
                    total = total + weight * p_coarse[(m - offset) // 2 + 2]
            p_mid[k + i] = jnp.where(z.holds_mid(m), total, 0.0)

    for g in range(0, s.sum_planes, 4):
        sum_group(g, min(4, s.sum_planes - g))
    edges = fine_edges()
    for k in range(0, z.coarse_all, BLOCK):
        coarse_block(k)
    for k in range(0, z.mid_all, BLOCK):
        mid_block(k)
    lane = iota((y.fine, x.fine), 1)
    for k in range(z.fine):
        total = fine[k]
        for offset, weight in WEIGHTS:
            if (k - offset) % 2 == 0:
                total = total + weight * p_mid[(k - offset) // 2 + 1]
        block, at = k // s.side, k % s.side * RADIUS
        low, high = (edge[:, block * x.fine : (block + 1) * x.fine] for edge in edges)
        low = pltpu.roll(low, -at % x.fine, 1) if at else low
        turn = (x.fine - RADIUS - at) % x.fine
        high = pltpu.roll(high, turn, 1) if turn else high
        total = total + jnp.where(lane < RADIUS, low, jnp.where(lane >= x.fine - RADIUS, high, 0.0))
        out[k] = total


def call(kernel, outs, ins, scratch=(), flops=10**7):
    specs = [SMEM if a.ndim == 3 and a.shape[-1] == TAPS else VMEM for a in ins]
    size = sum(a.size * a.dtype.itemsize for a in ins) + sum(o.size * o.dtype.itemsize for o in outs)
    return pl.pallas_call(
        kernel,
        out_shape=tuple(outs),
        in_specs=specs,
        out_specs=tuple(VMEM for _ in outs),
        scratch_shapes=list(scratch),
        compiler_params=PARAMS,
        cost_estimate=pl.CostEstimate(flops=flops, bytes_accessed=size, transcendentals=0),
    )(*ins)


def array(*shape, dtype=F32):
    return jax.ShapeDtypeStruct(shape, dtype)


def local(charges, kernel_taps):
    z, y, x = (Cut(name, size) for name, size in zip(("gz", "gy", "gx"), charges.shape))
    s = Sizes(z, y, x)
    n = x.fine
    nz, nz2 = len(s.z_routes), len(s.z2_routes)

    def bound(kernel, *static):
        return lambda *refs: kernel(s, *static, *refs)

    rows = up8(y.mid_all)
    held, own, ahead, behind, *messages = call(
        bound(restrict_kernel, nz),
        [array(*charges.shape), array(z.mid_all, rows, n)] + [array(s.y_rows, n)] * 2 + [array(s.z_rows, n)] * nz + [array(s.z2_rows, n)] * nz2,
        [charges],
        [
            pltpu.VMEM((z.fine, y.fine + 16, n), F32),
            pltpu.VMEM((z.mid_all, rows, n), F32),
            pltpu.VMEM((z.mid_all, up8(y.mid + 24), n), F32),
            pltpu.VMEM((z.mid_all, rows, n), F32),
        ],
    )
    z_got = [route(m) for route, m in zip(s.z_routes + s.z2_routes, messages)]
    sides = [s.y_routes[0](ahead), s.y_routes[1](behind)]
    operators = call(
        bound(operator_kernel),
        [
            array(3 * n, TERMS * n, dtype=BF16),
            array(3 * n + 256, 2 * TERMS * n, dtype=BF16),
            array(2 * TERMS, 3 * s.fine_groups * n, z_columns(s), dtype=BF16),
            array(TERMS * y.fine, 3 * s.fine_rows, dtype=BF16),
            array(TERMS * y.fine, 3 * s.sum_rows, dtype=BF16),
            array(TERMS * y.fine, 3 * s.sum_rows, dtype=BF16),
        ],
        [kernel_taps],
    )
    ahead, behind, far = call(
        bound(spread_kernel, nz, nz2),
        [array(s.slab_rows, n), array(s.slab_rows, n), array(s.far_rows, n)],
        [operators[-1], own, *z_got],
        [pltpu.VMEM((s.far_groups, s.far_rows, n), F32)],
    )
    sides += [s.y_routes[0](ahead), s.y_routes[1](behind)]
    far = s.y2_routes[0](far)
    fine, sums, first, second = call(
        bound(collect_kernel, nz, nz2),
        [
            array(s.fine_planes, s.fine_rows, n),
            array(s.sum_planes, s.sum_rows, n),
            array(s.x_rows, n),
            array(s.x_rows, n),
        ],
        [held, own, *z_got, *sides, far],
        [pltpu.VMEM((s.slab_planes, s.sum_rows, n), F32), pltpu.VMEM((s.far_groups, s.far_rows, n), F32)],
    )
    first, second = s.x_routes[0](first), s.x_routes[1](second)
    x_fine, x_sums, ends, y_fine, y_mid, y_coarse = operators
    fine, sums = call(
        bound(own_kernel),
        [array(z.fine, y.fine, n), array(s.sum_planes * s.sum_rows, 2 * TERMS * n)],
        [kernel_taps, fine, sums, x_fine, x_sums, y_fine],
        [pltpu.VMEM((z.fine + 2 * RADIUS, TERMS, y.fine, n), F32)],
    )
    (out,) = call(
        bound(sum_kernel),
        [array(z.fine, y.fine, n)],
        [kernel_taps, fine, sums, first, second, x_sums, ends, y_fine, y_mid, y_coarse],
        [
            pltpu.VMEM((s.sum_blocks * 128, n), F32),
            pltpu.VMEM((z.mid + 2 * RADIUS + 3, TERMS, y.fine, n), F32),
            pltpu.VMEM((z.coarse + 2 * RADIUS + 5, TERMS, y.fine, n), F32),
            pltpu.VMEM((z.mid_all, y.fine, n), F32),
            pltpu.VMEM((z.coarse_all, y.fine, n), F32),
        ],
    )
    return out


def solution(mesh):
    return jax.shard_map(
        local,
        mesh=mesh,
        in_specs=(P("gz", "gy", "gx"), P()),
        out_specs=P("gz", "gy", "gx"),
        check_vma=False,
    )
```

```python
import jax
import jax.numpy as jnp
from jax import lax
from jax.experimental import pallas as pl
from jax.experimental.pallas import tpu as pltpu
from jax.sharding import PartitionSpec as P

RADIUS = 8
TAPS = 17
TERMS = 2
WEIGHTS = ((-3, -0.0625), (-1, 0.5625), (0, 1.0), (1, 0.5625), (3, -0.0625))
EXACT = lax.Precision.HIGHEST
SPAN = RADIUS + 5
EDGE = RADIUS + 3
F32, BF16 = jnp.float32, jnp.bfloat16
PARAMS = pltpu.CompilerParams(vmem_limit_bytes=32 * 1024 * 1024)
VMEM = pl.BlockSpec(memory_space=pltpu.VMEM)
SMEM = pl.BlockSpec(memory_space=pltpu.SMEM)


def up8(n):
    return -(-n // 8) * 8


def iota(shape, dim):
    return lax.broadcasted_iota(jnp.int32, shape, dim)


def weight_of(difference):
    size = jnp.abs(difference)
    out = jnp.where(size == 1, 0.5625, jnp.where(size == 3, -0.0625, 0.0))
    return jnp.where(size == 0, 1.0, out)


def choose(condition, a, b):
    return jnp.where(condition, jnp.where(a, 1, 0), jnp.where(b, 1, 0)) != 0


class Cut:
    def __init__(self, name, length):
        self.name, self.fine = name, length
        self.count = lax.axis_size(name)
        self.mid, self.coarse = length // 2, length // 4
        self.mid_all, self.coarse_all = self.mid + 3, self.coarse + 5
        self.second = max(SPAN - self.coarse, 0)

    def index(self):
        return lax.axis_index(self.name)

    def holds_mid(self, k):
        k = k + self.index() * self.mid
        return (k >= 0) & (k < self.mid * self.count)

    def holds_coarse(self, k):
        k = k + self.index() * self.coarse
        return (k >= 0) & (k < self.coarse * self.count)


class Route:
    def __init__(self, names, pairs, up, below):
        self.names, self.pairs, self.up, self.below = names, pairs, up, below

    def __call__(self, x):
        return lax.ppermute(x, self.names, self.pairs)


def flip(pairs):
    return [(b, a) for a, b in pairs]


def swap(cut, steps):
    pairs = [(i, i + steps) for i in range(cut.count - steps)]

    def up():
        return cut.index() + steps < cut.count

    return [Route(cut.name, pairs + flip(pairs), up, lambda: ~up())]


def both_ways(cut, steps):
    pairs = [(i, i + steps) for i in range(cut.count - steps)]
    yes, no = (lambda: cut.index() >= 0), (lambda: cut.index() < 0)
    return [Route(cut.name, pairs, yes, yes), Route(cut.name, flip(pairs), no, no)]


def folded(cut, beside, names):
    n, m = cut.count, lax.axis_size(beside)

    def place(c, i):
        return c * n + i if names[0] == beside else i * m + c

    pairs = []
    for c in range(0, m, 2):
        cycle = [place(c, i) for i in range(n)] + [place(c + 1, i) for i in reversed(range(n))]
        pairs += list(zip(cycle, cycle[1:] + cycle[:1]))

    def even():
        return lax.axis_index(beside) % 2 == 0

    def odd():
        return lax.axis_index(beside) % 2 == 1

    return [Route(names, pairs, even, even), Route(names, flip(pairs), odd, odd)]


def split(x):
    high = x.astype(BF16)
    return high, (x - high.astype(F32)).astype(BF16)


def pick(selector, x):
    nt = (((1,), (1,)), ((), ()))
    a = x.astype(BF16)
    rest = x - a.astype(F32)
    b = rest.astype(BF16)
    c = (rest - b.astype(F32)).astype(BF16)
    out = lax.dot_general(selector, c, nt, preferred_element_type=F32)
    out = out + lax.dot_general(selector, b, nt, preferred_element_type=F32)
    return out + lax.dot_general(selector, a, nt, preferred_element_type=F32)


class Sizes:
    def __init__(self, z, y, x):
        self.z, self.y, self.x = z, y, x
        self.z_routes = swap(z, 1) if z.count <= 2 else both_ways(z, 1)
        self.z2_routes = [] if z.count <= 2 else swap(z, 2) if z.count <= 4 else both_ways(z, 2)
        self.y_routes = folded(y, x.name, (x.name, y.name))
        self.y2_routes = swap(y, 2)
        self.x_routes = folded(x, z.name, (x.name, z.name))
        self.z_fine = RADIUS * y.fine
        self.z_sums = max(EDGE * y.mid_all, SPAN * y.coarse_all)
        self.z_rows = up8(self.z_fine + self.z_sums)
        self.z2_rows = up8(z.second * y.coarse_all)
        self.slab_planes = SPAN * len(self.z_routes) + z.second * len(self.z2_routes)
        self.fine_planes = z.fine + RADIUS * len(self.z_routes)
        self.sum_planes = z.mid_all + RADIUS * len(self.z_routes)
        self.coarse_rows = -(-y.coarse_all // 16) * 16
        self.y_fine = RADIUS * z.fine
        self.y_rows = up8(self.y_fine + SPAN * z.mid_all)
        self.slab_fine = RADIUS * RADIUS * len(self.z_routes)
        self.slab_rows = up8(self.slab_fine + SPAN * self.slab_planes)
        self.far_groups = x.fine // x.coarse_all
        self.far_planes = -(-(z.coarse_all + self.slab_planes) // self.far_groups)
        self.far_rows = up8(y.second * self.far_planes)
        self.fine_rows = y.fine + 2 * RADIUS
        self.far = y.coarse_all
        self.low = y.mid_all
        self.high = self.low + SPAN
        self.sum_rows = -(-(self.high + SPAN) // 16) * 16
        self.edge_sums = EDGE + SPAN
        self.side = x.fine // RADIUS
        self.fine_groups = -(-self.fine_planes // self.side)
        self.fine_ends = self.fine_groups * self.fine_rows
        self.sum_blocks = -(-self.sum_planes * self.sum_rows // 128)
        self.x_rows = self.fine_ends + self.sum_blocks * self.edge_sums
        assert x.mid_all + x.coarse_all <= x.fine
        assert self.far + y.second <= self.low and y.coarse_all == SPAN
        assert z.coarse >= RADIUS and y.coarse >= RADIUS and y.count == 4


def restrict_kernel(s, nz, source, charges, own, ahead, behind, *rest):
    messages, (wide, mid, high, coarse, packed) = rest[:-5], rest[-5:]
    z, y, x = s.z, s.y, s.x
    lanes = (x.fine, x.fine)
    cell, lane = iota(lanes, 0), iota(lanes, 1)
    k = lane - 1
    to_mid = jnp.where((lane < x.mid_all) & x.holds_mid(k), weight_of(cell - 2 * k), 0.0)
    c = lane - x.mid_all - 2
    inside = (lane >= x.mid_all) & (lane < x.mid_all + x.coarse_all) & x.holds_coarse(c)
    to_coarse = jnp.where(inside, weight_of(cell - 1 - 2 * c), 0.0)
    narrow = to_mid + jnp.dot(to_mid, to_coarse, precision=EXACT, preferred_element_type=F32)
    wide[...] = jnp.zeros(wide.shape, F32)
    charges[...] = source[...]
    cells = source[...].reshape(z.fine * y.fine, x.fine)
    top, rest = cells.astype(BF16), cells
    rest = rest - top.astype(F32)
    middle = rest.astype(BF16)
    low = (rest - middle.astype(F32)).astype(BF16)
    weights = jnp.concatenate(split(narrow), axis=1)
    both = jnp.dot(low, weights, preferred_element_type=F32)
    both = both + jnp.dot(
        jnp.concatenate([top, middle], axis=1), jnp.concatenate([weights, weights], axis=0), preferred_element_type=F32
    )
    reduced = both[:, : x.fine] + both[:, x.fine :]
    wide[:, 8 : 8 + y.fine, :] = reduced.reshape(z.fine, y.fine, x.fine)
    rows = 0.0
    for offset, weight in WEIGHTS:
        rows = rows + weight * wide[:, pl.ds(6 + offset, y.mid_all, stride=2), :]
    keep = y.holds_mid(iota((y.mid_all, x.fine), 0) - 1)
    mid[...] = jnp.zeros(mid.shape, F32)
    coarse[...] = jnp.zeros(coarse.shape, F32)
    high[...] = jnp.zeros(high.shape, F32)
    for p in range(z.mid_all):
        total = 0.0
        for offset, weight in WEIGHTS:
            at = 2 * (p - 1) + offset
            if 0 <= at < z.fine:
                total = total + weight * rows[at]
        total = jnp.where(keep & z.holds_mid(p - 1), total, 0.0)
        mid[p, : y.mid_all] = total
        high[p, 8 : 8 + y.mid_all] = total
    rows = 0.0
    for offset, weight in WEIGHTS:
        rows = rows + weight * high[:, pl.ds(5 + offset, y.coarse_all, stride=2), :]
    keep = y.holds_coarse(iota((y.coarse_all, x.fine), 0) - 2)
    for p in range(z.coarse_all):
        total = 0.0
        for offset, weight in WEIGHTS:
            at = 2 * (p - 2) + offset + 1
            if 0 <= at < z.mid_all:
                total = total + weight * rows[at]
        coarse[p, : y.coarse_all] = jnp.where(keep & z.holds_coarse(p - 2), total, 0.0)
    is_mid = iota(mid.shape[1:], 1) < x.mid_all
    for p in range(z.mid_all):
        own[p] = jnp.where(is_mid, mid[p], coarse[p]) if p < z.coarse_all else jnp.where(is_mid, mid[p], 0.0)
    is_side = iota((SPAN, x.fine), 1) < x.mid_all
    for message, route in zip((ahead, behind), s.y_routes):
        up = route.up()
        edge = jnp.where(up, charges[:, y.fine - RADIUS :, :], charges[:, :RADIUS, :])
        message[: s.y_fine] = edge.reshape(s.y_fine, x.fine)
        for p in range(z.mid_all):
            last = jnp.where(is_side, own[p, y.mid_all - SPAN : y.mid_all], own[p, y.coarse_all - SPAN : y.coarse_all])
            at = s.y_fine + p * SPAN
            message[at : at + SPAN] = jnp.where(up, last, own[p, :SPAN])
        filled = s.y_fine + SPAN * z.mid_all
        if filled < s.y_rows:
            message[filled:] = jnp.zeros((s.y_rows - filled, x.fine), F32)
    for message, route in zip(messages, s.z_routes):
        up = route.up().astype(jnp.int32)
        message[: s.z_fine] = charges[pl.ds(up * (z.fine - RADIUS), RADIUS)].reshape(s.z_fine, x.fine)
        packed[...] = jnp.zeros(packed.shape, F32)
        for p in range(EDGE):
            packed[0, p * y.mid_all : (p + 1) * y.mid_all] = mid[up * (z.mid_all - EDGE) + p][: y.mid_all]
        for p in range(SPAN):
            plane = coarse[up * (z.coarse_all - SPAN) + p]
            packed[1, p * y.coarse_all : (p + 1) * y.coarse_all] = plane[: y.coarse_all]
        is_mid = iota(packed.shape[1:], 1) < x.mid_all
        message[s.z_fine :] = jnp.where(is_mid, packed[0], packed[1])
    for message, route in zip(messages[nz:], s.z2_routes):
        up = route.up().astype(jnp.int32)
        message[...] = jnp.zeros(message.shape, F32)
        for p in range(z.second):
            plane = coarse[up * (z.coarse_all - z.second) + p]
            message[p * y.coarse_all : (p + 1) * y.coarse_all] = plane[: y.coarse_all]


class Slab:
    def __init__(self, message, mid, coarse):
        self.message, self.mid, self.coarse = message, mid, coarse

    def coarse_rows(self, first, count):
        return self.message[self.coarse + first : self.coarse + first + count]

    def rows(self, is_mid, first_mid, first_coarse, count):
        coarse = 0.0 if first_coarse is None else self.coarse_rows(first_coarse, count)
        mid = 0.0 if self.mid is None else self.message[self.mid + first_mid : self.mid + first_mid + count]
        return jnp.where(is_mid, mid, coarse)


def slabs(s, z_messages, z2_messages):
    out = []
    for message in z_messages:
        for p in range(SPAN):
            mid = s.z_fine + p * s.y.mid_all if p < EDGE else None
            out.append(Slab(message, mid, s.z_fine + p * s.y.coarse_all))
    for message in z2_messages:
        out += [Slab(message, None, p * s.y.coarse_all) for p in range(s.z.second)]
    return out


def spread_kernel(s, nz, nz2, _, own, *rest):
    z_messages, z2_messages = rest[:nz], rest[nz : nz + nz2]
    ahead, behind, far, rows = rest[-4:]
    z, y, x = s.z, s.y, s.x
    is_mid = iota((SPAN, x.fine), 1) < x.mid_all
    planes = slabs(s, z_messages, z2_messages)
    for message, route in zip((ahead, behind), s.y_routes):
        up = route.up()
        at = 0
        for z_message in z_messages:
            slab = z_message[: s.z_fine].reshape(RADIUS, y.fine, x.fine)
            edge = jnp.where(up, slab[:, y.fine - RADIUS :], slab[:, :RADIUS])
            message[at : at + RADIUS * RADIUS] = edge.reshape(RADIUS * RADIUS, x.fine)
            at += RADIUS * RADIUS
        for plane in planes:
            last = plane.rows(is_mid, y.mid_all - SPAN, y.coarse_all - SPAN, SPAN)
            message[at : at + SPAN] = jnp.where(up, last, plane.rows(is_mid, 0, 0, SPAN))
            at += SPAN
        if at < s.slab_rows:
            message[at:] = jnp.zeros((s.slab_rows - at, x.fine), F32)
    up = s.y2_routes[0].up()
    count, end = y.second, y.coarse_all
    rows[...] = jnp.zeros(rows.shape, F32)
    pairs = [(own[p, end - count : end], own[p, :count]) for p in range(z.coarse_all)]
    pairs += [(plane.coarse_rows(end - count, count), plane.coarse_rows(0, count)) for plane in planes]
    for p, (last, start) in enumerate(pairs):
        g, at = p // s.far_planes, p % s.far_planes * count
        rows[g, at : at + count] = jnp.where(up, last, start)
    lane = iota(far.shape, 1)
    total = jnp.zeros(far.shape, F32)
    for g in range(s.far_groups):
        start = g * x.coarse_all
        turned = pltpu.roll(rows[g], (start - x.mid_all) % x.fine, 1)
        total = jnp.where((lane >= start) & (lane < start + x.coarse_all), turned, total)
    far[...] = total


def collect_kernel(s, nz, nz2, charges, own, *rest):
    z_messages, z2_messages = rest[:nz], rest[nz : nz + nz2]
    rest = rest[nz + nz2 :]
    pairs = rest[:4]
    far, fine, sums, first, second, raw, rows = rest[4:]
    z, y, x = s.z, s.y, s.x
    below = s.y_routes[0].below()
    planes = slabs(s, z_messages, z2_messages)

    def sides(which, start, count):
        a, b = (message[start : start + count] for message in pairs[2 * which : 2 * which + 2])
        return jnp.where(below, a, b), jnp.where(below, b, a)

    def fine_planes(at, count, body, which, row):
        low, high = sides(which, row, RADIUS * count)
        fine[at : at + count, : y.fine] = body
        fine[at : at + count, y.fine : y.fine + RADIUS] = low.reshape(count, RADIUS, x.fine)
        fine[at : at + count, y.fine + RADIUS :] = high.reshape(count, RADIUS, x.fine)

    fine_planes(0, z.fine, charges[...], 0, 0)
    at = z.fine
    for n, z_message in enumerate(z_messages):
        slab = z_message[: s.z_fine].reshape(RADIUS, y.fine, x.fine)
        fine_planes(at, RADIUS, slab, 1, n * RADIUS * RADIUS)
        at += RADIUS
    sums[...] = jnp.zeros(sums.shape, F32)
    raw[...] = jnp.zeros(raw.shape, F32)
    for g in range(s.far_groups):
        rows[g] = pltpu.roll(far[...], (x.mid_all - g * x.coarse_all) % x.fine, 1)
    is_mid = iota((y.second, x.fine), 1) < x.mid_all

    def rows_of_plane(out, p, body, which, row, far_plane):
        low, high = sides(which, row, SPAN)
        out[p, : y.mid_all] = body
        out[p, s.low : s.low + SPAN] = low
        out[p, s.high : s.high + SPAN] = high
        if far_plane is not None:
            at = slice(s.far, s.far + y.second)
            start = far_plane % s.far_planes * y.second
            out[p, at] = jnp.where(is_mid, out[p, at], rows[far_plane // s.far_planes, start : start + y.second])

    for p in range(z.mid_all):
        far_plane = p if p < z.coarse_all else None
        rows_of_plane(sums, p, own[p, : y.mid_all], 0, s.y_fine + p * SPAN, far_plane)
    is_mid_row = iota((SPAN, x.fine), 1) < x.mid_all
    is_mid_rest = iota((y.mid_all - SPAN, x.fine), 1) < x.mid_all
    for p, plane in enumerate(planes):
        body = [plane.rows(is_mid_row, 0, 0, SPAN), plane.rows(is_mid_rest, SPAN, None, y.mid_all - SPAN)]
        rows_of_plane(raw, p, jnp.concatenate(body, axis=0), 1, s.slab_fine + p * SPAN, z.coarse_all + p)
    is_mid = iota((s.sum_rows, x.fine), 1) < x.mid_all

    def number(condition, a, b):
        return jnp.where(condition, a, b)

    for n, route in enumerate(s.z_routes):
        lower, base = route.below(), n * SPAN
        for j in range(RADIUS):
            a = raw[base + number(lower, 0, 3) + j]
            b = raw[base + number(lower, SPAN - 5 - RADIUS, 5) + j]
            sums[z.mid_all + n * RADIUS + j] = jnp.where(is_mid, a, b)
        for i in range(3):
            at = number(lower, 0, z.mid) + i
            sums[at] = sums[at] + jnp.where(is_mid, raw[base + number(lower, EDGE - 3, 0) + i], 0.0)
        for i in range(5):
            at = number(lower, 0, z.coarse) + i
            sums[at] = sums[at] + jnp.where(is_mid, 0.0, raw[base + number(lower, SPAN - 5, 0) + i])
    for n, route in enumerate(s.z2_routes):
        base = len(s.z_routes) * SPAN + n * z.second
        start = z.mid_all + number(route.below(), RADIUS - z.coarse, RADIUS + z.coarse - 5)
        for p in range(z.second):
            sums[start + p] = sums[start + p] + jnp.where(is_mid, 0.0, raw[base + p])

    up = s.x_routes[0].up()
    lane = iota((s.fine_rows, x.fine), 1)
    for g in range(s.fine_groups):
        ends = [jnp.zeros(lane.shape, F32)] * 2
        for j in range(min(s.side, s.fine_planes - g * s.side)):
            plane = fine[g * s.side + j]
            here = (lane >= RADIUS * j) & (lane < RADIUS * (j + 1))
            for n, start in enumerate((x.fine - RADIUS, 0)):
                shift = (RADIUS * j - start) % x.fine
                ends[n] = jnp.where(here, pltpu.roll(plane, shift, 1) if shift else plane, ends[n])
        rows = slice(g * s.fine_rows, (g + 1) * s.fine_rows)
        first[rows] = jnp.where(up, ends[0], ends[1])
        second[rows] = jnp.where(up, ends[1], ends[0])
    width = EDGE + SPAN
    row, lane = iota((2 * width, x.fine), 0), iota((2 * width, x.fine), 1)
    is_first = row < width
    goes_up = choose(up, is_first, ~is_first)
    slot = jnp.where(is_first, row, row - width)
    from_mid = jnp.where(goes_up, x.mid_all - EDGE + slot, slot)
    from_coarse = slot - EDGE + jnp.where(goes_up, x.mid_all + x.coarse_all - SPAN, x.mid_all)
    wanted = jnp.where(slot < EDGE, from_mid, from_coarse)
    picked_sums = pick((lane == wanted).astype(BF16), sums[...].reshape(s.sum_planes * s.sum_rows, x.fine))
    spare = s.sum_blocks * 128 - picked_sums.shape[1]
    if spare:
        picked_sums = jnp.concatenate([picked_sums, jnp.zeros((2 * width, spare), F32)], axis=1)
    for n, message in enumerate((first, second)):
        for b in range(s.sum_blocks):
            at = s.fine_ends + b * width
            message[at : at + width] = picked_sums[n * width : (n + 1) * width, b * 128 : (b + 1) * 128]


def band(taps, level, offset, valid):
    at = jnp.where(valid, offset + RADIUS, -1)
    out = [jnp.zeros(at.shape, F32) for _ in range(TERMS)]
    for tap in range(TAPS):
        here = at == tap
        out = [jnp.where(here, taps[level, term, tap], total) for term, total in enumerate(out)]
    return out


def dot(a, b):
    return jnp.dot(a, b, precision=EXACT, preferred_element_type=F32)


def z_columns(s):
    return s.z.fine * RADIUS


def lower_x(x):
    return x.index() > 0


def higher_x(x):
    return x.index() < x.count - 1


def operator_kernel(s, taps, x_fine, x_sums, ends, y_fine, y_mid, y_coarse, widen_x, widen_y):
    y, x = s.y, s.x
    own, edge = x.fine, 64
    shape = (own + edge, x.fine)
    row, lane = iota(shape, 0), iota(shape, 1)
    t = row - own
    lower, higher = x.index() > 0, x.index() < x.count - 1
    is_own = row < own

    def place(half, own_place, own_valid, first, count, low_place, high_place):
        is_low = t < half
        r = jnp.where(is_low, t, t - half) - first
        there = (r >= 0) & (r < count) & (t < 2 * half) & choose(is_low, lower, higher)
        valid = choose(is_own, own_valid, there)
        return jnp.where(is_own, own_place, jnp.where(is_low, low_place + r, high_place + r)), valid

    half = s.edge_sums
    fine = band(taps, 0, row - lane, is_own)
    where, valid = place(half, row - 1, row < x.mid_all, 0, EDGE, 2 - EDGE, x.mid - 1)
    mid = band(taps, 1, where - (lane - 1), valid & (lane < x.mid_all))
    first = x.mid_all
    inside = (row >= first) & (row < first + x.coarse_all)
    where, valid = place(half, row - first - 2, inside, EDGE, SPAN, 3 - SPAN, x.coarse - 2)
    side = x.fine // TERMS
    column = lane % side
    terms = band(taps, 2, where - (column - 2), valid & (column < x.coarse_all))
    coarse = terms[0]
    for term in range(1, TERMS):
        coarse = jnp.where(lane >= term * side, terms[term], coarse)
    a, b = iota((x.fine, x.fine), 0), iota((x.fine, x.fine), 1)
    from_mid = jnp.where((a < x.mid_all) & x.holds_mid(a - 1), weight_of(b - 2 * (a - 1)), 0.0)
    c = a % side
    from_coarse = jnp.where((c < x.coarse_all) & x.holds_coarse(c - 2), weight_of(b - 1 - 2 * (c - 2)), 0.0)
    high, low = split(dot(from_coarse, from_mid))
    widen_x[:own] = high
    widen_x[own : 2 * own] = high
    widen_x[2 * own :] = low
    columns = [(x_fine, 0, 0, fine)]
    columns += [(x_sums, half, 0, [dot(m, from_mid) for m in mid])]
    columns += [(x_sums, half, TERMS * x.fine, [coarse])]
    for out, half, at, terms in columns:
        for term, matrix in enumerate(terms):
            high, low = split(matrix)
            cols = slice(at + term * x.fine, at + (term + 1) * x.fine)
            n = 2 * half
            out[0:own, cols] = high[:own]
            out[own : 2 * own, cols] = high[:own]
            out[2 * own : 3 * own, cols] = low[:own]
            if n:
                out[3 * own :, cols] = jnp.zeros((out.shape[0] - 3 * own, x.fine), BF16)
                out[3 * own : 3 * own + n, cols] = high[own : own + n]
                out[3 * own + n : 3 * own + 2 * n, cols] = high[own : own + n]
                out[3 * own + 128 : 3 * own + 128 + n, cols] = low[own : own + n]

    z, slots, wide = s.z, s.side * s.fine_groups, z_columns(s)
    slot, column = iota((slots, wide), 0), iota((slots, wide), 1)
    where, valid = slot, slot < z.fine
    for n, route in enumerate(s.z_routes):
        lower, i, first = route.below(), z.index(), z.fine + n * RADIUS
        here = (slot >= first) & (slot < first + RADIUS)
        where = jnp.where(here, slot - first + jnp.where(lower, -RADIUS, z.fine), where)
        valid = choose(here, choose(lower, i >= 1, i + 1 < z.count), valid)
    planes = band(taps, 0, where - column // RADIUS, valid)
    r, c = iota((RADIUS, wide), 0), iota((RADIUS, wide), 1) % RADIUS
    cells = (slots, RADIUS, wide)
    for side, (offset, valid) in enumerate(((r - c - RADIUS, lower_x(x)), (r - c + RADIUS, higher_x(x)))):
        columns = band(taps, 0, offset, choose(valid, r >= 0, r < 0))
        for term in range(TERMS):
            joint = jnp.broadcast_to(planes[term][:, None, :], cells) * jnp.broadcast_to(columns[term][None], cells)
            high, low = split(joint.reshape(slots * RADIUS, wide))
            at = 2 * term + side
            ends[at, : slots * RADIUS] = high
            ends[at, slots * RADIUS : 2 * slots * RADIUS] = high
            ends[at, 2 * slots * RADIUS :] = low

    lower, higher = y.index() > 0, y.index() < y.count - 1
    far_below = s.y2_routes[0].below()
    n = up8(y.mid_all)

    def write(out, size, terms):
        part = iota(terms[0].shape, 1) >= 2 * size
        for term, matrix in enumerate(terms):
            high, low = split(matrix)
            n = matrix.shape[0]
            out[term * n : (term + 1) * n] = jnp.where(part, low.astype(F32), high.astype(F32)).astype(BF16)

    def columns_of(rows, size):
        lane = iota((rows, 3 * size), 1)
        return jnp.where(lane >= 2 * size, lane - 2 * size, jnp.where(lane >= size, lane - size, lane))

    c = columns_of(y.fine, s.fine_rows)
    is_low = (c >= y.fine) & (c < y.fine + RADIUS)
    is_high = c >= y.fine + RADIUS
    where = jnp.where(is_low, c - y.fine - RADIUS, jnp.where(is_high, c - RADIUS, c))
    valid = choose(is_low, lower, choose(is_high, higher, c >= 0))
    write(y_fine, s.fine_rows, band(taps, 0, where - iota(c.shape, 0), valid))

    c = columns_of(n, s.sum_rows)
    r = iota(c.shape, 0)
    is_low = (c >= s.low) & (c < s.low + SPAN)
    is_high = (c >= s.high) & (c < s.high + SPAN)
    is_far = (c >= s.far) & (c < s.far + y.second)
    where = jnp.where(is_low, c - s.low + 2 - SPAN, jnp.where(is_high, c - s.high + y.mid - 1, c - 1))
    valid = choose(is_low, lower, choose(is_high, higher, c < y.mid_all))
    mid = band(taps, 1, where - (r - 1), valid & (r < y.mid_all))
    far = jnp.where(far_below, -2 - y.coarse, 2 * y.coarse - 2)
    where = jnp.where(is_low, c - s.low + 3 - SPAN, jnp.where(is_high, c - s.high + y.coarse - 2, c - 2))
    where = jnp.where(is_far, c - s.far + far, where)
    valid = choose(is_low, lower, choose(is_high, higher, (c < y.coarse_all) | is_far))
    coarse = band(taps, 2, where - (r - 2), valid & (r < y.coarse_all))
    o, k = iota((y.fine, n), 0), iota((y.fine, n), 1)
    from_mid = jnp.where((k < y.mid_all) & y.holds_mid(k - 1), weight_of(o - 2 * (k - 1)), 0.0)
    m = s.coarse_rows
    c = columns_of(n, m)
    k = iota(c.shape, 0)
    from_coarse = jnp.where((c < y.coarse_all) & y.holds_coarse(c - 2), weight_of(k - 1 - 2 * (c - 2)), 0.0)
    write(y_mid, s.sum_rows, [dot(from_mid, matrix) for matrix in mid])
    write(y_coarse, s.sum_rows, [matrix[:m] for matrix in coarse])
    write(widen_y, m, [dot(from_mid, from_coarse)])


def contract_y(s, weights, high, low):
    joined = jnp.concatenate([high, low, high], axis=0)
    result = jnp.dot(weights[...], joined, preferred_element_type=F32)
    n, m = s.y.fine, s.x.fine
    return [result[t * n : (t + 1) * n, t * m : (t + 1) * m] for t in range(TERMS)]


def contract_z(weight, held, base, count):
    totals = [None] * count
    for t in range(held.shape[1]):
        for j in range(count + TAPS - 1):
            plane = held[base + j, t]
            for i in range(max(0, j - TAPS + 1), min(count, j + 1)):
                term = weight(t, j - i) * plane
                totals[i] = term if totals[i] is None else totals[i] + term
    return totals


def slab_starts(s, below_at, above_at):
    result = []
    for route in s.z_routes:
        lower, i = route.below(), s.z.index()
        valid = choose(lower, i >= 1, i + 1 < s.z.count)
        result.append((jnp.where(lower, below_at, above_at), valid))
    return result


def store_terms(held, at, valid, parts):
    for t, part in enumerate(parts):
        held[at, t] = part if valid is None else jnp.where(valid, part, 0.0)


BLOCK = 4


def own_kernel(s, taps, fine, sums, x_fine, x_sums, y_fine, fine_part, sums_part, t_fine):
    z, x = s.z, s.x

    def along_x(grid, weights):
        high, low = split(grid)
        joined = jnp.concatenate([high, low, high], axis=1)
        return jnp.dot(joined, weights[: 3 * x.fine], preferred_element_type=F32)

    t_fine[...] = jnp.zeros(t_fine.shape, F32)
    fine_at = [(RADIUS + p, None) for p in range(z.fine)]
    for start, valid in slab_starts(s, 0, z.fine + RADIUS):
        fine_at += [(start + p, valid) for p in range(RADIUS)]

    def fine_group(g, count):
        n = s.fine_rows
        a, b = split(along_x(fine[g : g + count].reshape(count * n, x.fine), x_fine))
        for p in range(count):
            rows = slice(p * n, (p + 1) * n)
            store_terms(t_fine, *fine_at[g + p], contract_y(s, y_fine, a[rows], b[rows]))

    def fine_block(k):
        for i, total in enumerate(contract_z(lambda t, d: taps[0, t, d], t_fine, k, BLOCK)):
            fine_part[k + i] = total

    def sum_part(g, count):
        n = s.sum_rows
        grid = sums[g : g + count].reshape(count * n, x.fine)
        sums_part[g * n : (g + count) * n] = along_x(grid, x_sums)

    later = []
    done = 0
    for g in list(range(z.fine, s.fine_planes, 8)) + list(range(0, z.fine, 8)):
        fine_group(g, 8)
        while later:
            later.pop(0)()
        if g < z.fine:
            ready = g if g + 8 < z.fine else z.fine
            later += [lambda k=k: fine_block(k) for k in range(done, ready, BLOCK)]
            done = max(done, ready)
    starts = list(range(0, s.sum_planes, 8))
    while later or starts:
        if starts:
            sum_part(starts[0], min(8, s.sum_planes - starts[0]))
            starts.pop(0)
        if later:
            later.pop(0)()


def sum_kernel(s, taps, fine, sums, first, second, x_sums, ends, y_fine, y_mid, y_coarse, widen_x, widen_y, out, *scratch):
    sums_ends, t_mid, t_coarse, p_mid, p_coarse, narrow = scratch
    z, y, x = s.z, s.y, s.x
    below = s.x_routes[0].below()
    half = s.edge_sums
    for b in range(s.sum_blocks):
        at = slice(s.fine_ends + b * half, s.fine_ends + (b + 1) * half)
        one, two = first[at], second[at]
        rows = [jnp.where(below, one, two), jnp.where(below, two, one)] * 2
        rows.append(jnp.zeros((128 - 4 * half, 128), F32))
        sums_ends[b * 128 : (b + 1) * 128] = jnp.concatenate(rows, axis=0).T

    def along_x(start, rows):
        edge_high, edge_low = split(sums_ends[start : start + rows])
        is_high = iota(edge_high.shape, 1) < 2 * half
        packed = jnp.where(is_high, edge_high.astype(F32), edge_low.astype(F32)).astype(BF16)
        joined = jnp.concatenate([packed, edge_high], axis=1)
        part = jnp.dot(joined, x_sums[3 * x.fine :], preferred_element_type=F32)
        return split(sums[start : start + rows] + part)

    def fine_edges():
        columns = []
        for flip in range(2):
            for g in range(s.fine_groups):
                at = slice(g * s.fine_rows, (g + 1) * s.fine_rows)
                pair = (first[at], second[at])
                columns.append(jnp.where(below, pair[flip], pair[1 - flip]))
        high, low = split(jnp.concatenate(columns, axis=1))
        joined = jnp.concatenate([high, low, high], axis=0)
        high, low = split(jnp.dot(y_fine[...], joined, preferred_element_type=F32))
        width = s.fine_groups * x.fine
        result = []
        for side in range(2):
            total = 0.0
            for t in range(TERMS):
                rows, cols = slice(t * y.fine, (t + 1) * y.fine), slice(side * width, (side + 1) * width)
                a, b = high[rows, cols], low[rows, cols]
                joined = jnp.concatenate([a, b, a], axis=1)
                total = total + jnp.dot(joined, ends[2 * t + side], preferred_element_type=F32)
            result.append(total)
        return result

    t_mid[...] = jnp.zeros(t_mid.shape, F32)
    t_coarse[...] = jnp.zeros(t_coarse.shape, F32)
    mid_at = [(RADIUS + p, None) for p in range(z.mid_all)]
    coarse_at = [(RADIUS + p if p < z.coarse_all else None, None) for p in range(z.mid_all)]
    for start, valid in slab_starts(s, 0, z.mid + 3 + RADIUS):
        mid_at += [(start + p, valid) for p in range(RADIUS)]
    for start, valid in slab_starts(s, 0, z.coarse + 5 + RADIUS):
        coarse_at += [(start + p, valid) for p in range(RADIUS)]
    is_second = iota((s.coarse_rows, x.fine), 1) >= x.fine // TERMS
    coarse_taps = [jnp.where(is_second, taps[2, 1, d], taps[2, 0, d]) for d in range(TAPS)]

    def sum_group(g, count):
        n = s.sum_rows
        a, b = along_x(g * n, count * n)
        for p in range(count):
            rows = slice(p * n, (p + 1) * n)
            at, valid = mid_at[g + p]
            cols = slice(0, TERMS * x.fine)
            store_terms(t_mid, at, valid, contract_y(s, y_mid, a[rows, cols], b[rows, cols]))
            at, valid = coarse_at[g + p]
            if at is not None:
                cols = slice(TERMS * x.fine, (TERMS + 1) * x.fine)
                joined = jnp.concatenate([a[rows, cols], b[rows, cols], a[rows, cols]], axis=0)
                both = jnp.dot(y_coarse[...], joined, preferred_element_type=F32)
                m = s.coarse_rows
                store_terms(t_coarse, at, valid, [jnp.where(is_second, both[m:], both[:m])])

    def coarse_block(k):
        count = min(BLOCK, z.coarse_all - k)
        for i, total in enumerate(contract_z(lambda t, d: coarse_taps[d], t_coarse, k, count)):
            narrow[k + i] = jnp.where(z.holds_coarse(k + i - 2), total, 0.0)

    def widen():
        m = s.coarse_rows
        high, low = split(narrow[...].reshape(z.coarse_all * m, x.fine))
        joined = jnp.concatenate([high, low, high], axis=1)
        high, low = split(jnp.dot(joined, widen_x[...], preferred_element_type=F32))
        for p in range(z.coarse_all):
            rows = slice(p * m, (p + 1) * m)
            joined = jnp.concatenate([high[rows], low[rows], high[rows]], axis=0)
            p_coarse[p] = jnp.dot(widen_y[...], joined, preferred_element_type=F32)

    def mid_block(k):
        count = min(BLOCK, z.mid_all - k)
        for i, total in enumerate(contract_z(lambda t, d: taps[1, t, d], t_mid, k, count)):
            m = k + i - 1
            for offset, weight in WEIGHTS:
                if (m - offset) % 2 == 0 and 0 <= (m - offset) // 2 + 2 < z.coarse_all:
                    total = total + weight * p_coarse[(m - offset) // 2 + 2]
            p_mid[k + i] = jnp.where(z.holds_mid(m), total, 0.0)

    groups = list(range(z.mid_all, s.sum_planes, 4)) + list(range(0, z.mid_all, 4))
    for g in groups:
        sum_group(g, min(4, s.sum_planes - g if g >= z.mid_all else z.mid_all - g))
    edges = fine_edges()
    for k in range(0, z.coarse_all, BLOCK):
        coarse_block(k)
    widen()
    for k in range(0, z.mid_all, BLOCK):
        mid_block(k)
    lane = iota((y.fine, x.fine), 1)
    for k in range(z.fine):
        total = fine[k]
        for offset, weight in WEIGHTS:
            if (k - offset) % 2 == 0:
                total = total + weight * p_mid[(k - offset) // 2 + 1]
        block, at = k // s.side, k % s.side * RADIUS
        low, high = (edge[:, block * x.fine : (block + 1) * x.fine] for edge in edges)
        low = pltpu.roll(low, -at % x.fine, 1) if at else low
        turn = (x.fine - RADIUS - at) % x.fine
        high = pltpu.roll(high, turn, 1) if turn else high
        total = total + jnp.where(lane < RADIUS, low, jnp.where(lane >= x.fine - RADIUS, high, 0.0))
        out[k] = total


def call(kernel, outs, ins, scratch=(), flops=10**7):
    specs = [SMEM if a.ndim == 3 and a.shape[-1] == TAPS else VMEM for a in ins]
    size = sum(a.size * a.dtype.itemsize for a in ins) + sum(o.size * o.dtype.itemsize for o in outs)
    return pl.pallas_call(
        kernel,
        out_shape=tuple(outs),
        in_specs=specs,
        out_specs=tuple(VMEM for _ in outs),
        scratch_shapes=list(scratch),
        compiler_params=PARAMS,
        cost_estimate=pl.CostEstimate(flops=flops, bytes_accessed=size, transcendentals=0),
    )(*ins)


def array(*shape, dtype=F32):
    return jax.ShapeDtypeStruct(shape, dtype)


def local(charges, kernel_taps):
    z, y, x = (Cut(name, size) for name, size in zip(("gz", "gy", "gx"), charges.shape))
    s = Sizes(z, y, x)
    n = x.fine
    nz, nz2 = len(s.z_routes), len(s.z2_routes)

    def bound(kernel, *static):
        return lambda *refs: kernel(s, *static, *refs)

    rows = up8(y.mid_all)
    held, own, ahead, behind, *messages = call(
        bound(restrict_kernel, nz),
        [array(*charges.shape), array(z.mid_all, rows, n)] + [array(s.y_rows, n)] * 2 + [array(s.z_rows, n)] * nz + [array(s.z2_rows, n)] * nz2,
        [charges],
        [
            pltpu.VMEM((z.fine, y.fine + 16, n), F32),
            pltpu.VMEM((z.mid_all, rows, n), F32),
            pltpu.VMEM((z.mid_all, up8(y.mid + 24), n), F32),
            pltpu.VMEM((z.mid_all, rows, n), F32),
            pltpu.VMEM((2, s.z_rows - s.z_fine, n), F32),
        ],
    )
    z_got = [route(m) for route, m in zip(s.z_routes + s.z2_routes, messages)]
    sides = [s.y_routes[0](ahead), s.y_routes[1](behind)]
    operators = call(
        bound(operator_kernel),
        [
            array(3 * n, TERMS * n, dtype=BF16),
            array(3 * n + 256, (TERMS + 1) * n, dtype=BF16),
            array(2 * TERMS, 3 * s.fine_groups * n, z_columns(s), dtype=BF16),
            array(TERMS * y.fine, 3 * s.fine_rows, dtype=BF16),
            array(TERMS * y.fine, 3 * s.sum_rows, dtype=BF16),
            array(TERMS * s.coarse_rows, 3 * s.sum_rows, dtype=BF16),
            array(3 * n, n, dtype=BF16),
            array(y.fine, 3 * s.coarse_rows, dtype=BF16),
        ],
        [kernel_taps],
    )
    ahead, behind, far = call(
        bound(spread_kernel, nz, nz2),
        [array(s.slab_rows, n), array(s.slab_rows, n), array(s.far_rows, n)],
        [operators[-1], own, *z_got],
        [pltpu.VMEM((s.far_groups, s.far_rows, n), F32)],
    )
    sides += [s.y_routes[0](ahead), s.y_routes[1](behind)]
    far = s.y2_routes[0](far)
    fine, sums, first, second = call(
        bound(collect_kernel, nz, nz2),
        [
            array(s.fine_planes, s.fine_rows, n),
            array(s.sum_planes, s.sum_rows, n),
            array(s.x_rows, n),
            array(s.x_rows, n),
        ],
        [held, own, *z_got, *sides, far],
        [pltpu.VMEM((s.slab_planes, s.sum_rows, n), F32), pltpu.VMEM((s.far_groups, s.far_rows, n), F32)],
    )
    first, second = s.x_routes[0](first), s.x_routes[1](second)
    x_fine, x_sums, ends, y_fine, y_mid, y_coarse, widen_x, widen_y = operators
    fine, sums = call(
        bound(own_kernel),
        [array(z.fine, y.fine, n), array(s.sum_planes * s.sum_rows, (TERMS + 1) * n)],
        [kernel_taps, fine, sums, x_fine, x_sums, y_fine],
        [pltpu.VMEM((z.fine + 2 * RADIUS, TERMS, y.fine, n), F32)],
    )
    (out,) = call(
        bound(sum_kernel),
        [array(z.fine, y.fine, n)],
        [kernel_taps, fine, sums, first, second, x_sums, ends, y_fine, y_mid, y_coarse, widen_x, widen_y],
        [
            pltpu.VMEM((s.sum_blocks * 128, n), F32),
            pltpu.VMEM((z.mid + 2 * RADIUS + 3, TERMS, y.fine, n), F32),
            pltpu.VMEM((z.coarse + 2 * RADIUS + 5, 1, s.coarse_rows, n), F32),
            pltpu.VMEM((z.mid_all, y.fine, n), F32),
            pltpu.VMEM((z.coarse_all, y.fine, n), F32),
            pltpu.VMEM((z.coarse_all, s.coarse_rows, n), F32),
        ],
    )
    return out


def solution(mesh):
    return jax.shard_map(
        local,
        mesh=mesh,
        in_specs=(P("gz", "gy", "gx"), P()),
        out_specs=P("gz", "gy", "gx"),
        check_vma=False,
    )
```

```python
import jax
import jax.numpy as jnp
from jax import lax
from jax.experimental import pallas as pl
from jax.experimental.pallas import tpu as pltpu
from jax.sharding import PartitionSpec as P

RADIUS = 8
TAPS = 17
TERMS = 2
WEIGHTS = ((-3, -0.0625), (-1, 0.5625), (0, 1.0), (1, 0.5625), (3, -0.0625))
EXACT = lax.Precision.HIGHEST
SPAN = RADIUS + 5
EDGE = RADIUS + 3
F32, BF16 = jnp.float32, jnp.bfloat16
PARAMS = pltpu.CompilerParams(vmem_limit_bytes=32 * 1024 * 1024)
VMEM = pl.BlockSpec(memory_space=pltpu.VMEM)
SMEM = pl.BlockSpec(memory_space=pltpu.SMEM)


def up8(n):
    return -(-n // 8) * 8


def iota(shape, dim):
    return lax.broadcasted_iota(jnp.int32, shape, dim)


def weight_of(difference):
    size = jnp.abs(difference)
    out = jnp.where(size == 1, 0.5625, jnp.where(size == 3, -0.0625, 0.0))
    return jnp.where(size == 0, 1.0, out)


def choose(condition, a, b):
    return jnp.where(condition, jnp.where(a, 1, 0), jnp.where(b, 1, 0)) != 0


class Cut:
    def __init__(self, name, length):
        self.name, self.fine = name, length
        self.count = lax.axis_size(name)
        self.mid, self.coarse = length // 2, length // 4
        self.mid_all, self.coarse_all = self.mid + 3, self.coarse + 5
        self.second = max(SPAN - self.coarse, 0)

    def index(self):
        return lax.axis_index(self.name)

    def holds_mid(self, k):
        k = k + self.index() * self.mid
        return (k >= 0) & (k < self.mid * self.count)

    def holds_coarse(self, k):
        k = k + self.index() * self.coarse
        return (k >= 0) & (k < self.coarse * self.count)


class Route:
    def __init__(self, names, pairs, up, below):
        self.names, self.pairs, self.up, self.below = names, pairs, up, below

    def __call__(self, x):
        return lax.ppermute(x, self.names, self.pairs)


def flip(pairs):
    return [(b, a) for a, b in pairs]


def swap(cut, steps):
    pairs = [(i, i + steps) for i in range(cut.count - steps)]

    def up():
        return cut.index() + steps < cut.count

    return [Route(cut.name, pairs + flip(pairs), up, lambda: ~up())]


def both_ways(cut, steps):
    pairs = [(i, i + steps) for i in range(cut.count - steps)]
    yes, no = (lambda: cut.index() >= 0), (lambda: cut.index() < 0)
    return [Route(cut.name, pairs, yes, yes), Route(cut.name, flip(pairs), no, no)]


def folded(cut, beside, names):
    n, m = cut.count, lax.axis_size(beside)

    def place(c, i):
        return c * n + i if names[0] == beside else i * m + c

    pairs = []
    for c in range(0, m, 2):
        cycle = [place(c, i) for i in range(n)] + [place(c + 1, i) for i in reversed(range(n))]
        pairs += list(zip(cycle, cycle[1:] + cycle[:1]))

    def even():
        return lax.axis_index(beside) % 2 == 0

    def odd():
        return lax.axis_index(beside) % 2 == 1

    return [Route(names, pairs, even, even), Route(names, flip(pairs), odd, odd)]


def split(x):
    high = x.astype(BF16)
    return high, (x - high.astype(F32)).astype(BF16)


def pick(selector, x):
    nt = (((1,), (1,)), ((), ()))
    a = x.astype(BF16)
    rest = x - a.astype(F32)
    b = rest.astype(BF16)
    c = (rest - b.astype(F32)).astype(BF16)
    out = lax.dot_general(selector, c, nt, preferred_element_type=F32)
    out = out + lax.dot_general(selector, b, nt, preferred_element_type=F32)
    return out + lax.dot_general(selector, a, nt, preferred_element_type=F32)


class Sizes:
    def __init__(self, z, y, x):
        self.z, self.y, self.x = z, y, x
        self.z_routes = swap(z, 1) if z.count <= 2 else both_ways(z, 1)
        self.z2_routes = [] if z.count <= 2 else swap(z, 2) if z.count <= 4 else both_ways(z, 2)
        self.y_routes = folded(y, x.name, (x.name, y.name))
        self.y2_routes = swap(y, 2)
        self.x_routes = folded(x, z.name, (x.name, z.name))
        self.z_fine = RADIUS * y.fine
        self.z_sums = max(EDGE * y.mid_all, SPAN * y.coarse_all)
        self.z_rows = up8(self.z_fine + self.z_sums)
        self.z2_rows = up8(z.second * y.coarse_all)
        self.slab_planes = SPAN * len(self.z_routes) + z.second * len(self.z2_routes)
        self.fine_planes = z.fine + RADIUS * len(self.z_routes)
        self.sum_planes = z.mid_all + RADIUS * len(self.z_routes)
        self.coarse_rows = -(-y.coarse_all // 16) * 16
        self.y_fine = RADIUS * z.fine
        self.y_rows = up8(self.y_fine + SPAN * z.mid_all)
        self.slab_fine = RADIUS * RADIUS * len(self.z_routes)
        self.slab_rows = up8(self.slab_fine + SPAN * self.slab_planes)
        self.far_groups = x.fine // x.coarse_all
        self.far_planes = -(-(z.coarse_all + self.slab_planes) // self.far_groups)
        self.far_rows = up8(y.second * self.far_planes)
        self.fine_rows = y.fine + 2 * RADIUS
        self.far = y.coarse_all
        self.low = y.mid_all
        self.high = self.low + SPAN
        self.sum_rows = -(-(self.high + SPAN) // 16) * 16
        self.edge_sums = EDGE + SPAN
        self.side = x.fine // RADIUS
        self.fine_groups = -(-self.fine_planes // self.side)
        self.fine_ends = self.fine_groups * self.fine_rows
        self.sum_blocks = -(-self.sum_planes * self.sum_rows // 128)
        self.x_rows = self.fine_ends + self.sum_blocks * self.edge_sums
        assert x.mid_all + x.coarse_all <= x.fine
        assert self.far + y.second <= self.low and y.coarse_all == SPAN
        assert z.coarse >= RADIUS and y.coarse >= RADIUS and y.count == 4


def restrict_kernel(s, nz, source, charges, own, ahead, behind, *rest):
    messages, (wide, mid, high, coarse, packed) = rest[:-5], rest[-5:]
    z, y, x = s.z, s.y, s.x
    lanes = (x.fine, x.fine)
    cell, lane = iota(lanes, 0), iota(lanes, 1)
    k = lane - 1
    to_mid = jnp.where((lane < x.mid_all) & x.holds_mid(k), weight_of(cell - 2 * k), 0.0)
    c = lane - x.mid_all - 2
    inside = (lane >= x.mid_all) & (lane < x.mid_all + x.coarse_all) & x.holds_coarse(c)
    to_coarse = jnp.where(inside, weight_of(cell - 1 - 2 * c), 0.0)
    narrow = to_mid + jnp.dot(to_mid, to_coarse, precision=EXACT, preferred_element_type=F32)
    wide[...] = jnp.zeros(wide.shape, F32)
    charges[...] = source[...]
    cells = source[...].reshape(z.fine * y.fine, x.fine)
    top, rest = cells.astype(BF16), cells
    rest = rest - top.astype(F32)
    middle = rest.astype(BF16)
    low = (rest - middle.astype(F32)).astype(BF16)
    weights = jnp.concatenate(split(narrow), axis=1)
    both = jnp.dot(low, weights, preferred_element_type=F32)
    both = both + jnp.dot(
        jnp.concatenate([top, middle], axis=1), jnp.concatenate([weights, weights], axis=0), preferred_element_type=F32
    )
    reduced = both[:, : x.fine] + both[:, x.fine :]
    wide[:, 8 : 8 + y.fine, :] = reduced.reshape(z.fine, y.fine, x.fine)
    rows = 0.0
    for offset, weight in WEIGHTS:
        rows = rows + weight * wide[:, pl.ds(6 + offset, y.mid_all, stride=2), :]
    keep = y.holds_mid(iota((y.mid_all, x.fine), 0) - 1)
    mid[...] = jnp.zeros(mid.shape, F32)
    coarse[...] = jnp.zeros(coarse.shape, F32)
    high[...] = jnp.zeros(high.shape, F32)
    for p in range(z.mid_all):
        total = 0.0
        for offset, weight in WEIGHTS:
            at = 2 * (p - 1) + offset
            if 0 <= at < z.fine:
                total = total + weight * rows[at]
        total = jnp.where(keep & z.holds_mid(p - 1), total, 0.0)
        mid[p, : y.mid_all] = total
        high[p, 8 : 8 + y.mid_all] = total
    rows = 0.0
    for offset, weight in WEIGHTS:
        rows = rows + weight * high[:, pl.ds(5 + offset, y.coarse_all, stride=2), :]
    keep = y.holds_coarse(iota((y.coarse_all, x.fine), 0) - 2)
    for p in range(z.coarse_all):
        total = 0.0
        for offset, weight in WEIGHTS:
            at = 2 * (p - 2) + offset + 1
            if 0 <= at < z.mid_all:
                total = total + weight * rows[at]
        coarse[p, : y.coarse_all] = jnp.where(keep & z.holds_coarse(p - 2), total, 0.0)
    is_mid = iota(mid.shape[1:], 1) < x.mid_all
    for p in range(z.mid_all):
        own[p] = jnp.where(is_mid, mid[p], coarse[p]) if p < z.coarse_all else jnp.where(is_mid, mid[p], 0.0)
    is_side = iota((SPAN, x.fine), 1) < x.mid_all
    for message, route in zip((ahead, behind), s.y_routes):
        up = route.up()
        edge = jnp.where(up, charges[:, y.fine - RADIUS :, :], charges[:, :RADIUS, :])
        message[: s.y_fine] = edge.reshape(s.y_fine, x.fine)
        for p in range(z.mid_all):
            last = jnp.where(is_side, own[p, y.mid_all - SPAN : y.mid_all], own[p, y.coarse_all - SPAN : y.coarse_all])
            at = s.y_fine + p * SPAN
            message[at : at + SPAN] = jnp.where(up, last, own[p, :SPAN])
        filled = s.y_fine + SPAN * z.mid_all
        if filled < s.y_rows:
            message[filled:] = jnp.zeros((s.y_rows - filled, x.fine), F32)
    for message, route in zip(messages, s.z_routes):
        up = route.up().astype(jnp.int32)
        message[: s.z_fine] = charges[pl.ds(up * (z.fine - RADIUS), RADIUS)].reshape(s.z_fine, x.fine)
        packed[...] = jnp.zeros(packed.shape, F32)
        for p in range(EDGE):
            packed[0, p * y.mid_all : (p + 1) * y.mid_all] = mid[up * (z.mid_all - EDGE) + p][: y.mid_all]
        for p in range(SPAN):
            plane = coarse[up * (z.coarse_all - SPAN) + p]
            packed[1, p * y.coarse_all : (p + 1) * y.coarse_all] = plane[: y.coarse_all]
        is_mid = iota(packed.shape[1:], 1) < x.mid_all
        message[s.z_fine :] = jnp.where(is_mid, packed[0], packed[1])
    for message, route in zip(messages[nz:], s.z2_routes):
        up = route.up().astype(jnp.int32)
        message[...] = jnp.zeros(message.shape, F32)
        for p in range(z.second):
            plane = coarse[up * (z.coarse_all - z.second) + p]
            message[p * y.coarse_all : (p + 1) * y.coarse_all] = plane[: y.coarse_all]


class Slab:
    def __init__(self, message, mid, coarse):
        self.message, self.mid, self.coarse = message, mid, coarse

    def coarse_rows(self, first, count):
        return self.message[self.coarse + first : self.coarse + first + count]

    def rows(self, is_mid, first_mid, first_coarse, count):
        coarse = 0.0 if first_coarse is None else self.coarse_rows(first_coarse, count)
        mid = 0.0 if self.mid is None else self.message[self.mid + first_mid : self.mid + first_mid + count]
        return jnp.where(is_mid, mid, coarse)


def slabs(s, z_messages, z2_messages):
    out = []
    for message in z_messages:
        for p in range(SPAN):
            mid = s.z_fine + p * s.y.mid_all if p < EDGE else None
            out.append(Slab(message, mid, s.z_fine + p * s.y.coarse_all))
    for message in z2_messages:
        out += [Slab(message, None, p * s.y.coarse_all) for p in range(s.z.second)]
    return out


def spread_kernel(s, nz, nz2, _, own, *rest):
    z_messages, z2_messages = rest[:nz], rest[nz : nz + nz2]
    ahead, behind, far, rows = rest[-4:]
    z, y, x = s.z, s.y, s.x
    is_mid = iota((SPAN, x.fine), 1) < x.mid_all
    planes = slabs(s, z_messages, z2_messages)
    for message, route in zip((ahead, behind), s.y_routes):
        up = route.up()
        at = 0
        for z_message in z_messages:
            slab = z_message[: s.z_fine].reshape(RADIUS, y.fine, x.fine)
            edge = jnp.where(up, slab[:, y.fine - RADIUS :], slab[:, :RADIUS])
            message[at : at + RADIUS * RADIUS] = edge.reshape(RADIUS * RADIUS, x.fine)
            at += RADIUS * RADIUS
        for plane in planes:
            last = plane.rows(is_mid, y.mid_all - SPAN, y.coarse_all - SPAN, SPAN)
            message[at : at + SPAN] = jnp.where(up, last, plane.rows(is_mid, 0, 0, SPAN))
            at += SPAN
        if at < s.slab_rows:
            message[at:] = jnp.zeros((s.slab_rows - at, x.fine), F32)
    up = s.y2_routes[0].up()
    count, end = y.second, y.coarse_all
    rows[...] = jnp.zeros(rows.shape, F32)
    pairs = [(own[p, end - count : end], own[p, :count]) for p in range(z.coarse_all)]
    pairs += [(plane.coarse_rows(end - count, count), plane.coarse_rows(0, count)) for plane in planes]
    for p, (last, start) in enumerate(pairs):
        g, at = p // s.far_planes, p % s.far_planes * count
        rows[g, at : at + count] = jnp.where(up, last, start)
    lane = iota(far.shape, 1)
    total = jnp.zeros(far.shape, F32)
    for g in range(s.far_groups):
        start = g * x.coarse_all
        turned = pltpu.roll(rows[g], (start - x.mid_all) % x.fine, 1)
        total = jnp.where((lane >= start) & (lane < start + x.coarse_all), turned, total)
    far[...] = total


def roll_ends(s, plane_rows, count):
    x = s.x
    lane = iota((count, x.fine), 1)
    for g in range(s.fine_groups):
        ends = [jnp.zeros(lane.shape, F32)] * 2
        for j in range(min(s.side, s.fine_planes - g * s.side)):
            plane = plane_rows(g * s.side + j)
            here = (lane >= RADIUS * j) & (lane < RADIUS * (j + 1))
            for n, start in enumerate((x.fine - RADIUS, 0)):
                shift = (RADIUS * j - start) % x.fine
                ends[n] = jnp.where(here, pltpu.roll(plane, shift, 1) if shift else plane, ends[n])
        yield g, ends


def early_kernel(s, nz, charges, *rest):
    z_messages = rest[:nz]
    x_fine, y_own, t_part, last, start, slab = rest[nz:]
    z, y, x = s.z, s.y, s.x
    for n, message in enumerate(z_messages):
        slab[n * RADIUS : (n + 1) * RADIUS] = message[: s.z_fine].reshape(RADIUS, y.fine, x.fine)

    def rows_of(p):
        return charges[p] if p < z.fine else slab[p - z.fine]

    t_part[...] = jnp.zeros(t_part.shape, F32)
    fine_at = fine_places(s)
    for g in range(0, s.fine_planes, 8):
        planes = charges[g : g + 8] if g < z.fine else slab[g - z.fine : g - z.fine + 8]
        a, b = split(contract_x(s, planes.reshape(8 * y.fine, x.fine), x_fine))
        for p in range(8):
            rows = slice(p * y.fine, (p + 1) * y.fine)
            store_terms(t_part, *fine_at[g + p], contract_y(s, y_own, a[rows], b[rows]))
    for g, ends in roll_ends(s, rows_of, y.fine):
        rows = slice(g * y.fine, (g + 1) * y.fine)
        last[rows], start[rows] = ends


def collect_kernel(s, nz, nz2, last, start, own, *rest):
    z_messages, z2_messages = rest[:nz], rest[nz : nz + nz2]
    rest = rest[nz + nz2 :]
    pairs = rest[:4]
    far, fine, sums, first, second, raw, rows = rest[4:]
    z, y, x = s.z, s.y, s.x
    below = s.y_routes[0].below()
    planes = slabs(s, z_messages, z2_messages)

    def sides(which, start, count):
        a, b = (message[start : start + count] for message in pairs[2 * which : 2 * which + 2])
        return jnp.where(below, a, b), jnp.where(below, b, a)

    parts = [(0, z.fine, 0, 0)] + [(z.fine + n * RADIUS, RADIUS, 1, n * RADIUS * RADIUS) for n in range(nz)]
    for at, count, which, row in parts:
        low, high = sides(which, row, RADIUS * count)
        fine[at : at + count, :RADIUS] = low.reshape(count, RADIUS, x.fine)
        fine[at : at + count, RADIUS:] = high.reshape(count, RADIUS, x.fine)
    sums[...] = jnp.zeros(sums.shape, F32)
    raw[...] = jnp.zeros(raw.shape, F32)
    for g in range(s.far_groups):
        rows[g] = pltpu.roll(far[...], (x.mid_all - g * x.coarse_all) % x.fine, 1)
    is_mid = iota((y.second, x.fine), 1) < x.mid_all

    def rows_of_plane(out, p, body, which, row, far_plane):
        low, high = sides(which, row, SPAN)
        out[p, : y.mid_all] = body
        out[p, s.low : s.low + SPAN] = low
        out[p, s.high : s.high + SPAN] = high
        if far_plane is not None:
            at = slice(s.far, s.far + y.second)
            start = far_plane % s.far_planes * y.second
            out[p, at] = jnp.where(is_mid, out[p, at], rows[far_plane // s.far_planes, start : start + y.second])

    for p in range(z.mid_all):
        far_plane = p if p < z.coarse_all else None
        rows_of_plane(sums, p, own[p, : y.mid_all], 0, s.y_fine + p * SPAN, far_plane)
    is_mid_row = iota((SPAN, x.fine), 1) < x.mid_all
    is_mid_rest = iota((y.mid_all - SPAN, x.fine), 1) < x.mid_all
    for p, plane in enumerate(planes):
        body = [plane.rows(is_mid_row, 0, 0, SPAN), plane.rows(is_mid_rest, SPAN, None, y.mid_all - SPAN)]
        rows_of_plane(raw, p, jnp.concatenate(body, axis=0), 1, s.slab_fine + p * SPAN, z.coarse_all + p)
    is_mid = iota((s.sum_rows, x.fine), 1) < x.mid_all

    def number(condition, a, b):
        return jnp.where(condition, a, b)

    for n, route in enumerate(s.z_routes):
        lower, base = route.below(), n * SPAN
        for j in range(RADIUS):
            a = raw[base + number(lower, 0, 3) + j]
            b = raw[base + number(lower, SPAN - 5 - RADIUS, 5) + j]
            sums[z.mid_all + n * RADIUS + j] = jnp.where(is_mid, a, b)
        for i in range(3):
            at = number(lower, 0, z.mid) + i
            sums[at] = sums[at] + jnp.where(is_mid, raw[base + number(lower, EDGE - 3, 0) + i], 0.0)
        for i in range(5):
            at = number(lower, 0, z.coarse) + i
            sums[at] = sums[at] + jnp.where(is_mid, 0.0, raw[base + number(lower, SPAN - 5, 0) + i])
    for n, route in enumerate(s.z2_routes):
        base = len(s.z_routes) * SPAN + n * z.second
        at = z.mid_all + number(route.below(), RADIUS - z.coarse, RADIUS + z.coarse - 5)
        for p in range(z.second):
            sums[at + p] = sums[at + p] + jnp.where(is_mid, 0.0, raw[base + p])

    up = s.x_routes[0].up()
    for g, ends in roll_ends(s, lambda p: fine[p], 2 * RADIUS):
        rows = slice(g * y.fine, (g + 1) * y.fine)
        at = slice(g * s.fine_rows, g * s.fine_rows + y.fine)
        first[at] = jnp.where(up, last[rows], start[rows])
        second[at] = jnp.where(up, start[rows], last[rows])
        at = slice(g * s.fine_rows + y.fine, (g + 1) * s.fine_rows)
        first[at] = jnp.where(up, ends[0], ends[1])
        second[at] = jnp.where(up, ends[1], ends[0])
    width = EDGE + SPAN
    row, lane = iota((2 * width, x.fine), 0), iota((2 * width, x.fine), 1)
    is_first = row < width
    goes_up = choose(up, is_first, ~is_first)
    slot = jnp.where(is_first, row, row - width)
    from_mid = jnp.where(goes_up, x.mid_all - EDGE + slot, slot)
    from_coarse = slot - EDGE + jnp.where(goes_up, x.mid_all + x.coarse_all - SPAN, x.mid_all)
    wanted = jnp.where(slot < EDGE, from_mid, from_coarse)
    picked_sums = pick((lane == wanted).astype(BF16), sums[...].reshape(s.sum_planes * s.sum_rows, x.fine))
    spare = s.sum_blocks * 128 - picked_sums.shape[1]
    if spare:
        picked_sums = jnp.concatenate([picked_sums, jnp.zeros((2 * width, spare), F32)], axis=1)
    for n, message in enumerate((first, second)):
        for b in range(s.sum_blocks):
            at = s.fine_ends + b * width
            message[at : at + width] = picked_sums[n * width : (n + 1) * width, b * 128 : (b + 1) * 128]


def band(taps, level, offset, valid):
    at = jnp.where(valid, offset + RADIUS, -1)
    out = [jnp.zeros(at.shape, F32) for _ in range(TERMS)]
    for tap in range(TAPS):
        here = at == tap
        out = [jnp.where(here, taps[level, term, tap], total) for term, total in enumerate(out)]
    return out


def dot(a, b):
    return jnp.dot(a, b, precision=EXACT, preferred_element_type=F32)


def z_columns(s):
    return s.z.fine * RADIUS


def lower_x(x):
    return x.index() > 0


def higher_x(x):
    return x.index() < x.count - 1


def operator_kernel(s, taps, x_fine, x_sums, ends, y_own, y_edge, y_fine, y_mid, y_coarse, widen_x, widen_y, table):
    y, x = s.y, s.x
    for level in range(2):
        for term in range(TERMS):
            for tap in range(TAPS):
                table[(level * TERMS + term) * TAPS + tap] = jnp.full((8, x.fine), taps[level, term, tap], F32)
    is_second = iota((8, x.fine), 1) >= x.fine // TERMS
    for tap in range(TAPS):
        table[2 * TERMS * TAPS + tap] = jnp.where(is_second, taps[2, 1, tap], taps[2, 0, tap])
    own, edge = x.fine, 64
    shape = (own + edge, x.fine)
    row, lane = iota(shape, 0), iota(shape, 1)
    t = row - own
    lower, higher = x.index() > 0, x.index() < x.count - 1
    is_own = row < own

    def place(half, own_place, own_valid, first, count, low_place, high_place):
        is_low = t < half
        r = jnp.where(is_low, t, t - half) - first
        there = (r >= 0) & (r < count) & (t < 2 * half) & choose(is_low, lower, higher)
        valid = choose(is_own, own_valid, there)
        return jnp.where(is_own, own_place, jnp.where(is_low, low_place + r, high_place + r)), valid

    half = s.edge_sums
    fine = band(taps, 0, row - lane, is_own)
    where, valid = place(half, row - 1, row < x.mid_all, 0, EDGE, 2 - EDGE, x.mid - 1)
    mid = band(taps, 1, where - (lane - 1), valid & (lane < x.mid_all))
    first = x.mid_all
    inside = (row >= first) & (row < first + x.coarse_all)
    where, valid = place(half, row - first - 2, inside, EDGE, SPAN, 3 - SPAN, x.coarse - 2)
    side = x.fine // TERMS
    column = lane % side
    terms = band(taps, 2, where - (column - 2), valid & (column < x.coarse_all))
    coarse = terms[0]
    for term in range(1, TERMS):
        coarse = jnp.where(lane >= term * side, terms[term], coarse)
    a, b = iota((x.fine, x.fine), 0), iota((x.fine, x.fine), 1)
    from_mid = jnp.where((a < x.mid_all) & x.holds_mid(a - 1), weight_of(b - 2 * (a - 1)), 0.0)
    c = a % side
    from_coarse = jnp.where((c < x.coarse_all) & x.holds_coarse(c - 2), weight_of(b - 1 - 2 * (c - 2)), 0.0)
    high, low = split(dot(from_coarse, from_mid))
    widen_x[:own] = high
    widen_x[own : 2 * own] = high
    widen_x[2 * own :] = low
    columns = [(x_fine, 0, 0, fine)]
    columns += [(x_sums, half, 0, [dot(m, from_mid) for m in mid])]
    columns += [(x_sums, half, TERMS * x.fine, [coarse])]
    for out, half, at, terms in columns:
        for term, matrix in enumerate(terms):
            high, low = split(matrix)
            cols = slice(at + term * x.fine, at + (term + 1) * x.fine)
            n = 2 * half
            out[0:own, cols] = high[:own]
            out[own : 2 * own, cols] = high[:own]
            out[2 * own : 3 * own, cols] = low[:own]
            if n:
                out[3 * own :, cols] = jnp.zeros((out.shape[0] - 3 * own, x.fine), BF16)
                out[3 * own : 3 * own + n, cols] = high[own : own + n]
                out[3 * own + n : 3 * own + 2 * n, cols] = high[own : own + n]
                out[3 * own + 128 : 3 * own + 128 + n, cols] = low[own : own + n]

    z, slots, wide = s.z, s.side * s.fine_groups, z_columns(s)
    slot, column = iota((slots, wide), 0), iota((slots, wide), 1)
    where, valid = slot, slot < z.fine
    for n, route in enumerate(s.z_routes):
        lower, i, first = route.below(), z.index(), z.fine + n * RADIUS
        here = (slot >= first) & (slot < first + RADIUS)
        where = jnp.where(here, slot - first + jnp.where(lower, -RADIUS, z.fine), where)
        valid = choose(here, choose(lower, i >= 1, i + 1 < z.count), valid)
    planes = band(taps, 0, where - column // RADIUS, valid)
    r, c = iota((RADIUS, wide), 0), iota((RADIUS, wide), 1) % RADIUS
    cells = (slots, RADIUS, wide)
    for side, (offset, valid) in enumerate(((r - c - RADIUS, lower_x(x)), (r - c + RADIUS, higher_x(x)))):
        columns = band(taps, 0, offset, choose(valid, r >= 0, r < 0))
        for term in range(TERMS):
            joint = jnp.broadcast_to(planes[term][:, None, :], cells) * jnp.broadcast_to(columns[term][None], cells)
            high, low = split(joint.reshape(slots * RADIUS, wide))
            at = 2 * term + side
            ends[at, : slots * RADIUS] = high
            ends[at, slots * RADIUS : 2 * slots * RADIUS] = high
            ends[at, 2 * slots * RADIUS :] = low

    lower, higher = y.index() > 0, y.index() < y.count - 1
    far_below = s.y2_routes[0].below()
    n = up8(y.mid_all)

    def write(out, size, terms):
        part = iota(terms[0].shape, 1) >= 2 * size
        for term, matrix in enumerate(terms):
            high, low = split(matrix)
            n = matrix.shape[0]
            out[term * n : (term + 1) * n] = jnp.where(part, low.astype(F32), high.astype(F32)).astype(BF16)

    def columns_of(rows, size):
        lane = iota((rows, 3 * size), 1)
        return jnp.where(lane >= 2 * size, lane - 2 * size, jnp.where(lane >= size, lane - size, lane))

    c = columns_of(y.fine, s.fine_rows)
    is_low = (c >= y.fine) & (c < y.fine + RADIUS)
    is_high = c >= y.fine + RADIUS
    where = jnp.where(is_low, c - y.fine - RADIUS, jnp.where(is_high, c - RADIUS, c))
    valid = choose(is_low, lower, choose(is_high, higher, c >= 0))
    write(y_fine, s.fine_rows, band(taps, 0, where - iota(c.shape, 0), valid))
    c = columns_of(y.fine, y.fine)
    write(y_own, y.fine, band(taps, 0, c - iota(c.shape, 0), c >= 0))
    c = columns_of(y.fine, 2 * RADIUS)
    where = jnp.where(c < RADIUS, c - RADIUS, c - RADIUS + y.fine)
    write(y_edge, 2 * RADIUS, band(taps, 0, where - iota(c.shape, 0), choose(c < RADIUS, lower, higher)))

    c = columns_of(n, s.sum_rows)
    r = iota(c.shape, 0)
    is_low = (c >= s.low) & (c < s.low + SPAN)
    is_high = (c >= s.high) & (c < s.high + SPAN)
    is_far = (c >= s.far) & (c < s.far + y.second)
    where = jnp.where(is_low, c - s.low + 2 - SPAN, jnp.where(is_high, c - s.high + y.mid - 1, c - 1))
    valid = choose(is_low, lower, choose(is_high, higher, c < y.mid_all))
    mid = band(taps, 1, where - (r - 1), valid & (r < y.mid_all))
    far = jnp.where(far_below, -2 - y.coarse, 2 * y.coarse - 2)
    where = jnp.where(is_low, c - s.low + 3 - SPAN, jnp.where(is_high, c - s.high + y.coarse - 2, c - 2))
    where = jnp.where(is_far, c - s.far + far, where)
    valid = choose(is_low, lower, choose(is_high, higher, (c < y.coarse_all) | is_far))
    coarse = band(taps, 2, where - (r - 2), valid & (r < y.coarse_all))
    o, k = iota((y.fine, n), 0), iota((y.fine, n), 1)
    from_mid = jnp.where((k < y.mid_all) & y.holds_mid(k - 1), weight_of(o - 2 * (k - 1)), 0.0)
    m = s.coarse_rows
    c = columns_of(n, m)
    k = iota(c.shape, 0)
    from_coarse = jnp.where((c < y.coarse_all) & y.holds_coarse(c - 2), weight_of(k - 1 - 2 * (c - 2)), 0.0)
    write(y_mid, s.sum_rows, [dot(from_mid, matrix) for matrix in mid])
    write(y_coarse, s.sum_rows, [matrix[:m] for matrix in coarse])
    write(widen_y, m, [dot(from_mid, from_coarse)])


def contract_y(s, weights, high, low):
    joined = jnp.concatenate([high, low, high], axis=0)
    result = jnp.dot(weights[...], joined, preferred_element_type=F32)
    n, m = s.y.fine, s.x.fine
    return [result[t * n : (t + 1) * n, t * m : (t + 1) * m] for t in range(TERMS)]


def contract_z(table, level, held, base, count):
    rows = held.shape[2:]
    totals = [None] * count
    for t in range(held.shape[1]):
        for j in range(count + TAPS - 1):
            plane = held[base + j, t].reshape(rows[0] // 8, 8, rows[1])
            for i in range(max(0, j - TAPS + 1), min(count, j + 1)):
                term = table[(level * TERMS + t) * TAPS + j - i][None] * plane
                totals[i] = term if totals[i] is None else totals[i] + term
    return [total.reshape(rows) for total in totals]


def slab_starts(s, below_at, above_at):
    result = []
    for route in s.z_routes:
        lower, i = route.below(), s.z.index()
        valid = choose(lower, i >= 1, i + 1 < s.z.count)
        result.append((jnp.where(lower, below_at, above_at), valid))
    return result


def store_terms(held, at, valid, parts):
    for t, part in enumerate(parts):
        held[at, t] = part if valid is None else jnp.where(valid, part, 0.0)


BLOCK = 4


def fine_places(s):
    places = [(RADIUS + p, None) for p in range(s.z.fine)]
    for start, valid in slab_starts(s, 0, s.z.fine + RADIUS):
        places += [(start + p, valid) for p in range(RADIUS)]
    return places


def contract_x(s, grid, weights):
    high, low = split(grid)
    joined = jnp.concatenate([high, low, high], axis=1)
    return jnp.dot(joined, weights[: 3 * s.x.fine], preferred_element_type=F32)


def own_kernel(s, table, t_part, fine, sums, x_fine, x_sums, y_edge, fine_part, sums_part, t_fine):
    z, x = s.z, s.x
    t_fine[...] = t_part[...]
    fine_at = fine_places(s)

    def fine_group(g, count):
        n = 2 * RADIUS
        a, b = split(contract_x(s, fine[g : g + count].reshape(count * n, x.fine), x_fine))
        for p in range(count):
            rows = slice(p * n, (p + 1) * n)
            at, valid = fine_at[g + p]
            for t, part in enumerate(contract_y(s, y_edge, a[rows], b[rows])):
                t_fine[at, t] = t_fine[at, t] + (part if valid is None else jnp.where(valid, part, 0.0))

    def fine_block(k):
        for i, total in enumerate(contract_z(table, 0, t_fine, k, BLOCK)):
            fine_part[k + i] = total

    def sum_part(g, count):
        n = s.sum_rows
        grid = sums[g : g + count].reshape(count * n, x.fine)
        sums_part[g * n : (g + count) * n] = contract_x(s, grid, x_sums)

    later = []
    done = 0
    for g in list(range(z.fine, s.fine_planes, 8)) + list(range(0, z.fine, 8)):
        fine_group(g, 8)
        while later:
            later.pop(0)()
        if g < z.fine:
            ready = g if g + 8 < z.fine else z.fine
            later += [lambda k=k: fine_block(k) for k in range(done, ready, BLOCK)]
            done = max(done, ready)
    starts = list(range(0, s.sum_planes, 8))
    while later or starts:
        if starts:
            sum_part(starts[0], min(8, s.sum_planes - starts[0]))
            starts.pop(0)
        if later:
            later.pop(0)()


def sum_kernel(s, table, fine, sums, first, second, x_sums, ends, y_fine, y_mid, y_coarse, widen_x, widen_y, result, *scratch):
    sums_ends, t_mid, t_coarse, p_mid, p_coarse, narrow, out, left = scratch
    z, y, x = s.z, s.y, s.x
    below = s.x_routes[0].below()
    half = s.edge_sums
    for b in range(s.sum_blocks):
        at = slice(s.fine_ends + b * half, s.fine_ends + (b + 1) * half)
        one, two = first[at], second[at]
        rows = [jnp.where(below, one, two), jnp.where(below, two, one)] * 2
        rows.append(jnp.zeros((128 - 4 * half, 128), F32))
        sums_ends[b * 128 : (b + 1) * 128] = jnp.concatenate(rows, axis=0).T

    def along_x(start, rows):
        edge_high, edge_low = split(sums_ends[start : start + rows])
        is_high = iota(edge_high.shape, 1) < 2 * half
        packed = jnp.where(is_high, edge_high.astype(F32), edge_low.astype(F32)).astype(BF16)
        joined = jnp.concatenate([packed, edge_high], axis=1)
        part = jnp.dot(joined, x_sums[3 * x.fine :], preferred_element_type=F32)
        return split(sums[start : start + rows] + part)

    def fine_edges():
        columns = []
        for flip in range(2):
            for g in range(s.fine_groups):
                at = slice(g * s.fine_rows, (g + 1) * s.fine_rows)
                pair = (first[at], second[at])
                columns.append(jnp.where(below, pair[flip], pair[1 - flip]))
        high, low = split(jnp.concatenate(columns, axis=1))
        joined = jnp.concatenate([high, low, high], axis=0)
        high, low = split(jnp.dot(y_fine[...], joined, preferred_element_type=F32))
        width = s.fine_groups * x.fine
        result = []
        for side in range(2):
            total = 0.0
            for t in range(TERMS):
                rows, cols = slice(t * y.fine, (t + 1) * y.fine), slice(side * width, (side + 1) * width)
                a, b = high[rows, cols], low[rows, cols]
                joined = jnp.concatenate([a, b, a], axis=1)
                total = total + jnp.dot(joined, ends[2 * t + side], preferred_element_type=F32)
            result.append(total)
        return result

    t_mid[...] = jnp.zeros(t_mid.shape, F32)
    t_coarse[...] = jnp.zeros(t_coarse.shape, F32)
    mid_at = [(RADIUS + p, None) for p in range(z.mid_all)]
    coarse_at = [(RADIUS + p if p < z.coarse_all else None, None) for p in range(z.mid_all)]
    for start, valid in slab_starts(s, 0, z.mid + 3 + RADIUS):
        mid_at += [(start + p, valid) for p in range(RADIUS)]
    for start, valid in slab_starts(s, 0, z.coarse + 5 + RADIUS):
        coarse_at += [(start + p, valid) for p in range(RADIUS)]
    is_second = iota((s.coarse_rows, x.fine), 1) >= x.fine // TERMS

    def sum_group(g, count):
        n = s.sum_rows
        a, b = along_x(g * n, count * n)
        for p in range(count):
            rows = slice(p * n, (p + 1) * n)
            at, valid = mid_at[g + p]
            cols = slice(0, TERMS * x.fine)
            store_terms(t_mid, at, valid, contract_y(s, y_mid, a[rows, cols], b[rows, cols]))
            at, valid = coarse_at[g + p]
            if at is not None:
                cols = slice(TERMS * x.fine, (TERMS + 1) * x.fine)
                joined = jnp.concatenate([a[rows, cols], b[rows, cols], a[rows, cols]], axis=0)
                both = jnp.dot(y_coarse[...], joined, preferred_element_type=F32)
                m = s.coarse_rows
                store_terms(t_coarse, at, valid, [jnp.where(is_second, both[m:], both[:m])])

    def coarse_block(k):
        count = min(BLOCK, z.coarse_all - k)
        for i, total in enumerate(contract_z(table, 2, t_coarse, k, count)):
            narrow[k + i] = jnp.where(z.holds_coarse(k + i - 2), total, 0.0)

    def widen():
        m = s.coarse_rows
        high, low = split(narrow[...].reshape(z.coarse_all * m, x.fine))
        joined = jnp.concatenate([high, low, high], axis=1)
        high, low = split(jnp.dot(joined, widen_x[...], preferred_element_type=F32))
        for p in range(z.coarse_all):
            rows = slice(p * m, (p + 1) * m)
            joined = jnp.concatenate([high[rows], low[rows], high[rows]], axis=0)
            p_coarse[p] = jnp.dot(widen_y[...], joined, preferred_element_type=F32)

    def mid_block(k):
        count = min(BLOCK, z.mid_all - k)
        for i, total in enumerate(contract_z(table, 1, t_mid, k, count)):
            m = k + i - 1
            for offset, weight in WEIGHTS:
                if (m - offset) % 2 == 0 and 0 <= (m - offset) // 2 + 2 < z.coarse_all:
                    total = total + weight * p_coarse[(m - offset) // 2 + 2]
            p_mid[k + i] = jnp.where(z.holds_mid(m), total, 0.0)

    groups = list(range(z.mid_all, s.sum_planes, 4)) + list(range(0, z.mid_all, 4))
    for g in groups:
        sum_group(g, min(4, s.sum_planes - g if g >= z.mid_all else z.mid_all - g))
    edges = fine_edges()
    for k in range(0, z.coarse_all, BLOCK):
        coarse_block(k)
    widen()
    lane = iota((y.fine, x.fine), 1)

    def finish(k):
        total = fine[k]
        for offset, weight in WEIGHTS:
            if (k - offset) % 2 == 0:
                total = total + weight * p_mid[(k - offset) // 2 + 1]
        block, at = k // s.side, k % s.side * RADIUS
        low, high = (edge[:, block * x.fine : (block + 1) * x.fine] for edge in edges)
        low = pltpu.roll(low, -at % x.fine, 1) if at else low
        turn = (x.fine - RADIUS - at) % x.fine
        high = pltpu.roll(high, turn, 1) if turn else high
        out[k] = total + jnp.where(lane < RADIUS, low, jnp.where(lane >= x.fine - RADIUS, high, 0.0))

    done, copies = 0, []
    for k in range(0, z.mid_all, BLOCK):
        mid_block(k)
        ready = z.fine if k + BLOCK >= z.mid_all else 2 * k + 2
        while done < ready:
            finish(done)
            done += 1
            if done % 8 == 0:
                part = pl.ds(done - 8, 8)
                copies.append(pltpu.make_async_copy(out.at[part], result.at[part], left.at[done // 8 - 1]))
                copies[-1].start()
    for copy in copies:
        copy.wait()


def call(kernel, outs, ins, scratch=(), flops=10**7, out_space=pltpu.VMEM):
    specs = [SMEM if a.ndim == 3 and a.shape[-1] == TAPS else VMEM for a in ins]
    size = sum(a.size * a.dtype.itemsize for a in ins) + sum(o.size * o.dtype.itemsize for o in outs)
    return pl.pallas_call(
        kernel,
        out_shape=tuple(outs),
        in_specs=specs,
        out_specs=tuple(pl.BlockSpec(memory_space=out_space) for _ in outs),
        scratch_shapes=list(scratch),
        compiler_params=PARAMS,
        cost_estimate=pl.CostEstimate(flops=flops, bytes_accessed=size, transcendentals=0),
    )(*ins)


def array(*shape, dtype=F32):
    return jax.ShapeDtypeStruct(shape, dtype)


def local(charges, kernel_taps):
    z, y, x = (Cut(name, size) for name, size in zip(("gz", "gy", "gx"), charges.shape))
    s = Sizes(z, y, x)
    n = x.fine
    nz, nz2 = len(s.z_routes), len(s.z2_routes)

    def bound(kernel, *static):
        return lambda *refs: kernel(s, *static, *refs)

    rows = up8(y.mid_all)
    held, own, ahead, behind, *messages = call(
        bound(restrict_kernel, nz),
        [array(*charges.shape), array(z.mid_all, rows, n)] + [array(s.y_rows, n)] * 2 + [array(s.z_rows, n)] * nz + [array(s.z2_rows, n)] * nz2,
        [charges],
        [
            pltpu.VMEM((z.fine, y.fine + 16, n), F32),
            pltpu.VMEM((z.mid_all, rows, n), F32),
            pltpu.VMEM((z.mid_all, up8(y.mid + 24), n), F32),
            pltpu.VMEM((z.mid_all, rows, n), F32),
            pltpu.VMEM((2, s.z_rows - s.z_fine, n), F32),
        ],
    )
    z_got = [route(m) for route, m in zip(s.z_routes + s.z2_routes, messages)]
    sides = [s.y_routes[0](ahead), s.y_routes[1](behind)]
    operators = call(
        bound(operator_kernel),
        [
            array(3 * n, TERMS * n, dtype=BF16),
            array(3 * n + 256, (TERMS + 1) * n, dtype=BF16),
            array(2 * TERMS, 3 * s.fine_groups * n, z_columns(s), dtype=BF16),
            array(TERMS * y.fine, 3 * y.fine, dtype=BF16),
            array(TERMS * y.fine, 6 * RADIUS, dtype=BF16),
            array(TERMS * y.fine, 3 * s.fine_rows, dtype=BF16),
            array(TERMS * y.fine, 3 * s.sum_rows, dtype=BF16),
            array(TERMS * s.coarse_rows, 3 * s.sum_rows, dtype=BF16),
            array(3 * n, n, dtype=BF16),
            array(y.fine, 3 * s.coarse_rows, dtype=BF16),
            array((2 * TERMS + 1) * TAPS, 8, n),
        ],
        [kernel_taps],
    )
    ahead, behind, far = call(
        bound(spread_kernel, nz, nz2),
        [array(s.slab_rows, n), array(s.slab_rows, n), array(s.far_rows, n)],
        [operators[-1], own, *z_got],
        [pltpu.VMEM((s.far_groups, s.far_rows, n), F32)],
    )
    sides += [s.y_routes[0](ahead), s.y_routes[1](behind)]
    far = s.y2_routes[0](far)
    x_fine, x_sums, ends, y_own, y_edge, y_fine, y_mid, y_coarse, widen_x, widen_y, table = operators
    t_part, last, start = call(
        bound(early_kernel, nz),
        [array(z.fine + 2 * RADIUS, TERMS, y.fine, n)] + [array(s.fine_groups * y.fine, n)] * 2,
        [held, *z_got[:nz], x_fine, y_own],
        [pltpu.VMEM((nz * RADIUS, y.fine, n), F32)],
    )
    fine, sums, first, second = call(
        bound(collect_kernel, nz, nz2),
        [
            array(s.fine_planes, 2 * RADIUS, n),
            array(s.sum_planes, s.sum_rows, n),
            array(s.x_rows, n),
            array(s.x_rows, n),
        ],
        [last, start, own, *z_got, *sides, far],
        [pltpu.VMEM((s.slab_planes, s.sum_rows, n), F32), pltpu.VMEM((s.far_groups, s.far_rows, n), F32)],
    )
    first, second = s.x_routes[0](first), s.x_routes[1](second)
    fine, sums = call(
        bound(own_kernel),
        [array(z.fine, y.fine, n), array(s.sum_planes * s.sum_rows, (TERMS + 1) * n)],
        [table, t_part, fine, sums, x_fine, x_sums, y_edge],
        [pltpu.VMEM((z.fine + 2 * RADIUS, TERMS, y.fine, n), F32)],
    )
    (out,) = call(
        bound(sum_kernel),
        [array(z.fine, y.fine, n)],
        [table, fine, sums, first, second, x_sums, ends, y_fine, y_mid, y_coarse, widen_x, widen_y],
        [
            pltpu.VMEM((s.sum_blocks * 128, n), F32),
            pltpu.VMEM((z.mid + 2 * RADIUS + 3, TERMS, y.fine, n), F32),
            pltpu.VMEM((z.coarse + 2 * RADIUS + 5, 1, s.coarse_rows, n), F32),
            pltpu.VMEM((z.mid_all, y.fine, n), F32),
            pltpu.VMEM((z.coarse_all, y.fine, n), F32),
            pltpu.VMEM((z.coarse_all, s.coarse_rows, n), F32),
            pltpu.VMEM((z.fine, y.fine, n), F32),
            pltpu.SemaphoreType.DMA((z.fine // 8,)),
        ],
        out_space=pltpu.HBM,
    )
    return out


def solution(mesh):
    return jax.shard_map(
        local,
        mesh=mesh,
        in_specs=(P("gz", "gy", "gx"), P()),
        out_specs=P("gz", "gy", "gx"),
        check_vma=False,
    )
```

```python
import jax
import jax.numpy as jnp
from jax import lax
from jax.experimental import pallas as pl
from jax.experimental.pallas import tpu as pltpu
from jax.sharding import PartitionSpec as P

RADIUS = 8
TAPS = 17
TERMS = 2
WEIGHTS = ((-3, -0.0625), (-1, 0.5625), (0, 1.0), (1, 0.5625), (3, -0.0625))
EXACT = lax.Precision.HIGHEST
SPAN = RADIUS + 5
EDGE = RADIUS + 3
F32, BF16 = jnp.float32, jnp.bfloat16
PARAMS = pltpu.CompilerParams(vmem_limit_bytes=32 * 1024 * 1024)
VMEM = pl.BlockSpec(memory_space=pltpu.VMEM)
SMEM = pl.BlockSpec(memory_space=pltpu.SMEM)


def up8(n):
    return -(-n // 8) * 8


def iota(shape, dim):
    return lax.broadcasted_iota(jnp.int32, shape, dim)


def weight_of(difference):
    size = jnp.abs(difference)
    out = jnp.where(size == 1, 0.5625, jnp.where(size == 3, -0.0625, 0.0))
    return jnp.where(size == 0, 1.0, out)


def choose(condition, a, b):
    return jnp.where(condition, jnp.where(a, 1, 0), jnp.where(b, 1, 0)) != 0


class Cut:
    def __init__(self, name, length):
        self.name, self.fine = name, length
        self.count = lax.axis_size(name)
        self.mid, self.coarse = length // 2, length // 4
        self.mid_all, self.coarse_all = self.mid + 3, self.coarse + 5
        self.second = max(SPAN - self.coarse, 0)

    def index(self):
        return lax.axis_index(self.name)

    def holds_mid(self, k):
        k = k + self.index() * self.mid
        return (k >= 0) & (k < self.mid * self.count)

    def holds_coarse(self, k):
        k = k + self.index() * self.coarse
        return (k >= 0) & (k < self.coarse * self.count)


class Route:
    def __init__(self, names, pairs, up, below):
        self.names, self.pairs, self.up, self.below = names, pairs, up, below

    def __call__(self, x):
        return lax.ppermute(x, self.names, self.pairs)


def flip(pairs):
    return [(b, a) for a, b in pairs]


def swap(cut, steps):
    pairs = [(i, i + steps) for i in range(cut.count - steps)]

    def up():
        return cut.index() + steps < cut.count

    return [Route(cut.name, pairs + flip(pairs), up, lambda: ~up())]


def both_ways(cut, steps):
    pairs = [(i, i + steps) for i in range(cut.count - steps)]
    yes, no = (lambda: cut.index() >= 0), (lambda: cut.index() < 0)
    return [Route(cut.name, pairs, yes, yes), Route(cut.name, flip(pairs), no, no)]


def folded(cut, beside, names):
    n, m = cut.count, lax.axis_size(beside)

    def place(c, i):
        return c * n + i if names[0] == beside else i * m + c

    pairs = []
    for c in range(0, m, 2):
        cycle = [place(c, i) for i in range(n)] + [place(c + 1, i) for i in reversed(range(n))]
        pairs += list(zip(cycle, cycle[1:] + cycle[:1]))

    def even():
        return lax.axis_index(beside) % 2 == 0

    def odd():
        return lax.axis_index(beside) % 2 == 1

    return [Route(names, pairs, even, even), Route(names, flip(pairs), odd, odd)]


def split(x):
    high = x.astype(BF16)
    return high, (x - high.astype(F32)).astype(BF16)


def pick(selector, x):
    nt = (((1,), (1,)), ((), ()))
    a = x.astype(BF16)
    rest = x - a.astype(F32)
    b = rest.astype(BF16)
    c = (rest - b.astype(F32)).astype(BF16)
    out = lax.dot_general(selector, c, nt, preferred_element_type=F32)
    out = out + lax.dot_general(selector, b, nt, preferred_element_type=F32)
    return out + lax.dot_general(selector, a, nt, preferred_element_type=F32)


class Sizes:
    def place_of(self, p):
        return p if p < self.slab_start else p + self.coarse_planes - self.slab_start

    def __init__(self, z, y, x):
        self.z, self.y, self.x = z, y, x
        self.z_routes = swap(z, 1) if z.count <= 2 else both_ways(z, 1)
        self.z2_routes = [] if z.count <= 2 else swap(z, 2) if z.count <= 4 else both_ways(z, 2)
        self.y_routes = folded(y, x.name, (x.name, y.name))
        self.y2_routes = swap(y, 2)
        self.x_routes = folded(x, z.name, (x.name, z.name))
        self.z_fine = RADIUS * y.fine
        self.z_sums = max(EDGE * y.mid_all, SPAN * y.coarse_all)
        self.z_rows = up8(self.z_fine + self.z_sums)
        self.z2_rows = up8(z.second * y.coarse_all)
        self.slab_planes = SPAN * len(self.z_routes) + z.second * len(self.z2_routes)
        self.fine_planes = z.fine + RADIUS * len(self.z_routes)
        self.sum_planes = z.mid_all + RADIUS * len(self.z_routes)
        self.coarse_rows = -(-y.coarse_all // 16) * 16
        self.y_fine = RADIUS * z.fine
        self.y_rows = up8(self.y_fine + SPAN * z.mid_all)
        self.slab_fine = RADIUS * RADIUS * len(self.z_routes)
        self.slab_rows = up8(self.slab_fine + SPAN * self.slab_planes)
        self.far_groups = x.fine // x.coarse_all
        self.far_planes = -(-(z.coarse_all + self.slab_planes) // self.far_groups)
        self.far_rows = up8(y.second * self.far_planes)
        self.slab_start = z.coarse_all
        self.coarse_planes = z.coarse_all + RADIUS * len(self.z_routes)
        self.fine_rows = y.fine + 2 * RADIUS
        self.far = y.coarse_all
        self.low = y.mid_all
        self.high = self.low + SPAN
        self.sum_rows = -(-(self.high + SPAN) // 16) * 16
        self.edge_sums = EDGE + SPAN
        self.side = x.fine // RADIUS
        self.fine_groups = -(-self.fine_planes // self.side)
        self.folded = 0 < self.fine_planes % self.side <= self.side // 2
        self.fine_ends = self.fine_groups * self.fine_rows - (self.fine_rows // 2 if self.folded else 0)
        self.sum_blocks = -(-self.sum_planes * self.sum_rows // 128)
        self.coarse_blocks = -(-self.coarse_planes * self.sum_rows // 128)
        self.mid_ends = self.fine_ends + self.coarse_blocks * self.edge_sums
        self.x_rows = self.mid_ends + (self.sum_blocks - self.coarse_blocks) * up8(EDGE)
        assert x.mid_all + x.coarse_all <= x.fine
        assert self.far + y.second <= self.low and y.coarse_all == SPAN
        assert z.coarse >= RADIUS and y.coarse >= RADIUS and y.count == 4


def narrow_kernel(s, out):
    x = s.x
    lanes = (x.fine, x.fine)
    cell, lane = iota(lanes, 0), iota(lanes, 1)
    k = lane - 1
    to_mid = jnp.where((lane < x.mid_all) & x.holds_mid(k), weight_of(cell - 2 * k), 0.0)
    c = lane - x.mid_all - 2
    inside = (lane >= x.mid_all) & (lane < x.mid_all + x.coarse_all) & x.holds_coarse(c)
    to_coarse = jnp.where(inside, weight_of(cell - 1 - 2 * c), 0.0)
    narrow = to_mid + jnp.dot(to_mid, to_coarse, precision=EXACT, preferred_element_type=F32)
    out[...] = jnp.concatenate(split(narrow), axis=1)


def restrict_kernel(s, nz, source, narrow, charges, own, ahead, behind, *rest):
    messages, (wide, mid, high, coarse, packed) = rest[:-5], rest[-5:]
    z, y, x = s.z, s.y, s.x
    wide[...] = jnp.zeros(wide.shape, F32)
    charges[...] = source[...]
    cells = source[...].reshape(z.fine * y.fine, x.fine)
    top, rest = cells.astype(BF16), cells
    rest = rest - top.astype(F32)
    middle = rest.astype(BF16)
    low = (rest - middle.astype(F32)).astype(BF16)
    weights = narrow[...]
    both = jnp.dot(low, weights, preferred_element_type=F32)
    both = both + jnp.dot(
        jnp.concatenate([top, middle], axis=1), jnp.concatenate([weights, weights], axis=0), preferred_element_type=F32
    )
    reduced = both[:, : x.fine] + both[:, x.fine :]
    wide[:, 8 : 8 + y.fine, :] = reduced.reshape(z.fine, y.fine, x.fine)
    rows = 0.0
    for offset, weight in WEIGHTS:
        rows = rows + weight * wide[:, pl.ds(6 + offset, y.mid_all, stride=2), :]
    keep = y.holds_mid(iota((y.mid_all, x.fine), 0) - 1)
    mid[...] = jnp.zeros(mid.shape, F32)
    coarse[...] = jnp.zeros(coarse.shape, F32)
    high[...] = jnp.zeros(high.shape, F32)
    for p in range(z.mid_all):
        total = 0.0
        for offset, weight in WEIGHTS:
            at = 2 * (p - 1) + offset
            if 0 <= at < z.fine:
                total = total + weight * rows[at]
        total = jnp.where(keep & z.holds_mid(p - 1), total, 0.0)
        mid[p, : y.mid_all] = total
        high[p, 8 : 8 + y.mid_all] = total
    rows = 0.0
    for offset, weight in WEIGHTS:
        rows = rows + weight * high[:, pl.ds(5 + offset, y.coarse_all, stride=2), :]
    keep = y.holds_coarse(iota((y.coarse_all, x.fine), 0) - 2)
    for p in range(z.coarse_all):
        total = 0.0
        for offset, weight in WEIGHTS:
            at = 2 * (p - 2) + offset + 1
            if 0 <= at < z.mid_all:
                total = total + weight * rows[at]
        coarse[p, : y.coarse_all] = jnp.where(keep & z.holds_coarse(p - 2), total, 0.0)
    is_mid = iota(mid.shape[1:], 1) < x.mid_all
    for p in range(z.mid_all):
        own[p] = jnp.where(is_mid, mid[p], coarse[p]) if p < z.coarse_all else jnp.where(is_mid, mid[p], 0.0)
    is_side = iota((SPAN, x.fine), 1) < x.mid_all
    for message, route in zip((ahead, behind), s.y_routes):
        up = route.up()
        edge = jnp.where(up, charges[:, y.fine - RADIUS :, :], charges[:, :RADIUS, :])
        message[: s.y_fine] = edge.reshape(s.y_fine, x.fine)
        for p in range(z.mid_all):
            last = jnp.where(is_side, own[p, y.mid_all - SPAN : y.mid_all], own[p, y.coarse_all - SPAN : y.coarse_all])
            at = s.y_fine + p * SPAN
            message[at : at + SPAN] = jnp.where(up, last, own[p, :SPAN])
        filled = s.y_fine + SPAN * z.mid_all
        if filled < s.y_rows:
            message[filled:] = jnp.zeros((s.y_rows - filled, x.fine), F32)
    for message, route in zip(messages, s.z_routes):
        up = route.up().astype(jnp.int32)
        message[: s.z_fine] = charges[pl.ds(up * (z.fine - RADIUS), RADIUS)].reshape(s.z_fine, x.fine)
        packed[...] = jnp.zeros(packed.shape, F32)
        for p in range(EDGE):
            packed[0, p * y.mid_all : (p + 1) * y.mid_all] = mid[up * (z.mid_all - EDGE) + p][: y.mid_all]
        for p in range(SPAN):
            plane = coarse[up * (z.coarse_all - SPAN) + p]
            packed[1, p * y.coarse_all : (p + 1) * y.coarse_all] = plane[: y.coarse_all]
        is_mid = iota(packed.shape[1:], 1) < x.mid_all
        message[s.z_fine :] = jnp.where(is_mid, packed[0], packed[1])
    for message, route in zip(messages[nz:], s.z2_routes):
        up = route.up().astype(jnp.int32)
        message[...] = jnp.zeros(message.shape, F32)
        for p in range(z.second):
            plane = coarse[up * (z.coarse_all - z.second) + p]
            message[p * y.coarse_all : (p + 1) * y.coarse_all] = plane[: y.coarse_all]


class Slab:
    def __init__(self, message, mid, coarse):
        self.message, self.mid, self.coarse = message, mid, coarse

    def coarse_rows(self, first, count):
        return self.message[self.coarse + first : self.coarse + first + count]

    def rows(self, is_mid, first_mid, first_coarse, count):
        coarse = 0.0 if first_coarse is None else self.coarse_rows(first_coarse, count)
        mid = 0.0 if self.mid is None else self.message[self.mid + first_mid : self.mid + first_mid + count]
        return jnp.where(is_mid, mid, coarse)


def slabs(s, z_messages, z2_messages):
    out = []
    for message in z_messages:
        for p in range(SPAN):
            mid = s.z_fine + p * s.y.mid_all if p < EDGE else None
            out.append(Slab(message, mid, s.z_fine + p * s.y.coarse_all))
    for message in z2_messages:
        out += [Slab(message, None, p * s.y.coarse_all) for p in range(s.z.second)]
    return out


def spread_kernel(s, nz, nz2, _, own, *rest):
    z_messages, z2_messages = rest[:nz], rest[nz : nz + nz2]
    ahead, behind, far, rows = rest[-4:]
    z, y, x = s.z, s.y, s.x
    is_mid = iota((SPAN, x.fine), 1) < x.mid_all
    planes = slabs(s, z_messages, z2_messages)
    for message, route in zip((ahead, behind), s.y_routes):
        up = route.up()
        at = 0
        for z_message in z_messages:
            slab = z_message[: s.z_fine].reshape(RADIUS, y.fine, x.fine)
            edge = jnp.where(up, slab[:, y.fine - RADIUS :], slab[:, :RADIUS])
            message[at : at + RADIUS * RADIUS] = edge.reshape(RADIUS * RADIUS, x.fine)
            at += RADIUS * RADIUS
        for plane in planes:
            last = plane.rows(is_mid, y.mid_all - SPAN, y.coarse_all - SPAN, SPAN)
            message[at : at + SPAN] = jnp.where(up, last, plane.rows(is_mid, 0, 0, SPAN))
            at += SPAN
        if at < s.slab_rows:
            message[at:] = jnp.zeros((s.slab_rows - at, x.fine), F32)
    up = s.y2_routes[0].up()
    count, end = y.second, y.coarse_all
    rows[...] = jnp.zeros(rows.shape, F32)
    pairs = [(own[p, end - count : end], own[p, :count]) for p in range(z.coarse_all)]
    pairs += [(plane.coarse_rows(end - count, count), plane.coarse_rows(0, count)) for plane in planes]
    for p, (last, start) in enumerate(pairs):
        g, at = p // s.far_planes, p % s.far_planes * count
        rows[g, at : at + count] = jnp.where(up, last, start)
    lane = iota(far.shape, 1)
    total = jnp.zeros(far.shape, F32)
    for g in range(s.far_groups):
        start = g * x.coarse_all
        turned = pltpu.roll(rows[g], (start - x.mid_all) % x.fine, 1)
        total = jnp.where((lane >= start) & (lane < start + x.coarse_all), turned, total)
    far[...] = total


def roll_ends(s, plane_rows, count):
    x = s.x
    lane = iota((count, x.fine), 1)
    for g in range(s.fine_groups):
        ends = [jnp.zeros(lane.shape, F32)] * 2
        for j in range(min(s.side, s.fine_planes - g * s.side)):
            plane = plane_rows(g * s.side + j)
            here = (lane >= RADIUS * j) & (lane < RADIUS * (j + 1))
            for n, start in enumerate((x.fine - RADIUS, 0)):
                shift = (RADIUS * j - start) % x.fine
                ends[n] = jnp.where(here, pltpu.roll(plane, shift, 1) if shift else plane, ends[n])
        yield g, ends


def early_kernel(s, nz, charges, *rest):
    z_messages = rest[:nz]
    x_fine, y_own, t_part, last, start, slab = rest[nz:]
    z, y, x = s.z, s.y, s.x
    for n, message in enumerate(z_messages):
        slab[n * RADIUS : (n + 1) * RADIUS] = message[: s.z_fine].reshape(RADIUS, y.fine, x.fine)

    def rows_of(p):
        return charges[p] if p < z.fine else slab[p - z.fine]

    t_part[...] = jnp.zeros(t_part.shape, F32)
    fine_at = fine_places(s)
    for g in range(0, s.fine_planes, 8):
        planes = charges[g : g + 8] if g < z.fine else slab[g - z.fine : g - z.fine + 8]
        a, b = split(contract_x(s, planes.reshape(8 * y.fine, x.fine), x_fine))
        for p in range(8):
            rows = slice(p * y.fine, (p + 1) * y.fine)
            store_terms(t_part, *fine_at[g + p], contract_y(s, y_own, a[rows], b[rows]))
    for g, ends in roll_ends(s, rows_of, y.fine):
        rows = slice(g * y.fine, (g + 1) * y.fine)
        last[rows], start[rows] = ends


def collect_kernel(s, nz, nz2, last, start, own, *rest):
    z_messages, z2_messages = rest[:nz], rest[nz : nz + nz2]
    rest = rest[nz + nz2 :]
    pairs = rest[:4]
    far, fine, sums, first, second, raw, rows = rest[4:]
    z, y, x = s.z, s.y, s.x
    below = s.y_routes[0].below()
    planes = slabs(s, z_messages, z2_messages)

    def sides(which, start, count):
        a, b = (message[start : start + count] for message in pairs[2 * which : 2 * which + 2])
        return jnp.where(below, a, b), jnp.where(below, b, a)

    parts = [(0, z.fine, 0, 0)] + [(z.fine + n * RADIUS, RADIUS, 1, n * RADIUS * RADIUS) for n in range(nz)]
    for at, count, which, row in parts:
        low, high = sides(which, row, RADIUS * count)
        fine[at : at + count, :RADIUS] = low.reshape(count, RADIUS, x.fine)
        fine[at : at + count, RADIUS:] = high.reshape(count, RADIUS, x.fine)
    sums[...] = jnp.zeros(sums.shape, F32)
    raw[...] = jnp.zeros(raw.shape, F32)
    for g in range(s.far_groups):
        rows[g] = pltpu.roll(far[...], (x.mid_all - g * x.coarse_all) % x.fine, 1)
    is_mid = iota((y.second, x.fine), 1) < x.mid_all

    def rows_of_plane(out, p, body, which, row, far_plane):
        low, high = sides(which, row, SPAN)
        out[p, : y.mid_all] = body
        out[p, s.low : s.low + SPAN] = low
        out[p, s.high : s.high + SPAN] = high
        if far_plane is not None:
            at = slice(s.far, s.far + y.second)
            start = far_plane % s.far_planes * y.second
            out[p, at] = jnp.where(is_mid, out[p, at], rows[far_plane // s.far_planes, start : start + y.second])

    for p in range(z.mid_all):
        far_plane = p if p < z.coarse_all else None
        rows_of_plane(sums, s.place_of(p), own[p, : y.mid_all], 0, s.y_fine + p * SPAN, far_plane)
    is_mid_row = iota((SPAN, x.fine), 1) < x.mid_all
    is_mid_rest = iota((y.mid_all - SPAN, x.fine), 1) < x.mid_all
    for p, plane in enumerate(planes):
        body = [plane.rows(is_mid_row, 0, 0, SPAN), plane.rows(is_mid_rest, SPAN, None, y.mid_all - SPAN)]
        rows_of_plane(raw, p, jnp.concatenate(body, axis=0), 1, s.slab_fine + p * SPAN, z.coarse_all + p)
    is_mid = iota((s.sum_rows, x.fine), 1) < x.mid_all

    def number(condition, a, b):
        return jnp.where(condition, a, b)

    for n, route in enumerate(s.z_routes):
        lower, base = route.below(), n * SPAN
        for j in range(RADIUS):
            a = raw[base + number(lower, 0, 3) + j]
            b = raw[base + number(lower, SPAN - 5 - RADIUS, 5) + j]
            sums[s.slab_start + n * RADIUS + j] = jnp.where(is_mid, a, b)
        for i in range(3):
            at = number(lower, 0, s.place_of(z.mid)) + i
            sums[at] = sums[at] + jnp.where(is_mid, raw[base + number(lower, EDGE - 3, 0) + i], 0.0)
        for i in range(5):
            at = number(lower, 0, z.coarse) + i
            sums[at] = sums[at] + jnp.where(is_mid, 0.0, raw[base + number(lower, SPAN - 5, 0) + i])
    for n, route in enumerate(s.z2_routes):
        base = len(s.z_routes) * SPAN + n * z.second
        at = s.slab_start + number(route.below(), RADIUS - z.coarse, RADIUS + z.coarse - 5)
        for p in range(z.second):
            sums[at + p] = sums[at + p] + jnp.where(is_mid, 0.0, raw[base + p])

    up = s.x_routes[0].up()
    half, shift = s.fine_rows // 2, x.fine // 2
    is_first_half = iota((half, x.fine), 1) < shift
    for g, ends in roll_ends(s, lambda p: fine[p], 2 * RADIUS):
        rows = slice(g * y.fine, (g + 1) * y.fine)
        both = [jnp.concatenate([old[rows], new], axis=0) for old, new in zip((last, start), ends)]
        if s.folded and g == s.fine_groups - 1:
            both = [jnp.where(is_first_half, e[:half], pltpu.roll(e[half:], shift, 1)) for e in both]
        at = slice(g * s.fine_rows, g * s.fine_rows + both[0].shape[0])
        first[at] = jnp.where(up, both[0], both[1])
        second[at] = jnp.where(up, both[1], both[0])
    width = EDGE + SPAN
    row, lane = iota((2 * width, x.fine), 0), iota((2 * width, x.fine), 1)
    is_first = row < width
    goes_up = choose(up, is_first, ~is_first)
    slot = jnp.where(is_first, row, row - width)
    from_mid = jnp.where(goes_up, x.mid_all - EDGE + slot, slot)
    from_coarse = slot - EDGE + jnp.where(goes_up, x.mid_all + x.coarse_all - SPAN, x.mid_all)
    wanted = jnp.where(slot < EDGE, from_mid, from_coarse)
    picked_sums = pick((lane == wanted).astype(BF16), sums[...].reshape(s.sum_planes * s.sum_rows, x.fine))
    spare = s.sum_blocks * 128 - picked_sums.shape[1]
    if spare:
        picked_sums = jnp.concatenate([picked_sums, jnp.zeros((2 * width, spare), F32)], axis=1)
    for n, message in enumerate((first, second)):
        rows = picked_sums[n * width : (n + 1) * width]
        for b in range(s.coarse_blocks):
            at = s.fine_ends + b * width
            message[at : at + width] = rows[:, b * 128 : (b + 1) * 128]
        for b in range(s.coarse_blocks, s.sum_blocks):
            at = s.mid_ends + (b - s.coarse_blocks) * up8(EDGE)
            message[at : at + up8(EDGE)] = rows[: up8(EDGE), b * 128 : (b + 1) * 128]


def band(taps, level, offset, valid):
    at = jnp.where(valid, offset + RADIUS, -1)
    out = [jnp.zeros(at.shape, F32) for _ in range(TERMS)]
    for tap in range(TAPS):
        here = at == tap
        out = [jnp.where(here, taps[level, term, tap], total) for term, total in enumerate(out)]
    return out


def dot(a, b):
    return jnp.dot(a, b, precision=EXACT, preferred_element_type=F32)


def z_columns(s):
    return s.z.fine * RADIUS


def lower_x(x):
    return x.index() > 0


def higher_x(x):
    return x.index() < x.count - 1


def operator_kernel(s, taps, x_fine, x_sums, ends, y_own, y_edge, y_fine, y_mid, y_coarse, widen_x, widen_y, table):
    y, x = s.y, s.x
    for level in range(2):
        for term in range(TERMS):
            for tap in range(TAPS):
                table[(level * TERMS + term) * TAPS + tap] = jnp.full((8, x.fine), taps[level, term, tap], F32)
    is_second = iota((8, x.fine), 1) >= x.fine // TERMS
    for tap in range(TAPS):
        table[2 * TERMS * TAPS + tap] = jnp.where(is_second, taps[2, 1, tap], taps[2, 0, tap])
    own, edge = x.fine, 64
    shape = (own + edge, x.fine)
    row, lane = iota(shape, 0), iota(shape, 1)
    t = row - own
    lower, higher = x.index() > 0, x.index() < x.count - 1
    is_own = row < own

    def place(half, own_place, own_valid, first, count, low_place, high_place):
        is_low = t < half
        r = jnp.where(is_low, t, t - half) - first
        there = (r >= 0) & (r < count) & (t < 2 * half) & choose(is_low, lower, higher)
        valid = choose(is_own, own_valid, there)
        return jnp.where(is_own, own_place, jnp.where(is_low, low_place + r, high_place + r)), valid

    half = s.edge_sums
    fine = band(taps, 0, row - lane, is_own)
    where, valid = place(half, row - 1, row < x.mid_all, 0, EDGE, 2 - EDGE, x.mid - 1)
    mid = band(taps, 1, where - (lane - 1), valid & (lane < x.mid_all))
    first = x.mid_all
    inside = (row >= first) & (row < first + x.coarse_all)
    where, valid = place(half, row - first - 2, inside, EDGE, SPAN, 3 - SPAN, x.coarse - 2)
    side = x.fine // TERMS
    column = lane % side
    terms = band(taps, 2, where - (column - 2), valid & (column < x.coarse_all))
    coarse = terms[0]
    for term in range(1, TERMS):
        coarse = jnp.where(lane >= term * side, terms[term], coarse)
    a, b = iota((x.fine, x.fine), 0), iota((x.fine, x.fine), 1)
    from_mid = jnp.where((a < x.mid_all) & x.holds_mid(a - 1), weight_of(b - 2 * (a - 1)), 0.0)
    c = a % side
    from_coarse = jnp.where((c < x.coarse_all) & x.holds_coarse(c - 2), weight_of(b - 1 - 2 * (c - 2)), 0.0)
    high, low = split(dot(from_coarse, from_mid))
    widen_x[:own] = high
    widen_x[own : 2 * own] = high
    widen_x[2 * own :] = low
    columns = [(x_fine, 0, 0, fine)]
    columns += [(x_sums, half, 0, [dot(m, from_mid) for m in mid])]
    columns += [(x_sums, half, TERMS * x.fine, [coarse])]
    for out, half, at, terms in columns:
        for term, matrix in enumerate(terms):
            high, low = split(matrix)
            cols = slice(at + term * x.fine, at + (term + 1) * x.fine)
            n = 2 * half
            out[0:own, cols] = high[:own]
            out[own : 2 * own, cols] = high[:own]
            out[2 * own : 3 * own, cols] = low[:own]
            if n:
                out[3 * own :, cols] = jnp.zeros((out.shape[0] - 3 * own, x.fine), BF16)
                out[3 * own : 3 * own + n, cols] = high[own : own + n]
                out[3 * own + n : 3 * own + 2 * n, cols] = high[own : own + n]
                out[3 * own + 128 : 3 * own + 128 + n, cols] = low[own : own + n]

    z, slots, wide = s.z, s.side * s.fine_groups, z_columns(s)
    slot, column = iota((slots, wide), 0), iota((slots, wide), 1)
    where, valid = slot, slot < z.fine
    for n, route in enumerate(s.z_routes):
        lower, i, first = route.below(), z.index(), z.fine + n * RADIUS
        here = (slot >= first) & (slot < first + RADIUS)
        where = jnp.where(here, slot - first + jnp.where(lower, -RADIUS, z.fine), where)
        valid = choose(here, choose(lower, i >= 1, i + 1 < z.count), valid)
    planes = band(taps, 0, where - column // RADIUS, valid)
    r, c = iota((RADIUS, wide), 0), iota((RADIUS, wide), 1) % RADIUS
    cells = (slots, RADIUS, wide)
    for side, (offset, valid) in enumerate(((r - c - RADIUS, lower_x(x)), (r - c + RADIUS, higher_x(x)))):
        columns = band(taps, 0, offset, choose(valid, r >= 0, r < 0))
        for term in range(TERMS):
            joint = jnp.broadcast_to(planes[term][:, None, :], cells) * jnp.broadcast_to(columns[term][None], cells)
            high, low = split(joint.reshape(slots * RADIUS, wide))
            at = 2 * term + side
            ends[at, : slots * RADIUS] = high
            ends[at, slots * RADIUS : 2 * slots * RADIUS] = high
            ends[at, 2 * slots * RADIUS :] = low

    lower, higher = y.index() > 0, y.index() < y.count - 1
    far_below = s.y2_routes[0].below()
    n = up8(y.mid_all)

    def write(out, size, terms):
        part = iota(terms[0].shape, 1) >= 2 * size
        for term, matrix in enumerate(terms):
            high, low = split(matrix)
            n = matrix.shape[0]
            out[term * n : (term + 1) * n] = jnp.where(part, low.astype(F32), high.astype(F32)).astype(BF16)

    def columns_of(rows, size):
        lane = iota((rows, 3 * size), 1)
        return jnp.where(lane >= 2 * size, lane - 2 * size, jnp.where(lane >= size, lane - size, lane))

    c = columns_of(y.fine, s.fine_rows)
    is_low = (c >= y.fine) & (c < y.fine + RADIUS)
    is_high = c >= y.fine + RADIUS
    where = jnp.where(is_low, c - y.fine - RADIUS, jnp.where(is_high, c - RADIUS, c))
    valid = choose(is_low, lower, choose(is_high, higher, c >= 0))
    write(y_fine, s.fine_rows, band(taps, 0, where - iota(c.shape, 0), valid))
    c = columns_of(y.fine, y.fine)
    write(y_own, y.fine, band(taps, 0, c - iota(c.shape, 0), c >= 0))
    c = columns_of(y.fine, 2 * RADIUS)
    where = jnp.where(c < RADIUS, c - RADIUS, c - RADIUS + y.fine)
    write(y_edge, 2 * RADIUS, band(taps, 0, where - iota(c.shape, 0), choose(c < RADIUS, lower, higher)))

    c = columns_of(n, s.sum_rows)
    r = iota(c.shape, 0)
    is_low = (c >= s.low) & (c < s.low + SPAN)
    is_high = (c >= s.high) & (c < s.high + SPAN)
    is_far = (c >= s.far) & (c < s.far + y.second)
    where = jnp.where(is_low, c - s.low + 2 - SPAN, jnp.where(is_high, c - s.high + y.mid - 1, c - 1))
    valid = choose(is_low, lower, choose(is_high, higher, c < y.mid_all))
    mid = band(taps, 1, where - (r - 1), valid & (r < y.mid_all))
    far = jnp.where(far_below, -2 - y.coarse, 2 * y.coarse - 2)
    where = jnp.where(is_low, c - s.low + 3 - SPAN, jnp.where(is_high, c - s.high + y.coarse - 2, c - 2))
    where = jnp.where(is_far, c - s.far + far, where)
    valid = choose(is_low, lower, choose(is_high, higher, (c < y.coarse_all) | is_far))
    coarse = band(taps, 2, where - (r - 2), valid & (r < y.coarse_all))
    o, k = iota((y.fine, n), 0), iota((y.fine, n), 1)
    from_mid = jnp.where((k < y.mid_all) & y.holds_mid(k - 1), weight_of(o - 2 * (k - 1)), 0.0)
    m = s.coarse_rows
    c = columns_of(n, m)
    k = iota(c.shape, 0)
    from_coarse = jnp.where((c < y.coarse_all) & y.holds_coarse(c - 2), weight_of(k - 1 - 2 * (c - 2)), 0.0)
    write(y_mid, s.sum_rows, [dot(from_mid, matrix) for matrix in mid])
    write(y_coarse, s.sum_rows, [matrix[:m] for matrix in coarse])
    write(widen_y, m, [dot(from_mid, from_coarse)])


def contract_y(s, weights, high, low):
    joined = jnp.concatenate([high, low, high], axis=0)
    result = jnp.dot(weights[...], joined, preferred_element_type=F32)
    n, m = s.y.fine, s.x.fine
    return [result[t * n : (t + 1) * n, t * m : (t + 1) * m] for t in range(TERMS)]


def contract_z(table, level, held, base, count):
    rows = held.shape[2:]
    totals = [None] * count
    for t in range(held.shape[1]):
        for j in range(count + TAPS - 1):
            plane = held[base + j, t].reshape(rows[0] // 8, 8, rows[1])
            for i in range(max(0, j - TAPS + 1), min(count, j + 1)):
                term = table[(level * TERMS + t) * TAPS + j - i][None] * plane
                totals[i] = term if totals[i] is None else totals[i] + term
    return [total.reshape(rows) for total in totals]


def slab_starts(s, below_at, above_at):
    result = []
    for route in s.z_routes:
        lower, i = route.below(), s.z.index()
        valid = choose(lower, i >= 1, i + 1 < s.z.count)
        result.append((jnp.where(lower, below_at, above_at), valid))
    return result


def store_terms(held, at, valid, parts):
    for t, part in enumerate(parts):
        held[at, t] = part if valid is None else jnp.where(valid, part, 0.0)


BLOCK = 4


def fine_places(s):
    places = [(RADIUS + p, None) for p in range(s.z.fine)]
    for start, valid in slab_starts(s, 0, s.z.fine + RADIUS):
        places += [(start + p, valid) for p in range(RADIUS)]
    return places


def contract_x(s, grid, weights):
    high, low = split(grid)
    joined = jnp.concatenate([high, low, high], axis=1)
    return jnp.dot(joined, weights[: 3 * s.x.fine], preferred_element_type=F32)


def own_kernel(s, table, t_part, fine, sums, x_fine, x_sums, y_edge, fine_part, sums_part, t_fine):
    z, x = s.z, s.x
    t_fine[...] = t_part[...]
    fine_at = fine_places(s)

    def fine_group(g, count):
        n = 2 * RADIUS
        a, b = split(contract_x(s, fine[g : g + count].reshape(count * n, x.fine), x_fine))
        for p in range(count):
            rows = slice(p * n, (p + 1) * n)
            at, valid = fine_at[g + p]
            for t, part in enumerate(contract_y(s, y_edge, a[rows], b[rows])):
                t_fine[at, t] = t_fine[at, t] + (part if valid is None else jnp.where(valid, part, 0.0))

    def fine_block(k):
        for i, total in enumerate(contract_z(table, 0, t_fine, k, BLOCK)):
            fine_part[k + i] = total

    def sum_part(g, count):
        n = s.sum_rows
        grid = sums[g : g + count].reshape(count * n, x.fine)
        sums_part[g * n : (g + count) * n] = contract_x(s, grid, x_sums)

    later = []
    done = 0
    for g in list(range(z.fine, s.fine_planes, 8)) + list(range(0, z.fine, 8)):
        fine_group(g, 8)
        while later:
            later.pop(0)()
        if g < z.fine:
            ready = g if g + 8 < z.fine else z.fine
            later += [lambda k=k: fine_block(k) for k in range(done, ready, BLOCK)]
            done = max(done, ready)
    starts = list(range(0, s.sum_planes, 8))
    while later or starts:
        if starts:
            sum_part(starts[0], min(8, s.sum_planes - starts[0]))
            starts.pop(0)
        if later:
            later.pop(0)()


def sum_kernel(s, table, fine, sums, first, second, x_sums, ends, y_fine, y_mid, y_coarse, widen_x, widen_y, result, *scratch):
    sums_ends, t_mid, t_coarse, p_mid, p_coarse, narrow, out, left = scratch
    z, y, x = s.z, s.y, s.x
    below = s.x_routes[0].below()
    half = s.edge_sums
    def ends_of(start, rows):
        one, two = first[start : start + rows], second[start : start + rows]
        return jnp.where(below, one, two), jnp.where(below, two, one)

    for b in range(s.sum_blocks):
        if b < s.coarse_blocks:
            pair = ends_of(s.fine_ends + b * half, half)
        else:
            rest = jnp.zeros((half - up8(EDGE), 128), F32)
            pair = ends_of(s.mid_ends + (b - s.coarse_blocks) * up8(EDGE), up8(EDGE))
            pair = [jnp.concatenate([ends, rest], axis=0) for ends in pair]
        rows = jnp.concatenate(pair, axis=0)
        zeros = jnp.zeros((128 - 4 * half, 128), F32)
        sums_ends[b * 128 : (b + 1) * 128] = jnp.concatenate([rows, rows, zeros], axis=0).T

    def along_x(start, rows):
        edge_high, edge_low = split(sums_ends[start : start + rows])
        is_high = iota(edge_high.shape, 1) < 2 * half
        packed = jnp.where(is_high, edge_high.astype(F32), edge_low.astype(F32)).astype(BF16)
        joined = jnp.concatenate([packed, edge_high], axis=1)
        part = jnp.dot(joined, x_sums[3 * x.fine :], preferred_element_type=F32)
        return split(sums[start : start + rows] + part)

    def fine_edges():
        columns = []
        for flip in range(2):
            for g in range(s.fine_groups):
                is_folded = s.folded and g == s.fine_groups - 1
                at = slice(g * s.fine_rows, s.fine_ends if is_folded else (g + 1) * s.fine_rows)
                pair = (first[at], second[at])
                ends_here = jnp.where(below, pair[flip], pair[1 - flip])
                if is_folded:
                    ends_here = jnp.concatenate([ends_here, pltpu.roll(ends_here, x.fine // 2, 1)], axis=0)
                columns.append(ends_here)
        high, low = split(jnp.concatenate(columns, axis=1))
        joined = jnp.concatenate([high, low, high], axis=0)
        high, low = split(jnp.dot(y_fine[...], joined, preferred_element_type=F32))
        width = s.fine_groups * x.fine
        result = []
        for side in range(2):
            total = 0.0
            for t in range(TERMS):
                rows, cols = slice(t * y.fine, (t + 1) * y.fine), slice(side * width, (side + 1) * width)
                a, b = high[rows, cols], low[rows, cols]
                joined = jnp.concatenate([a, b, a], axis=1)
                total = total + jnp.dot(joined, ends[2 * t + side], preferred_element_type=F32)
            result.append(total)
        return result

    t_mid[...] = jnp.zeros(t_mid.shape, F32)
    t_coarse[...] = jnp.zeros(t_coarse.shape, F32)
    mid_at = [(RADIUS + p, None) for p in range(z.mid_all)]
    mid_at, rest_at = mid_at[: z.coarse_all], mid_at[z.coarse_all :]
    coarse_at = [(RADIUS + p, None) for p in range(z.coarse_all)]
    for start, valid in slab_starts(s, 0, z.mid + 3 + RADIUS):
        mid_at += [(start + p, valid) for p in range(RADIUS)]
    mid_at += rest_at
    for start, valid in slab_starts(s, 0, z.coarse + 5 + RADIUS):
        coarse_at += [(start + p, valid) for p in range(RADIUS)]
    coarse_at += [(None, None)] * len(rest_at)
    is_second = iota((s.coarse_rows, x.fine), 1) >= x.fine // TERMS

    def sum_group(g, count):
        n = s.sum_rows
        a, b = along_x(g * n, count * n)
        for p in range(count):
            rows = slice(p * n, (p + 1) * n)
            at, valid = mid_at[g + p]
            cols = slice(0, TERMS * x.fine)
            store_terms(t_mid, at, valid, contract_y(s, y_mid, a[rows, cols], b[rows, cols]))
            at, valid = coarse_at[g + p]
            if at is not None:
                cols = slice(TERMS * x.fine, (TERMS + 1) * x.fine)
                joined = jnp.concatenate([a[rows, cols], b[rows, cols], a[rows, cols]], axis=0)
                both = jnp.dot(y_coarse[...], joined, preferred_element_type=F32)
                m = s.coarse_rows
                store_terms(t_coarse, at, valid, [jnp.where(is_second, both[m:], both[:m])])

    def coarse_block(k):
        count = min(BLOCK, z.coarse_all - k)
        for i, total in enumerate(contract_z(table, 2, t_coarse, k, count)):
            narrow[k + i] = jnp.where(z.holds_coarse(k + i - 2), total, 0.0)

    def widen():
        m = s.coarse_rows
        high, low = split(narrow[...].reshape(z.coarse_all * m, x.fine))
        joined = jnp.concatenate([high, low, high], axis=1)
        high, low = split(jnp.dot(joined, widen_x[...], preferred_element_type=F32))
        for p in range(z.coarse_all):
            rows = slice(p * m, (p + 1) * m)
            joined = jnp.concatenate([high[rows], low[rows], high[rows]], axis=0)
            p_coarse[p] = jnp.dot(widen_y[...], joined, preferred_element_type=F32)

    def mid_block(k):
        count = min(BLOCK, z.mid_all - k)
        for i, total in enumerate(contract_z(table, 1, t_mid, k, count)):
            m = k + i - 1
            for offset, weight in WEIGHTS:
                if (m - offset) % 2 == 0 and 0 <= (m - offset) // 2 + 2 < z.coarse_all:
                    total = total + weight * p_coarse[(m - offset) // 2 + 2]
            p_mid[k + i] = jnp.where(z.holds_mid(m), total, 0.0)

    edges = fine_edges()
    lane = iota((y.fine, x.fine), 1)

    def begin(k):
        block, at = k // s.side, k % s.side * RADIUS
        low, high = (edge[:, block * x.fine : (block + 1) * x.fine] for edge in edges)
        low = pltpu.roll(low, -at % x.fine, 1) if at else low
        turn = (x.fine - RADIUS - at) % x.fine
        high = pltpu.roll(high, turn, 1) if turn else high
        out[k] = fine[k] + jnp.where(lane < RADIUS, low, jnp.where(lane >= x.fine - RADIUS, high, 0.0))

    def finish(k):
        total = out[k]
        for offset, weight in WEIGHTS:
            if (k - offset) % 2 == 0:
                total = total + weight * p_mid[(k - offset) // 2 + 1]
        out[k] = total

    groups = list(range(0, s.sum_planes, 4))
    share = -(-z.fine // len(groups))
    for n, g in enumerate(groups):
        sum_group(g, min(4, s.sum_planes - g))
        for k in range(n * share, min((n + 1) * share, z.fine)):
            begin(k)
    for k in range(0, z.coarse_all, BLOCK):
        coarse_block(k)
    widen()
    done, copies = 0, []
    for k in range(0, z.mid_all, BLOCK):
        mid_block(k)
        ready = z.fine if k + BLOCK >= z.mid_all else 2 * k + 2
        while done < ready:
            finish(done)
            done += 1
            if done % 8 == 0:
                part = pl.ds(done - 8, 8)
                copies.append(pltpu.make_async_copy(out.at[part], result.at[part], left.at[done // 8 - 1]))
                copies[-1].start()
    for copy in copies:
        copy.wait()


def call(kernel, outs, ins, scratch=(), flops=10**7, out_space=pltpu.VMEM):
    specs = [SMEM if a.ndim == 3 and a.shape[-1] == TAPS else VMEM for a in ins]
    size = sum(a.size * a.dtype.itemsize for a in ins) + sum(o.size * o.dtype.itemsize for o in outs)
    return pl.pallas_call(
        kernel,
        out_shape=tuple(outs),
        in_specs=specs,
        out_specs=tuple(pl.BlockSpec(memory_space=out_space) for _ in outs),
        scratch_shapes=list(scratch),
        compiler_params=PARAMS,
        cost_estimate=pl.CostEstimate(flops=flops, bytes_accessed=size, transcendentals=0),
    )(*ins)


def array(*shape, dtype=F32):
    return jax.ShapeDtypeStruct(shape, dtype)


def local(charges, kernel_taps):
    z, y, x = (Cut(name, size) for name, size in zip(("gz", "gy", "gx"), charges.shape))
    s = Sizes(z, y, x)
    n = x.fine
    nz, nz2 = len(s.z_routes), len(s.z2_routes)

    def bound(kernel, *static):
        return lambda *refs: kernel(s, *static, *refs)

    rows = up8(y.mid_all)
    (weights,) = call(bound(narrow_kernel), [array(n, 2 * n, dtype=BF16)], [], flops=10**10)
    held, own, ahead, behind, *messages = call(
        bound(restrict_kernel, nz),
        [array(*charges.shape), array(z.mid_all, rows, n)] + [array(s.y_rows, n)] * 2 + [array(s.z_rows, n)] * nz + [array(s.z2_rows, n)] * nz2,
        [charges, weights],
        [
            pltpu.VMEM((z.fine, y.fine + 16, n), F32),
            pltpu.VMEM((z.mid_all, rows, n), F32),
            pltpu.VMEM((z.mid_all, up8(y.mid + 24), n), F32),
            pltpu.VMEM((z.mid_all, rows, n), F32),
            pltpu.VMEM((2, s.z_rows - s.z_fine, n), F32),
        ],
    )
    z_got = [route(m) for route, m in zip(s.z_routes + s.z2_routes, messages)]
    sides = [s.y_routes[0](ahead), s.y_routes[1](behind)]
    operators = call(
        bound(operator_kernel),
        [
            array(3 * n, TERMS * n, dtype=BF16),
            array(3 * n + 256, (TERMS + 1) * n, dtype=BF16),
            array(2 * TERMS, 3 * s.fine_groups * n, z_columns(s), dtype=BF16),
            array(TERMS * y.fine, 3 * y.fine, dtype=BF16),
            array(TERMS * y.fine, 6 * RADIUS, dtype=BF16),
            array(TERMS * y.fine, 3 * s.fine_rows, dtype=BF16),
            array(TERMS * y.fine, 3 * s.sum_rows, dtype=BF16),
            array(TERMS * s.coarse_rows, 3 * s.sum_rows, dtype=BF16),
            array(3 * n, n, dtype=BF16),
            array(y.fine, 3 * s.coarse_rows, dtype=BF16),
            array((2 * TERMS + 1) * TAPS, 8, n),
        ],
        [kernel_taps],
    )
    ahead, behind, far = call(
        bound(spread_kernel, nz, nz2),
        [array(s.slab_rows, n), array(s.slab_rows, n), array(s.far_rows, n)],
        [operators[-1], own, *z_got],
        [pltpu.VMEM((s.far_groups, s.far_rows, n), F32)],
    )
    sides += [s.y_routes[0](ahead), s.y_routes[1](behind)]
    far = s.y2_routes[0](far)
    x_fine, x_sums, ends, y_own, y_edge, y_fine, y_mid, y_coarse, widen_x, widen_y, table = operators
    t_part, last, start = call(
        bound(early_kernel, nz),
        [array(z.fine + 2 * RADIUS, TERMS, y.fine, n)] + [array(s.fine_groups * y.fine, n)] * 2,
        [held, *z_got[:nz], x_fine, y_own],
        [pltpu.VMEM((nz * RADIUS, y.fine, n), F32)],
    )
    fine, sums, first, second = call(
        bound(collect_kernel, nz, nz2),
        [
            array(s.fine_planes, 2 * RADIUS, n),
            array(s.sum_planes, s.sum_rows, n),
            array(s.x_rows, n),
            array(s.x_rows, n),
        ],
        [last, start, own, *z_got, *sides, far],
        [pltpu.VMEM((s.slab_planes, s.sum_rows, n), F32), pltpu.VMEM((s.far_groups, s.far_rows, n), F32)],
    )
    first, second = s.x_routes[0](first), s.x_routes[1](second)
    fine, sums = call(
        bound(own_kernel),
        [array(z.fine, y.fine, n), array(s.sum_planes * s.sum_rows, (TERMS + 1) * n)],
        [table, t_part, fine, sums, x_fine, x_sums, y_edge],
        [pltpu.VMEM((z.fine + 2 * RADIUS, TERMS, y.fine, n), F32)],
    )
    (out,) = call(
        bound(sum_kernel),
        [array(z.fine, y.fine, n)],
        [table, fine, sums, first, second, x_sums, ends, y_fine, y_mid, y_coarse, widen_x, widen_y],
        [
            pltpu.VMEM((s.sum_blocks * 128, n), F32),
            pltpu.VMEM((z.mid + 2 * RADIUS + 3, TERMS, y.fine, n), F32),
            pltpu.VMEM((z.coarse + 2 * RADIUS + 5, 1, s.coarse_rows, n), F32),
            pltpu.VMEM((z.mid_all, y.fine, n), F32),
            pltpu.VMEM((z.coarse_all, y.fine, n), F32),
            pltpu.VMEM((z.coarse_all, s.coarse_rows, n), F32),
            pltpu.VMEM((z.fine, y.fine, n), F32),
            pltpu.SemaphoreType.DMA((z.fine // 8,)),
        ],
        out_space=pltpu.HBM,
    )
    return out


def solution(mesh):
    return jax.shard_map(
        local,
        mesh=mesh,
        in_specs=(P("gz", "gy", "gx"), P()),
        out_specs=P("gz", "gy", "gx"),
        check_vma=False,
    )
```

```python
import jax
import jax.numpy as jnp
from jax import lax
from jax.experimental import pallas as pl
from jax.experimental.pallas import tpu as pltpu
from jax.sharding import PartitionSpec as P

RADIUS = 8
TAPS = 17
TERMS = 2
WEIGHTS = ((-3, -0.0625), (-1, 0.5625), (0, 1.0), (1, 0.5625), (3, -0.0625))
EXACT = lax.Precision.HIGHEST
SPAN = RADIUS + 5
EDGE = RADIUS + 3
F32, BF16 = jnp.float32, jnp.bfloat16
PARAMS = pltpu.CompilerParams(vmem_limit_bytes=32 * 1024 * 1024)
VMEM = pl.BlockSpec(memory_space=pltpu.VMEM)
SMEM = pl.BlockSpec(memory_space=pltpu.SMEM)


def up8(n):
    return -(-n // 8) * 8


def iota(shape, dim):
    return lax.broadcasted_iota(jnp.int32, shape, dim)


def weight_of(difference):
    size = jnp.abs(difference)
    out = jnp.where(size == 1, 0.5625, jnp.where(size == 3, -0.0625, 0.0))
    return jnp.where(size == 0, 1.0, out)


def choose(condition, a, b):
    return jnp.where(condition, jnp.where(a, 1, 0), jnp.where(b, 1, 0)) != 0


class Cut:
    def __init__(self, name, length):
        self.name, self.fine = name, length
        self.count = lax.axis_size(name)
        self.mid, self.coarse = length // 2, length // 4
        self.mid_all, self.coarse_all = self.mid + 3, self.coarse + 5
        self.second = max(SPAN - self.coarse, 0)

    def index(self):
        return lax.axis_index(self.name)

    def holds_mid(self, k):
        k = k + self.index() * self.mid
        return (k >= 0) & (k < self.mid * self.count)

    def holds_coarse(self, k):
        k = k + self.index() * self.coarse
        return (k >= 0) & (k < self.coarse * self.count)


class Route:
    def __init__(self, names, pairs, up, below):
        self.names, self.pairs, self.up, self.below = names, pairs, up, below

    def __call__(self, x):
        return lax.ppermute(x, self.names, self.pairs)


def flip(pairs):
    return [(b, a) for a, b in pairs]


def swap(cut, steps):
    pairs = [(i, i + steps) for i in range(cut.count - steps)]

    def up():
        return cut.index() + steps < cut.count

    return [Route(cut.name, pairs + flip(pairs), up, lambda: ~up())]


def both_ways(cut, steps):
    pairs = [(i, i + steps) for i in range(cut.count - steps)]
    yes, no = (lambda: cut.index() >= 0), (lambda: cut.index() < 0)
    return [Route(cut.name, pairs, yes, yes), Route(cut.name, flip(pairs), no, no)]


def folded(cut, beside, names):
    n, m = cut.count, lax.axis_size(beside)

    def place(c, i):
        return c * n + i if names[0] == beside else i * m + c

    pairs = []
    for c in range(0, m, 2):
        cycle = [place(c, i) for i in range(n)] + [place(c + 1, i) for i in reversed(range(n))]
        pairs += list(zip(cycle, cycle[1:] + cycle[:1]))

    def even():
        return lax.axis_index(beside) % 2 == 0

    def odd():
        return lax.axis_index(beside) % 2 == 1

    return [Route(names, pairs, even, even), Route(names, flip(pairs), odd, odd)]


def split(x):
    high = x.astype(BF16)
    return high, (x - high.astype(F32)).astype(BF16)


def pick(selector, x):
    nt = (((1,), (1,)), ((), ()))
    a = x.astype(BF16)
    rest = x - a.astype(F32)
    b = rest.astype(BF16)
    c = (rest - b.astype(F32)).astype(BF16)
    out = lax.dot_general(selector, c, nt, preferred_element_type=F32)
    out = out + lax.dot_general(selector, b, nt, preferred_element_type=F32)
    return out + lax.dot_general(selector, a, nt, preferred_element_type=F32)


class Sizes:
    def place_of(self, p):
        return p if p < self.slab_start else p + self.coarse_planes - self.slab_start

    def __init__(self, z, y, x):
        self.z, self.y, self.x = z, y, x
        self.z_routes = swap(z, 1) if z.count <= 2 else both_ways(z, 1)
        self.z2_routes = [] if z.count <= 2 else swap(z, 2) if z.count <= 4 else both_ways(z, 2)
        self.y_routes = folded(y, x.name, (x.name, y.name))
        self.y2_routes = swap(y, 2)
        self.x_routes = folded(x, z.name, (x.name, z.name))
        self.z_fine = RADIUS * y.fine
        self.z_sums = max(EDGE * y.mid_all, SPAN * y.coarse_all)
        self.z_rows = up8(self.z_fine + self.z_sums)
        self.z2_rows = up8(z.second * y.coarse_all)
        self.slab_planes = SPAN * len(self.z_routes) + z.second * len(self.z2_routes)
        self.fine_planes = z.fine + RADIUS * len(self.z_routes)
        self.sum_planes = z.mid_all + RADIUS * len(self.z_routes)
        self.coarse_rows = -(-y.coarse_all // 16) * 16
        self.y_fine = RADIUS * z.fine
        self.y_rows = up8(self.y_fine + SPAN * z.mid_all)
        self.slab_fine = RADIUS * RADIUS * len(self.z_routes)
        self.slab_rows = up8(self.slab_fine + SPAN * self.slab_planes)
        self.far_groups = x.fine // x.coarse_all
        self.far_planes = -(-z.coarse_all // self.far_groups)
        self.far_rows = up8(y.second * self.far_planes)
        self.slab_start = z.coarse_all
        self.coarse_planes = z.coarse_all + RADIUS * len(self.z_routes)
        self.fine_rows = y.fine + 2 * RADIUS
        self.far = y.coarse_all
        self.low = y.mid_all
        self.high = self.low + SPAN
        self.sum_rows = -(-(self.high + SPAN) // 16) * 16
        self.edge_sums = EDGE + SPAN
        self.side = x.fine // RADIUS
        self.fine_groups = -(-self.fine_planes // self.side)
        self.folded = 0 < self.fine_planes % self.side <= self.side // 2
        self.fine_ends = self.fine_groups * self.fine_rows - (self.fine_rows // 2 if self.folded else 0)
        self.sum_blocks = -(-self.sum_planes * self.sum_rows // 128)
        self.coarse_blocks = -(-self.coarse_planes * self.sum_rows // 128)
        self.mid_ends = self.fine_ends + self.coarse_blocks * self.edge_sums
        self.x_rows = self.mid_ends + (self.sum_blocks - self.coarse_blocks) * up8(EDGE)
        assert x.mid_all + x.coarse_all <= x.fine
        assert self.far + y.second <= self.low and y.second <= 8 and y.coarse_all == SPAN and z.coarse_all == SPAN
        assert z.coarse >= RADIUS and y.coarse >= RADIUS and y.count == 4


def narrow_kernel(s, out):
    x = s.x
    lanes = (x.fine, x.fine)
    cell, lane = iota(lanes, 0), iota(lanes, 1)
    k = lane - 1
    to_mid = jnp.where((lane < x.mid_all) & x.holds_mid(k), weight_of(cell - 2 * k), 0.0)
    c = lane - x.mid_all - 2
    inside = (lane >= x.mid_all) & (lane < x.mid_all + x.coarse_all) & x.holds_coarse(c)
    to_coarse = jnp.where(inside, weight_of(cell - 1 - 2 * c), 0.0)
    narrow = to_mid + jnp.dot(to_mid, to_coarse, precision=EXACT, preferred_element_type=F32)
    out[...] = jnp.concatenate(split(narrow), axis=1)


def restrict_kernel(s, nz, source, narrow, charges, own, ahead, behind, far, *rest):
    messages, (wide, mid, high, coarse, packed, groups) = rest[:-6], rest[-6:]
    z, y, x = s.z, s.y, s.x
    wide[...] = jnp.zeros(wide.shape, F32)
    charges[...] = source[...]
    cells = source[...].reshape(z.fine * y.fine, x.fine)
    top, rest = cells.astype(BF16), cells
    rest = rest - top.astype(F32)
    middle = rest.astype(BF16)
    low = (rest - middle.astype(F32)).astype(BF16)
    weights = narrow[...]
    both = jnp.dot(low, weights, preferred_element_type=F32)
    both = both + jnp.dot(
        jnp.concatenate([top, middle], axis=1), jnp.concatenate([weights, weights], axis=0), preferred_element_type=F32
    )
    reduced = both[:, : x.fine] + both[:, x.fine :]
    wide[:, 8 : 8 + y.fine, :] = reduced.reshape(z.fine, y.fine, x.fine)
    rows = 0.0
    for offset, weight in WEIGHTS:
        rows = rows + weight * wide[:, pl.ds(6 + offset, y.mid_all, stride=2), :]
    keep = y.holds_mid(iota((y.mid_all, x.fine), 0) - 1)
    mid[...] = jnp.zeros(mid.shape, F32)
    coarse[...] = jnp.zeros(coarse.shape, F32)
    high[...] = jnp.zeros(high.shape, F32)
    for p in range(z.mid_all):
        total = 0.0
        for offset, weight in WEIGHTS:
            at = 2 * (p - 1) + offset
            if 0 <= at < z.fine:
                total = total + weight * rows[at]
        total = jnp.where(keep & z.holds_mid(p - 1), total, 0.0)
        mid[p, : y.mid_all] = total
        high[p, 8 : 8 + y.mid_all] = total
    rows = 0.0
    for offset, weight in WEIGHTS:
        rows = rows + weight * high[:, pl.ds(5 + offset, y.coarse_all, stride=2), :]
    keep = y.holds_coarse(iota((y.coarse_all, x.fine), 0) - 2)
    for p in range(z.coarse_all):
        total = 0.0
        for offset, weight in WEIGHTS:
            at = 2 * (p - 2) + offset + 1
            if 0 <= at < z.mid_all:
                total = total + weight * rows[at]
        coarse[p, : y.coarse_all] = jnp.where(keep & z.holds_coarse(p - 2), total, 0.0)
    is_mid = iota(mid.shape[1:], 1) < x.mid_all
    for p in range(z.mid_all):
        own[p] = jnp.where(is_mid, mid[p], coarse[p]) if p < z.coarse_all else jnp.where(is_mid, mid[p], 0.0)
    up = s.y2_routes[0].up()
    count, end = y.second, y.coarse_all
    groups[...] = jnp.zeros(groups.shape, F32)
    for p in range(z.coarse_all):
        g, at = p // s.far_planes, p % s.far_planes * count
        groups[g, at : at + count] = jnp.where(up, own[p, end - count : end], own[p, :count])
    lane = iota(far.shape, 1)
    total = jnp.zeros(far.shape, F32)
    for g in range(s.far_groups):
        first = g * x.coarse_all
        turned = pltpu.roll(groups[g], (first - x.mid_all) % x.fine, 1)
        total = jnp.where((lane >= first) & (lane < first + x.coarse_all), turned, total)
    far[...] = total
    is_side = iota((SPAN, x.fine), 1) < x.mid_all
    for message, route in zip((ahead, behind), s.y_routes):
        up = route.up()
        edge = jnp.where(up, charges[:, y.fine - RADIUS :, :], charges[:, :RADIUS, :])
        message[: s.y_fine] = edge.reshape(s.y_fine, x.fine)
        for p in range(z.mid_all):
            last = jnp.where(is_side, own[p, y.mid_all - SPAN : y.mid_all], own[p, y.coarse_all - SPAN : y.coarse_all])
            at = s.y_fine + p * SPAN
            message[at : at + SPAN] = jnp.where(up, last, own[p, :SPAN])
        filled = s.y_fine + SPAN * z.mid_all
        if filled < s.y_rows:
            message[filled:] = jnp.zeros((s.y_rows - filled, x.fine), F32)
    for message, route in zip(messages, s.z_routes):
        up = route.up().astype(jnp.int32)
        message[: s.z_fine] = charges[pl.ds(up * (z.fine - RADIUS), RADIUS)].reshape(s.z_fine, x.fine)
        packed[...] = jnp.zeros(packed.shape, F32)
        for p in range(EDGE):
            packed[0, p * y.mid_all : (p + 1) * y.mid_all] = mid[up * (z.mid_all - EDGE) + p][: y.mid_all]
        for p in range(SPAN):
            plane = coarse[up * (z.coarse_all - SPAN) + p]
            packed[1, p * y.coarse_all : (p + 1) * y.coarse_all] = plane[: y.coarse_all]
        is_mid = iota(packed.shape[1:], 1) < x.mid_all
        message[s.z_fine :] = jnp.where(is_mid, packed[0], packed[1])
    for message, route in zip(messages[nz:], s.z2_routes):
        up = route.up().astype(jnp.int32)
        message[...] = jnp.zeros(message.shape, F32)
        for p in range(z.second):
            plane = coarse[up * (z.coarse_all - z.second) + p]
            message[p * y.coarse_all : (p + 1) * y.coarse_all] = plane[: y.coarse_all]


class Slab:
    def __init__(self, message, mid, coarse):
        self.message, self.mid, self.coarse = message, mid, coarse

    def coarse_rows(self, first, count):
        return self.message[self.coarse + first : self.coarse + first + count]

    def rows(self, is_mid, first_mid, first_coarse, count):
        coarse = 0.0 if first_coarse is None else self.coarse_rows(first_coarse, count)
        mid = 0.0 if self.mid is None else self.message[self.mid + first_mid : self.mid + first_mid + count]
        return jnp.where(is_mid, mid, coarse)


def slabs(s, z_messages, z2_messages):
    out = []
    for message in z_messages:
        for p in range(SPAN):
            mid = s.z_fine + p * s.y.mid_all if p < EDGE else None
            out.append(Slab(message, mid, s.z_fine + p * s.y.coarse_all))
    for message in z2_messages:
        out += [Slab(message, None, p * s.y.coarse_all) for p in range(s.z.second)]
    return out


def spread_kernel(s, nz, nz2, _, *rest):
    z_messages, z2_messages = rest[:nz], rest[nz : nz + nz2]
    ahead, behind = rest[-2:]
    z, y, x = s.z, s.y, s.x
    is_mid = iota((SPAN, x.fine), 1) < x.mid_all
    planes = slabs(s, z_messages, z2_messages)
    for message, route in zip((ahead, behind), s.y_routes):
        up = route.up()
        at = 0
        for z_message in z_messages:
            slab = z_message[: s.z_fine].reshape(RADIUS, y.fine, x.fine)
            edge = jnp.where(up, slab[:, y.fine - RADIUS :], slab[:, :RADIUS])
            message[at : at + RADIUS * RADIUS] = edge.reshape(RADIUS * RADIUS, x.fine)
            at += RADIUS * RADIUS
        for plane in planes:
            last = plane.rows(is_mid, y.mid_all - SPAN, y.coarse_all - SPAN, SPAN)
            message[at : at + SPAN] = jnp.where(up, last, plane.rows(is_mid, 0, 0, SPAN))
            at += SPAN
        if at < s.slab_rows:
            message[at:] = jnp.zeros((s.slab_rows - at, x.fine), F32)


def pass_kernel(s, far, out):
    out[...] = far[...]


def roll_ends(s, plane_rows, count):
    x = s.x
    lane = iota((count, x.fine), 1)
    for g in range(s.fine_groups):
        ends = [jnp.zeros(lane.shape, F32)] * 2
        for j in range(min(s.side, s.fine_planes - g * s.side)):
            plane = plane_rows(g * s.side + j)
            here = (lane >= RADIUS * j) & (lane < RADIUS * (j + 1))
            for n, start in enumerate((x.fine - RADIUS, 0)):
                shift = (RADIUS * j - start) % x.fine
                ends[n] = jnp.where(here, pltpu.roll(plane, shift, 1) if shift else plane, ends[n])
        yield g, ends


def early_kernel(s, nz, charges, *rest):
    z_messages = rest[:nz]
    x_fine, y_own, t_part, last, start, slab = rest[nz:]
    z, y, x = s.z, s.y, s.x
    for n, message in enumerate(z_messages):
        slab[n * RADIUS : (n + 1) * RADIUS] = message[: s.z_fine].reshape(RADIUS, y.fine, x.fine)

    def rows_of(p):
        return charges[p] if p < z.fine else slab[p - z.fine]

    t_part[...] = jnp.zeros(t_part.shape, F32)
    fine_at = fine_places(s)
    for g in range(0, s.fine_planes, 8):
        planes = charges[g : g + 8] if g < z.fine else slab[g - z.fine : g - z.fine + 8]
        a, b = split(contract_x(s, planes.reshape(8 * y.fine, x.fine), x_fine))
        for p in range(8):
            rows = slice(p * y.fine, (p + 1) * y.fine)
            store_terms(t_part, *fine_at[g + p], contract_y(s, y_own, a[rows], b[rows]))
    for g, ends in roll_ends(s, rows_of, y.fine):
        rows = slice(g * y.fine, (g + 1) * y.fine)
        last[rows], start[rows] = ends


def collect_kernel(s, nz, nz2, last, start, own, *rest):
    z_messages, z2_messages = rest[:nz], rest[nz : nz + nz2]
    rest = rest[nz + nz2 :]
    pairs = rest[:4]
    fars = rest[4 : 5 + nz + nz2]
    fine, sums, first, second, raw, rows = rest[5 + nz + nz2 :]
    z, y, x = s.z, s.y, s.x
    below = s.y_routes[0].below()
    planes = slabs(s, z_messages, z2_messages)

    def sides(which, start, count):
        a, b = (message[start : start + count] for message in pairs[2 * which : 2 * which + 2])
        return jnp.where(below, a, b), jnp.where(below, b, a)

    parts = [(0, z.fine, 0, 0)] + [(z.fine + n * RADIUS, RADIUS, 1, n * RADIUS * RADIUS) for n in range(nz)]
    for at, count, which, row in parts:
        low, high = sides(which, row, RADIUS * count)
        fine[at : at + count, :RADIUS] = low.reshape(count, RADIUS, x.fine)
        fine[at : at + count, RADIUS:] = high.reshape(count, RADIUS, x.fine)
    sums[...] = jnp.zeros(sums.shape, F32)
    raw[...] = jnp.zeros(raw.shape, F32)
    for n, far in enumerate(fars):
        for g in range(s.far_groups):
            turned = pltpu.roll(far[...], (x.mid_all - g * x.coarse_all) % x.fine, 1)
            for p in range(g * s.far_planes, min((g + 1) * s.far_planes, z.coarse_all)):
                at = p % s.far_planes * y.second
                rows[n, p, : y.second] = turned[at : at + y.second]
    is_mid = iota((y.second, x.fine), 1) < x.mid_all

    def rows_of_plane(out, p, body, which, row, far_plane):
        low, high = sides(which, row, SPAN)
        out[p, : y.mid_all] = body
        out[p, s.low : s.low + SPAN] = low
        out[p, s.high : s.high + SPAN] = high
        if far_plane is not None:
            at = slice(s.far, s.far + y.second)
            out[p, at] = jnp.where(is_mid, out[p, at], rows[far_plane][: y.second])

    for p in range(z.mid_all):
        far_plane = (0, p) if p < z.coarse_all else None
        rows_of_plane(sums, s.place_of(p), own[p, : y.mid_all], 0, s.y_fine + p * SPAN, far_plane)
    is_mid_row = iota((SPAN, x.fine), 1) < x.mid_all
    is_mid_rest = iota((y.mid_all - SPAN, x.fine), 1) < x.mid_all
    slab_far = [(1 + n, p) for n in range(nz) for p in range(SPAN)]
    for n, route in enumerate(s.z2_routes):
        at = jnp.where(route.below(), z.coarse_all - z.second, 0)
        slab_far += [(1 + nz + n, at + p) for p in range(z.second)]
    for p, plane in enumerate(planes):
        body = [plane.rows(is_mid_row, 0, 0, SPAN), plane.rows(is_mid_rest, SPAN, None, y.mid_all - SPAN)]
        rows_of_plane(raw, p, jnp.concatenate(body, axis=0), 1, s.slab_fine + p * SPAN, slab_far[p])
    is_mid = iota((s.sum_rows, x.fine), 1) < x.mid_all

    def number(condition, a, b):
        return jnp.where(condition, a, b)

    for n, route in enumerate(s.z_routes):
        lower, base = route.below(), n * SPAN
        for j in range(RADIUS):
            a = raw[base + number(lower, 0, 3) + j]
            b = raw[base + number(lower, SPAN - 5 - RADIUS, 5) + j]
            sums[s.slab_start + n * RADIUS + j] = jnp.where(is_mid, a, b)
        for i in range(3):
            at = number(lower, 0, s.place_of(z.mid)) + i
            sums[at] = sums[at] + jnp.where(is_mid, raw[base + number(lower, EDGE - 3, 0) + i], 0.0)
        for i in range(5):
            at = number(lower, 0, z.coarse) + i
            sums[at] = sums[at] + jnp.where(is_mid, 0.0, raw[base + number(lower, SPAN - 5, 0) + i])
    for n, route in enumerate(s.z2_routes):
        base = len(s.z_routes) * SPAN + n * z.second
        at = s.slab_start + number(route.below(), RADIUS - z.coarse, RADIUS + z.coarse - 5)
        for p in range(z.second):
            sums[at + p] = sums[at + p] + jnp.where(is_mid, 0.0, raw[base + p])

    up = s.x_routes[0].up()
    half, shift = s.fine_rows // 2, x.fine // 2
    is_first_half = iota((half, x.fine), 1) < shift
    for g, ends in roll_ends(s, lambda p: fine[p], 2 * RADIUS):
        rows = slice(g * y.fine, (g + 1) * y.fine)
        both = [jnp.concatenate([old[rows], new], axis=0) for old, new in zip((last, start), ends)]
        if s.folded and g == s.fine_groups - 1:
            both = [jnp.where(is_first_half, e[:half], pltpu.roll(e[half:], shift, 1)) for e in both]
        at = slice(g * s.fine_rows, g * s.fine_rows + both[0].shape[0])
        first[at] = jnp.where(up, both[0], both[1])
        second[at] = jnp.where(up, both[1], both[0])
    width = EDGE + SPAN
    row, lane = iota((2 * width, x.fine), 0), iota((2 * width, x.fine), 1)
    is_first = row < width
    goes_up = choose(up, is_first, ~is_first)
    slot = jnp.where(is_first, row, row - width)
    from_mid = jnp.where(goes_up, x.mid_all - EDGE + slot, slot)
    from_coarse = slot - EDGE + jnp.where(goes_up, x.mid_all + x.coarse_all - SPAN, x.mid_all)
    wanted = jnp.where(slot < EDGE, from_mid, from_coarse)
    picked_sums = pick((lane == wanted).astype(BF16), sums[...].reshape(s.sum_planes * s.sum_rows, x.fine))
    spare = s.sum_blocks * 128 - picked_sums.shape[1]
    if spare:
        picked_sums = jnp.concatenate([picked_sums, jnp.zeros((2 * width, spare), F32)], axis=1)
    for n, message in enumerate((first, second)):
        rows = picked_sums[n * width : (n + 1) * width]
        for b in range(s.coarse_blocks):
            at = s.fine_ends + b * width
            message[at : at + width] = rows[:, b * 128 : (b + 1) * 128]
        for b in range(s.coarse_blocks, s.sum_blocks):
            at = s.mid_ends + (b - s.coarse_blocks) * up8(EDGE)
            message[at : at + up8(EDGE)] = rows[: up8(EDGE), b * 128 : (b + 1) * 128]


def band(taps, level, offset, valid):
    at = jnp.where(valid, offset + RADIUS, -1)
    out = [jnp.zeros(at.shape, F32) for _ in range(TERMS)]
    for tap in range(TAPS):
        here = at == tap
        out = [jnp.where(here, taps[level, term, tap], total) for term, total in enumerate(out)]
    return out


def dot(a, b):
    return jnp.dot(a, b, precision=EXACT, preferred_element_type=F32)


def z_columns(s):
    return s.z.fine * RADIUS


def lower_x(x):
    return x.index() > 0


def higher_x(x):
    return x.index() < x.count - 1


def operator_kernel(s, taps, x_fine, x_sums, ends, y_own, y_edge, y_fine, y_mid, y_coarse, widen_x, widen_y, table):
    y, x = s.y, s.x
    for level in range(2):
        for term in range(TERMS):
            for tap in range(TAPS):
                table[(level * TERMS + term) * TAPS + tap] = jnp.full((8, x.fine), taps[level, term, tap], F32)
    is_second = iota((8, x.fine), 1) >= x.fine // TERMS
    for tap in range(TAPS):
        table[2 * TERMS * TAPS + tap] = jnp.where(is_second, taps[2, 1, tap], taps[2, 0, tap])
    own, edge = x.fine, 64
    shape = (own + edge, x.fine)
    row, lane = iota(shape, 0), iota(shape, 1)
    t = row - own
    lower, higher = x.index() > 0, x.index() < x.count - 1
    is_own = row < own

    def place(half, own_place, own_valid, first, count, low_place, high_place):
        is_low = t < half
        r = jnp.where(is_low, t, t - half) - first
        there = (r >= 0) & (r < count) & (t < 2 * half) & choose(is_low, lower, higher)
        valid = choose(is_own, own_valid, there)
        return jnp.where(is_own, own_place, jnp.where(is_low, low_place + r, high_place + r)), valid

    half = s.edge_sums
    fine = band(taps, 0, row - lane, is_own)
    where, valid = place(half, row - 1, row < x.mid_all, 0, EDGE, 2 - EDGE, x.mid - 1)
    mid = band(taps, 1, where - (lane - 1), valid & (lane < x.mid_all))
    first = x.mid_all
    inside = (row >= first) & (row < first + x.coarse_all)
    where, valid = place(half, row - first - 2, inside, EDGE, SPAN, 3 - SPAN, x.coarse - 2)
    side = x.fine // TERMS
    column = lane % side
    terms = band(taps, 2, where - (column - 2), valid & (column < x.coarse_all))
    coarse = terms[0]
    for term in range(1, TERMS):
        coarse = jnp.where(lane >= term * side, terms[term], coarse)
    a, b = iota((x.fine, x.fine), 0), iota((x.fine, x.fine), 1)
    from_mid = jnp.where((a < x.mid_all) & x.holds_mid(a - 1), weight_of(b - 2 * (a - 1)), 0.0)
    c = a % side
    from_coarse = jnp.where((c < x.coarse_all) & x.holds_coarse(c - 2), weight_of(b - 1 - 2 * (c - 2)), 0.0)
    high, low = split(dot(from_coarse, from_mid))
    widen_x[:own] = high
    widen_x[own : 2 * own] = high
    widen_x[2 * own :] = low
    columns = [(x_fine, 0, 0, fine)]
    columns += [(x_sums, half, 0, [dot(m, from_mid) for m in mid])]
    columns += [(x_sums, half, TERMS * x.fine, [coarse])]
    for out, half, at, terms in columns:
        for term, matrix in enumerate(terms):
            high, low = split(matrix)
            cols = slice(at + term * x.fine, at + (term + 1) * x.fine)
            n = 2 * half
            out[0:own, cols] = high[:own]
            out[own : 2 * own, cols] = high[:own]
            out[2 * own : 3 * own, cols] = low[:own]
            if n:
                out[3 * own :, cols] = jnp.zeros((out.shape[0] - 3 * own, x.fine), BF16)
                out[3 * own : 3 * own + n, cols] = high[own : own + n]
                out[3 * own + n : 3 * own + 2 * n, cols] = high[own : own + n]
                out[3 * own + 128 : 3 * own + 128 + n, cols] = low[own : own + n]

    z, slots, wide = s.z, s.side * s.fine_groups, z_columns(s)
    slot, column = iota((slots, wide), 0), iota((slots, wide), 1)
    where, valid = slot, slot < z.fine
    for n, route in enumerate(s.z_routes):
        lower, i, first = route.below(), z.index(), z.fine + n * RADIUS
        here = (slot >= first) & (slot < first + RADIUS)
        where = jnp.where(here, slot - first + jnp.where(lower, -RADIUS, z.fine), where)
        valid = choose(here, choose(lower, i >= 1, i + 1 < z.count), valid)
    planes = band(taps, 0, where - column // RADIUS, valid)
    r, c = iota((RADIUS, wide), 0), iota((RADIUS, wide), 1) % RADIUS
    cells = (slots, RADIUS, wide)
    for side, (offset, valid) in enumerate(((r - c - RADIUS, lower_x(x)), (r - c + RADIUS, higher_x(x)))):
        columns = band(taps, 0, offset, choose(valid, r >= 0, r < 0))
        for term in range(TERMS):
            joint = jnp.broadcast_to(planes[term][:, None, :], cells) * jnp.broadcast_to(columns[term][None], cells)
            high, low = split(joint.reshape(slots * RADIUS, wide))
            at = 2 * term + side
            ends[at, : slots * RADIUS] = high
            ends[at, slots * RADIUS : 2 * slots * RADIUS] = high
            ends[at, 2 * slots * RADIUS :] = low

    lower, higher = y.index() > 0, y.index() < y.count - 1
    far_below = s.y2_routes[0].below()
    n = up8(y.mid_all)

    def write(out, size, terms):
        part = iota(terms[0].shape, 1) >= 2 * size
        for term, matrix in enumerate(terms):
            high, low = split(matrix)
            n = matrix.shape[0]
            out[term * n : (term + 1) * n] = jnp.where(part, low.astype(F32), high.astype(F32)).astype(BF16)

    def columns_of(rows, size):
        lane = iota((rows, 3 * size), 1)
        return jnp.where(lane >= 2 * size, lane - 2 * size, jnp.where(lane >= size, lane - size, lane))

    c = columns_of(y.fine, s.fine_rows)
    is_low = (c >= y.fine) & (c < y.fine + RADIUS)
    is_high = c >= y.fine + RADIUS
    where = jnp.where(is_low, c - y.fine - RADIUS, jnp.where(is_high, c - RADIUS, c))
    valid = choose(is_low, lower, choose(is_high, higher, c >= 0))
    write(y_fine, s.fine_rows, band(taps, 0, where - iota(c.shape, 0), valid))
    c = columns_of(y.fine, y.fine)
    write(y_own, y.fine, band(taps, 0, c - iota(c.shape, 0), c >= 0))
    c = columns_of(y.fine, 2 * RADIUS)
    where = jnp.where(c < RADIUS, c - RADIUS, c - RADIUS + y.fine)
    write(y_edge, 2 * RADIUS, band(taps, 0, where - iota(c.shape, 0), choose(c < RADIUS, lower, higher)))

    c = columns_of(n, s.sum_rows)
    r = iota(c.shape, 0)
    is_low = (c >= s.low) & (c < s.low + SPAN)
    is_high = (c >= s.high) & (c < s.high + SPAN)
    is_far = (c >= s.far) & (c < s.far + y.second)
    where = jnp.where(is_low, c - s.low + 2 - SPAN, jnp.where(is_high, c - s.high + y.mid - 1, c - 1))
    valid = choose(is_low, lower, choose(is_high, higher, c < y.mid_all))
    mid = band(taps, 1, where - (r - 1), valid & (r < y.mid_all))
    far = jnp.where(far_below, -2 - y.coarse, 2 * y.coarse - 2)
    where = jnp.where(is_low, c - s.low + 3 - SPAN, jnp.where(is_high, c - s.high + y.coarse - 2, c - 2))
    where = jnp.where(is_far, c - s.far + far, where)
    valid = choose(is_low, lower, choose(is_high, higher, (c < y.coarse_all) | is_far))
    coarse = band(taps, 2, where - (r - 2), valid & (r < y.coarse_all))
    o, k = iota((y.fine, n), 0), iota((y.fine, n), 1)
    from_mid = jnp.where((k < y.mid_all) & y.holds_mid(k - 1), weight_of(o - 2 * (k - 1)), 0.0)
    m = s.coarse_rows
    c = columns_of(n, m)
    k = iota(c.shape, 0)
    from_coarse = jnp.where((c < y.coarse_all) & y.holds_coarse(c - 2), weight_of(k - 1 - 2 * (c - 2)), 0.0)
    write(y_mid, s.sum_rows, [dot(from_mid, matrix) for matrix in mid])
    write(y_coarse, s.sum_rows, [matrix[:m] for matrix in coarse])
    write(widen_y, m, [dot(from_mid, from_coarse)])


def contract_y(s, weights, high, low):
    joined = jnp.concatenate([high, low, high], axis=0)
    result = jnp.dot(weights[...], joined, preferred_element_type=F32)
    n, m = s.y.fine, s.x.fine
    return [result[t * n : (t + 1) * n, t * m : (t + 1) * m] for t in range(TERMS)]


def contract_z(table, level, held, base, count):
    rows = held.shape[2:]
    totals = [None] * count
    for t in range(held.shape[1]):
        for j in range(count + TAPS - 1):
            plane = held[base + j, t].reshape(rows[0] // 8, 8, rows[1])
            for i in range(max(0, j - TAPS + 1), min(count, j + 1)):
                term = table[(level * TERMS + t) * TAPS + j - i][None] * plane
                totals[i] = term if totals[i] is None else totals[i] + term
    return [total.reshape(rows) for total in totals]


def slab_starts(s, below_at, above_at):
    result = []
    for route in s.z_routes:
        lower, i = route.below(), s.z.index()
        valid = choose(lower, i >= 1, i + 1 < s.z.count)
        result.append((jnp.where(lower, below_at, above_at), valid))
    return result


def store_terms(held, at, valid, parts):
    for t, part in enumerate(parts):
        held[at, t] = part if valid is None else jnp.where(valid, part, 0.0)


BLOCK = 4


def fine_places(s):
    places = [(RADIUS + p, None) for p in range(s.z.fine)]
    for start, valid in slab_starts(s, 0, s.z.fine + RADIUS):
        places += [(start + p, valid) for p in range(RADIUS)]
    return places


def contract_x(s, grid, weights):
    high, low = split(grid)
    joined = jnp.concatenate([high, low, high], axis=1)
    return jnp.dot(joined, weights[: 3 * s.x.fine], preferred_element_type=F32)


def own_kernel(s, table, t_part, fine, sums, x_fine, x_sums, y_edge, fine_part, sums_part, t_fine):
    z, x = s.z, s.x
    t_fine[...] = t_part[...]
    fine_at = fine_places(s)

    def fine_group(g, count):
        n = 2 * RADIUS
        a, b = split(contract_x(s, fine[g : g + count].reshape(count * n, x.fine), x_fine))
        for p in range(count):
            rows = slice(p * n, (p + 1) * n)
            at, valid = fine_at[g + p]
            for t, part in enumerate(contract_y(s, y_edge, a[rows], b[rows])):
                t_fine[at, t] = t_fine[at, t] + (part if valid is None else jnp.where(valid, part, 0.0))

    def fine_block(k):
        for i, total in enumerate(contract_z(table, 0, t_fine, k, BLOCK)):
            fine_part[k + i] = total

    def sum_part(g, count):
        n = s.sum_rows
        grid = sums[g : g + count].reshape(count * n, x.fine)
        sums_part[g * n : (g + count) * n] = contract_x(s, grid, x_sums)

    later = []
    done = 0
    for g in list(range(z.fine, s.fine_planes, 8)) + list(range(0, z.fine, 8)):
        fine_group(g, 8)
        while later:
            later.pop(0)()
        if g < z.fine:
            ready = g if g + 8 < z.fine else z.fine
            later += [lambda k=k: fine_block(k) for k in range(done, ready, BLOCK)]
            done = max(done, ready)
    starts = list(range(0, s.sum_planes, 8))
    while later or starts:
        if starts:
            sum_part(starts[0], min(8, s.sum_planes - starts[0]))
            starts.pop(0)
        if later:
            later.pop(0)()


def sum_kernel(s, table, fine, sums, first, second, x_sums, ends, y_fine, y_mid, y_coarse, widen_x, widen_y, result, *scratch):
    sums_ends, t_mid, t_coarse, p_mid, p_coarse, narrow, out, left = scratch
    z, y, x = s.z, s.y, s.x
    below = s.x_routes[0].below()
    half = s.edge_sums
    def ends_of(start, rows):
        one, two = first[start : start + rows], second[start : start + rows]
        return jnp.where(below, one, two), jnp.where(below, two, one)

    for b in range(s.sum_blocks):
        if b < s.coarse_blocks:
            pair = ends_of(s.fine_ends + b * half, half)
        else:
            rest = jnp.zeros((half - up8(EDGE), 128), F32)
            pair = ends_of(s.mid_ends + (b - s.coarse_blocks) * up8(EDGE), up8(EDGE))
            pair = [jnp.concatenate([ends, rest], axis=0) for ends in pair]
        rows = jnp.concatenate(pair, axis=0)
        zeros = jnp.zeros((128 - 4 * half, 128), F32)
        sums_ends[b * 128 : (b + 1) * 128] = jnp.concatenate([rows, rows, zeros], axis=0).T

    def along_x(start, rows):
        edge_high, edge_low = split(sums_ends[start : start + rows])
        is_high = iota(edge_high.shape, 1) < 2 * half
        packed = jnp.where(is_high, edge_high.astype(F32), edge_low.astype(F32)).astype(BF16)
        joined = jnp.concatenate([packed, edge_high], axis=1)
        part = jnp.dot(joined, x_sums[3 * x.fine :], preferred_element_type=F32)
        return split(sums[start : start + rows] + part)

    def fine_edges():
        columns = []
        for flip in range(2):
            for g in range(s.fine_groups):
                is_folded = s.folded and g == s.fine_groups - 1
                at = slice(g * s.fine_rows, s.fine_ends if is_folded else (g + 1) * s.fine_rows)
                pair = (first[at], second[at])
                ends_here = jnp.where(below, pair[flip], pair[1 - flip])
                if is_folded:
                    ends_here = jnp.concatenate([ends_here, pltpu.roll(ends_here, x.fine // 2, 1)], axis=0)
                columns.append(ends_here)
        high, low = split(jnp.concatenate(columns, axis=1))
        joined = jnp.concatenate([high, low, high], axis=0)
        high, low = split(jnp.dot(y_fine[...], joined, preferred_element_type=F32))
        width = s.fine_groups * x.fine
        result = []
        for side in range(2):
            total = 0.0
            for t in range(TERMS):
                rows, cols = slice(t * y.fine, (t + 1) * y.fine), slice(side * width, (side + 1) * width)
                a, b = high[rows, cols], low[rows, cols]
                joined = jnp.concatenate([a, b, a], axis=1)
                total = total + jnp.dot(joined, ends[2 * t + side], preferred_element_type=F32)
            result.append(total)
        return result

    t_mid[...] = jnp.zeros(t_mid.shape, F32)
    t_coarse[...] = jnp.zeros(t_coarse.shape, F32)
    mid_at = [(RADIUS + p, None) for p in range(z.mid_all)]
    mid_at, rest_at = mid_at[: z.coarse_all], mid_at[z.coarse_all :]
    coarse_at = [(RADIUS + p, None) for p in range(z.coarse_all)]
    for start, valid in slab_starts(s, 0, z.mid + 3 + RADIUS):
        mid_at += [(start + p, valid) for p in range(RADIUS)]
    mid_at += rest_at
    for start, valid in slab_starts(s, 0, z.coarse + 5 + RADIUS):
        coarse_at += [(start + p, valid) for p in range(RADIUS)]
    coarse_at += [(None, None)] * len(rest_at)
    is_second = iota((s.coarse_rows, x.fine), 1) >= x.fine // TERMS

    def sum_group(g, count):
        n = s.sum_rows
        a, b = along_x(g * n, count * n)
        for p in range(count):
            rows = slice(p * n, (p + 1) * n)
            at, valid = mid_at[g + p]
            cols = slice(0, TERMS * x.fine)
            store_terms(t_mid, at, valid, contract_y(s, y_mid, a[rows, cols], b[rows, cols]))
            at, valid = coarse_at[g + p]
            if at is not None:
                cols = slice(TERMS * x.fine, (TERMS + 1) * x.fine)
                joined = jnp.concatenate([a[rows, cols], b[rows, cols], a[rows, cols]], axis=0)
                both = jnp.dot(y_coarse[...], joined, preferred_element_type=F32)
                m = s.coarse_rows
                store_terms(t_coarse, at, valid, [jnp.where(is_second, both[m:], both[:m])])

    def coarse_block(k):
        count = min(BLOCK, z.coarse_all - k)
        for i, total in enumerate(contract_z(table, 2, t_coarse, k, count)):
            narrow[k + i] = jnp.where(z.holds_coarse(k + i - 2), total, 0.0)

    def widen():
        m = s.coarse_rows
        high, low = split(narrow[...].reshape(z.coarse_all * m, x.fine))
        joined = jnp.concatenate([high, low, high], axis=1)
        high, low = split(jnp.dot(joined, widen_x[...], preferred_element_type=F32))
        for p in range(z.coarse_all):
            rows = slice(p * m, (p + 1) * m)
            joined = jnp.concatenate([high[rows], low[rows], high[rows]], axis=0)
            p_coarse[p] = jnp.dot(widen_y[...], joined, preferred_element_type=F32)

    def mid_block(k):
        count = min(BLOCK, z.mid_all - k)
        for i, total in enumerate(contract_z(table, 1, t_mid, k, count)):
            m = k + i - 1
            for offset, weight in WEIGHTS:
                if (m - offset) % 2 == 0 and 0 <= (m - offset) // 2 + 2 < z.coarse_all:
                    total = total + weight * p_coarse[(m - offset) // 2 + 2]
            p_mid[k + i] = jnp.where(z.holds_mid(m), total, 0.0)

    edges = fine_edges()
    lane = iota((y.fine, x.fine), 1)

    def begin(k):
        block, at = k // s.side, k % s.side * RADIUS
        low, high = (edge[:, block * x.fine : (block + 1) * x.fine] for edge in edges)
        low = pltpu.roll(low, -at % x.fine, 1) if at else low
        turn = (x.fine - RADIUS - at) % x.fine
        high = pltpu.roll(high, turn, 1) if turn else high
        out[k] = fine[k] + jnp.where(lane < RADIUS, low, jnp.where(lane >= x.fine - RADIUS, high, 0.0))

    def finish(k):
        total = out[k]
        for offset, weight in WEIGHTS:
            if (k - offset) % 2 == 0:
                total = total + weight * p_mid[(k - offset) // 2 + 1]
        out[k] = total

    groups = list(range(0, s.sum_planes, 4))
    share = -(-z.fine // len(groups))
    for n, g in enumerate(groups):
        sum_group(g, min(4, s.sum_planes - g))
        for k in range(n * share, min((n + 1) * share, z.fine)):
            begin(k)
    for k in range(0, z.coarse_all, BLOCK):
        coarse_block(k)
    widen()
    done, copies = 0, []
    for k in range(0, z.mid_all, BLOCK):
        mid_block(k)
        ready = z.fine if k + BLOCK >= z.mid_all else 2 * k + 2
        while done < ready:
            finish(done)
            done += 1
            if done % 8 == 0:
                part = pl.ds(done - 8, 8)
                copies.append(pltpu.make_async_copy(out.at[part], result.at[part], left.at[done // 8 - 1]))
                copies[-1].start()
    for copy in copies:
        copy.wait()


def call(kernel, outs, ins, scratch=(), flops=10**7, out_space=pltpu.VMEM):
    specs = [SMEM if a.ndim == 3 and a.shape[-1] == TAPS else VMEM for a in ins]
    size = sum(a.size * a.dtype.itemsize for a in ins) + sum(o.size * o.dtype.itemsize for o in outs)
    return pl.pallas_call(
        kernel,
        out_shape=tuple(outs),
        in_specs=specs,
        out_specs=tuple(pl.BlockSpec(memory_space=out_space) for _ in outs),
        scratch_shapes=list(scratch),
        compiler_params=PARAMS,
        cost_estimate=pl.CostEstimate(flops=flops, bytes_accessed=size, transcendentals=0),
    )(*ins)


def array(*shape, dtype=F32):
    return jax.ShapeDtypeStruct(shape, dtype)


def local(charges, kernel_taps):
    z, y, x = (Cut(name, size) for name, size in zip(("gz", "gy", "gx"), charges.shape))
    s = Sizes(z, y, x)
    n = x.fine
    nz, nz2 = len(s.z_routes), len(s.z2_routes)

    def bound(kernel, *static):
        return lambda *refs: kernel(s, *static, *refs)

    rows = up8(y.mid_all)
    (weights,) = call(bound(narrow_kernel), [array(n, 2 * n, dtype=BF16)], [], flops=10**10)
    held, own, ahead, behind, far, *messages = call(
        bound(restrict_kernel, nz),
        [array(*charges.shape), array(z.mid_all, rows, n)] + [array(s.y_rows, n)] * 2 + [array(s.far_rows, n)] + [array(s.z_rows, n)] * nz + [array(s.z2_rows, n)] * nz2,
        [charges, weights],
        [
            pltpu.VMEM((z.fine, y.fine + 16, n), F32),
            pltpu.VMEM((z.mid_all, rows, n), F32),
            pltpu.VMEM((z.mid_all, up8(y.mid + 24), n), F32),
            pltpu.VMEM((z.mid_all, rows, n), F32),
            pltpu.VMEM((2, s.z_rows - s.z_fine, n), F32),
            pltpu.VMEM((s.far_groups, s.far_rows, n), F32),
        ],
    )
    z_got = [route(m) for route, m in zip(s.z_routes + s.z2_routes, messages)]
    sides = [s.y_routes[0](ahead), s.y_routes[1](behind)]
    far = s.y2_routes[0](far)
    (passed,) = call(bound(pass_kernel), [array(s.far_rows, n)], [far], flops=2*10**9)
    operators = call(
        bound(operator_kernel),
        [
            array(3 * n, TERMS * n, dtype=BF16),
            array(3 * n + 256, (TERMS + 1) * n, dtype=BF16),
            array(2 * TERMS, 3 * s.fine_groups * n, z_columns(s), dtype=BF16),
            array(TERMS * y.fine, 3 * y.fine, dtype=BF16),
            array(TERMS * y.fine, 6 * RADIUS, dtype=BF16),
            array(TERMS * y.fine, 3 * s.fine_rows, dtype=BF16),
            array(TERMS * y.fine, 3 * s.sum_rows, dtype=BF16),
            array(TERMS * s.coarse_rows, 3 * s.sum_rows, dtype=BF16),
            array(3 * n, n, dtype=BF16),
            array(y.fine, 3 * s.coarse_rows, dtype=BF16),
            array((2 * TERMS + 1) * TAPS, 8, n),
        ],
        [kernel_taps],
    )
    ahead, behind = call(
        bound(spread_kernel, nz, nz2),
        [array(s.slab_rows, n), array(s.slab_rows, n)],
        [passed, *z_got],
    )
    sides += [s.y_routes[0](ahead), s.y_routes[1](behind)]
    fars = [far] + [route(passed) for route in s.z_routes + s.z2_routes]
    x_fine, x_sums, ends, y_own, y_edge, y_fine, y_mid, y_coarse, widen_x, widen_y, table = operators
    t_part, last, start = call(
        bound(early_kernel, nz),
        [array(z.fine + 2 * RADIUS, TERMS, y.fine, n)] + [array(s.fine_groups * y.fine, n)] * 2,
        [held, *z_got[:nz], x_fine, y_own],
        [pltpu.VMEM((nz * RADIUS, y.fine, n), F32)],
    )
    fine, sums, first, second = call(
        bound(collect_kernel, nz, nz2),
        [
            array(s.fine_planes, 2 * RADIUS, n),
            array(s.sum_planes, s.sum_rows, n),
            array(s.x_rows, n),
            array(s.x_rows, n),
        ],
        [last, start, own, *z_got, *sides, *fars],
        [pltpu.VMEM((s.slab_planes, s.sum_rows, n), F32), pltpu.VMEM((1 + nz + nz2, z.coarse_all, 8, n), F32)],
    )
    first, second = s.x_routes[0](first), s.x_routes[1](second)
    fine, sums = call(
        bound(own_kernel),
        [array(z.fine, y.fine, n), array(s.sum_planes * s.sum_rows, (TERMS + 1) * n)],
        [table, t_part, fine, sums, x_fine, x_sums, y_edge],
        [pltpu.VMEM((z.fine + 2 * RADIUS, TERMS, y.fine, n), F32)],
    )
    (out,) = call(
        bound(sum_kernel),
        [array(z.fine, y.fine, n)],
        [table, fine, sums, first, second, x_sums, ends, y_fine, y_mid, y_coarse, widen_x, widen_y],
        [
            pltpu.VMEM((s.sum_blocks * 128, n), F32),
            pltpu.VMEM((z.mid + 2 * RADIUS + 3, TERMS, y.fine, n), F32),
            pltpu.VMEM((z.coarse + 2 * RADIUS + 5, 1, s.coarse_rows, n), F32),
            pltpu.VMEM((z.mid_all, y.fine, n), F32),
            pltpu.VMEM((z.coarse_all, y.fine, n), F32),
            pltpu.VMEM((z.coarse_all, s.coarse_rows, n), F32),
            pltpu.VMEM((z.fine, y.fine, n), F32),
            pltpu.SemaphoreType.DMA((z.fine // 8,)),
        ],
        out_space=pltpu.HBM,
    )
    return out


def solution(mesh):
    return jax.shard_map(
        local,
        mesh=mesh,
        in_specs=(P("gz", "gy", "gx"), P()),
        out_specs=P("gz", "gy", "gx"),
        check_vma=False,
    )
```

```python
import jax
import jax.numpy as jnp
from jax import lax
from jax.experimental import pallas as pl
from jax.experimental.pallas import tpu as pltpu
from jax.sharding import PartitionSpec as P

RADIUS = 8
TAPS = 17
TERMS = 2
WEIGHTS = ((-3, -0.0625), (-1, 0.5625), (0, 1.0), (1, 0.5625), (3, -0.0625))
EXACT = lax.Precision.HIGHEST
SPAN = RADIUS + 5
EDGE = RADIUS + 3
F32, BF16 = jnp.float32, jnp.bfloat16
PARAMS = pltpu.CompilerParams(vmem_limit_bytes=32 * 1024 * 1024)
VMEM = pl.BlockSpec(memory_space=pltpu.VMEM)
SMEM = pl.BlockSpec(memory_space=pltpu.SMEM)


def up8(n):
    return -(-n // 8) * 8


def iota(shape, dim):
    return lax.broadcasted_iota(jnp.int32, shape, dim)


def weight_of(difference):
    size = jnp.abs(difference)
    out = jnp.where(size == 1, 0.5625, jnp.where(size == 3, -0.0625, 0.0))
    return jnp.where(size == 0, 1.0, out)


def choose(condition, a, b):
    return jnp.where(condition, jnp.where(a, 1, 0), jnp.where(b, 1, 0)) != 0


class Cut:
    def __init__(self, name, length):
        self.name, self.fine = name, length
        self.count = lax.axis_size(name)
        self.mid, self.coarse = length // 2, length // 4
        self.mid_all, self.coarse_all = self.mid + 3, self.coarse + 5
        self.second = max(SPAN - self.coarse, 0)

    def index(self):
        return lax.axis_index(self.name)

    def holds_mid(self, k):
        k = k + self.index() * self.mid
        return (k >= 0) & (k < self.mid * self.count)

    def holds_coarse(self, k):
        k = k + self.index() * self.coarse
        return (k >= 0) & (k < self.coarse * self.count)


class Route:
    def __init__(self, names, pairs, up, below):
        self.names, self.pairs, self.up, self.below = names, pairs, up, below

    def __call__(self, x):
        return lax.ppermute(x, self.names, self.pairs)


def flip(pairs):
    return [(b, a) for a, b in pairs]


def swap(cut, steps):
    pairs = [(i, i + steps) for i in range(cut.count - steps)]

    def up():
        return cut.index() + steps < cut.count

    return [Route(cut.name, pairs + flip(pairs), up, lambda: ~up())]


def both_ways(cut, steps):
    pairs = [(i, i + steps) for i in range(cut.count - steps)]
    yes, no = (lambda: cut.index() >= 0), (lambda: cut.index() < 0)
    return [Route(cut.name, pairs, yes, yes), Route(cut.name, flip(pairs), no, no)]


def folded(cut, beside, names):
    n, m = cut.count, lax.axis_size(beside)

    def place(c, i):
        return c * n + i if names[0] == beside else i * m + c

    pairs = []
    for c in range(0, m, 2):
        cycle = [place(c, i) for i in range(n)] + [place(c + 1, i) for i in reversed(range(n))]
        pairs += list(zip(cycle, cycle[1:] + cycle[:1]))

    def even():
        return lax.axis_index(beside) % 2 == 0

    def odd():
        return lax.axis_index(beside) % 2 == 1

    return [Route(names, pairs, even, even), Route(names, flip(pairs), odd, odd)]


def split(x):
    high = x.astype(BF16)
    return high, (x - high.astype(F32)).astype(BF16)


def pick(selector, x):
    nt = (((1,), (1,)), ((), ()))
    a = x.astype(BF16)
    rest = x - a.astype(F32)
    b = rest.astype(BF16)
    c = (rest - b.astype(F32)).astype(BF16)
    out = lax.dot_general(selector, c, nt, preferred_element_type=F32)
    out = out + lax.dot_general(selector, b, nt, preferred_element_type=F32)
    return out + lax.dot_general(selector, a, nt, preferred_element_type=F32)


class Sizes:
    def place_of(self, p):
        return p if p < self.slab_start else p + self.coarse_planes - self.slab_start

    def __init__(self, z, y, x):
        self.z, self.y, self.x = z, y, x
        self.z_routes = swap(z, 1) if z.count <= 2 else both_ways(z, 1)
        self.z2_routes = [] if z.count <= 2 else swap(z, 2) if z.count <= 4 else both_ways(z, 2)
        self.y_routes = folded(y, x.name, (x.name, y.name))
        self.y2_routes = swap(y, 2)
        self.x_routes = folded(x, z.name, (x.name, z.name))
        self.z_fine = RADIUS * y.fine
        self.z_sums = max(EDGE * y.mid_all, SPAN * y.coarse_all)
        self.z_rows = up8(self.z_fine + self.z_sums)
        self.z2_rows = up8(z.second * y.coarse_all)
        self.slab_planes = SPAN * len(self.z_routes) + z.second * len(self.z2_routes)
        self.fine_planes = z.fine + RADIUS * len(self.z_routes)
        self.sum_planes = z.mid_all + RADIUS * len(self.z_routes)
        self.coarse_rows = -(-y.coarse_all // 16) * 16
        self.y_fine = RADIUS * z.fine
        self.y_sums = max(EDGE * z.mid_all, SPAN * z.coarse_all)
        self.y_rows = up8(self.y_fine + self.y_sums)
        self.slab_fine = RADIUS * RADIUS * len(self.z_routes)
        self.slab_mid = EDGE * EDGE * len(self.z_routes)
        self.slab_coarse = SPAN * self.slab_planes
        self.extra = max(self.slab_coarse - self.slab_mid, 0)
        self.spare = x.fine - x.mid_all - x.coarse_all
        self.pieces = -(-x.coarse_all // max(self.spare, 1))
        if self.pieces * self.extra > self.slab_mid:
            self.extra = 0
        self.slab_sums = max(self.slab_mid, self.slab_coarse - self.extra)
        self.slab_rows = up8(self.slab_fine + self.slab_sums)
        self.far_groups = x.fine // x.coarse_all
        self.far_planes = -(-z.coarse_all // self.far_groups)
        self.far_rows = up8(y.second * self.far_planes)
        self.slab_start = z.coarse_all
        self.coarse_planes = z.coarse_all + RADIUS * len(self.z_routes)
        self.fine_rows = y.fine + 2 * RADIUS
        self.far = y.coarse_all
        self.low = y.mid_all
        self.high = self.low + SPAN
        self.sum_rows = -(-(self.high + SPAN) // 16) * 16
        self.edge_sums = EDGE + SPAN
        self.side = x.fine // RADIUS
        self.fine_groups = -(-self.fine_planes // self.side)
        self.folded = 0 < self.fine_planes % self.side <= self.side // 2
        self.fine_ends = self.fine_groups * self.fine_rows - (self.fine_rows // 2 if self.folded else 0)
        self.sum_blocks = -(-self.sum_planes * self.sum_rows // 128)
        self.coarse_blocks = -(-self.coarse_planes * self.sum_rows // 128)
        self.mid_ends = self.fine_ends + self.coarse_blocks * self.edge_sums
        self.x_rows = self.mid_ends + (self.sum_blocks - self.coarse_blocks) * up8(EDGE)
        assert x.mid_all + x.coarse_all <= x.fine
        assert self.far + y.second <= self.low and y.second <= 8 and y.coarse_all == SPAN and z.coarse_all == SPAN
        assert z.coarse >= RADIUS and y.coarse >= RADIUS and y.count == 4


def narrow_kernel(s, out):
    x = s.x
    lanes = (x.fine, x.fine)
    cell, lane = iota(lanes, 0), iota(lanes, 1)
    k = lane - 1
    to_mid = jnp.where((lane < x.mid_all) & x.holds_mid(k), weight_of(cell - 2 * k), 0.0)
    c = lane - x.mid_all - 2
    inside = (lane >= x.mid_all) & (lane < x.mid_all + x.coarse_all) & x.holds_coarse(c)
    to_coarse = jnp.where(inside, weight_of(cell - 1 - 2 * c), 0.0)
    narrow = to_mid + jnp.dot(to_mid, to_coarse, precision=EXACT, preferred_element_type=F32)
    out[...] = jnp.concatenate(split(narrow), axis=1)


def restrict_kernel(s, nz, source, narrow, charges, own, ahead, behind, far, *rest):
    messages, (wide, mid, high, coarse, packed, groups) = rest[:-6], rest[-6:]
    z, y, x = s.z, s.y, s.x
    wide[...] = jnp.zeros(wide.shape, F32)
    charges[...] = source[...]
    cells = source[...].reshape(z.fine * y.fine, x.fine)
    top, rest = cells.astype(BF16), cells
    rest = rest - top.astype(F32)
    middle = rest.astype(BF16)
    low = (rest - middle.astype(F32)).astype(BF16)
    weights = narrow[...]
    both = jnp.dot(low, weights, preferred_element_type=F32)
    both = both + jnp.dot(
        jnp.concatenate([top, middle], axis=1), jnp.concatenate([weights, weights], axis=0), preferred_element_type=F32
    )
    reduced = both[:, : x.fine] + both[:, x.fine :]
    wide[:, 8 : 8 + y.fine, :] = reduced.reshape(z.fine, y.fine, x.fine)
    rows = 0.0
    for offset, weight in WEIGHTS:
        rows = rows + weight * wide[:, pl.ds(6 + offset, y.mid_all, stride=2), :]
    keep = y.holds_mid(iota((y.mid_all, x.fine), 0) - 1)
    mid[...] = jnp.zeros(mid.shape, F32)
    coarse[...] = jnp.zeros(coarse.shape, F32)
    high[...] = jnp.zeros(high.shape, F32)
    for p in range(z.mid_all):
        total = 0.0
        for offset, weight in WEIGHTS:
            at = 2 * (p - 1) + offset
            if 0 <= at < z.fine:
                total = total + weight * rows[at]
        total = jnp.where(keep & z.holds_mid(p - 1), total, 0.0)
        mid[p, : y.mid_all] = total
        high[p, 8 : 8 + y.mid_all] = total
    rows = 0.0
    for offset, weight in WEIGHTS:
        rows = rows + weight * high[:, pl.ds(5 + offset, y.coarse_all, stride=2), :]
    keep = y.holds_coarse(iota((y.coarse_all, x.fine), 0) - 2)
    for p in range(z.coarse_all):
        total = 0.0
        for offset, weight in WEIGHTS:
            at = 2 * (p - 2) + offset + 1
            if 0 <= at < z.mid_all:
                total = total + weight * rows[at]
        coarse[p, : y.coarse_all] = jnp.where(keep & z.holds_coarse(p - 2), total, 0.0)
    is_mid = iota(mid.shape[1:], 1) < x.mid_all
    for p in range(z.mid_all):
        own[p] = jnp.where(is_mid, mid[p], coarse[p]) if p < z.coarse_all else jnp.where(is_mid, mid[p], 0.0)
    up = s.y2_routes[0].up()
    count, end = y.second, y.coarse_all
    groups[...] = jnp.zeros(groups.shape, F32)
    for p in range(z.coarse_all):
        g, at = p // s.far_planes, p % s.far_planes * count
        groups[g, at : at + count] = jnp.where(up, own[p, end - count : end], own[p, :count])
    lane = iota(far.shape, 1)
    total = jnp.zeros(far.shape, F32)
    for g in range(s.far_groups):
        first = g * x.coarse_all
        turned = pltpu.roll(groups[g], (first - x.mid_all) % x.fine, 1)
        total = jnp.where((lane >= first) & (lane < first + x.coarse_all), turned, total)
    far[...] = total
    for message, route in zip((ahead, behind), s.y_routes):
        up = route.up()
        edge = jnp.where(up, charges[:, y.fine - RADIUS :, :], charges[:, :RADIUS, :])
        message[: s.y_fine] = edge.reshape(s.y_fine, x.fine)
        packed[...] = jnp.zeros(packed.shape, F32)
        for p in range(z.mid_all):
            packed[0, p * EDGE : (p + 1) * EDGE] = jnp.where(up, mid[p, y.mid_all - EDGE : y.mid_all], mid[p, :EDGE])
        for p in range(z.coarse_all):
            packed[1, p * SPAN : (p + 1) * SPAN] = coarse[p, :SPAN]
        rows = s.y_rows - s.y_fine
        is_mid = iota((rows, x.fine), 1) < x.mid_all
        message[s.y_fine :] = jnp.where(is_mid, packed[0, :rows], packed[1, :rows])
    for message, route in zip(messages, s.z_routes):
        up = route.up().astype(jnp.int32)
        message[: s.z_fine] = charges[pl.ds(up * (z.fine - RADIUS), RADIUS)].reshape(s.z_fine, x.fine)
        packed[...] = jnp.zeros(packed.shape, F32)
        for p in range(EDGE):
            packed[0, p * y.mid_all : (p + 1) * y.mid_all] = mid[up * (z.mid_all - EDGE) + p][: y.mid_all]
        for p in range(SPAN):
            plane = coarse[up * (z.coarse_all - SPAN) + p]
            packed[1, p * y.coarse_all : (p + 1) * y.coarse_all] = plane[: y.coarse_all]
        rows = s.z_rows - s.z_fine
        is_mid = iota((rows, x.fine), 1) < x.mid_all
        message[s.z_fine :] = jnp.where(is_mid, packed[0, :rows], packed[1, :rows])
    for message, route in zip(messages[nz:], s.z2_routes):
        up = route.up().astype(jnp.int32)
        message[...] = jnp.zeros(message.shape, F32)
        for p in range(z.second):
            plane = coarse[up * (z.coarse_all - z.second) + p]
            message[p * y.coarse_all : (p + 1) * y.coarse_all] = plane[: y.coarse_all]


class Slab:
    def __init__(self, message, mid, coarse):
        self.message, self.mid, self.coarse = message, mid, coarse

    def mid_rows(self, first, count):
        return self.message[self.mid + first : self.mid + first + count]

    def coarse_rows(self, first, count):
        return self.message[self.coarse + first : self.coarse + first + count]

    def rows(self, is_mid, first_mid, first_coarse, count):
        coarse = 0.0 if first_coarse is None else self.coarse_rows(first_coarse, count)
        mid = 0.0 if self.mid is None else self.message[self.mid + first_mid : self.mid + first_mid + count]
        return jnp.where(is_mid, mid, coarse)


def slabs(s, z_messages, z2_messages):
    out = []
    for message in z_messages:
        for p in range(SPAN):
            mid = s.z_fine + p * s.y.mid_all if p < EDGE else None
            out.append(Slab(message, mid, s.z_fine + p * s.y.coarse_all))
    for message in z2_messages:
        out += [Slab(message, None, p * s.y.coarse_all) for p in range(s.z.second)]
    return out


def spread_kernel(s, nz, nz2, _, __, *rest):
    z_messages, z2_messages = rest[:nz], rest[nz : nz + nz2]
    ahead, behind, packed = rest[-3:]
    z, y, x = s.z, s.y, s.x
    planes = slabs(s, z_messages, z2_messages)
    count = s.slab_rows - s.slab_fine
    lane = iota((count, x.fine), 1)
    packed[...] = jnp.zeros(packed.shape, F32)
    for p, plane in enumerate(planes):
        packed[1, p * SPAN : (p + 1) * SPAN] = plane.coarse_rows(0, SPAN)
    for n in range(s.pieces if s.extra else 0):
        first = x.mid_all + n * s.spare
        turned = pltpu.roll(packed[1, s.slab_mid : s.slab_mid + up8(s.extra)], x.fine - s.spare - first, 1)
        packed[2, n * s.extra : (n + 1) * s.extra] = turned[: s.extra]
    coarse = jnp.where(lane < x.fine - s.spare, packed[1, :count], packed[2, :count])
    for message, route in zip((ahead, behind), s.y_routes):
        up = route.up()
        at = 0
        for z_message in z_messages:
            slab = z_message[: s.z_fine].reshape(RADIUS, y.fine, x.fine)
            edge = jnp.where(up, slab[:, y.fine - RADIUS :], slab[:, :RADIUS])
            message[at : at + RADIUS * RADIUS] = edge.reshape(RADIUS * RADIUS, x.fine)
            at += RADIUS * RADIUS
        at = 0
        for plane in planes:
            if plane.mid is not None:
                first, last = plane.mid_rows(0, EDGE), plane.mid_rows(y.mid_all - EDGE, EDGE)
                packed[0, at : at + EDGE] = jnp.where(up, last, first)
                at += EDGE
        message[s.slab_fine :] = jnp.where(lane < x.mid_all, packed[0, :count], coarse)


def pass_kernel(s, far, out):
    out[...] = far[...]


def roll_ends(s, plane_rows, count):
    x = s.x
    lane = iota((count, x.fine), 1)
    for g in range(s.fine_groups):
        ends = [jnp.zeros(lane.shape, F32)] * 2
        for j in range(min(s.side, s.fine_planes - g * s.side)):
            plane = plane_rows(g * s.side + j)
            here = (lane >= RADIUS * j) & (lane < RADIUS * (j + 1))
            for n, start in enumerate((x.fine - RADIUS, 0)):
                shift = (RADIUS * j - start) % x.fine
                ends[n] = jnp.where(here, pltpu.roll(plane, shift, 1) if shift else plane, ends[n])
        yield g, ends


def early_kernel(s, nz, charges, *rest):
    z_messages = rest[:nz]
    x_fine, y_own, t_part, last, start, slab = rest[nz:]
    z, y, x = s.z, s.y, s.x
    for n, message in enumerate(z_messages):
        slab[n * RADIUS : (n + 1) * RADIUS] = message[: s.z_fine].reshape(RADIUS, y.fine, x.fine)

    def rows_of(p):
        return charges[p] if p < z.fine else slab[p - z.fine]

    t_part[...] = jnp.zeros(t_part.shape, F32)
    fine_at = fine_places(s)
    for g in range(0, s.fine_planes, 8):
        planes = charges[g : g + 8] if g < z.fine else slab[g - z.fine : g - z.fine + 8]
        a, b = split(contract_x(s, planes.reshape(8 * y.fine, x.fine), x_fine))
        for p in range(8):
            rows = slice(p * y.fine, (p + 1) * y.fine)
            store_terms(t_part, *fine_at[g + p], contract_y(s, y_own, a[rows], b[rows]))
    for g, ends in roll_ends(s, rows_of, y.fine):
        rows = slice(g * y.fine, (g + 1) * y.fine)
        last[rows], start[rows] = ends


def collect_kernel(s, nz, nz2, last, start, own, *rest):
    z_messages, z2_messages = rest[:nz], rest[nz : nz + nz2]
    rest = rest[nz + nz2 :]
    pairs = rest[:4]
    fars = rest[4 : 5 + nz + nz2]
    fine, sums, first, second, raw, rows, near = rest[5 + nz + nz2 :]
    z, y, x = s.z, s.y, s.x
    below = s.y_routes[0].below()
    planes = slabs(s, z_messages, z2_messages)

    def sides(which, start, count):
        a, b = (message[start : start + count] for message in pairs[2 * which : 2 * which + 2])
        return jnp.where(below, a, b), jnp.where(below, b, a)

    parts = [(0, z.fine, 0, 0)] + [(z.fine + n * RADIUS, RADIUS, 1, n * RADIUS * RADIUS) for n in range(nz)]
    for at, count, which, row in parts:
        low, high = sides(which, row, RADIUS * count)
        fine[at : at + count, :RADIUS] = low.reshape(count, RADIUS, x.fine)
        fine[at : at + count, RADIUS:] = high.reshape(count, RADIUS, x.fine)
    sums[...] = jnp.zeros(sums.shape, F32)
    raw[...] = jnp.zeros(raw.shape, F32)
    for n, far in enumerate(fars):
        for g in range(s.far_groups):
            turned = pltpu.roll(far[...], (x.mid_all - g * x.coarse_all) % x.fine, 1)
            for p in range(g * s.far_planes, min((g + 1) * s.far_planes, z.coarse_all)):
                at = p % s.far_planes * y.second
                rows[n, p, : y.second] = turned[at : at + y.second]
    is_mid = iota((y.second, x.fine), 1) < x.mid_all

    lane = iota((up8(s.extra), x.fine), 1)
    for side, got in enumerate(sides(1, s.slab_fine, s.slab_sums)):
        near[side, : s.slab_sums] = got
        if s.extra:
            total = jnp.zeros(lane.shape, F32)
            for n in range(s.pieces):
                begin = x.mid_all + n * s.spare
                piece = near[side, n * s.extra : n * s.extra + up8(s.extra)]
                turned = pltpu.roll(piece, begin + s.spare, 1)
                total = jnp.where(lane >= begin, turned, total)
            near[side, s.slab_mid : s.slab_mid + s.extra] = total[: s.extra]
    is_mid_edge = iota((EDGE, x.fine), 1) < x.mid_all
    is_mid_span = iota((SPAN, x.fine), 1) < x.mid_all

    def rows_of_plane(out, p, body, mids, coarses, far_plane):
        out[p, : y.mid_all] = body
        for base, shift, n in ((s.low, SPAN - EDGE, 0), (s.high, 0, 1)):
            if coarses is not None:
                out[p, base : base + SPAN] = jnp.where(is_mid_span, 0.0, coarses[n])
            if mids is not None:
                at = slice(base + shift, base + shift + EDGE)
                out[p, at] = jnp.where(is_mid_edge, mids[n], out[p, at])
        if far_plane is not None:
            at = slice(s.far, s.far + y.second)
            out[p, at] = jnp.where(is_mid, out[p, at], rows[far_plane][: y.second])

    for p in range(z.mid_all):
        far_plane = (0, p) if p < z.coarse_all else None
        mids = sides(0, s.y_fine + p * EDGE, EDGE)
        coarses = sides(0, s.y_fine + p * SPAN, SPAN) if p < z.coarse_all else None
        rows_of_plane(sums, s.place_of(p), own[p, : y.mid_all], mids, coarses, far_plane)
    is_mid_row = iota((SPAN, x.fine), 1) < x.mid_all
    is_mid_rest = iota((y.mid_all - SPAN, x.fine), 1) < x.mid_all
    slab_far = [(1 + n, p) for n in range(nz) for p in range(SPAN)]
    for n, route in enumerate(s.z2_routes):
        at = jnp.where(route.below(), z.coarse_all - z.second, 0)
        slab_far += [(1 + nz + n, at + p) for p in range(z.second)]
    held = 0
    for p, plane in enumerate(planes):
        body = [plane.rows(is_mid_row, 0, 0, SPAN), plane.rows(is_mid_rest, SPAN, None, y.mid_all - SPAN)]
        mids = None
        if plane.mid is not None:
            mids = sides(1, s.slab_fine + held * EDGE, EDGE)
            held += 1
        coarses = [near[side, p * SPAN : (p + 1) * SPAN] for side in range(2)]
        rows_of_plane(raw, p, jnp.concatenate(body, axis=0), mids, coarses, slab_far[p])
    is_mid = iota((s.sum_rows, x.fine), 1) < x.mid_all

    def number(condition, a, b):
        return jnp.where(condition, a, b)

    for n, route in enumerate(s.z_routes):
        lower, base = route.below(), n * SPAN
        for j in range(RADIUS):
            a = raw[base + number(lower, 0, 3) + j]
            b = raw[base + number(lower, SPAN - 5 - RADIUS, 5) + j]
            sums[s.slab_start + n * RADIUS + j] = jnp.where(is_mid, a, b)
        for i in range(3):
            at = number(lower, 0, s.place_of(z.mid)) + i
            sums[at] = sums[at] + jnp.where(is_mid, raw[base + number(lower, EDGE - 3, 0) + i], 0.0)
        for i in range(5):
            at = number(lower, 0, z.coarse) + i
            sums[at] = sums[at] + jnp.where(is_mid, 0.0, raw[base + number(lower, SPAN - 5, 0) + i])
    for n, route in enumerate(s.z2_routes):
        base = len(s.z_routes) * SPAN + n * z.second
        at = s.slab_start + number(route.below(), RADIUS - z.coarse, RADIUS + z.coarse - 5)
        for p in range(z.second):
            sums[at + p] = sums[at + p] + jnp.where(is_mid, 0.0, raw[base + p])

    up = s.x_routes[0].up()
    half, shift = s.fine_rows // 2, x.fine // 2
    is_first_half = iota((half, x.fine), 1) < shift
    for g, ends in roll_ends(s, lambda p: fine[p], 2 * RADIUS):
        rows = slice(g * y.fine, (g + 1) * y.fine)
        both = [jnp.concatenate([old[rows], new], axis=0) for old, new in zip((last, start), ends)]
        if s.folded and g == s.fine_groups - 1:
            both = [jnp.where(is_first_half, e[:half], pltpu.roll(e[half:], shift, 1)) for e in both]
        at = slice(g * s.fine_rows, g * s.fine_rows + both[0].shape[0])
        first[at] = jnp.where(up, both[0], both[1])
        second[at] = jnp.where(up, both[1], both[0])
    width = EDGE + SPAN
    row, lane = iota((2 * width, x.fine), 0), iota((2 * width, x.fine), 1)
    is_first = row < width
    goes_up = choose(up, is_first, ~is_first)
    slot = jnp.where(is_first, row, row - width)
    from_mid = jnp.where(goes_up, x.mid_all - EDGE + slot, slot)
    from_coarse = slot - EDGE + jnp.where(goes_up, x.mid_all + x.coarse_all - SPAN, x.mid_all)
    wanted = jnp.where(slot < EDGE, from_mid, from_coarse)
    picked_sums = pick((lane == wanted).astype(BF16), sums[...].reshape(s.sum_planes * s.sum_rows, x.fine))
    spare = s.sum_blocks * 128 - picked_sums.shape[1]
    if spare:
        picked_sums = jnp.concatenate([picked_sums, jnp.zeros((2 * width, spare), F32)], axis=1)
    for n, message in enumerate((first, second)):
        rows = picked_sums[n * width : (n + 1) * width]
        for b in range(s.coarse_blocks):
            at = s.fine_ends + b * width
            message[at : at + width] = rows[:, b * 128 : (b + 1) * 128]
        for b in range(s.coarse_blocks, s.sum_blocks):
            at = s.mid_ends + (b - s.coarse_blocks) * up8(EDGE)
            message[at : at + up8(EDGE)] = rows[: up8(EDGE), b * 128 : (b + 1) * 128]


def band(taps, level, offset, valid):
    at = jnp.where(valid, offset + RADIUS, -1)
    out = [jnp.zeros(at.shape, F32) for _ in range(TERMS)]
    for tap in range(TAPS):
        here = at == tap
        out = [jnp.where(here, taps[level, term, tap], total) for term, total in enumerate(out)]
    return out


def dot(a, b):
    return jnp.dot(a, b, precision=EXACT, preferred_element_type=F32)


def z_columns(s):
    return s.z.fine * RADIUS


def lower_x(x):
    return x.index() > 0


def higher_x(x):
    return x.index() < x.count - 1


def later_kernel(s, taps, ends, table):
    y, x = s.y, s.x
    for level in range(2):
        for term in range(TERMS):
            for tap in range(TAPS):
                table[(level * TERMS + term) * TAPS + tap] = jnp.full((8, x.fine), taps[level, term, tap], F32)
    is_second = iota((8, x.fine), 1) >= x.fine // TERMS
    for tap in range(TAPS):
        table[2 * TERMS * TAPS + tap] = jnp.where(is_second, taps[2, 1, tap], taps[2, 0, tap])

    z, slots, wide = s.z, s.side * s.fine_groups, z_columns(s)
    slot, column = iota((slots, wide), 0), iota((slots, wide), 1)
    where, valid = slot, slot < z.fine
    for n, route in enumerate(s.z_routes):
        lower, i, first = route.below(), z.index(), z.fine + n * RADIUS
        here = (slot >= first) & (slot < first + RADIUS)
        where = jnp.where(here, slot - first + jnp.where(lower, -RADIUS, z.fine), where)
        valid = choose(here, choose(lower, i >= 1, i + 1 < z.count), valid)
    planes = band(taps, 0, where - column // RADIUS, valid)
    r, c = iota((RADIUS, wide), 0), iota((RADIUS, wide), 1) % RADIUS
    cells = (slots, RADIUS, wide)
    for side, (offset, valid) in enumerate(((r - c - RADIUS, lower_x(x)), (r - c + RADIUS, higher_x(x)))):
        columns = band(taps, 0, offset, choose(valid, r >= 0, r < 0))
        for term in range(TERMS):
            joint = jnp.broadcast_to(planes[term][:, None, :], cells) * jnp.broadcast_to(columns[term][None], cells)
            high, low = split(joint.reshape(slots * RADIUS, wide))
            at = 2 * term + side
            ends[at, : slots * RADIUS] = high
            ends[at, slots * RADIUS : 2 * slots * RADIUS] = high
            ends[at, 2 * slots * RADIUS :] = low

def operator_kernel(s, taps, x_fine, x_sums, y_own, y_edge, y_fine, y_mid, y_coarse, widen_x, widen_y):
    y, x = s.y, s.x
    own, edge = x.fine, 64
    shape = (own + edge, x.fine)
    row, lane = iota(shape, 0), iota(shape, 1)
    t = row - own
    lower, higher = x.index() > 0, x.index() < x.count - 1
    is_own = row < own

    def place(half, own_place, own_valid, first, count, low_place, high_place):
        is_low = t < half
        r = jnp.where(is_low, t, t - half) - first
        there = (r >= 0) & (r < count) & (t < 2 * half) & choose(is_low, lower, higher)
        valid = choose(is_own, own_valid, there)
        return jnp.where(is_own, own_place, jnp.where(is_low, low_place + r, high_place + r)), valid

    half = s.edge_sums
    fine = band(taps, 0, row - lane, is_own)
    where, valid = place(half, row - 1, row < x.mid_all, 0, EDGE, 2 - EDGE, x.mid - 1)
    mid = band(taps, 1, where - (lane - 1), valid & (lane < x.mid_all))
    first = x.mid_all
    inside = (row >= first) & (row < first + x.coarse_all)
    where, valid = place(half, row - first - 2, inside, EDGE, SPAN, 3 - SPAN, x.coarse - 2)
    side = x.fine // TERMS
    column = lane % side
    terms = band(taps, 2, where - (column - 2), valid & (column < x.coarse_all))
    coarse = terms[0]
    for term in range(1, TERMS):
        coarse = jnp.where(lane >= term * side, terms[term], coarse)
    a, b = iota((x.fine, x.fine), 0), iota((x.fine, x.fine), 1)
    from_mid = jnp.where((a < x.mid_all) & x.holds_mid(a - 1), weight_of(b - 2 * (a - 1)), 0.0)
    c = a % side
    from_coarse = jnp.where((c < x.coarse_all) & x.holds_coarse(c - 2), weight_of(b - 1 - 2 * (c - 2)), 0.0)
    high, low = split(dot(from_coarse, from_mid))
    widen_x[:own] = high
    widen_x[own : 2 * own] = high
    widen_x[2 * own :] = low
    columns = [(x_fine, 0, 0, fine)]
    columns += [(x_sums, half, 0, [dot(m, from_mid) for m in mid])]
    columns += [(x_sums, half, TERMS * x.fine, [coarse])]
    for out, half, at, terms in columns:
        for term, matrix in enumerate(terms):
            high, low = split(matrix)
            cols = slice(at + term * x.fine, at + (term + 1) * x.fine)
            n = 2 * half
            out[0:own, cols] = high[:own]
            out[own : 2 * own, cols] = high[:own]
            out[2 * own : 3 * own, cols] = low[:own]
            if n:
                out[3 * own :, cols] = jnp.zeros((out.shape[0] - 3 * own, x.fine), BF16)
                out[3 * own : 3 * own + n, cols] = high[own : own + n]
                out[3 * own + n : 3 * own + 2 * n, cols] = high[own : own + n]
                out[3 * own + 128 : 3 * own + 128 + n, cols] = low[own : own + n]

    lower, higher = y.index() > 0, y.index() < y.count - 1
    far_below = s.y2_routes[0].below()
    n = up8(y.mid_all)

    def write(out, size, terms):
        part = iota(terms[0].shape, 1) >= 2 * size
        for term, matrix in enumerate(terms):
            high, low = split(matrix)
            n = matrix.shape[0]
            out[term * n : (term + 1) * n] = jnp.where(part, low.astype(F32), high.astype(F32)).astype(BF16)

    def columns_of(rows, size):
        lane = iota((rows, 3 * size), 1)
        return jnp.where(lane >= 2 * size, lane - 2 * size, jnp.where(lane >= size, lane - size, lane))

    c = columns_of(y.fine, s.fine_rows)
    is_low = (c >= y.fine) & (c < y.fine + RADIUS)
    is_high = c >= y.fine + RADIUS
    where = jnp.where(is_low, c - y.fine - RADIUS, jnp.where(is_high, c - RADIUS, c))
    valid = choose(is_low, lower, choose(is_high, higher, c >= 0))
    write(y_fine, s.fine_rows, band(taps, 0, where - iota(c.shape, 0), valid))
    c = columns_of(y.fine, y.fine)
    write(y_own, y.fine, band(taps, 0, c - iota(c.shape, 0), c >= 0))
    c = columns_of(y.fine, 2 * RADIUS)
    where = jnp.where(c < RADIUS, c - RADIUS, c - RADIUS + y.fine)
    write(y_edge, 2 * RADIUS, band(taps, 0, where - iota(c.shape, 0), choose(c < RADIUS, lower, higher)))

    c = columns_of(n, s.sum_rows)
    r = iota(c.shape, 0)
    is_low = (c >= s.low) & (c < s.low + SPAN)
    is_high = (c >= s.high) & (c < s.high + SPAN)
    is_far = (c >= s.far) & (c < s.far + y.second)
    where = jnp.where(is_low, c - s.low + 2 - SPAN, jnp.where(is_high, c - s.high + y.mid - 1, c - 1))
    valid = choose(is_low, lower, choose(is_high, higher, c < y.mid_all))
    mid = band(taps, 1, where - (r - 1), valid & (r < y.mid_all))
    far = jnp.where(far_below, -2 - y.coarse, 2 * y.coarse - 2)
    where = jnp.where(is_low, c - s.low + 3 - SPAN, jnp.where(is_high, c - s.high + y.coarse - 2, c - 2))
    where = jnp.where(is_far, c - s.far + far, where)
    valid = choose(is_low, lower, choose(is_high, higher, (c < y.coarse_all) | is_far))
    coarse = band(taps, 2, where - (r - 2), valid & (r < y.coarse_all))
    o, k = iota((y.fine, n), 0), iota((y.fine, n), 1)
    from_mid = jnp.where((k < y.mid_all) & y.holds_mid(k - 1), weight_of(o - 2 * (k - 1)), 0.0)
    m = s.coarse_rows
    c = columns_of(n, m)
    k = iota(c.shape, 0)
    from_coarse = jnp.where((c < y.coarse_all) & y.holds_coarse(c - 2), weight_of(k - 1 - 2 * (c - 2)), 0.0)
    write(y_mid, s.sum_rows, [dot(from_mid, matrix) for matrix in mid])
    write(y_coarse, s.sum_rows, [matrix[:m] for matrix in coarse])
    write(widen_y, m, [dot(from_mid, from_coarse)])


def contract_y(s, weights, high, low):
    joined = jnp.concatenate([high, low, high], axis=0)
    result = jnp.dot(weights[...], joined, preferred_element_type=F32)
    n, m = s.y.fine, s.x.fine
    return [result[t * n : (t + 1) * n, t * m : (t + 1) * m] for t in range(TERMS)]


def contract_z(table, level, held, base, count):
    rows = held.shape[2:]
    totals = [None] * count
    for t in range(held.shape[1]):
        for j in range(count + TAPS - 1):
            plane = held[base + j, t].reshape(rows[0] // 8, 8, rows[1])
            for i in range(max(0, j - TAPS + 1), min(count, j + 1)):
                term = table[(level * TERMS + t) * TAPS + j - i][None] * plane
                totals[i] = term if totals[i] is None else totals[i] + term
    return [total.reshape(rows) for total in totals]


def slab_starts(s, below_at, above_at):
    result = []
    for route in s.z_routes:
        lower, i = route.below(), s.z.index()
        valid = choose(lower, i >= 1, i + 1 < s.z.count)
        result.append((jnp.where(lower, below_at, above_at), valid))
    return result


def store_terms(held, at, valid, parts):
    for t, part in enumerate(parts):
        held[at, t] = part if valid is None else jnp.where(valid, part, 0.0)


BLOCK = 4


def fine_places(s):
    places = [(RADIUS + p, None) for p in range(s.z.fine)]
    for start, valid in slab_starts(s, 0, s.z.fine + RADIUS):
        places += [(start + p, valid) for p in range(RADIUS)]
    return places


def contract_x(s, grid, weights):
    high, low = split(grid)
    joined = jnp.concatenate([high, low, high], axis=1)
    return jnp.dot(joined, weights[: 3 * s.x.fine], preferred_element_type=F32)


def own_kernel(s, table, t_part, fine, sums, x_fine, x_sums, y_edge, fine_part, sums_part, t_fine):
    z, x = s.z, s.x
    t_fine[...] = t_part[...]
    fine_at = fine_places(s)

    def fine_group(g, count):
        n = 2 * RADIUS
        a, b = split(contract_x(s, fine[g : g + count].reshape(count * n, x.fine), x_fine))
        for p in range(count):
            rows = slice(p * n, (p + 1) * n)
            at, valid = fine_at[g + p]
            for t, part in enumerate(contract_y(s, y_edge, a[rows], b[rows])):
                t_fine[at, t] = t_fine[at, t] + (part if valid is None else jnp.where(valid, part, 0.0))

    def fine_block(k):
        for i, total in enumerate(contract_z(table, 0, t_fine, k, BLOCK)):
            fine_part[k + i] = total

    def sum_part(g, count):
        n = s.sum_rows
        grid = sums[g : g + count].reshape(count * n, x.fine)
        sums_part[g * n : (g + count) * n] = contract_x(s, grid, x_sums)

    later = []
    done = 0
    for g in list(range(z.fine, s.fine_planes, 8)) + list(range(0, z.fine, 8)):
        fine_group(g, 8)
        while later:
            later.pop(0)()
        if g < z.fine:
            ready = g if g + 8 < z.fine else z.fine
            later += [lambda k=k: fine_block(k) for k in range(done, ready, BLOCK)]
            done = max(done, ready)
    starts = list(range(0, s.sum_planes, 8))
    while later or starts:
        if starts:
            sum_part(starts[0], min(8, s.sum_planes - starts[0]))
            starts.pop(0)
        if later:
            later.pop(0)()


def sum_kernel(s, table, fine, sums, first, second, x_sums, ends, y_fine, y_mid, y_coarse, widen_x, widen_y, result, *scratch):
    sums_ends, t_mid, t_coarse, p_mid, p_coarse, narrow, out, left = scratch
    z, y, x = s.z, s.y, s.x
    below = s.x_routes[0].below()
    half = s.edge_sums
    def ends_of(start, rows):
        one, two = first[start : start + rows], second[start : start + rows]
        return jnp.where(below, one, two), jnp.where(below, two, one)

    for b in range(s.sum_blocks):
        if b < s.coarse_blocks:
            pair = ends_of(s.fine_ends + b * half, half)
        else:
            rest = jnp.zeros((half - up8(EDGE), 128), F32)
            pair = ends_of(s.mid_ends + (b - s.coarse_blocks) * up8(EDGE), up8(EDGE))
            pair = [jnp.concatenate([ends, rest], axis=0) for ends in pair]
        rows = jnp.concatenate(pair, axis=0)
        zeros = jnp.zeros((128 - 4 * half, 128), F32)
        sums_ends[b * 128 : (b + 1) * 128] = jnp.concatenate([rows, rows, zeros], axis=0).T

    def along_x(start, rows):
        edge_high, edge_low = split(sums_ends[start : start + rows])
        is_high = iota(edge_high.shape, 1) < 2 * half
        packed = jnp.where(is_high, edge_high.astype(F32), edge_low.astype(F32)).astype(BF16)
        joined = jnp.concatenate([packed, edge_high], axis=1)
        part = jnp.dot(joined, x_sums[3 * x.fine :], preferred_element_type=F32)
        return split(sums[start : start + rows] + part)

    def fine_edges():
        columns = []
        for flip in range(2):
            for g in range(s.fine_groups):
                is_folded = s.folded and g == s.fine_groups - 1
                at = slice(g * s.fine_rows, s.fine_ends if is_folded else (g + 1) * s.fine_rows)
                pair = (first[at], second[at])
                ends_here = jnp.where(below, pair[flip], pair[1 - flip])
                if is_folded:
                    ends_here = jnp.concatenate([ends_here, pltpu.roll(ends_here, x.fine // 2, 1)], axis=0)
                columns.append(ends_here)
        high, low = split(jnp.concatenate(columns, axis=1))
        joined = jnp.concatenate([high, low, high], axis=0)
        high, low = split(jnp.dot(y_fine[...], joined, preferred_element_type=F32))
        width = s.fine_groups * x.fine
        result = []
        for side in range(2):
            total = 0.0
            for t in range(TERMS):
                rows, cols = slice(t * y.fine, (t + 1) * y.fine), slice(side * width, (side + 1) * width)
                a, b = high[rows, cols], low[rows, cols]
                joined = jnp.concatenate([a, b, a], axis=1)
                total = total + jnp.dot(joined, ends[2 * t + side], preferred_element_type=F32)
            result.append(total)
        return result

    t_mid[...] = jnp.zeros(t_mid.shape, F32)
    t_coarse[...] = jnp.zeros(t_coarse.shape, F32)
    mid_at = [(RADIUS + p, None) for p in range(z.mid_all)]
    mid_at, rest_at = mid_at[: z.coarse_all], mid_at[z.coarse_all :]
    coarse_at = [(RADIUS + p, None) for p in range(z.coarse_all)]
    for start, valid in slab_starts(s, 0, z.mid + 3 + RADIUS):
        mid_at += [(start + p, valid) for p in range(RADIUS)]
    mid_at += rest_at
    for start, valid in slab_starts(s, 0, z.coarse + 5 + RADIUS):
        coarse_at += [(start + p, valid) for p in range(RADIUS)]
    coarse_at += [(None, None)] * len(rest_at)
    is_second = iota((s.coarse_rows, x.fine), 1) >= x.fine // TERMS

    def sum_group(g, count):
        n = s.sum_rows
        a, b = along_x(g * n, count * n)
        for p in range(count):
            rows = slice(p * n, (p + 1) * n)
            at, valid = mid_at[g + p]
            cols = slice(0, TERMS * x.fine)
            store_terms(t_mid, at, valid, contract_y(s, y_mid, a[rows, cols], b[rows, cols]))
            at, valid = coarse_at[g + p]
            if at is not None:
                cols = slice(TERMS * x.fine, (TERMS + 1) * x.fine)
                joined = jnp.concatenate([a[rows, cols], b[rows, cols], a[rows, cols]], axis=0)
                both = jnp.dot(y_coarse[...], joined, preferred_element_type=F32)
                m = s.coarse_rows
                store_terms(t_coarse, at, valid, [jnp.where(is_second, both[m:], both[:m])])

    def coarse_block(k):
        count = min(BLOCK, z.coarse_all - k)
        for i, total in enumerate(contract_z(table, 2, t_coarse, k, count)):
            narrow[k + i] = jnp.where(z.holds_coarse(k + i - 2), total, 0.0)

    def widen():
        m = s.coarse_rows
        high, low = split(narrow[...].reshape(z.coarse_all * m, x.fine))
        joined = jnp.concatenate([high, low, high], axis=1)
        high, low = split(jnp.dot(joined, widen_x[...], preferred_element_type=F32))
        for p in range(z.coarse_all):
            rows = slice(p * m, (p + 1) * m)
            joined = jnp.concatenate([high[rows], low[rows], high[rows]], axis=0)
            p_coarse[p] = jnp.dot(widen_y[...], joined, preferred_element_type=F32)

    def mid_block(k):
        count = min(BLOCK, z.mid_all - k)
        for i, total in enumerate(contract_z(table, 1, t_mid, k, count)):
            m = k + i - 1
            for offset, weight in WEIGHTS:
                if (m - offset) % 2 == 0 and 0 <= (m - offset) // 2 + 2 < z.coarse_all:
                    total = total + weight * p_coarse[(m - offset) // 2 + 2]
            p_mid[k + i] = jnp.where(z.holds_mid(m), total, 0.0)

    edges = fine_edges()
    lane = iota((y.fine, x.fine), 1)

    def begin(k):
        block, at = k // s.side, k % s.side * RADIUS
        low, high = (edge[:, block * x.fine : (block + 1) * x.fine] for edge in edges)
        low = pltpu.roll(low, -at % x.fine, 1) if at else low
        turn = (x.fine - RADIUS - at) % x.fine
        high = pltpu.roll(high, turn, 1) if turn else high
        out[k] = fine[k] + jnp.where(lane < RADIUS, low, jnp.where(lane >= x.fine - RADIUS, high, 0.0))

    def finish(k):
        total = out[k]
        for offset, weight in WEIGHTS:
            if (k - offset) % 2 == 0:
                total = total + weight * p_mid[(k - offset) // 2 + 1]
        out[k] = total

    groups = list(range(0, s.sum_planes, 4))
    share = -(-z.fine // len(groups))
    for n, g in enumerate(groups):
        sum_group(g, min(4, s.sum_planes - g))
        for k in range(n * share, min((n + 1) * share, z.fine)):
            begin(k)
    for k in range(0, z.coarse_all, BLOCK):
        coarse_block(k)
    widen()
    done, copies = 0, []
    for k in range(0, z.mid_all, BLOCK):
        mid_block(k)
        ready = z.fine if k + BLOCK >= z.mid_all else 2 * k + 2
        while done < ready:
            finish(done)
            done += 1
            if done % 8 == 0:
                part = pl.ds(done - 8, 8)
                copies.append(pltpu.make_async_copy(out.at[part], result.at[part], left.at[done // 8 - 1]))
                copies[-1].start()
    for copy in copies:
        copy.wait()


def call(kernel, outs, ins, scratch=(), flops=10**7, out_space=pltpu.VMEM):
    specs = [SMEM if a.ndim == 3 and a.shape[-1] == TAPS else VMEM for a in ins]
    size = sum(a.size * a.dtype.itemsize for a in ins) + sum(o.size * o.dtype.itemsize for o in outs)
    return pl.pallas_call(
        kernel,
        out_shape=tuple(outs),
        in_specs=specs,
        out_specs=tuple(pl.BlockSpec(memory_space=out_space) for _ in outs),
        scratch_shapes=list(scratch),
        compiler_params=PARAMS,
        cost_estimate=pl.CostEstimate(flops=flops, bytes_accessed=size, transcendentals=0),
    )(*ins)


def array(*shape, dtype=F32):
    return jax.ShapeDtypeStruct(shape, dtype)


def local(charges, kernel_taps):
    z, y, x = (Cut(name, size) for name, size in zip(("gz", "gy", "gx"), charges.shape))
    s = Sizes(z, y, x)
    n = x.fine
    nz, nz2 = len(s.z_routes), len(s.z2_routes)

    def bound(kernel, *static):
        return lambda *refs: kernel(s, *static, *refs)

    rows = up8(y.mid_all)
    (weights,) = call(bound(narrow_kernel), [array(n, 2 * n, dtype=BF16)], [], flops=10**10)
    held, own, ahead, behind, far, *messages = call(
        bound(restrict_kernel, nz),
        [array(*charges.shape), array(z.mid_all, rows, n)] + [array(s.y_rows, n)] * 2 + [array(s.far_rows, n)] + [array(s.z_rows, n)] * nz + [array(s.z2_rows, n)] * nz2,
        [charges, weights],
        [
            pltpu.VMEM((z.fine, y.fine + 16, n), F32),
            pltpu.VMEM((z.mid_all, rows, n), F32),
            pltpu.VMEM((z.mid_all, up8(y.mid + 24), n), F32),
            pltpu.VMEM((z.mid_all, rows, n), F32),
            pltpu.VMEM((2, max(s.z_rows - s.z_fine, s.y_rows - s.y_fine), n), F32),
            pltpu.VMEM((s.far_groups, s.far_rows, n), F32),
        ],
    )
    z_got = [route(m) for route, m in zip(s.z_routes + s.z2_routes, messages)]
    sides = [s.y_routes[0](ahead), s.y_routes[1](behind)]
    far = s.y2_routes[0](far)
    (passed,) = call(bound(pass_kernel), [array(s.far_rows, n)], [far], flops=2*10**9)
    operators = call(
        bound(operator_kernel),
        [
            array(3 * n, TERMS * n, dtype=BF16),
            array(3 * n + 256, (TERMS + 1) * n, dtype=BF16),
            array(TERMS * y.fine, 3 * y.fine, dtype=BF16),
            array(TERMS * y.fine, 6 * RADIUS, dtype=BF16),
            array(TERMS * y.fine, 3 * s.fine_rows, dtype=BF16),
            array(TERMS * y.fine, 3 * s.sum_rows, dtype=BF16),
            array(TERMS * s.coarse_rows, 3 * s.sum_rows, dtype=BF16),
            array(3 * n, n, dtype=BF16),
            array(y.fine, 3 * s.coarse_rows, dtype=BF16),
        ],
        [kernel_taps],
    )
    later = call(
        bound(later_kernel),
        [array(2 * TERMS, 3 * s.fine_groups * n, z_columns(s), dtype=BF16), array((2 * TERMS + 1) * TAPS, 8, n)],
        [kernel_taps],
    )
    ends, table = later
    ahead, behind = call(
        bound(spread_kernel, nz, nz2),
        [array(s.slab_rows, n), array(s.slab_rows, n)],
        [passed, later[1], *z_got],
        [pltpu.VMEM((3, up8(max(s.slab_coarse, s.slab_rows - s.slab_fine)) + 8, n), F32)],
    )
    sides += [s.y_routes[0](ahead), s.y_routes[1](behind)]
    fars = [far] + [route(passed) for route in s.z_routes + s.z2_routes]
    x_fine, x_sums, y_own, y_edge, y_fine, y_mid, y_coarse, widen_x, widen_y = operators
    t_part, last, start = call(
        bound(early_kernel, nz),
        [array(z.fine + 2 * RADIUS, TERMS, y.fine, n)] + [array(s.fine_groups * y.fine, n)] * 2,
        [held, *z_got[:nz], x_fine, y_own],
        [pltpu.VMEM((nz * RADIUS, y.fine, n), F32)],
    )
    fine, sums, first, second = call(
        bound(collect_kernel, nz, nz2),
        [
            array(s.fine_planes, 2 * RADIUS, n),
            array(s.sum_planes, s.sum_rows, n),
            array(s.x_rows, n),
            array(s.x_rows, n),
        ],
        [last, start, own, *z_got, *sides, *fars],
        [
            pltpu.VMEM((s.slab_planes, s.sum_rows, n), F32),
            pltpu.VMEM((1 + nz + nz2, z.coarse_all, 8, n), F32),
            pltpu.VMEM((2, up8(s.slab_coarse) + 8, n), F32),
        ],
    )
    first, second = s.x_routes[0](first), s.x_routes[1](second)
    fine, sums = call(
        bound(own_kernel),
        [array(z.fine, y.fine, n), array(s.sum_planes * s.sum_rows, (TERMS + 1) * n)],
        [table, t_part, fine, sums, x_fine, x_sums, y_edge],
        [pltpu.VMEM((z.fine + 2 * RADIUS, TERMS, y.fine, n), F32)],
    )
    (out,) = call(
        bound(sum_kernel),
        [array(z.fine, y.fine, n)],
        [table, fine, sums, first, second, x_sums, ends, y_fine, y_mid, y_coarse, widen_x, widen_y],
        [
            pltpu.VMEM((s.sum_blocks * 128, n), F32),
            pltpu.VMEM((z.mid + 2 * RADIUS + 3, TERMS, y.fine, n), F32),
            pltpu.VMEM((z.coarse + 2 * RADIUS + 5, 1, s.coarse_rows, n), F32),
            pltpu.VMEM((z.mid_all, y.fine, n), F32),
            pltpu.VMEM((z.coarse_all, y.fine, n), F32),
            pltpu.VMEM((z.coarse_all, s.coarse_rows, n), F32),
            pltpu.VMEM((z.fine, y.fine, n), F32),
            pltpu.SemaphoreType.DMA((z.fine // 8,)),
        ],
        out_space=pltpu.HBM,
    )
    return out


def solution(mesh):
    return jax.shard_map(
        local,
        mesh=mesh,
        in_specs=(P("gz", "gy", "gx"), P()),
        out_specs=P("gz", "gy", "gx"),
        check_vma=False,
    )
```

```python
import jax
import jax.numpy as jnp
from jax import lax
from jax.experimental import pallas as pl
from jax.experimental.pallas import tpu as pltpu
from jax.sharding import PartitionSpec as P

RADIUS = 8
TAPS = 17
TERMS = 2
WEIGHTS = ((-3, -0.0625), (-1, 0.5625), (0, 1.0), (1, 0.5625), (3, -0.0625))
EXACT = lax.Precision.HIGHEST
SPAN = RADIUS + 5
EDGE = RADIUS + 3
F32, BF16 = jnp.float32, jnp.bfloat16
PARAMS = pltpu.CompilerParams(vmem_limit_bytes=32 * 1024 * 1024)
VMEM = pl.BlockSpec(memory_space=pltpu.VMEM)
SMEM = pl.BlockSpec(memory_space=pltpu.SMEM)


def up8(n):
    return -(-n // 8) * 8


def iota(shape, dim):
    return lax.broadcasted_iota(jnp.int32, shape, dim)


def weight_of(difference):
    size = jnp.abs(difference)
    out = jnp.where(size == 1, 0.5625, jnp.where(size == 3, -0.0625, 0.0))
    return jnp.where(size == 0, 1.0, out)


def choose(condition, a, b):
    return jnp.where(condition, jnp.where(a, 1, 0), jnp.where(b, 1, 0)) != 0


class Cut:
    def __init__(self, name, length):
        self.name, self.fine = name, length
        self.count = lax.axis_size(name)
        self.mid, self.coarse = length // 2, length // 4
        self.mid_all, self.coarse_all = self.mid + 3, self.coarse + 5
        self.second = max(SPAN - self.coarse, 0)

    def index(self):
        return lax.axis_index(self.name)

    def holds_mid(self, k):
        k = k + self.index() * self.mid
        return (k >= 0) & (k < self.mid * self.count)

    def holds_coarse(self, k):
        k = k + self.index() * self.coarse
        return (k >= 0) & (k < self.coarse * self.count)


class Route:
    def __init__(self, names, pairs, up, below):
        self.names, self.pairs, self.up, self.below = names, pairs, up, below

    def __call__(self, x):
        return lax.ppermute(x, self.names, self.pairs)


def flip(pairs):
    return [(b, a) for a, b in pairs]


def swap(cut, steps):
    pairs = [(i, i + steps) for i in range(cut.count - steps)]

    def up():
        return cut.index() + steps < cut.count

    return [Route(cut.name, pairs + flip(pairs), up, lambda: ~up())]


def both_ways(cut, steps):
    pairs = [(i, i + steps) for i in range(cut.count - steps)]
    yes, no = (lambda: cut.index() >= 0), (lambda: cut.index() < 0)
    return [Route(cut.name, pairs, yes, yes), Route(cut.name, flip(pairs), no, no)]


def folded(cut, beside, names):
    n, m = cut.count, lax.axis_size(beside)

    def place(c, i):
        return c * n + i if names[0] == beside else i * m + c

    pairs = []
    for c in range(0, m, 2):
        cycle = [place(c, i) for i in range(n)] + [place(c + 1, i) for i in reversed(range(n))]
        pairs += list(zip(cycle, cycle[1:] + cycle[:1]))

    def even():
        return lax.axis_index(beside) % 2 == 0

    def odd():
        return lax.axis_index(beside) % 2 == 1

    return [Route(names, pairs, even, even), Route(names, flip(pairs), odd, odd)]


def split(x):
    high = x.astype(BF16)
    return high, (x - high.astype(F32)).astype(BF16)


def pick(selector, x):
    nt = (((1,), (1,)), ((), ()))
    a = x.astype(BF16)
    rest = x - a.astype(F32)
    b = rest.astype(BF16)
    c = (rest - b.astype(F32)).astype(BF16)
    out = lax.dot_general(selector, c, nt, preferred_element_type=F32)
    out = out + lax.dot_general(selector, b, nt, preferred_element_type=F32)
    return out + lax.dot_general(selector, a, nt, preferred_element_type=F32)


class Sizes:
    def place_of(self, p):
        return p if p < self.slab_start else p + self.coarse_planes - self.slab_start

    def __init__(self, z, y, x):
        self.z, self.y, self.x = z, y, x
        self.z_routes = swap(z, 1) if z.count <= 2 else both_ways(z, 1)
        self.z2_routes = [] if z.count <= 2 else swap(z, 2) if z.count <= 4 else both_ways(z, 2)
        self.y_routes = folded(y, x.name, (x.name, y.name))
        self.y2_routes = swap(y, 2)
        self.x_routes = folded(x, z.name, (x.name, z.name))
        self.z_fine = RADIUS * y.fine
        self.z_sums = max(EDGE * y.mid_all, SPAN * y.coarse_all)
        self.z_rows = up8(self.z_fine + self.z_sums)
        self.z2_rows = up8(z.second * y.coarse_all)
        self.slab_planes = SPAN * len(self.z_routes) + z.second * len(self.z2_routes)
        self.fine_planes = z.fine + RADIUS * len(self.z_routes)
        self.sum_planes = z.mid_all + RADIUS * len(self.z_routes)
        self.coarse_rows = -(-y.coarse_all // 16) * 16
        self.y_fine = RADIUS * z.fine
        self.y_sums = max(EDGE * z.mid_all, SPAN * z.coarse_all)
        self.y_rows = up8(self.y_fine + self.y_sums)
        self.slab_fine = RADIUS * RADIUS * len(self.z_routes)
        self.slab_mid = EDGE * EDGE * len(self.z_routes)
        self.slab_coarse = SPAN * self.slab_planes
        self.extra = max(self.slab_coarse - self.slab_mid, 0)
        self.spare = x.fine - x.mid_all - x.coarse_all
        self.pieces = -(-x.coarse_all // max(self.spare, 1))
        if self.pieces * self.extra > self.slab_mid:
            self.extra = 0
        self.slab_sums = max(self.slab_mid, self.slab_coarse - self.extra)
        self.slab_rows = up8(self.slab_fine + self.slab_sums)
        self.far_groups = x.fine // x.coarse_all
        self.far_planes = -(-z.coarse_all // self.far_groups)
        self.far_rows = up8(y.second * self.far_planes)
        self.slab_start = z.coarse_all
        self.coarse_planes = z.coarse_all + RADIUS * len(self.z_routes)
        self.fine_rows = y.fine + 2 * RADIUS
        self.far = y.coarse_all
        self.low = y.mid_all
        self.high = self.low + SPAN
        self.sum_rows = -(-(self.high + SPAN) // 16) * 16
        self.edge_sums = EDGE + SPAN
        self.side = x.fine // RADIUS
        self.fine_groups = -(-self.fine_planes // self.side)
        self.folded = 0 < self.fine_planes % self.side <= self.side // 2
        self.fine_ends = self.fine_groups * self.fine_rows - (self.fine_rows // 2 if self.folded else 0)
        self.sum_blocks = -(-self.sum_planes * self.sum_rows // 128)
        self.coarse_blocks = -(-self.coarse_planes * self.sum_rows // 128)
        self.mid_ends = self.fine_ends + self.coarse_blocks * self.edge_sums
        self.x_rows = self.mid_ends + (self.sum_blocks - self.coarse_blocks) * up8(EDGE)
        assert x.mid_all + x.coarse_all <= x.fine
        assert self.far + y.second <= self.low and y.second <= 8 and y.coarse_all == SPAN and z.coarse_all == SPAN
        assert z.coarse >= RADIUS and y.coarse >= RADIUS and y.count == 4


def narrow_kernel(s, out):
    x = s.x
    lanes = (x.fine, x.fine)
    cell, lane = iota(lanes, 0), iota(lanes, 1)
    k = lane - 1
    to_mid = jnp.where((lane < x.mid_all) & x.holds_mid(k), weight_of(cell - 2 * k), 0.0)
    c = lane - x.mid_all - 2
    inside = (lane >= x.mid_all) & (lane < x.mid_all + x.coarse_all) & x.holds_coarse(c)
    to_coarse = jnp.where(inside, weight_of(cell - 1 - 2 * c), 0.0)
    narrow = to_mid + jnp.dot(to_mid, to_coarse, precision=EXACT, preferred_element_type=F32)
    out[...] = jnp.concatenate(split(narrow), axis=1)


def restrict_kernel(s, nz, source, narrow, charges, own, ahead, behind, far, *rest):
    messages, (wide, mid, high, coarse, packed, groups) = rest[:-6], rest[-6:]
    z, y, x = s.z, s.y, s.x
    wide[...] = jnp.zeros(wide.shape, F32)
    charges[...] = source[...]
    cells = source[...].reshape(z.fine * y.fine, x.fine)
    top, rest = cells.astype(BF16), cells
    rest = rest - top.astype(F32)
    middle = rest.astype(BF16)
    low = (rest - middle.astype(F32)).astype(BF16)
    weights = narrow[...]
    both = jnp.dot(low, weights, preferred_element_type=F32)
    both = both + jnp.dot(
        jnp.concatenate([top, middle], axis=1), jnp.concatenate([weights, weights], axis=0), preferred_element_type=F32
    )
    reduced = both[:, : x.fine] + both[:, x.fine :]
    wide[:, 8 : 8 + y.fine, :] = reduced.reshape(z.fine, y.fine, x.fine)
    rows = 0.0
    for offset, weight in WEIGHTS:
        rows = rows + weight * wide[:, pl.ds(6 + offset, y.mid_all, stride=2), :]
    keep = y.holds_mid(iota((y.mid_all, x.fine), 0) - 1)
    mid[...] = jnp.zeros(mid.shape, F32)
    coarse[...] = jnp.zeros(coarse.shape, F32)
    high[...] = jnp.zeros(high.shape, F32)
    for p in range(z.mid_all):
        total = 0.0
        for offset, weight in WEIGHTS:
            at = 2 * (p - 1) + offset
            if 0 <= at < z.fine:
                total = total + weight * rows[at]
        total = jnp.where(keep & z.holds_mid(p - 1), total, 0.0)
        mid[p, : y.mid_all] = total
        high[p, 8 : 8 + y.mid_all] = total
    rows = 0.0
    for offset, weight in WEIGHTS:
        rows = rows + weight * high[:, pl.ds(5 + offset, y.coarse_all, stride=2), :]
    keep = y.holds_coarse(iota((y.coarse_all, x.fine), 0) - 2)
    for p in range(z.coarse_all):
        total = 0.0
        for offset, weight in WEIGHTS:
            at = 2 * (p - 2) + offset + 1
            if 0 <= at < z.mid_all:
                total = total + weight * rows[at]
        coarse[p, : y.coarse_all] = jnp.where(keep & z.holds_coarse(p - 2), total, 0.0)
    is_mid = iota(mid.shape[1:], 1) < x.mid_all
    for p in range(z.mid_all):
        own[p] = jnp.where(is_mid, mid[p], coarse[p]) if p < z.coarse_all else jnp.where(is_mid, mid[p], 0.0)
    up = s.y2_routes[0].up()
    count, end = y.second, y.coarse_all
    groups[...] = jnp.zeros(groups.shape, F32)
    for p in range(z.coarse_all):
        g, at = p // s.far_planes, p % s.far_planes * count
        groups[g, at : at + count] = jnp.where(up, own[p, end - count : end], own[p, :count])
    lane = iota(far.shape, 1)
    total = jnp.zeros(far.shape, F32)
    for g in range(s.far_groups):
        first = g * x.coarse_all
        turned = pltpu.roll(groups[g], (first - x.mid_all) % x.fine, 1)
        total = jnp.where((lane >= first) & (lane < first + x.coarse_all), turned, total)
    far[...] = total
    for message, route in zip((ahead, behind), s.y_routes):
        up = route.up()
        edge = jnp.where(up, charges[:, y.fine - RADIUS :, :], charges[:, :RADIUS, :])
        message[: s.y_fine] = edge.reshape(s.y_fine, x.fine)
        packed[...] = jnp.zeros(packed.shape, F32)
        for p in range(z.mid_all):
            packed[0, p * EDGE : (p + 1) * EDGE] = jnp.where(up, mid[p, y.mid_all - EDGE : y.mid_all], mid[p, :EDGE])
        for p in range(z.coarse_all):
            packed[1, p * SPAN : (p + 1) * SPAN] = coarse[p, :SPAN]
        rows = s.y_rows - s.y_fine
        is_mid = iota((rows, x.fine), 1) < x.mid_all
        message[s.y_fine :] = jnp.where(is_mid, packed[0, :rows], packed[1, :rows])
    for message, route in zip(messages, s.z_routes):
        up = route.up().astype(jnp.int32)
        message[: s.z_fine] = charges[pl.ds(up * (z.fine - RADIUS), RADIUS)].reshape(s.z_fine, x.fine)
        packed[...] = jnp.zeros(packed.shape, F32)
        for p in range(EDGE):
            packed[0, p * y.mid_all : (p + 1) * y.mid_all] = mid[up * (z.mid_all - EDGE) + p][: y.mid_all]
        for p in range(SPAN):
            plane = coarse[up * (z.coarse_all - SPAN) + p]
            packed[1, p * y.coarse_all : (p + 1) * y.coarse_all] = plane[: y.coarse_all]
        rows = s.z_rows - s.z_fine
        is_mid = iota((rows, x.fine), 1) < x.mid_all
        message[s.z_fine :] = jnp.where(is_mid, packed[0, :rows], packed[1, :rows])
    for message, route in zip(messages[nz:], s.z2_routes):
        up = route.up().astype(jnp.int32)
        message[...] = jnp.zeros(message.shape, F32)
        for p in range(z.second):
            plane = coarse[up * (z.coarse_all - z.second) + p]
            message[p * y.coarse_all : (p + 1) * y.coarse_all] = plane[: y.coarse_all]


class Slab:
    def __init__(self, message, mid, coarse):
        self.message, self.mid, self.coarse = message, mid, coarse

    def mid_rows(self, first, count):
        return self.message[self.mid + first : self.mid + first + count]

    def coarse_rows(self, first, count):
        return self.message[self.coarse + first : self.coarse + first + count]

    def rows(self, is_mid, first_mid, first_coarse, count):
        coarse = 0.0 if first_coarse is None else self.coarse_rows(first_coarse, count)
        mid = 0.0 if self.mid is None else self.message[self.mid + first_mid : self.mid + first_mid + count]
        return jnp.where(is_mid, mid, coarse)


def slabs(s, z_messages, z2_messages):
    out = []
    for message in z_messages:
        for p in range(SPAN):
            mid = s.z_fine + p * s.y.mid_all if p < EDGE else None
            out.append(Slab(message, mid, s.z_fine + p * s.y.coarse_all))
    for message in z2_messages:
        out += [Slab(message, None, p * s.y.coarse_all) for p in range(s.z.second)]
    return out


def spread_kernel(s, nz, nz2, _, __, *rest):
    z_messages, z2_messages = rest[:nz], rest[nz : nz + nz2]
    ahead, behind, packed = rest[-3:]
    z, y, x = s.z, s.y, s.x
    planes = slabs(s, z_messages, z2_messages)
    count = s.slab_rows - s.slab_fine
    lane = iota((count, x.fine), 1)
    packed[...] = jnp.zeros(packed.shape, F32)
    for p, plane in enumerate(planes):
        packed[1, p * SPAN : (p + 1) * SPAN] = plane.coarse_rows(0, SPAN)
    for n in range(s.pieces if s.extra else 0):
        first = x.mid_all + n * s.spare
        turned = pltpu.roll(packed[1, s.slab_mid : s.slab_mid + up8(s.extra)], x.fine - s.spare - first, 1)
        packed[2, n * s.extra : (n + 1) * s.extra] = turned[: s.extra]
    coarse = jnp.where(lane < x.fine - s.spare, packed[1, :count], packed[2, :count])
    for message, route in zip((ahead, behind), s.y_routes):
        up = route.up()
        at = 0
        for z_message in z_messages:
            slab = z_message[: s.z_fine].reshape(RADIUS, y.fine, x.fine)
            edge = jnp.where(up, slab[:, y.fine - RADIUS :], slab[:, :RADIUS])
            message[at : at + RADIUS * RADIUS] = edge.reshape(RADIUS * RADIUS, x.fine)
            at += RADIUS * RADIUS
        at = 0
        for plane in planes:
            if plane.mid is not None:
                first, last = plane.mid_rows(0, EDGE), plane.mid_rows(y.mid_all - EDGE, EDGE)
                packed[0, at : at + EDGE] = jnp.where(up, last, first)
                at += EDGE
        message[s.slab_fine :] = jnp.where(lane < x.mid_all, packed[0, :count], coarse)


def pass_kernel(s, far, out):
    out[...] = far[...]


def roll_ends(s, plane_rows, count):
    x = s.x
    lane = iota((count, x.fine), 1)
    for g in range(s.fine_groups):
        ends = [jnp.zeros(lane.shape, F32)] * 2
        for j in range(min(s.side, s.fine_planes - g * s.side)):
            plane = plane_rows(g * s.side + j)
            here = (lane >= RADIUS * j) & (lane < RADIUS * (j + 1))
            for n, start in enumerate((x.fine - RADIUS, 0)):
                shift = (RADIUS * j - start) % x.fine
                ends[n] = jnp.where(here, pltpu.roll(plane, shift, 1) if shift else plane, ends[n])
        yield g, ends


def early_kernel(s, nz, charges, *rest):
    z_messages = rest[:nz]
    x_fine, y_own, t_part, last, start, slab = rest[nz:]
    z, y, x = s.z, s.y, s.x
    for n, message in enumerate(z_messages):
        slab[n * RADIUS : (n + 1) * RADIUS] = message[: s.z_fine].reshape(RADIUS, y.fine, x.fine)

    def rows_of(p):
        return charges[p] if p < z.fine else slab[p - z.fine]

    t_part[...] = jnp.zeros(t_part.shape, F32)
    fine_at = fine_places(s)
    for g in range(0, s.fine_planes, 8):
        planes = charges[g : g + 8] if g < z.fine else slab[g - z.fine : g - z.fine + 8]
        a, b = split(contract_x(s, planes.reshape(8 * y.fine, x.fine), x_fine))
        for p in range(8):
            rows = slice(p * y.fine, (p + 1) * y.fine)
            store_terms(t_part, *fine_at[g + p], contract_y(s, y_own, a[rows], b[rows]))
    for g, ends in roll_ends(s, rows_of, y.fine):
        rows = slice(g * y.fine, (g + 1) * y.fine)
        last[rows], start[rows] = ends


def collect_kernel(s, nz, nz2, last, start, own, *rest):
    z_messages, z2_messages = rest[:nz], rest[nz : nz + nz2]
    rest = rest[nz + nz2 :]
    pairs = rest[:4]
    fars = rest[4 : 5 + nz + nz2]
    fine, sums, first, second, raw, rows, near = rest[5 + nz + nz2 :]
    z, y, x = s.z, s.y, s.x
    below = s.y_routes[0].below()
    planes = slabs(s, z_messages, z2_messages)

    def sides(which, start, count):
        a, b = (message[start : start + count] for message in pairs[2 * which : 2 * which + 2])
        return jnp.where(below, a, b), jnp.where(below, b, a)

    parts = [(0, z.fine, 0, 0)] + [(z.fine + n * RADIUS, RADIUS, 1, n * RADIUS * RADIUS) for n in range(nz)]
    for at, count, which, row in parts:
        low, high = sides(which, row, RADIUS * count)
        fine[at : at + count, :RADIUS] = low.reshape(count, RADIUS, x.fine)
        fine[at : at + count, RADIUS:] = high.reshape(count, RADIUS, x.fine)
    sums[...] = jnp.zeros(sums.shape, F32)
    raw[...] = jnp.zeros(raw.shape, F32)
    for n, far in enumerate(fars):
        for g in range(s.far_groups):
            turned = pltpu.roll(far[...], (x.mid_all - g * x.coarse_all) % x.fine, 1)
            for p in range(g * s.far_planes, min((g + 1) * s.far_planes, z.coarse_all)):
                at = p % s.far_planes * y.second
                rows[n, p, : y.second] = turned[at : at + y.second]
    is_mid = iota((y.second, x.fine), 1) < x.mid_all

    lane = iota((up8(s.extra), x.fine), 1)
    for side, got in enumerate(sides(1, s.slab_fine, s.slab_sums)):
        near[side, : s.slab_sums] = got
        if s.extra:
            total = jnp.zeros(lane.shape, F32)
            for n in range(s.pieces):
                begin = x.mid_all + n * s.spare
                piece = near[side, n * s.extra : n * s.extra + up8(s.extra)]
                turned = pltpu.roll(piece, begin + s.spare, 1)
                total = jnp.where(lane >= begin, turned, total)
            near[side, s.slab_mid : s.slab_mid + s.extra] = total[: s.extra]
    is_mid_edge = iota((EDGE, x.fine), 1) < x.mid_all
    is_mid_span = iota((SPAN, x.fine), 1) < x.mid_all

    def rows_of_plane(out, p, body, mids, coarses, far_plane):
        out[p, : y.mid_all] = body
        for base, shift, n in ((s.low, SPAN - EDGE, 0), (s.high, 0, 1)):
            if coarses is not None:
                out[p, base : base + SPAN] = jnp.where(is_mid_span, 0.0, coarses[n])
            if mids is not None:
                at = slice(base + shift, base + shift + EDGE)
                out[p, at] = jnp.where(is_mid_edge, mids[n], out[p, at])
        if far_plane is not None:
            at = slice(s.far, s.far + y.second)
            out[p, at] = jnp.where(is_mid, out[p, at], rows[far_plane][: y.second])

    for p in range(z.mid_all):
        far_plane = (0, p) if p < z.coarse_all else None
        mids = sides(0, s.y_fine + p * EDGE, EDGE)
        coarses = sides(0, s.y_fine + p * SPAN, SPAN) if p < z.coarse_all else None
        rows_of_plane(sums, s.place_of(p), own[p, : y.mid_all], mids, coarses, far_plane)
    is_mid_row = iota((SPAN, x.fine), 1) < x.mid_all
    is_mid_rest = iota((y.mid_all - SPAN, x.fine), 1) < x.mid_all
    slab_far = [(1 + n, p) for n in range(nz) for p in range(SPAN)]
    for n, route in enumerate(s.z2_routes):
        at = jnp.where(route.below(), z.coarse_all - z.second, 0)
        slab_far += [(1 + nz + n, at + p) for p in range(z.second)]
    held = 0
    for p, plane in enumerate(planes):
        body = [plane.rows(is_mid_row, 0, 0, SPAN), plane.rows(is_mid_rest, SPAN, None, y.mid_all - SPAN)]
        mids = None
        if plane.mid is not None:
            mids = sides(1, s.slab_fine + held * EDGE, EDGE)
            held += 1
        coarses = [near[side, p * SPAN : (p + 1) * SPAN] for side in range(2)]
        rows_of_plane(raw, p, jnp.concatenate(body, axis=0), mids, coarses, slab_far[p])
    is_mid = iota((s.sum_rows, x.fine), 1) < x.mid_all

    def number(condition, a, b):
        return jnp.where(condition, a, b)

    for n, route in enumerate(s.z_routes):
        lower, base = route.below(), n * SPAN
        for j in range(RADIUS):
            a = raw[base + number(lower, 0, 3) + j]
            b = raw[base + number(lower, SPAN - 5 - RADIUS, 5) + j]
            sums[s.slab_start + n * RADIUS + j] = jnp.where(is_mid, a, b)
        for i in range(3):
            at = number(lower, 0, s.place_of(z.mid)) + i
            sums[at] = sums[at] + jnp.where(is_mid, raw[base + number(lower, EDGE - 3, 0) + i], 0.0)
        for i in range(5):
            at = number(lower, 0, z.coarse) + i
            sums[at] = sums[at] + jnp.where(is_mid, 0.0, raw[base + number(lower, SPAN - 5, 0) + i])
    for n, route in enumerate(s.z2_routes):
        base = len(s.z_routes) * SPAN + n * z.second
        at = s.slab_start + number(route.below(), RADIUS - z.coarse, RADIUS + z.coarse - 5)
        for p in range(z.second):
            sums[at + p] = sums[at + p] + jnp.where(is_mid, 0.0, raw[base + p])

    up = s.x_routes[0].up()
    half, shift = s.fine_rows // 2, x.fine // 2
    is_first_half = iota((half, x.fine), 1) < shift
    for g, ends in roll_ends(s, lambda p: fine[p], 2 * RADIUS):
        rows = slice(g * y.fine, (g + 1) * y.fine)
        both = [jnp.concatenate([old[rows], new], axis=0) for old, new in zip((last, start), ends)]
        if s.folded and g == s.fine_groups - 1:
            both = [jnp.where(is_first_half, e[:half], pltpu.roll(e[half:], shift, 1)) for e in both]
        at = slice(g * s.fine_rows, g * s.fine_rows + both[0].shape[0])
        first[at] = jnp.where(up, both[0], both[1])
        second[at] = jnp.where(up, both[1], both[0])
    width = EDGE + SPAN
    row, lane = iota((2 * width, x.fine), 0), iota((2 * width, x.fine), 1)
    is_first = row < width
    goes_up = choose(up, is_first, ~is_first)
    slot = jnp.where(is_first, row, row - width)
    from_mid = jnp.where(goes_up, x.mid_all - EDGE + slot, slot)
    from_coarse = slot - EDGE + jnp.where(goes_up, x.mid_all + x.coarse_all - SPAN, x.mid_all)
    wanted = jnp.where(slot < EDGE, from_mid, from_coarse)
    picked_sums = pick((lane == wanted).astype(BF16), sums[...].reshape(s.sum_planes * s.sum_rows, x.fine))
    spare = s.sum_blocks * 128 - picked_sums.shape[1]
    if spare:
        picked_sums = jnp.concatenate([picked_sums, jnp.zeros((2 * width, spare), F32)], axis=1)
    for n, message in enumerate((first, second)):
        rows = picked_sums[n * width : (n + 1) * width]
        for b in range(s.coarse_blocks):
            at = s.fine_ends + b * width
            message[at : at + width] = rows[:, b * 128 : (b + 1) * 128]
        for b in range(s.coarse_blocks, s.sum_blocks):
            at = s.mid_ends + (b - s.coarse_blocks) * up8(EDGE)
            message[at : at + up8(EDGE)] = rows[: up8(EDGE), b * 128 : (b + 1) * 128]


def band(taps, level, offset, valid):
    at = jnp.where(valid, offset + RADIUS, -1)
    out = [jnp.zeros(at.shape, F32) for _ in range(TERMS)]
    for tap in range(TAPS):
        here = at == tap
        out = [jnp.where(here, taps[level, term, tap], total) for term, total in enumerate(out)]
    return out


def dot(a, b):
    return jnp.dot(a, b, precision=EXACT, preferred_element_type=F32)


def z_columns(s):
    return s.z.fine * RADIUS


def lower_x(x):
    return x.index() > 0


def higher_x(x):
    return x.index() < x.count - 1


def later_kernel(s, taps, ends, table):
    y, x = s.y, s.x
    for level in range(2):
        for term in range(TERMS):
            for tap in range(TAPS):
                table[(level * TERMS + term) * TAPS + tap] = jnp.full((8, x.fine), taps[level, term, tap], F32)
    is_second = iota((8, x.fine), 1) >= x.fine // TERMS
    for tap in range(TAPS):
        table[2 * TERMS * TAPS + tap] = jnp.where(is_second, taps[2, 1, tap], taps[2, 0, tap])

    z, slots, wide = s.z, s.side * s.fine_groups, z_columns(s)
    slot, column = iota((slots, wide), 0), iota((slots, wide), 1)
    where, valid = slot, slot < z.fine
    for n, route in enumerate(s.z_routes):
        lower, i, first = route.below(), z.index(), z.fine + n * RADIUS
        here = (slot >= first) & (slot < first + RADIUS)
        where = jnp.where(here, slot - first + jnp.where(lower, -RADIUS, z.fine), where)
        valid = choose(here, choose(lower, i >= 1, i + 1 < z.count), valid)
    planes = band(taps, 0, where - column // RADIUS, valid)
    r, c = iota((RADIUS, wide), 0), iota((RADIUS, wide), 1) % RADIUS
    cells = (slots, RADIUS, wide)
    for side, (offset, valid) in enumerate(((r - c - RADIUS, lower_x(x)), (r - c + RADIUS, higher_x(x)))):
        columns = band(taps, 0, offset, choose(valid, r >= 0, r < 0))
        for term in range(TERMS):
            joint = jnp.broadcast_to(planes[term][:, None, :], cells) * jnp.broadcast_to(columns[term][None], cells)
            high, low = split(joint.reshape(slots * RADIUS, wide))
            at = 2 * term + side
            ends[at, : slots * RADIUS] = high
            ends[at, slots * RADIUS : 2 * slots * RADIUS] = high
            ends[at, 2 * slots * RADIUS :] = low

def operator_kernel(s, taps, x_fine, x_sums, y_own, y_edge, y_fine, y_mid, y_coarse, widen_x, widen_y):
    y, x = s.y, s.x
    own, edge = x.fine, 64
    shape = (own + edge, x.fine)
    row, lane = iota(shape, 0), iota(shape, 1)
    t = row - own
    lower, higher = x.index() > 0, x.index() < x.count - 1
    is_own = row < own

    def place(half, own_place, own_valid, first, count, low_place, high_place):
        is_low = t < half
        r = jnp.where(is_low, t, t - half) - first
        there = (r >= 0) & (r < count) & (t < 2 * half) & choose(is_low, lower, higher)
        valid = choose(is_own, own_valid, there)
        return jnp.where(is_own, own_place, jnp.where(is_low, low_place + r, high_place + r)), valid

    half = s.edge_sums
    cell, column = iota((own, x.fine), 0), iota((own, x.fine), 1)
    fine = band(taps, 0, cell - column, cell >= 0)
    where, valid = place(half, row - 1, row < x.mid_all, 0, EDGE, 2 - EDGE, x.mid - 1)
    mid = band(taps, 1, where - (lane - 1), valid & (lane < x.mid_all))
    first = x.mid_all
    inside = (row >= first) & (row < first + x.coarse_all)
    where, valid = place(half, row - first - 2, inside, EDGE, SPAN, 3 - SPAN, x.coarse - 2)
    side = x.fine // TERMS
    column = lane % side
    terms = band(taps, 2, where - (column - 2), valid & (column < x.coarse_all))
    coarse = terms[0]
    for term in range(1, TERMS):
        coarse = jnp.where(lane >= term * side, terms[term], coarse)
    a, b = iota((x.fine, x.fine), 0), iota((x.fine, x.fine), 1)
    from_mid = jnp.where((a < x.mid_all) & x.holds_mid(a - 1), weight_of(b - 2 * (a - 1)), 0.0)
    c = a % side
    from_coarse = jnp.where((c < x.coarse_all) & x.holds_coarse(c - 2), weight_of(b - 1 - 2 * (c - 2)), 0.0)
    high, low = split(dot(from_coarse, from_mid))
    widen_x[:own] = high
    widen_x[own : 2 * own] = high
    widen_x[2 * own :] = low
    columns = [(x_fine, 0, 0, fine)]
    columns += [(x_sums, half, 0, [dot(m, from_mid) for m in mid])]
    columns += [(x_sums, half, TERMS * x.fine, [coarse])]
    for out, half, at, terms in columns:
        for term, matrix in enumerate(terms):
            high, low = split(matrix)
            cols = slice(at + term * x.fine, at + (term + 1) * x.fine)
            n = 2 * half
            out[0:own, cols] = high[:own]
            out[own : 2 * own, cols] = high[:own]
            out[2 * own : 3 * own, cols] = low[:own]
            if n:
                out[3 * own :, cols] = jnp.zeros((out.shape[0] - 3 * own, x.fine), BF16)
                out[3 * own : 3 * own + n, cols] = high[own : own + n]
                out[3 * own + n : 3 * own + 2 * n, cols] = high[own : own + n]
                out[3 * own + 128 : 3 * own + 128 + n, cols] = low[own : own + n]

    lower, higher = y.index() > 0, y.index() < y.count - 1
    far_below = s.y2_routes[0].below()
    n = up8(y.mid_all)

    def write(out, size, terms):
        part = iota(terms[0].shape, 1) >= 2 * size
        for term, matrix in enumerate(terms):
            high, low = split(matrix)
            n = matrix.shape[0]
            out[term * n : (term + 1) * n] = jnp.where(part, low.astype(F32), high.astype(F32)).astype(BF16)

    def columns_of(rows, size):
        lane = iota((rows, 3 * size), 1)
        return jnp.where(lane >= 2 * size, lane - 2 * size, jnp.where(lane >= size, lane - size, lane))

    c = columns_of(y.fine, s.fine_rows)
    is_low = (c >= y.fine) & (c < y.fine + RADIUS)
    is_high = c >= y.fine + RADIUS
    where = jnp.where(is_low, c - y.fine - RADIUS, jnp.where(is_high, c - RADIUS, c))
    valid = choose(is_low, lower, choose(is_high, higher, c >= 0))
    write(y_fine, s.fine_rows, band(taps, 0, where - iota(c.shape, 0), valid))
    c = columns_of(y.fine, y.fine)
    write(y_own, y.fine, band(taps, 0, c - iota(c.shape, 0), c >= 0))
    c = columns_of(y.fine, 2 * RADIUS)
    where = jnp.where(c < RADIUS, c - RADIUS, c - RADIUS + y.fine)
    write(y_edge, 2 * RADIUS, band(taps, 0, where - iota(c.shape, 0), choose(c < RADIUS, lower, higher)))

    c = columns_of(n, s.sum_rows)
    r = iota(c.shape, 0)
    is_low = (c >= s.low) & (c < s.low + SPAN)
    is_high = (c >= s.high) & (c < s.high + SPAN)
    is_far = (c >= s.far) & (c < s.far + y.second)
    where = jnp.where(is_low, c - s.low + 2 - SPAN, jnp.where(is_high, c - s.high + y.mid - 1, c - 1))
    valid = choose(is_low, lower, choose(is_high, higher, c < y.mid_all))
    mid = band(taps, 1, where - (r - 1), valid & (r < y.mid_all))
    far = jnp.where(far_below, -2 - y.coarse, 2 * y.coarse - 2)
    where = jnp.where(is_low, c - s.low + 3 - SPAN, jnp.where(is_high, c - s.high + y.coarse - 2, c - 2))
    where = jnp.where(is_far, c - s.far + far, where)
    valid = choose(is_low, lower, choose(is_high, higher, (c < y.coarse_all) | is_far))
    coarse = band(taps, 2, where - (r - 2), valid & (r < y.coarse_all))
    o, k = iota((y.fine, n), 0), iota((y.fine, n), 1)
    from_mid = jnp.where((k < y.mid_all) & y.holds_mid(k - 1), weight_of(o - 2 * (k - 1)), 0.0)
    m = s.coarse_rows
    c = columns_of(n, m)
    k = iota(c.shape, 0)
    from_coarse = jnp.where((c < y.coarse_all) & y.holds_coarse(c - 2), weight_of(k - 1 - 2 * (c - 2)), 0.0)
    write(y_mid, s.sum_rows, [dot(from_mid, matrix) for matrix in mid])
    write(y_coarse, s.sum_rows, [matrix[:m] for matrix in coarse])
    write(widen_y, m, [dot(from_mid, from_coarse)])


def contract_y(s, weights, high, low):
    joined = jnp.concatenate([high, low, high], axis=0)
    result = jnp.dot(weights[...], joined, preferred_element_type=F32)
    n, m = s.y.fine, s.x.fine
    return [result[t * n : (t + 1) * n, t * m : (t + 1) * m] for t in range(TERMS)]


def contract_z(table, level, held, base, count):
    rows = held.shape[2:]
    totals = [None] * count
    for t in range(held.shape[1]):
        for j in range(count + TAPS - 1):
            plane = held[base + j, t].reshape(rows[0] // 8, 8, rows[1])
            for i in range(max(0, j - TAPS + 1), min(count, j + 1)):
                term = table[(level * TERMS + t) * TAPS + j - i][None] * plane
                totals[i] = term if totals[i] is None else totals[i] + term
    return [total.reshape(rows) for total in totals]


def slab_starts(s, below_at, above_at):
    result = []
    for route in s.z_routes:
        lower, i = route.below(), s.z.index()
        valid = choose(lower, i >= 1, i + 1 < s.z.count)
        result.append((jnp.where(lower, below_at, above_at), valid))
    return result


def store_terms(held, at, valid, parts):
    for t, part in enumerate(parts):
        held[at, t] = part if valid is None else jnp.where(valid, part, 0.0)


BLOCK = 4


def fine_places(s):
    places = [(RADIUS + p, None) for p in range(s.z.fine)]
    for start, valid in slab_starts(s, 0, s.z.fine + RADIUS):
        places += [(start + p, valid) for p in range(RADIUS)]
    return places


def contract_x(s, grid, weights):
    high, low = split(grid)
    joined = jnp.concatenate([high, low, high], axis=1)
    return jnp.dot(joined, weights[: 3 * s.x.fine], preferred_element_type=F32)


def own_kernel(s, table, t_part, fine, sums, x_fine, x_sums, y_edge, fine_part, sums_part, t_fine):
    z, x = s.z, s.x
    t_fine[...] = t_part[...]
    fine_at = fine_places(s)

    def fine_group(g, count):
        n = 2 * RADIUS
        a, b = split(contract_x(s, fine[g : g + count].reshape(count * n, x.fine), x_fine))
        for p in range(count):
            rows = slice(p * n, (p + 1) * n)
            at, valid = fine_at[g + p]
            for t, part in enumerate(contract_y(s, y_edge, a[rows], b[rows])):
                t_fine[at, t] = t_fine[at, t] + (part if valid is None else jnp.where(valid, part, 0.0))

    def fine_block(k):
        for i, total in enumerate(contract_z(table, 0, t_fine, k, BLOCK)):
            fine_part[k + i] = total

    def sum_part(g, count):
        n = s.sum_rows
        grid = sums[g : g + count].reshape(count * n, x.fine)
        sums_part[g * n : (g + count) * n] = contract_x(s, grid, x_sums)

    later = []
    done = 0
    for g in list(range(z.fine, s.fine_planes, 8)) + list(range(0, z.fine, 8)):
        fine_group(g, 8)
        while later:
            later.pop(0)()
        if g < z.fine:
            ready = g if g + 8 < z.fine else z.fine
            later += [lambda k=k: fine_block(k) for k in range(done, ready, BLOCK)]
            done = max(done, ready)
    starts = list(range(0, s.sum_planes, 8))
    while later or starts:
        if starts:
            sum_part(starts[0], min(8, s.sum_planes - starts[0]))
            starts.pop(0)
        if later:
            later.pop(0)()


def sum_kernel(s, table, fine, sums, first, second, x_sums, ends, y_fine, y_mid, y_coarse, widen_x, widen_y, result, *scratch):
    sums_ends, t_mid, t_coarse, p_mid, p_coarse, narrow, out, left = scratch
    z, y, x = s.z, s.y, s.x
    below = s.x_routes[0].below()
    half = s.edge_sums
    def ends_of(start, rows):
        one, two = first[start : start + rows], second[start : start + rows]
        return jnp.where(below, one, two), jnp.where(below, two, one)

    for b in range(s.sum_blocks):
        if b < s.coarse_blocks:
            pair = ends_of(s.fine_ends + b * half, half)
        else:
            rest = jnp.zeros((half - up8(EDGE), 128), F32)
            pair = ends_of(s.mid_ends + (b - s.coarse_blocks) * up8(EDGE), up8(EDGE))
            pair = [jnp.concatenate([ends, rest], axis=0) for ends in pair]
        rows = jnp.concatenate(pair, axis=0)
        zeros = jnp.zeros((128 - 4 * half, 128), F32)
        sums_ends[b * 128 : (b + 1) * 128] = jnp.concatenate([rows, rows, zeros], axis=0).T

    def along_x(start, rows):
        edge_high, edge_low = split(sums_ends[start : start + rows])
        is_high = iota(edge_high.shape, 1) < 2 * half
        packed = jnp.where(is_high, edge_high.astype(F32), edge_low.astype(F32)).astype(BF16)
        joined = jnp.concatenate([packed, edge_high], axis=1)
        part = jnp.dot(joined, x_sums[3 * x.fine :], preferred_element_type=F32)
        return split(sums[start : start + rows] + part)

    def fine_edges():
        columns = []
        for flip in range(2):
            for g in range(s.fine_groups):
                is_folded = s.folded and g == s.fine_groups - 1
                at = slice(g * s.fine_rows, s.fine_ends if is_folded else (g + 1) * s.fine_rows)
                pair = (first[at], second[at])
                ends_here = jnp.where(below, pair[flip], pair[1 - flip])
                if is_folded:
                    ends_here = jnp.concatenate([ends_here, pltpu.roll(ends_here, x.fine // 2, 1)], axis=0)
                columns.append(ends_here)
        high, low = split(jnp.concatenate(columns, axis=1))
        joined = jnp.concatenate([high, low, high], axis=0)
        high, low = split(jnp.dot(y_fine[...], joined, preferred_element_type=F32))
        width = s.fine_groups * x.fine
        result = []
        for side in range(2):
            total = 0.0
            for t in range(TERMS):
                rows, cols = slice(t * y.fine, (t + 1) * y.fine), slice(side * width, (side + 1) * width)
                a, b = high[rows, cols], low[rows, cols]
                joined = jnp.concatenate([a, b, a], axis=1)
                total = total + jnp.dot(joined, ends[2 * t + side], preferred_element_type=F32)
            result.append(total)
        return result

    t_mid[...] = jnp.zeros(t_mid.shape, F32)
    t_coarse[...] = jnp.zeros(t_coarse.shape, F32)
    mid_at = [(RADIUS + p, None) for p in range(z.mid_all)]
    mid_at, rest_at = mid_at[: z.coarse_all], mid_at[z.coarse_all :]
    coarse_at = [(RADIUS + p, None) for p in range(z.coarse_all)]
    for start, valid in slab_starts(s, 0, z.mid + 3 + RADIUS):
        mid_at += [(start + p, valid) for p in range(RADIUS)]
    mid_at += rest_at
    for start, valid in slab_starts(s, 0, z.coarse + 5 + RADIUS):
        coarse_at += [(start + p, valid) for p in range(RADIUS)]
    coarse_at += [(None, None)] * len(rest_at)
    is_second = iota((s.coarse_rows, x.fine), 1) >= x.fine // TERMS

    def sum_group(g, count):
        n = s.sum_rows
        a, b = along_x(g * n, count * n)
        for p in range(count):
            rows = slice(p * n, (p + 1) * n)
            at, valid = mid_at[g + p]
            cols = slice(0, TERMS * x.fine)
            store_terms(t_mid, at, valid, contract_y(s, y_mid, a[rows, cols], b[rows, cols]))
            at, valid = coarse_at[g + p]
            if at is not None:
                cols = slice(TERMS * x.fine, (TERMS + 1) * x.fine)
                joined = jnp.concatenate([a[rows, cols], b[rows, cols], a[rows, cols]], axis=0)
                both = jnp.dot(y_coarse[...], joined, preferred_element_type=F32)
                m = s.coarse_rows
                store_terms(t_coarse, at, valid, [jnp.where(is_second, both[m:], both[:m])])

    def coarse_block(k):
        count = min(BLOCK, z.coarse_all - k)
        for i, total in enumerate(contract_z(table, 2, t_coarse, k, count)):
            narrow[k + i] = jnp.where(z.holds_coarse(k + i - 2), total, 0.0)

    def widen():
        m = s.coarse_rows
        high, low = split(narrow[...].reshape(z.coarse_all * m, x.fine))
        joined = jnp.concatenate([high, low, high], axis=1)
        high, low = split(jnp.dot(joined, widen_x[...], preferred_element_type=F32))
        for p in range(z.coarse_all):
            rows = slice(p * m, (p + 1) * m)
            joined = jnp.concatenate([high[rows], low[rows], high[rows]], axis=0)
            p_coarse[p] = jnp.dot(widen_y[...], joined, preferred_element_type=F32)

    def mid_block(k):
        count = min(BLOCK, z.mid_all - k)
        for i, total in enumerate(contract_z(table, 1, t_mid, k, count)):
            m = k + i - 1
            for offset, weight in WEIGHTS:
                if (m - offset) % 2 == 0 and 0 <= (m - offset) // 2 + 2 < z.coarse_all:
                    total = total + weight * p_coarse[(m - offset) // 2 + 2]
            p_mid[k + i] = jnp.where(z.holds_mid(m), total, 0.0)

    edges = fine_edges()
    lane = iota((y.fine, x.fine), 1)

    def begin(k):
        block, at = k // s.side, k % s.side * RADIUS
        low, high = (edge[:, block * x.fine : (block + 1) * x.fine] for edge in edges)
        low = pltpu.roll(low, -at % x.fine, 1) if at else low
        turn = (x.fine - RADIUS - at) % x.fine
        high = pltpu.roll(high, turn, 1) if turn else high
        out[k] = fine[k] + jnp.where(lane < RADIUS, low, jnp.where(lane >= x.fine - RADIUS, high, 0.0))

    def finish(k):
        total = out[k]
        for offset, weight in WEIGHTS:
            if (k - offset) % 2 == 0:
                total = total + weight * p_mid[(k - offset) // 2 + 1]
        out[k] = total

    groups = list(range(0, s.sum_planes, 4))
    share = -(-z.fine // len(groups))
    for n, g in enumerate(groups):
        sum_group(g, min(4, s.sum_planes - g))
        for k in range(n * share, min((n + 1) * share, z.fine)):
            begin(k)
    for k in range(0, z.coarse_all, BLOCK):
        coarse_block(k)
    widen()
    done, copies = 0, []
    for k in range(0, z.mid_all, BLOCK):
        mid_block(k)
        ready = z.fine if k + BLOCK >= z.mid_all else 2 * k + 2
        while done < ready:
            finish(done)
            done += 1
            if done % 8 == 0:
                part = pl.ds(done - 8, 8)
                copies.append(pltpu.make_async_copy(out.at[part], result.at[part], left.at[done // 8 - 1]))
                copies[-1].start()
    for copy in copies:
        copy.wait()


def call(kernel, outs, ins, scratch=(), flops=10**7, out_space=pltpu.VMEM):
    specs = [SMEM if a.ndim == 3 and a.shape[-1] == TAPS else VMEM for a in ins]
    size = sum(a.size * a.dtype.itemsize for a in ins) + sum(o.size * o.dtype.itemsize for o in outs)
    return pl.pallas_call(
        kernel,
        out_shape=tuple(outs),
        in_specs=specs,
        out_specs=tuple(pl.BlockSpec(memory_space=out_space) for _ in outs),
        scratch_shapes=list(scratch),
        compiler_params=PARAMS,
        cost_estimate=pl.CostEstimate(flops=flops, bytes_accessed=size, transcendentals=0),
    )(*ins)


def array(*shape, dtype=F32):
    return jax.ShapeDtypeStruct(shape, dtype)


def local(charges, kernel_taps):
    z, y, x = (Cut(name, size) for name, size in zip(("gz", "gy", "gx"), charges.shape))
    s = Sizes(z, y, x)
    n = x.fine
    nz, nz2 = len(s.z_routes), len(s.z2_routes)

    def bound(kernel, *static):
        return lambda *refs: kernel(s, *static, *refs)

    rows = up8(y.mid_all)
    (weights,) = call(bound(narrow_kernel), [array(n, 2 * n, dtype=BF16)], [], flops=10**10)
    held, own, ahead, behind, far, *messages = call(
        bound(restrict_kernel, nz),
        [array(*charges.shape), array(z.mid_all, rows, n)] + [array(s.y_rows, n)] * 2 + [array(s.far_rows, n)] + [array(s.z_rows, n)] * nz + [array(s.z2_rows, n)] * nz2,
        [charges, weights],
        [
            pltpu.VMEM((z.fine, y.fine + 32, n), F32),
            pltpu.VMEM((z.mid_all, rows, n), F32),
            pltpu.VMEM((z.mid_all, up8(y.mid + 24), n), F32),
            pltpu.VMEM((z.mid_all, rows, n), F32),
            pltpu.VMEM((2, max(s.z_rows - s.z_fine, s.y_rows - s.y_fine), n), F32),
            pltpu.VMEM((s.far_groups, s.far_rows, n), F32),
        ],
    )
    z_got = [route(m) for route, m in zip(s.z_routes + s.z2_routes, messages)]
    sides = [s.y_routes[0](ahead), s.y_routes[1](behind)]
    far = s.y2_routes[0](far)
    (passed,) = call(bound(pass_kernel), [array(s.far_rows, n)], [far], flops=2*10**9)
    operators = call(
        bound(operator_kernel),
        [
            array(3 * n, TERMS * n, dtype=BF16),
            array(3 * n + 256, (TERMS + 1) * n, dtype=BF16),
            array(TERMS * y.fine, 3 * y.fine, dtype=BF16),
            array(TERMS * y.fine, 6 * RADIUS, dtype=BF16),
            array(TERMS * y.fine, 3 * s.fine_rows, dtype=BF16),
            array(TERMS * y.fine, 3 * s.sum_rows, dtype=BF16),
            array(TERMS * s.coarse_rows, 3 * s.sum_rows, dtype=BF16),
            array(3 * n, n, dtype=BF16),
            array(y.fine, 3 * s.coarse_rows, dtype=BF16),
        ],
        [kernel_taps],
    )
    later = call(
        bound(later_kernel),
        [array(2 * TERMS, 3 * s.fine_groups * n, z_columns(s), dtype=BF16), array((2 * TERMS + 1) * TAPS, 8, n)],
        [kernel_taps],
    )
    ends, table = later
    ahead, behind = call(
        bound(spread_kernel, nz, nz2),
        [array(s.slab_rows, n), array(s.slab_rows, n)],
        [passed, later[1], *z_got],
        [pltpu.VMEM((3, up8(max(s.slab_coarse, s.slab_rows - s.slab_fine)) + 8, n), F32)],
    )
    sides += [s.y_routes[0](ahead), s.y_routes[1](behind)]
    fars = [far] + [route(passed) for route in s.z_routes + s.z2_routes]
    x_fine, x_sums, y_own, y_edge, y_fine, y_mid, y_coarse, widen_x, widen_y = operators
    t_part, last, start = call(
        bound(early_kernel, nz),
        [array(z.fine + 2 * RADIUS, TERMS, y.fine, n)] + [array(s.fine_groups * y.fine, n)] * 2,
        [held, *z_got[:nz], x_fine, y_own],
        [pltpu.VMEM((nz * RADIUS, y.fine, n), F32)],
    )
    fine, sums, first, second = call(
        bound(collect_kernel, nz, nz2),
        [
            array(s.fine_planes, 2 * RADIUS, n),
            array(s.sum_planes, s.sum_rows, n),
            array(s.x_rows, n),
            array(s.x_rows, n),
        ],
        [last, start, own, *z_got, *sides, *fars],
        [
            pltpu.VMEM((s.slab_planes, s.sum_rows, n), F32),
            pltpu.VMEM((1 + nz + nz2, z.coarse_all, 8, n), F32),
            pltpu.VMEM((2, up8(s.slab_coarse) + 8, n), F32),
        ],
    )
    first, second = s.x_routes[0](first), s.x_routes[1](second)
    fine, sums = call(
        bound(own_kernel),
        [array(z.fine, y.fine, n), array(s.sum_planes * s.sum_rows, (TERMS + 1) * n)],
        [table, t_part, fine, sums, x_fine, x_sums, y_edge],
        [pltpu.VMEM((z.fine + 2 * RADIUS, TERMS, y.fine, n), F32)],
    )
    (out,) = call(
        bound(sum_kernel),
        [array(z.fine, y.fine, n)],
        [table, fine, sums, first, second, x_sums, ends, y_fine, y_mid, y_coarse, widen_x, widen_y],
        [
            pltpu.VMEM((s.sum_blocks * 128, n), F32),
            pltpu.VMEM((z.mid + 2 * RADIUS + 3, TERMS, y.fine, n), F32),
            pltpu.VMEM((z.coarse + 2 * RADIUS + 5, 1, s.coarse_rows, n), F32),
            pltpu.VMEM((z.mid_all, y.fine, n), F32),
            pltpu.VMEM((z.coarse_all, y.fine, n), F32),
            pltpu.VMEM((z.coarse_all, s.coarse_rows, n), F32),
            pltpu.VMEM((z.fine, y.fine, n), F32),
            pltpu.SemaphoreType.DMA((z.fine // 8,)),
        ],
        out_space=pltpu.HBM,
    )
    return out


def solution(mesh):
    return jax.shard_map(
        local,
        mesh=mesh,
        in_specs=(P("gz", "gy", "gx"), P()),
        out_specs=P("gz", "gy", "gx"),
        check_vma=False,
    )
```

```python
import jax
import jax.numpy as jnp
from jax import lax
from jax.experimental import pallas as pl
from jax.experimental.pallas import tpu as pltpu
from jax.sharding import PartitionSpec as P

RADIUS = 8
TAPS = 17
TERMS = 2
WEIGHTS = ((-3, -0.0625), (-1, 0.5625), (0, 1.0), (1, 0.5625), (3, -0.0625))
EXACT = lax.Precision.HIGHEST
SPAN = RADIUS + 5
EDGE = RADIUS + 3
F32, BF16 = jnp.float32, jnp.bfloat16
PARAMS = pltpu.CompilerParams(vmem_limit_bytes=32 * 1024 * 1024)
VMEM = pl.BlockSpec(memory_space=pltpu.VMEM)
SMEM = pl.BlockSpec(memory_space=pltpu.SMEM)


def up8(n):
    return -(-n // 8) * 8


def iota(shape, dim):
    return lax.broadcasted_iota(jnp.int32, shape, dim)


def weight_of(difference):
    size = jnp.abs(difference)
    out = jnp.where(size == 1, 0.5625, jnp.where(size == 3, -0.0625, 0.0))
    return jnp.where(size == 0, 1.0, out)


def choose(condition, a, b):
    return jnp.where(condition, jnp.where(a, 1, 0), jnp.where(b, 1, 0)) != 0


class Cut:
    def __init__(self, name, length):
        self.name, self.fine = name, length
        self.count = lax.axis_size(name)
        self.mid, self.coarse = length // 2, length // 4
        self.mid_all, self.coarse_all = self.mid + 3, self.coarse + 5
        self.second = max(SPAN - self.coarse, 0)

    def index(self):
        return lax.axis_index(self.name)

    def holds_mid(self, k):
        k = k + self.index() * self.mid
        return (k >= 0) & (k < self.mid * self.count)

    def holds_coarse(self, k):
        k = k + self.index() * self.coarse
        return (k >= 0) & (k < self.coarse * self.count)


class Route:
    def __init__(self, names, pairs, up, below):
        self.names, self.pairs, self.up, self.below = names, pairs, up, below

    def __call__(self, x):
        return lax.ppermute(x, self.names, self.pairs)


def flip(pairs):
    return [(b, a) for a, b in pairs]


def swap(cut, steps):
    pairs = [(i, i + steps) for i in range(cut.count - steps)]

    def up():
        return cut.index() + steps < cut.count

    return [Route(cut.name, pairs + flip(pairs), up, lambda: ~up())]


def both_ways(cut, steps):
    pairs = [(i, i + steps) for i in range(cut.count - steps)]
    yes, no = (lambda: cut.index() >= 0), (lambda: cut.index() < 0)
    return [Route(cut.name, pairs, yes, yes), Route(cut.name, flip(pairs), no, no)]


def folded(cut, beside, names):
    n, m = cut.count, lax.axis_size(beside)

    def place(c, i):
        return c * n + i if names[0] == beside else i * m + c

    pairs = []
    for c in range(0, m, 2):
        cycle = [place(c, i) for i in range(n)] + [place(c + 1, i) for i in reversed(range(n))]
        pairs += list(zip(cycle, cycle[1:] + cycle[:1]))

    def even():
        return lax.axis_index(beside) % 2 == 0

    def odd():
        return lax.axis_index(beside) % 2 == 1

    return [Route(names, pairs, even, even), Route(names, flip(pairs), odd, odd)]


def split(x):
    high = x.astype(BF16)
    return high, (x - high.astype(F32)).astype(BF16)


def pick(selector, x):
    nt = (((1,), (1,)), ((), ()))
    a = x.astype(BF16)
    rest = x - a.astype(F32)
    b = rest.astype(BF16)
    c = (rest - b.astype(F32)).astype(BF16)
    out = lax.dot_general(selector, c, nt, preferred_element_type=F32)
    out = out + lax.dot_general(selector, b, nt, preferred_element_type=F32)
    return out + lax.dot_general(selector, a, nt, preferred_element_type=F32)


class Sizes:
    def place_of(self, p):
        return p if p < self.slab_start else p + self.coarse_planes - self.slab_start

    def __init__(self, z, y, x):
        self.z, self.y, self.x = z, y, x
        self.z_routes = swap(z, 1) if z.count <= 2 else both_ways(z, 1)
        self.z2_routes = [] if z.count <= 2 else swap(z, 2) if z.count <= 4 else both_ways(z, 2)
        self.y_routes = folded(y, x.name, (x.name, y.name))
        self.y2_routes = swap(y, 2)
        self.x_routes = folded(x, z.name, (x.name, z.name))
        self.inner = y.fine - 2 * RADIUS
        self.z_fine = RADIUS * 2 * RADIUS
        self.z_sums = max(EDGE * y.mid_all, SPAN * y.coarse_all)
        self.z_rows = up8(self.z_fine + self.z_sums)
        self.z2_rows = up8(z.second * y.coarse_all)
        self.slab_planes = SPAN * len(self.z_routes) + z.second * len(self.z2_routes)
        self.fine_planes = z.fine + RADIUS * len(self.z_routes)
        self.sum_planes = z.mid_all + RADIUS * len(self.z_routes)
        self.coarse_rows = -(-y.coarse_all // 16) * 16
        self.y_fine = RADIUS * z.fine
        self.y_sums = max(EDGE * z.mid_all, SPAN * z.coarse_all)
        self.y_rows = up8(self.y_fine + self.y_sums)
        self.slab_fine = RADIUS * RADIUS * len(self.z_routes)
        self.slab_mid = EDGE * EDGE * len(self.z_routes)
        self.slab_coarse = SPAN * self.slab_planes
        self.extra = max(self.slab_coarse - self.slab_mid, 0)
        self.spare = x.fine - x.mid_all - x.coarse_all
        self.pieces = -(-x.coarse_all // max(self.spare, 1))
        if self.pieces * self.extra > self.slab_mid:
            self.extra = 0
        self.slab_sums = max(self.slab_mid, self.slab_coarse - self.extra)
        self.slab_rows = up8(self.slab_fine + self.slab_sums)
        self.far_groups = x.fine // x.coarse_all
        self.far_planes = -(-z.coarse_all // self.far_groups)
        self.far_rows = up8(y.second * self.far_planes)
        self.slab_start = z.coarse_all
        self.coarse_planes = z.coarse_all + RADIUS * len(self.z_routes)
        self.fine_rows = y.fine + 2 * RADIUS
        self.far = y.coarse_all
        self.low = y.mid_all
        self.high = self.low + SPAN
        self.sum_rows = -(-(self.high + SPAN) // 16) * 16
        self.edge_sums = EDGE + SPAN
        self.side = x.fine // RADIUS
        self.fine_groups = -(-self.fine_planes // self.side)
        assert z.fine % self.side == 0
        self.own_groups = z.fine // self.side
        self.folded = 0 < self.fine_planes % self.side <= self.side // 2
        self.fine_ends = self.fine_groups * self.fine_rows - (self.fine_rows // 2 if self.folded else 0)
        self.sum_blocks = -(-self.sum_planes * self.sum_rows // 128)
        self.coarse_blocks = -(-self.coarse_planes * self.sum_rows // 128)
        self.mid_ends = self.fine_ends + self.coarse_blocks * self.edge_sums
        self.x_rows = self.mid_ends + (self.sum_blocks - self.coarse_blocks) * up8(EDGE)
        assert x.mid_all + x.coarse_all <= x.fine
        assert self.far + y.second <= self.low and y.second <= 8 and y.coarse_all == SPAN and z.coarse_all == SPAN
        assert z.coarse >= RADIUS and y.coarse >= RADIUS and y.count == 4


def narrow_kernel(s, out):
    x = s.x
    lanes = (x.fine, x.fine)
    cell, lane = iota(lanes, 0), iota(lanes, 1)
    k = lane - 1
    to_mid = jnp.where((lane < x.mid_all) & x.holds_mid(k), weight_of(cell - 2 * k), 0.0)
    c = lane - x.mid_all - 2
    inside = (lane >= x.mid_all) & (lane < x.mid_all + x.coarse_all) & x.holds_coarse(c)
    to_coarse = jnp.where(inside, weight_of(cell - 1 - 2 * c), 0.0)
    narrow = to_mid + jnp.dot(to_mid, to_coarse, precision=EXACT, preferred_element_type=F32)
    out[...] = jnp.concatenate(split(narrow), axis=1)


def restrict_kernel(s, nz, source, narrow, charges, own, ahead, behind, far, *rest):
    messages, (wide, mid, high, coarse, packed, groups) = rest[:-6], rest[-6:]
    z, y, x = s.z, s.y, s.x
    wide[...] = jnp.zeros(wide.shape, F32)
    charges[...] = source[...]
    cells = source[...].reshape(z.fine * y.fine, x.fine)
    top, rest = cells.astype(BF16), cells
    rest = rest - top.astype(F32)
    middle = rest.astype(BF16)
    low = (rest - middle.astype(F32)).astype(BF16)
    weights = narrow[...]
    both = jnp.dot(low, weights, preferred_element_type=F32)
    both = both + jnp.dot(
        jnp.concatenate([top, middle], axis=1), jnp.concatenate([weights, weights], axis=0), preferred_element_type=F32
    )
    reduced = both[:, : x.fine] + both[:, x.fine :]
    wide[:, 8 : 8 + y.fine, :] = reduced.reshape(z.fine, y.fine, x.fine)
    rows = 0.0
    for offset, weight in WEIGHTS:
        rows = rows + weight * wide[:, pl.ds(6 + offset, y.mid_all, stride=2), :]
    keep = y.holds_mid(iota((y.mid_all, x.fine), 0) - 1)
    mid[...] = jnp.zeros(mid.shape, F32)
    coarse[...] = jnp.zeros(coarse.shape, F32)
    high[...] = jnp.zeros(high.shape, F32)
    for p in range(z.mid_all):
        total = 0.0
        for offset, weight in WEIGHTS:
            at = 2 * (p - 1) + offset
            if 0 <= at < z.fine:
                total = total + weight * rows[at]
        total = jnp.where(keep & z.holds_mid(p - 1), total, 0.0)
        mid[p, : y.mid_all] = total
        high[p, 8 : 8 + y.mid_all] = total
    rows = 0.0
    for offset, weight in WEIGHTS:
        rows = rows + weight * high[:, pl.ds(5 + offset, y.coarse_all, stride=2), :]
    keep = y.holds_coarse(iota((y.coarse_all, x.fine), 0) - 2)
    for p in range(z.coarse_all):
        total = 0.0
        for offset, weight in WEIGHTS:
            at = 2 * (p - 2) + offset + 1
            if 0 <= at < z.mid_all:
                total = total + weight * rows[at]
        coarse[p, : y.coarse_all] = jnp.where(keep & z.holds_coarse(p - 2), total, 0.0)
    is_mid = iota(mid.shape[1:], 1) < x.mid_all
    for p in range(z.mid_all):
        own[p] = jnp.where(is_mid, mid[p], coarse[p]) if p < z.coarse_all else jnp.where(is_mid, mid[p], 0.0)
    up = s.y2_routes[0].up()
    count, end = y.second, y.coarse_all
    groups[...] = jnp.zeros(groups.shape, F32)
    for p in range(z.coarse_all):
        g, at = p // s.far_planes, p % s.far_planes * count
        groups[g, at : at + count] = jnp.where(up, own[p, end - count : end], own[p, :count])
    lane = iota(far.shape, 1)
    total = jnp.zeros(far.shape, F32)
    for g in range(s.far_groups):
        first = g * x.coarse_all
        turned = pltpu.roll(groups[g], (first - x.mid_all) % x.fine, 1)
        total = jnp.where((lane >= first) & (lane < first + x.coarse_all), turned, total)
    far[...] = total
    for message, route in zip((ahead, behind), s.y_routes):
        up = route.up()
        edge = jnp.where(up, charges[:, y.fine - RADIUS :, :], charges[:, :RADIUS, :])
        message[: s.y_fine] = edge.reshape(s.y_fine, x.fine)
        packed[...] = jnp.zeros(packed.shape, F32)
        for p in range(z.mid_all):
            packed[0, p * EDGE : (p + 1) * EDGE] = jnp.where(up, mid[p, y.mid_all - EDGE : y.mid_all], mid[p, :EDGE])
        for p in range(z.coarse_all):
            packed[1, p * SPAN : (p + 1) * SPAN] = coarse[p, :SPAN]
        rows = s.y_rows - s.y_fine
        is_mid = iota((rows, x.fine), 1) < x.mid_all
        message[s.y_fine :] = jnp.where(is_mid, packed[0, :rows], packed[1, :rows])
    for message, route in zip(messages, s.z_routes):
        up = route.up().astype(jnp.int32)
        planes = charges[pl.ds(up * (z.fine - RADIUS), RADIUS)]
        outer = jnp.concatenate([planes[:, :RADIUS], planes[:, y.fine - RADIUS :]], axis=1)
        message[: s.z_fine] = outer.reshape(s.z_fine, x.fine)
        packed[...] = jnp.zeros(packed.shape, F32)
        for p in range(EDGE):
            packed[0, p * y.mid_all : (p + 1) * y.mid_all] = mid[up * (z.mid_all - EDGE) + p][: y.mid_all]
        for p in range(SPAN):
            plane = coarse[up * (z.coarse_all - SPAN) + p]
            packed[1, p * y.coarse_all : (p + 1) * y.coarse_all] = plane[: y.coarse_all]
        rows = s.z_rows - s.z_fine
        is_mid = iota((rows, x.fine), 1) < x.mid_all
        message[s.z_fine :] = jnp.where(is_mid, packed[0, :rows], packed[1, :rows])
    for message, route in zip(messages[nz:], s.z2_routes):
        up = route.up().astype(jnp.int32)
        message[...] = jnp.zeros(message.shape, F32)
        for p in range(z.second):
            plane = coarse[up * (z.coarse_all - z.second) + p]
            message[p * y.coarse_all : (p + 1) * y.coarse_all] = plane[: y.coarse_all]


class Slab:
    def __init__(self, message, mid, coarse):
        self.message, self.mid, self.coarse = message, mid, coarse

    def mid_rows(self, first, count):
        return self.message[self.mid + first : self.mid + first + count]

    def coarse_rows(self, first, count):
        return self.message[self.coarse + first : self.coarse + first + count]

    def rows(self, is_mid, first_mid, first_coarse, count):
        coarse = 0.0 if first_coarse is None else self.coarse_rows(first_coarse, count)
        mid = 0.0 if self.mid is None else self.message[self.mid + first_mid : self.mid + first_mid + count]
        return jnp.where(is_mid, mid, coarse)


def slabs(s, z_messages, z2_messages):
    out = []
    for message in z_messages:
        for p in range(SPAN):
            mid = s.z_fine + p * s.y.mid_all if p < EDGE else None
            out.append(Slab(message, mid, s.z_fine + p * s.y.coarse_all))
    for message in z2_messages:
        out += [Slab(message, None, p * s.y.coarse_all) for p in range(s.z.second)]
    return out


def spread_kernel(s, nz, nz2, _, __, *rest):
    z_messages, z2_messages = rest[:nz], rest[nz : nz + nz2]
    ahead, behind, packed = rest[-3:]
    z, y, x = s.z, s.y, s.x
    planes = slabs(s, z_messages, z2_messages)
    count = s.slab_rows - s.slab_fine
    lane = iota((count, x.fine), 1)
    packed[...] = jnp.zeros(packed.shape, F32)
    for p, plane in enumerate(planes):
        packed[1, p * SPAN : (p + 1) * SPAN] = plane.coarse_rows(0, SPAN)
    for n in range(s.pieces if s.extra else 0):
        first = x.mid_all + n * s.spare
        turned = pltpu.roll(packed[1, s.slab_mid : s.slab_mid + up8(s.extra)], x.fine - s.spare - first, 1)
        packed[2, n * s.extra : (n + 1) * s.extra] = turned[: s.extra]
    coarse = jnp.where(lane < x.fine - s.spare, packed[1, :count], packed[2, :count])
    for message, route in zip((ahead, behind), s.y_routes):
        up = route.up()
        at = 0
        for z_message in z_messages:
            slab = z_message[: s.z_fine].reshape(RADIUS, 2 * RADIUS, x.fine)
            edge = jnp.where(up, slab[:, RADIUS:], slab[:, :RADIUS])
            message[at : at + RADIUS * RADIUS] = edge.reshape(RADIUS * RADIUS, x.fine)
            at += RADIUS * RADIUS
        at = 0
        for plane in planes:
            if plane.mid is not None:
                first, last = plane.mid_rows(0, EDGE), plane.mid_rows(y.mid_all - EDGE, EDGE)
                packed[0, at : at + EDGE] = jnp.where(up, last, first)
                at += EDGE
        message[s.slab_fine :] = jnp.where(lane < x.mid_all, packed[0, :count], coarse)


def pass_kernel(s, nz, far, charges, *outs):
    z, x = s.z, s.x
    rows = RADIUS * s.inner
    for out, route in zip(outs, s.z_routes):
        planes = charges[pl.ds(route.up().astype(jnp.int32) * (z.fine - RADIUS), RADIUS)]
        out[:rows] = planes[:, RADIUS : RADIUS + s.inner].reshape(rows, x.fine)
        out[rows:] = far[...]
    for out in outs[nz:]:
        out[...] = far[...]


def roll_ends(s, plane_rows, count, groups):
    x = s.x
    lane = iota((count, x.fine), 1)
    for g in groups:
        ends = [jnp.zeros(lane.shape, F32)] * 2
        for j in range(min(s.side, s.fine_planes - g * s.side)):
            plane = plane_rows(g * s.side + j)
            here = (lane >= RADIUS * j) & (lane < RADIUS * (j + 1))
            for n, start in enumerate((x.fine - RADIUS, 0)):
                shift = (RADIUS * j - start) % x.fine
                ends[n] = jnp.where(here, pltpu.roll(plane, shift, 1) if shift else plane, ends[n])
        yield g, ends


def early_kernel(s, charges, x_fine, y_own, t_part, last, start):
    z, y, x = s.z, s.y, s.x
    t_part[...] = jnp.zeros(t_part.shape, F32)
    for g in range(0, z.fine, 8):
        a, b = split(contract_x(s, charges[g : g + 8].reshape(8 * y.fine, x.fine), x_fine))
        for p in range(8):
            rows = slice(p * y.fine, (p + 1) * y.fine)
            store_terms(t_part, RADIUS + g + p, None, contract_y(s, y_own, a[rows], b[rows]))
    for g, ends in roll_ends(s, lambda p: charges[p], y.fine, range(s.own_groups)):
        rows = slice(g * y.fine, (g + 1) * y.fine)
        last[rows], start[rows] = ends


def collect_kernel(s, nz, nz2, last, start, own, *rest):
    z_messages, z2_messages = rest[:nz], rest[nz : nz + nz2]
    rest = rest[nz + nz2 :]
    pairs = rest[:4]
    fars = rest[4 : 5 + nz + nz2]
    fine, slab, sums, first, second, raw, rows, near = rest[5 + nz + nz2 :]
    z, y, x = s.z, s.y, s.x
    below = s.y_routes[0].below()
    planes = slabs(s, z_messages, z2_messages)

    def sides(which, start, count):
        a, b = (message[start : start + count] for message in pairs[2 * which : 2 * which + 2])
        return jnp.where(below, a, b), jnp.where(below, b, a)

    parts = [(0, z.fine, 0, 0)] + [(z.fine + n * RADIUS, RADIUS, 1, n * RADIUS * RADIUS) for n in range(nz)]
    for at, count, which, row in parts:
        low, high = sides(which, row, RADIUS * count)
        fine[at : at + count, :RADIUS] = low.reshape(count, RADIUS, x.fine)
        fine[at : at + count, RADIUS:] = high.reshape(count, RADIUS, x.fine)
    sums[...] = jnp.zeros(sums.shape, F32)
    raw[...] = jnp.zeros(raw.shape, F32)
    inner_rows = RADIUS * s.inner
    for n, far in enumerate(fars):
        is_joint = 0 < n <= nz
        if is_joint:
            outer = z_messages[n - 1][: s.z_fine].reshape(RADIUS, 2 * RADIUS, x.fine)
            planes_here = slice((n - 1) * RADIUS, n * RADIUS)
            slab[planes_here, :RADIUS] = outer[:, :RADIUS]
            slab[planes_here, RADIUS : RADIUS + s.inner] = far[:inner_rows].reshape(RADIUS, s.inner, x.fine)
            slab[planes_here, RADIUS + s.inner :] = outer[:, RADIUS:]
        two_away = far[inner_rows:] if is_joint else far[...]
        for g in range(s.far_groups):
            turned = pltpu.roll(two_away, (x.mid_all - g * x.coarse_all) % x.fine, 1)
            for p in range(g * s.far_planes, min((g + 1) * s.far_planes, z.coarse_all)):
                at = p % s.far_planes * y.second
                rows[n, p, : y.second] = turned[at : at + y.second]
    is_mid = iota((y.second, x.fine), 1) < x.mid_all

    lane = iota((up8(s.extra), x.fine), 1)
    for side, got in enumerate(sides(1, s.slab_fine, s.slab_sums)):
        near[side, : s.slab_sums] = got
        if s.extra:
            total = jnp.zeros(lane.shape, F32)
            for n in range(s.pieces):
                begin = x.mid_all + n * s.spare
                piece = near[side, n * s.extra : n * s.extra + up8(s.extra)]
                turned = pltpu.roll(piece, begin + s.spare, 1)
                total = jnp.where(lane >= begin, turned, total)
            near[side, s.slab_mid : s.slab_mid + s.extra] = total[: s.extra]
    is_mid_edge = iota((EDGE, x.fine), 1) < x.mid_all
    is_mid_span = iota((SPAN, x.fine), 1) < x.mid_all

    def rows_of_plane(out, p, body, mids, coarses, far_plane):
        out[p, : y.mid_all] = body
        for base, shift, n in ((s.low, SPAN - EDGE, 0), (s.high, 0, 1)):
            if coarses is not None:
                out[p, base : base + SPAN] = jnp.where(is_mid_span, 0.0, coarses[n])
            if mids is not None:
                at = slice(base + shift, base + shift + EDGE)
                out[p, at] = jnp.where(is_mid_edge, mids[n], out[p, at])
        if far_plane is not None:
            at = slice(s.far, s.far + y.second)
            out[p, at] = jnp.where(is_mid, out[p, at], rows[far_plane][: y.second])

    for p in range(z.mid_all):
        far_plane = (0, p) if p < z.coarse_all else None
        mids = sides(0, s.y_fine + p * EDGE, EDGE)
        coarses = sides(0, s.y_fine + p * SPAN, SPAN) if p < z.coarse_all else None
        rows_of_plane(sums, s.place_of(p), own[p, : y.mid_all], mids, coarses, far_plane)
    is_mid_row = iota((SPAN, x.fine), 1) < x.mid_all
    is_mid_rest = iota((y.mid_all - SPAN, x.fine), 1) < x.mid_all
    slab_far = [(1 + n, p) for n in range(nz) for p in range(SPAN)]
    for n, route in enumerate(s.z2_routes):
        at = jnp.where(route.below(), z.coarse_all - z.second, 0)
        slab_far += [(1 + nz + n, at + p) for p in range(z.second)]
    held = 0
    for p, plane in enumerate(planes):
        body = [plane.rows(is_mid_row, 0, 0, SPAN), plane.rows(is_mid_rest, SPAN, None, y.mid_all - SPAN)]
        mids = None
        if plane.mid is not None:
            mids = sides(1, s.slab_fine + held * EDGE, EDGE)
            held += 1
        coarses = [near[side, p * SPAN : (p + 1) * SPAN] for side in range(2)]
        rows_of_plane(raw, p, jnp.concatenate(body, axis=0), mids, coarses, slab_far[p])
    is_mid = iota((s.sum_rows, x.fine), 1) < x.mid_all

    def number(condition, a, b):
        return jnp.where(condition, a, b)

    for n, route in enumerate(s.z_routes):
        lower, base = route.below(), n * SPAN
        for j in range(RADIUS):
            a = raw[base + number(lower, 0, 3) + j]
            b = raw[base + number(lower, SPAN - 5 - RADIUS, 5) + j]
            sums[s.slab_start + n * RADIUS + j] = jnp.where(is_mid, a, b)
        for i in range(3):
            at = number(lower, 0, s.place_of(z.mid)) + i
            sums[at] = sums[at] + jnp.where(is_mid, raw[base + number(lower, EDGE - 3, 0) + i], 0.0)
        for i in range(5):
            at = number(lower, 0, z.coarse) + i
            sums[at] = sums[at] + jnp.where(is_mid, 0.0, raw[base + number(lower, SPAN - 5, 0) + i])
    for n, route in enumerate(s.z2_routes):
        base = len(s.z_routes) * SPAN + n * z.second
        at = s.slab_start + number(route.below(), RADIUS - z.coarse, RADIUS + z.coarse - 5)
        for p in range(z.second):
            sums[at + p] = sums[at + p] + jnp.where(is_mid, 0.0, raw[base + p])

    up = s.x_routes[0].up()
    half, shift = s.fine_rows // 2, x.fine // 2
    is_first_half = iota((half, x.fine), 1) < shift
    own_ends = roll_ends(s, lambda p: fine[p], 2 * RADIUS, range(s.own_groups))
    slab_rows = [jnp.concatenate([slab[p], fine[z.fine + p]], axis=0) for p in range(nz * RADIUS)]
    slab_ends = roll_ends(s, lambda p: slab_rows[p - z.fine], s.fine_rows, range(s.own_groups, s.fine_groups))
    for g, ends in list(own_ends) + list(slab_ends):
        both = ends
        if g < s.own_groups:
            rows = slice(g * y.fine, (g + 1) * y.fine)
            both = [jnp.concatenate([old[rows], new], axis=0) for old, new in zip((last, start), ends)]
        if s.folded and g == s.fine_groups - 1:
            both = [jnp.where(is_first_half, e[:half], pltpu.roll(e[half:], shift, 1)) for e in both]
        at = slice(g * s.fine_rows, g * s.fine_rows + both[0].shape[0])
        first[at] = jnp.where(up, both[0], both[1])
        second[at] = jnp.where(up, both[1], both[0])
    width = EDGE + SPAN
    row, lane = iota((2 * width, x.fine), 0), iota((2 * width, x.fine), 1)
    is_first = row < width
    goes_up = choose(up, is_first, ~is_first)
    slot = jnp.where(is_first, row, row - width)
    from_mid = jnp.where(goes_up, x.mid_all - EDGE + slot, slot)
    from_coarse = slot - EDGE + jnp.where(goes_up, x.mid_all + x.coarse_all - SPAN, x.mid_all)
    wanted = jnp.where(slot < EDGE, from_mid, from_coarse)
    picked_sums = pick((lane == wanted).astype(BF16), sums[...].reshape(s.sum_planes * s.sum_rows, x.fine))
    spare = s.sum_blocks * 128 - picked_sums.shape[1]
    if spare:
        picked_sums = jnp.concatenate([picked_sums, jnp.zeros((2 * width, spare), F32)], axis=1)
    for n, message in enumerate((first, second)):
        rows = picked_sums[n * width : (n + 1) * width]
        for b in range(s.coarse_blocks):
            at = s.fine_ends + b * width
            message[at : at + width] = rows[:, b * 128 : (b + 1) * 128]
        for b in range(s.coarse_blocks, s.sum_blocks):
            at = s.mid_ends + (b - s.coarse_blocks) * up8(EDGE)
            message[at : at + up8(EDGE)] = rows[: up8(EDGE), b * 128 : (b + 1) * 128]


def band(taps, level, offset, valid):
    at = jnp.where(valid, offset + RADIUS, -1)
    out = [jnp.zeros(at.shape, F32) for _ in range(TERMS)]
    for tap in range(TAPS):
        here = at == tap
        out = [jnp.where(here, taps[level, term, tap], total) for term, total in enumerate(out)]
    return out


def dot(a, b):
    return jnp.dot(a, b, precision=EXACT, preferred_element_type=F32)


def z_columns(s):
    return s.z.fine * RADIUS


def lower_x(x):
    return x.index() > 0


def higher_x(x):
    return x.index() < x.count - 1


def later_kernel(s, taps, ends, table):
    y, x = s.y, s.x
    for level in range(2):
        for term in range(TERMS):
            for tap in range(TAPS):
                table[(level * TERMS + term) * TAPS + tap] = jnp.full((8, x.fine), taps[level, term, tap], F32)
    is_second = iota((8, x.fine), 1) >= x.fine // TERMS
    for tap in range(TAPS):
        table[2 * TERMS * TAPS + tap] = jnp.where(is_second, taps[2, 1, tap], taps[2, 0, tap])

    z, slots, wide = s.z, s.side * s.fine_groups, z_columns(s)
    slot, column = iota((slots, wide), 0), iota((slots, wide), 1)
    where, valid = slot, slot < z.fine
    for n, route in enumerate(s.z_routes):
        lower, i, first = route.below(), z.index(), z.fine + n * RADIUS
        here = (slot >= first) & (slot < first + RADIUS)
        where = jnp.where(here, slot - first + jnp.where(lower, -RADIUS, z.fine), where)
        valid = choose(here, choose(lower, i >= 1, i + 1 < z.count), valid)
    planes = band(taps, 0, where - column // RADIUS, valid)
    r, c = iota((RADIUS, wide), 0), iota((RADIUS, wide), 1) % RADIUS
    cells = (slots, RADIUS, wide)
    for side, (offset, valid) in enumerate(((r - c - RADIUS, lower_x(x)), (r - c + RADIUS, higher_x(x)))):
        columns = band(taps, 0, offset, choose(valid, r >= 0, r < 0))
        for term in range(TERMS):
            joint = jnp.broadcast_to(planes[term][:, None, :], cells) * jnp.broadcast_to(columns[term][None], cells)
            high, low = split(joint.reshape(slots * RADIUS, wide))
            at = 2 * term + side
            ends[at, : slots * RADIUS] = high
            ends[at, slots * RADIUS : 2 * slots * RADIUS] = high
            ends[at, 2 * slots * RADIUS :] = low

def operator_kernel(s, taps, x_fine, x_sums, y_own, y_edge, y_fine, y_mid, y_coarse, widen_x, widen_y):
    y, x = s.y, s.x
    own, edge = x.fine, 64
    shape = (own + edge, x.fine)
    row, lane = iota(shape, 0), iota(shape, 1)
    t = row - own
    lower, higher = x.index() > 0, x.index() < x.count - 1
    is_own = row < own

    def place(half, own_place, own_valid, first, count, low_place, high_place):
        is_low = t < half
        r = jnp.where(is_low, t, t - half) - first
        there = (r >= 0) & (r < count) & (t < 2 * half) & choose(is_low, lower, higher)
        valid = choose(is_own, own_valid, there)
        return jnp.where(is_own, own_place, jnp.where(is_low, low_place + r, high_place + r)), valid

    half = s.edge_sums
    cell, column = iota((own, x.fine), 0), iota((own, x.fine), 1)
    fine = band(taps, 0, cell - column, cell >= 0)
    where, valid = place(half, row - 1, row < x.mid_all, 0, EDGE, 2 - EDGE, x.mid - 1)
    mid = band(taps, 1, where - (lane - 1), valid & (lane < x.mid_all))
    first = x.mid_all
    inside = (row >= first) & (row < first + x.coarse_all)
    where, valid = place(half, row - first - 2, inside, EDGE, SPAN, 3 - SPAN, x.coarse - 2)
    side = x.fine // TERMS
    column = lane % side
    terms = band(taps, 2, where - (column - 2), valid & (column < x.coarse_all))
    coarse = terms[0]
    for term in range(1, TERMS):
        coarse = jnp.where(lane >= term * side, terms[term], coarse)
    a, b = iota((x.fine, x.fine), 0), iota((x.fine, x.fine), 1)
    from_mid = jnp.where((a < x.mid_all) & x.holds_mid(a - 1), weight_of(b - 2 * (a - 1)), 0.0)
    c = a % side
    from_coarse = jnp.where((c < x.coarse_all) & x.holds_coarse(c - 2), weight_of(b - 1 - 2 * (c - 2)), 0.0)
    high, low = split(dot(from_coarse, from_mid))
    widen_x[:own] = high
    widen_x[own : 2 * own] = high
    widen_x[2 * own :] = low
    columns = [(x_fine, 0, 0, fine)]
    columns += [(x_sums, half, 0, [dot(m, from_mid) for m in mid])]
    columns += [(x_sums, half, TERMS * x.fine, [coarse])]
    for out, half, at, terms in columns:
        for term, matrix in enumerate(terms):
            high, low = split(matrix)
            cols = slice(at + term * x.fine, at + (term + 1) * x.fine)
            n = 2 * half
            out[0:own, cols] = high[:own]
            out[own : 2 * own, cols] = high[:own]
            out[2 * own : 3 * own, cols] = low[:own]
            if n:
                out[3 * own :, cols] = jnp.zeros((out.shape[0] - 3 * own, x.fine), BF16)
                out[3 * own : 3 * own + n, cols] = high[own : own + n]
                out[3 * own + n : 3 * own + 2 * n, cols] = high[own : own + n]
                out[3 * own + 128 : 3 * own + 128 + n, cols] = low[own : own + n]

    lower, higher = y.index() > 0, y.index() < y.count - 1
    far_below = s.y2_routes[0].below()
    n = up8(y.mid_all)

    def write(out, size, terms):
        part = iota(terms[0].shape, 1) >= 2 * size
        for term, matrix in enumerate(terms):
            high, low = split(matrix)
            n = matrix.shape[0]
            out[term * n : (term + 1) * n] = jnp.where(part, low.astype(F32), high.astype(F32)).astype(BF16)

    def columns_of(rows, size):
        lane = iota((rows, 3 * size), 1)
        return jnp.where(lane >= 2 * size, lane - 2 * size, jnp.where(lane >= size, lane - size, lane))

    c = columns_of(y.fine, s.fine_rows)
    is_low = (c >= y.fine) & (c < y.fine + RADIUS)
    is_high = c >= y.fine + RADIUS
    where = jnp.where(is_low, c - y.fine - RADIUS, jnp.where(is_high, c - RADIUS, c))
    valid = choose(is_low, lower, choose(is_high, higher, c >= 0))
    write(y_fine, s.fine_rows, band(taps, 0, where - iota(c.shape, 0), valid))
    c = columns_of(y.fine, y.fine)
    write(y_own, y.fine, band(taps, 0, c - iota(c.shape, 0), c >= 0))
    c = columns_of(y.fine, 2 * RADIUS)
    where = jnp.where(c < RADIUS, c - RADIUS, c - RADIUS + y.fine)
    write(y_edge, 2 * RADIUS, band(taps, 0, where - iota(c.shape, 0), choose(c < RADIUS, lower, higher)))

    c = columns_of(n, s.sum_rows)
    r = iota(c.shape, 0)
    is_low = (c >= s.low) & (c < s.low + SPAN)
    is_high = (c >= s.high) & (c < s.high + SPAN)
    is_far = (c >= s.far) & (c < s.far + y.second)
    where = jnp.where(is_low, c - s.low + 2 - SPAN, jnp.where(is_high, c - s.high + y.mid - 1, c - 1))
    valid = choose(is_low, lower, choose(is_high, higher, c < y.mid_all))
    mid = band(taps, 1, where - (r - 1), valid & (r < y.mid_all))
    far = jnp.where(far_below, -2 - y.coarse, 2 * y.coarse - 2)
    where = jnp.where(is_low, c - s.low + 3 - SPAN, jnp.where(is_high, c - s.high + y.coarse - 2, c - 2))
    where = jnp.where(is_far, c - s.far + far, where)
    valid = choose(is_low, lower, choose(is_high, higher, (c < y.coarse_all) | is_far))
    coarse = band(taps, 2, where - (r - 2), valid & (r < y.coarse_all))
    o, k = iota((y.fine, n), 0), iota((y.fine, n), 1)
    from_mid = jnp.where((k < y.mid_all) & y.holds_mid(k - 1), weight_of(o - 2 * (k - 1)), 0.0)
    m = s.coarse_rows
    c = columns_of(n, m)
    k = iota(c.shape, 0)
    from_coarse = jnp.where((c < y.coarse_all) & y.holds_coarse(c - 2), weight_of(k - 1 - 2 * (c - 2)), 0.0)
    write(y_mid, s.sum_rows, [dot(from_mid, matrix) for matrix in mid])
    write(y_coarse, s.sum_rows, [matrix[:m] for matrix in coarse])
    write(widen_y, m, [dot(from_mid, from_coarse)])


def contract_y(s, weights, high, low):
    joined = jnp.concatenate([high, low, high], axis=0)
    result = jnp.dot(weights[...], joined, preferred_element_type=F32)
    n, m = s.y.fine, s.x.fine
    return [result[t * n : (t + 1) * n, t * m : (t + 1) * m] for t in range(TERMS)]


def contract_z(table, level, held, base, count):
    rows = held.shape[2:]
    totals = [None] * count
    for t in range(held.shape[1]):
        for j in range(count + TAPS - 1):
            plane = held[base + j, t].reshape(rows[0] // 8, 8, rows[1])
            for i in range(max(0, j - TAPS + 1), min(count, j + 1)):
                term = table[(level * TERMS + t) * TAPS + j - i][None] * plane
                totals[i] = term if totals[i] is None else totals[i] + term
    return [total.reshape(rows) for total in totals]


def slab_starts(s, below_at, above_at):
    result = []
    for route in s.z_routes:
        lower, i = route.below(), s.z.index()
        valid = choose(lower, i >= 1, i + 1 < s.z.count)
        result.append((jnp.where(lower, below_at, above_at), valid))
    return result


def store_terms(held, at, valid, parts):
    for t, part in enumerate(parts):
        held[at, t] = part if valid is None else jnp.where(valid, part, 0.0)


BLOCK = 4


def fine_places(s):
    places = [(RADIUS + p, None) for p in range(s.z.fine)]
    for start, valid in slab_starts(s, 0, s.z.fine + RADIUS):
        places += [(start + p, valid) for p in range(RADIUS)]
    return places


def contract_x(s, grid, weights):
    high, low = split(grid)
    joined = jnp.concatenate([high, low, high], axis=1)
    return jnp.dot(joined, weights[: 3 * s.x.fine], preferred_element_type=F32)


def own_kernel(s, table, t_part, fine, slab, sums, x_fine, x_sums, y_edge, y_fine, fine_part, sums_part, t_fine):
    z, x = s.z, s.x
    t_fine[...] = t_part[...]
    fine_at = fine_places(s)

    def slab_group(g, count):
        n = s.fine_rows
        planes = jnp.concatenate([slab[g : g + count], fine[z.fine + g : z.fine + g + count]], axis=1)
        a, b = split(contract_x(s, planes.reshape(count * n, x.fine), x_fine))
        for p in range(count):
            rows = slice(p * n, (p + 1) * n)
            store_terms(t_fine, *fine_at[z.fine + g + p], contract_y(s, y_fine, a[rows], b[rows]))

    def fine_group(g, count):
        n = 2 * RADIUS
        a, b = split(contract_x(s, fine[g : g + count].reshape(count * n, x.fine), x_fine))
        for p in range(count):
            rows = slice(p * n, (p + 1) * n)
            at, valid = fine_at[g + p]
            for t, part in enumerate(contract_y(s, y_edge, a[rows], b[rows])):
                t_fine[at, t] = t_fine[at, t] + (part if valid is None else jnp.where(valid, part, 0.0))

    def fine_block(k):
        for i, total in enumerate(contract_z(table, 0, t_fine, k, BLOCK)):
            fine_part[k + i] = total

    def sum_part(g, count):
        n = s.sum_rows
        grid = sums[g : g + count].reshape(count * n, x.fine)
        sums_part[g * n : (g + count) * n] = contract_x(s, grid, x_sums)

    later = []
    done = 0
    for g in range(0, s.fine_planes - z.fine, 8):
        slab_group(g, 8)
    for g in range(0, z.fine, 8):
        fine_group(g, 8)
        while later:
            later.pop(0)()
        if g >= 0:
            ready = g if g + 8 < z.fine else z.fine
            later += [lambda k=k: fine_block(k) for k in range(done, ready, BLOCK)]
            done = max(done, ready)
    starts = list(range(0, s.sum_planes, 8))
    while later or starts:
        if starts:
            sum_part(starts[0], min(8, s.sum_planes - starts[0]))
            starts.pop(0)
        if later:
            later.pop(0)()


def sum_kernel(s, table, fine, sums, first, second, x_sums, ends, y_fine, y_mid, y_coarse, widen_x, widen_y, result, *scratch):
    sums_ends, t_mid, t_coarse, p_mid, p_coarse, narrow, out, left = scratch
    z, y, x = s.z, s.y, s.x
    below = s.x_routes[0].below()
    half = s.edge_sums
    def ends_of(start, rows):
        one, two = first[start : start + rows], second[start : start + rows]
        return jnp.where(below, one, two), jnp.where(below, two, one)

    for b in range(s.sum_blocks):
        if b < s.coarse_blocks:
            pair = ends_of(s.fine_ends + b * half, half)
        else:
            rest = jnp.zeros((half - up8(EDGE), 128), F32)
            pair = ends_of(s.mid_ends + (b - s.coarse_blocks) * up8(EDGE), up8(EDGE))
            pair = [jnp.concatenate([ends, rest], axis=0) for ends in pair]
        rows = jnp.concatenate(pair, axis=0)
        zeros = jnp.zeros((128 - 4 * half, 128), F32)
        sums_ends[b * 128 : (b + 1) * 128] = jnp.concatenate([rows, rows, zeros], axis=0).T

    def along_x(start, rows):
        edge_high, edge_low = split(sums_ends[start : start + rows])
        is_high = iota(edge_high.shape, 1) < 2 * half
        packed = jnp.where(is_high, edge_high.astype(F32), edge_low.astype(F32)).astype(BF16)
        joined = jnp.concatenate([packed, edge_high], axis=1)
        part = jnp.dot(joined, x_sums[3 * x.fine :], preferred_element_type=F32)
        return split(sums[start : start + rows] + part)

    def fine_edges():
        columns = []
        for flip in range(2):
            for g in range(s.fine_groups):
                is_folded = s.folded and g == s.fine_groups - 1
                at = slice(g * s.fine_rows, s.fine_ends if is_folded else (g + 1) * s.fine_rows)
                pair = (first[at], second[at])
                ends_here = jnp.where(below, pair[flip], pair[1 - flip])
                if is_folded:
                    ends_here = jnp.concatenate([ends_here, pltpu.roll(ends_here, x.fine // 2, 1)], axis=0)
                columns.append(ends_here)
        high, low = split(jnp.concatenate(columns, axis=1))
        joined = jnp.concatenate([high, low, high], axis=0)
        high, low = split(jnp.dot(y_fine[...], joined, preferred_element_type=F32))
        width = s.fine_groups * x.fine
        result = []
        for side in range(2):
            total = 0.0
            for t in range(TERMS):
                rows, cols = slice(t * y.fine, (t + 1) * y.fine), slice(side * width, (side + 1) * width)
                a, b = high[rows, cols], low[rows, cols]
                joined = jnp.concatenate([a, b, a], axis=1)
                total = total + jnp.dot(joined, ends[2 * t + side], preferred_element_type=F32)
            result.append(total)
        return result

    t_mid[...] = jnp.zeros(t_mid.shape, F32)
    t_coarse[...] = jnp.zeros(t_coarse.shape, F32)
    mid_at = [(RADIUS + p, None) for p in range(z.mid_all)]
    mid_at, rest_at = mid_at[: z.coarse_all], mid_at[z.coarse_all :]
    coarse_at = [(RADIUS + p, None) for p in range(z.coarse_all)]
    for start, valid in slab_starts(s, 0, z.mid + 3 + RADIUS):
        mid_at += [(start + p, valid) for p in range(RADIUS)]
    mid_at += rest_at
    for start, valid in slab_starts(s, 0, z.coarse + 5 + RADIUS):
        coarse_at += [(start + p, valid) for p in range(RADIUS)]
    coarse_at += [(None, None)] * len(rest_at)
    is_second = iota((s.coarse_rows, x.fine), 1) >= x.fine // TERMS

    def sum_group(g, count):
        n = s.sum_rows
        a, b = along_x(g * n, count * n)
        for p in range(count):
            rows = slice(p * n, (p + 1) * n)
            at, valid = mid_at[g + p]
            cols = slice(0, TERMS * x.fine)
            store_terms(t_mid, at, valid, contract_y(s, y_mid, a[rows, cols], b[rows, cols]))
            at, valid = coarse_at[g + p]
            if at is not None:
                cols = slice(TERMS * x.fine, (TERMS + 1) * x.fine)
                joined = jnp.concatenate([a[rows, cols], b[rows, cols], a[rows, cols]], axis=0)
                both = jnp.dot(y_coarse[...], joined, preferred_element_type=F32)
                m = s.coarse_rows
                store_terms(t_coarse, at, valid, [jnp.where(is_second, both[m:], both[:m])])

    def coarse_block(k):
        count = min(BLOCK, z.coarse_all - k)
        for i, total in enumerate(contract_z(table, 2, t_coarse, k, count)):
            narrow[k + i] = jnp.where(z.holds_coarse(k + i - 2), total, 0.0)

    def widen():
        m = s.coarse_rows
        high, low = split(narrow[...].reshape(z.coarse_all * m, x.fine))
        joined = jnp.concatenate([high, low, high], axis=1)
        high, low = split(jnp.dot(joined, widen_x[...], preferred_element_type=F32))
        for p in range(z.coarse_all):
            rows = slice(p * m, (p + 1) * m)
            joined = jnp.concatenate([high[rows], low[rows], high[rows]], axis=0)
            p_coarse[p] = jnp.dot(widen_y[...], joined, preferred_element_type=F32)

    def mid_block(k):
        count = min(BLOCK, z.mid_all - k)
        for i, total in enumerate(contract_z(table, 1, t_mid, k, count)):
            m = k + i - 1
            for offset, weight in WEIGHTS:
                if (m - offset) % 2 == 0 and 0 <= (m - offset) // 2 + 2 < z.coarse_all:
                    total = total + weight * p_coarse[(m - offset) // 2 + 2]
            p_mid[k + i] = jnp.where(z.holds_mid(m), total, 0.0)

    edges = fine_edges()
    lane = iota((y.fine, x.fine), 1)

    def begin(k):
        block, at = k // s.side, k % s.side * RADIUS
        low, high = (edge[:, block * x.fine : (block + 1) * x.fine] for edge in edges)
        low = pltpu.roll(low, -at % x.fine, 1) if at else low
        turn = (x.fine - RADIUS - at) % x.fine
        high = pltpu.roll(high, turn, 1) if turn else high
        out[k] = fine[k] + jnp.where(lane < RADIUS, low, jnp.where(lane >= x.fine - RADIUS, high, 0.0))

    def finish(k):
        total = out[k]
        for offset, weight in WEIGHTS:
            if (k - offset) % 2 == 0:
                total = total + weight * p_mid[(k - offset) // 2 + 1]
        out[k] = total

    groups = list(range(0, s.sum_planes, 4))
    share = -(-z.fine // len(groups))
    for n, g in enumerate(groups):
        sum_group(g, min(4, s.sum_planes - g))
        for k in range(n * share, min((n + 1) * share, z.fine)):
            begin(k)
    for k in range(0, z.coarse_all, BLOCK):
        coarse_block(k)
    widen()
    done, copies = 0, []
    for k in range(0, z.mid_all, BLOCK):
        mid_block(k)
        ready = z.fine if k + BLOCK >= z.mid_all else 2 * k + 2
        while done < ready:
            finish(done)
            done += 1
            if done % 8 == 0:
                part = pl.ds(done - 8, 8)
                copies.append(pltpu.make_async_copy(out.at[part], result.at[part], left.at[done // 8 - 1]))
                copies[-1].start()
    for copy in copies:
        copy.wait()


def call(kernel, outs, ins, scratch=(), flops=10**7, out_space=pltpu.VMEM):
    specs = [SMEM if a.ndim == 3 and a.shape[-1] == TAPS else VMEM for a in ins]
    size = sum(a.size * a.dtype.itemsize for a in ins) + sum(o.size * o.dtype.itemsize for o in outs)
    return pl.pallas_call(
        kernel,
        out_shape=tuple(outs),
        in_specs=specs,
        out_specs=tuple(pl.BlockSpec(memory_space=out_space) for _ in outs),
        scratch_shapes=list(scratch),
        compiler_params=PARAMS,
        cost_estimate=pl.CostEstimate(flops=flops, bytes_accessed=size, transcendentals=0),
    )(*ins)


def array(*shape, dtype=F32):
    return jax.ShapeDtypeStruct(shape, dtype)


def local(charges, kernel_taps):
    z, y, x = (Cut(name, size) for name, size in zip(("gz", "gy", "gx"), charges.shape))
    s = Sizes(z, y, x)
    n = x.fine
    nz, nz2 = len(s.z_routes), len(s.z2_routes)

    def bound(kernel, *static):
        return lambda *refs: kernel(s, *static, *refs)

    rows = up8(y.mid_all)
    (weights,) = call(bound(narrow_kernel), [array(n, 2 * n, dtype=BF16)], [], flops=10**10)
    held, own, ahead, behind, far, *messages = call(
        bound(restrict_kernel, nz),
        [array(*charges.shape), array(z.mid_all, rows, n)] + [array(s.y_rows, n)] * 2 + [array(s.far_rows, n)] + [array(s.z_rows, n)] * nz + [array(s.z2_rows, n)] * nz2,
        [charges, weights],
        [
            pltpu.VMEM((z.fine, y.fine + 32, n), F32),
            pltpu.VMEM((z.mid_all, rows, n), F32),
            pltpu.VMEM((z.mid_all, up8(y.mid + 24), n), F32),
            pltpu.VMEM((z.mid_all, rows, n), F32),
            pltpu.VMEM((2, max(s.z_rows - s.z_fine, s.y_rows - s.y_fine), n), F32),
            pltpu.VMEM((s.far_groups, s.far_rows, n), F32),
        ],
    )
    z_got = [route(m) for route, m in zip(s.z_routes + s.z2_routes, messages)]
    sides = [s.y_routes[0](ahead), s.y_routes[1](behind)]
    far = s.y2_routes[0](far)
    passed = call(
        bound(pass_kernel, nz),
        [array(RADIUS * s.inner + s.far_rows, n)] * nz + [array(s.far_rows, n)] * nz2,
        [far, held],
        flops=15 * 10**8,
    )
    operators = call(
        bound(operator_kernel),
        [
            array(3 * n, TERMS * n, dtype=BF16),
            array(3 * n + 256, (TERMS + 1) * n, dtype=BF16),
            array(TERMS * y.fine, 3 * y.fine, dtype=BF16),
            array(TERMS * y.fine, 6 * RADIUS, dtype=BF16),
            array(TERMS * y.fine, 3 * s.fine_rows, dtype=BF16),
            array(TERMS * y.fine, 3 * s.sum_rows, dtype=BF16),
            array(TERMS * s.coarse_rows, 3 * s.sum_rows, dtype=BF16),
            array(3 * n, n, dtype=BF16),
            array(y.fine, 3 * s.coarse_rows, dtype=BF16),
        ],
        [kernel_taps],
    )
    later = call(
        bound(later_kernel),
        [array(2 * TERMS, 3 * s.fine_groups * n, z_columns(s), dtype=BF16), array((2 * TERMS + 1) * TAPS, 8, n)],
        [kernel_taps],
    )
    ends, table = later
    ahead, behind = call(
        bound(spread_kernel, nz, nz2),
        [array(s.slab_rows, n), array(s.slab_rows, n)],
        [passed[0], later[1], *z_got],
        [pltpu.VMEM((3, up8(max(s.slab_coarse, s.slab_rows - s.slab_fine)) + 8, n), F32)],
    )
    sides += [s.y_routes[0](ahead), s.y_routes[1](behind)]
    fars = [far] + [route(m) for route, m in zip(s.z_routes + s.z2_routes, passed)]
    x_fine, x_sums, y_own, y_edge, y_fine, y_mid, y_coarse, widen_x, widen_y = operators
    t_part, last, start = call(
        bound(early_kernel),
        [array(z.fine + 2 * RADIUS, TERMS, y.fine, n)] + [array(s.own_groups * y.fine, n)] * 2,
        [held, x_fine, y_own],
    )
    fine, slab, sums, first, second = call(
        bound(collect_kernel, nz, nz2),
        [
            array(s.fine_planes, 2 * RADIUS, n),
            array(nz * RADIUS, y.fine, n),
            array(s.sum_planes, s.sum_rows, n),
            array(s.x_rows, n),
            array(s.x_rows, n),
        ],
        [last, start, own, *z_got, *sides, *fars],
        [
            pltpu.VMEM((s.slab_planes, s.sum_rows, n), F32),
            pltpu.VMEM((1 + nz + nz2, z.coarse_all, 8, n), F32),
            pltpu.VMEM((2, up8(s.slab_coarse) + 8, n), F32),
        ],
    )
    first, second = s.x_routes[0](first), s.x_routes[1](second)
    fine, sums = call(
        bound(own_kernel),
        [array(z.fine, y.fine, n), array(s.sum_planes * s.sum_rows, (TERMS + 1) * n)],
        [table, t_part, fine, slab, sums, x_fine, x_sums, y_edge, y_fine],
        [pltpu.VMEM((z.fine + 2 * RADIUS, TERMS, y.fine, n), F32)],
    )
    (out,) = call(
        bound(sum_kernel),
        [array(z.fine, y.fine, n)],
        [table, fine, sums, first, second, x_sums, ends, y_fine, y_mid, y_coarse, widen_x, widen_y],
        [
            pltpu.VMEM((s.sum_blocks * 128, n), F32),
            pltpu.VMEM((z.mid + 2 * RADIUS + 3, TERMS, y.fine, n), F32),
            pltpu.VMEM((z.coarse + 2 * RADIUS + 5, 1, s.coarse_rows, n), F32),
            pltpu.VMEM((z.mid_all, y.fine, n), F32),
            pltpu.VMEM((z.coarse_all, y.fine, n), F32),
            pltpu.VMEM((z.coarse_all, s.coarse_rows, n), F32),
            pltpu.VMEM((z.fine, y.fine, n), F32),
            pltpu.SemaphoreType.DMA((z.fine // 8,)),
        ],
        out_space=pltpu.HBM,
    )
    return out


def solution(mesh):
    return jax.shard_map(
        local,
        mesh=mesh,
        in_specs=(P("gz", "gy", "gx"), P()),
        out_specs=P("gz", "gy", "gx"),
        check_vma=False,
    )
```

```python
import jax
import jax.numpy as jnp
from jax import lax
from jax.experimental import pallas as pl
from jax.experimental.pallas import tpu as pltpu
from jax.sharding import PartitionSpec as P

RADIUS = 8
TAPS = 17
TERMS = 2
WEIGHTS = ((-3, -0.0625), (-1, 0.5625), (0, 1.0), (1, 0.5625), (3, -0.0625))
EXACT = lax.Precision.HIGHEST
SPAN = RADIUS + 5
EDGE = RADIUS + 3
F32, BF16 = jnp.float32, jnp.bfloat16
PARAMS = pltpu.CompilerParams(vmem_limit_bytes=32 * 1024 * 1024)
VMEM = pl.BlockSpec(memory_space=pltpu.VMEM)
SMEM = pl.BlockSpec(memory_space=pltpu.SMEM)


def up8(n):
    return -(-n // 8) * 8


def iota(shape, dim):
    return lax.broadcasted_iota(jnp.int32, shape, dim)


def weight_of(difference):
    size = jnp.abs(difference)
    out = jnp.where(size == 1, 0.5625, jnp.where(size == 3, -0.0625, 0.0))
    return jnp.where(size == 0, 1.0, out)


def choose(condition, a, b):
    return jnp.where(condition, jnp.where(a, 1, 0), jnp.where(b, 1, 0)) != 0


class Cut:
    def __init__(self, name, length):
        self.name, self.fine = name, length
        self.count = lax.axis_size(name)
        self.mid, self.coarse = length // 2, length // 4
        self.mid_all, self.coarse_all = self.mid + 3, self.coarse + 5
        self.second = max(SPAN - self.coarse, 0)

    def index(self):
        return lax.axis_index(self.name)

    def holds_mid(self, k):
        k = k + self.index() * self.mid
        return (k >= 0) & (k < self.mid * self.count)

    def holds_coarse(self, k):
        k = k + self.index() * self.coarse
        return (k >= 0) & (k < self.coarse * self.count)


class Route:
    def __init__(self, names, pairs, up, below):
        self.names, self.pairs, self.up, self.below = names, pairs, up, below

    def __call__(self, x):
        return lax.ppermute(x, self.names, self.pairs)


def flip(pairs):
    return [(b, a) for a, b in pairs]


def swap(cut, steps):
    pairs = [(i, i + steps) for i in range(cut.count - steps)]

    def up():
        return cut.index() + steps < cut.count

    return [Route(cut.name, pairs + flip(pairs), up, lambda: ~up())]


def both_ways(cut, steps):
    pairs = [(i, i + steps) for i in range(cut.count - steps)]
    yes, no = (lambda: cut.index() >= 0), (lambda: cut.index() < 0)
    return [Route(cut.name, pairs, yes, yes), Route(cut.name, flip(pairs), no, no)]


def folded(cut, beside, names):
    n, m = cut.count, lax.axis_size(beside)

    def place(c, i):
        return c * n + i if names[0] == beside else i * m + c

    pairs = []
    for c in range(0, m, 2):
        cycle = [place(c, i) for i in range(n)] + [place(c + 1, i) for i in reversed(range(n))]
        pairs += list(zip(cycle, cycle[1:] + cycle[:1]))

    def even():
        return lax.axis_index(beside) % 2 == 0

    def odd():
        return lax.axis_index(beside) % 2 == 1

    return [Route(names, pairs, even, even), Route(names, flip(pairs), odd, odd)]


def split(x):
    high = x.astype(BF16)
    return high, (x - high.astype(F32)).astype(BF16)


def pick(selector, x):
    nt = (((1,), (1,)), ((), ()))
    a = x.astype(BF16)
    rest = x - a.astype(F32)
    b = rest.astype(BF16)
    c = (rest - b.astype(F32)).astype(BF16)
    out = lax.dot_general(selector, c, nt, preferred_element_type=F32)
    out = out + lax.dot_general(selector, b, nt, preferred_element_type=F32)
    return out + lax.dot_general(selector, a, nt, preferred_element_type=F32)


class Sizes:
    def place_of(self, p):
        return p if p < self.slab_start else p + self.coarse_planes - self.slab_start

    def __init__(self, z, y, x):
        self.z, self.y, self.x = z, y, x
        self.z_routes = swap(z, 1) if z.count <= 2 else both_ways(z, 1)
        self.z2_routes = [] if z.count <= 2 else swap(z, 2) if z.count <= 4 else both_ways(z, 2)
        self.y_routes = folded(y, x.name, (x.name, y.name))
        self.y2_routes = swap(y, 2)
        self.x_routes = folded(x, z.name, (x.name, z.name))
        self.inner = y.fine - 2 * RADIUS
        self.z_fine = RADIUS * 2 * RADIUS
        self.z_sums = max(EDGE * y.mid_all, SPAN * y.coarse_all)
        self.z_rows = up8(self.z_fine + self.z_sums)
        self.z2_rows = up8(z.second * y.coarse_all)
        self.slab_planes = SPAN * len(self.z_routes) + z.second * len(self.z2_routes)
        self.fine_planes = z.fine + RADIUS * len(self.z_routes)
        self.sum_planes = z.mid_all + RADIUS * len(self.z_routes)
        self.coarse_rows = -(-y.coarse_all // 16) * 16
        self.y_fine = RADIUS * z.fine
        self.y_sums = max(EDGE * z.mid_all, SPAN * z.coarse_all)
        self.y_rows = up8(self.y_fine + self.y_sums)
        self.slab_fine = RADIUS * RADIUS * len(self.z_routes)
        self.slab_mid = EDGE * EDGE * len(self.z_routes)
        self.slab_coarse = SPAN * self.slab_planes
        self.extra = max(self.slab_coarse - self.slab_mid, 0)
        self.spare = x.fine - x.mid_all - x.coarse_all
        self.pieces = -(-x.coarse_all // max(self.spare, 1))
        if self.pieces * self.extra > self.slab_mid:
            self.extra = 0
        self.slab_sums = max(self.slab_mid, self.slab_coarse - self.extra)
        self.slab_rows = up8(self.slab_fine + self.slab_sums)
        self.far_groups = x.fine // x.coarse_all
        self.far_planes = -(-z.coarse_all // self.far_groups)
        self.far_rows = up8(y.second * self.far_planes)
        self.slab_start = z.coarse_all
        self.coarse_planes = z.coarse_all + RADIUS * len(self.z_routes)
        self.fine_rows = y.fine + 2 * RADIUS
        self.far = y.coarse_all
        self.low = y.mid_all
        self.high = self.low + SPAN
        self.sum_rows = -(-(self.high + SPAN) // 16) * 16
        self.edge_sums = EDGE + SPAN
        self.side = x.fine // RADIUS
        self.fine_groups = -(-self.fine_planes // self.side)
        assert z.fine % self.side == 0
        self.own_groups = z.fine // self.side
        self.folded = 0 < self.fine_planes % self.side <= self.side // 2
        self.fine_ends = self.fine_groups * self.fine_rows - (self.fine_rows // 2 if self.folded else 0)
        self.sum_blocks = -(-self.sum_planes * self.sum_rows // 128)
        self.coarse_blocks = -(-self.coarse_planes * self.sum_rows // 128)
        self.mid_ends = self.fine_ends + self.coarse_blocks * self.edge_sums
        self.x_rows = self.mid_ends + (self.sum_blocks - self.coarse_blocks) * up8(EDGE)
        assert x.mid_all + x.coarse_all <= x.fine
        assert self.far + y.second <= self.low and y.second <= 8 and y.coarse_all == SPAN and z.coarse_all == SPAN
        assert z.coarse >= RADIUS and y.coarse >= RADIUS and y.count == 4


def narrow_kernel(s, out):
    x = s.x
    lanes = (x.fine, x.fine)
    cell, lane = iota(lanes, 0), iota(lanes, 1)
    k = lane - 1
    to_mid = jnp.where((lane < x.mid_all) & x.holds_mid(k), weight_of(cell - 2 * k), 0.0)
    c = lane - x.mid_all - 2
    inside = (lane >= x.mid_all) & (lane < x.mid_all + x.coarse_all) & x.holds_coarse(c)
    to_coarse = jnp.where(inside, weight_of(cell - 1 - 2 * c), 0.0)
    narrow = to_mid + jnp.dot(to_mid, to_coarse, precision=EXACT, preferred_element_type=F32)
    out[...] = jnp.concatenate(split(narrow), axis=1)


def restrict_kernel(s, nz, source, narrow, charges, own, ahead, behind, far, *rest):
    messages, (wide, mid, high, coarse, packed, groups) = rest[:-6], rest[-6:]
    z, y, x = s.z, s.y, s.x
    wide[...] = jnp.zeros(wide.shape, F32)
    charges[...] = source[...]
    cells = source[...].reshape(z.fine * y.fine, x.fine)
    top, rest = cells.astype(BF16), cells
    rest = rest - top.astype(F32)
    middle = rest.astype(BF16)
    low = (rest - middle.astype(F32)).astype(BF16)
    weights = narrow[...]
    both = jnp.dot(low, weights, preferred_element_type=F32)
    both = both + jnp.dot(
        jnp.concatenate([top, middle], axis=1), jnp.concatenate([weights, weights], axis=0), preferred_element_type=F32
    )
    reduced = both[:, : x.fine] + both[:, x.fine :]
    wide[:, 8 : 8 + y.fine, :] = reduced.reshape(z.fine, y.fine, x.fine)
    rows = 0.0
    for offset, weight in WEIGHTS:
        rows = rows + weight * wide[:, pl.ds(6 + offset, y.mid_all, stride=2), :]
    keep = y.holds_mid(iota((y.mid_all, x.fine), 0) - 1)
    mid[...] = jnp.zeros(mid.shape, F32)
    coarse[...] = jnp.zeros(coarse.shape, F32)
    high[...] = jnp.zeros(high.shape, F32)
    for p in range(z.mid_all):
        total = 0.0
        for offset, weight in WEIGHTS:
            at = 2 * (p - 1) + offset
            if 0 <= at < z.fine:
                total = total + weight * rows[at]
        total = jnp.where(keep & z.holds_mid(p - 1), total, 0.0)
        mid[p, : y.mid_all] = total
        high[p, 8 : 8 + y.mid_all] = total
    rows = 0.0
    for offset, weight in WEIGHTS:
        rows = rows + weight * high[:, pl.ds(5 + offset, y.coarse_all, stride=2), :]
    keep = y.holds_coarse(iota((y.coarse_all, x.fine), 0) - 2)
    for p in range(z.coarse_all):
        total = 0.0
        for offset, weight in WEIGHTS:
            at = 2 * (p - 2) + offset + 1
            if 0 <= at < z.mid_all:
                total = total + weight * rows[at]
        coarse[p, : y.coarse_all] = jnp.where(keep & z.holds_coarse(p - 2), total, 0.0)
    is_mid = iota(mid.shape[1:], 1) < x.mid_all
    for p in range(z.mid_all):
        own[p] = jnp.where(is_mid, mid[p], coarse[p]) if p < z.coarse_all else jnp.where(is_mid, mid[p], 0.0)
    up = s.y2_routes[0].up()
    count, end = y.second, y.coarse_all
    groups[...] = jnp.zeros(groups.shape, F32)
    for p in range(z.coarse_all):
        g, at = p // s.far_planes, p % s.far_planes * count
        groups[g, at : at + count] = jnp.where(up, own[p, end - count : end], own[p, :count])
    lane = iota(far.shape, 1)
    total = jnp.zeros(far.shape, F32)
    for g in range(s.far_groups):
        first = g * x.coarse_all
        turned = pltpu.roll(groups[g], (first - x.mid_all) % x.fine, 1)
        total = jnp.where((lane >= first) & (lane < first + x.coarse_all), turned, total)
    far[...] = total
    for message, route in zip((ahead, behind), s.y_routes):
        up = route.up()
        edge = jnp.where(up, charges[:, y.fine - RADIUS :, :], charges[:, :RADIUS, :])
        message[: s.y_fine] = edge.reshape(s.y_fine, x.fine)
        packed[...] = jnp.zeros(packed.shape, F32)
        for p in range(z.mid_all):
            packed[0, p * EDGE : (p + 1) * EDGE] = jnp.where(up, mid[p, y.mid_all - EDGE : y.mid_all], mid[p, :EDGE])
        for p in range(z.coarse_all):
            packed[1, p * SPAN : (p + 1) * SPAN] = coarse[p, :SPAN]
        rows = s.y_rows - s.y_fine
        is_mid = iota((rows, x.fine), 1) < x.mid_all
        message[s.y_fine :] = jnp.where(is_mid, packed[0, :rows], packed[1, :rows])
    for message, route in zip(messages, s.z_routes):
        up = route.up().astype(jnp.int32)
        planes = charges[pl.ds(up * (z.fine - RADIUS), RADIUS)]
        outer = jnp.concatenate([planes[:, :RADIUS], planes[:, y.fine - RADIUS :]], axis=1)
        message[: s.z_fine] = outer.reshape(s.z_fine, x.fine)
        packed[...] = jnp.zeros(packed.shape, F32)
        for p in range(EDGE):
            packed[0, p * y.mid_all : (p + 1) * y.mid_all] = mid[up * (z.mid_all - EDGE) + p][: y.mid_all]
        for p in range(SPAN):
            plane = coarse[up * (z.coarse_all - SPAN) + p]
            packed[1, p * y.coarse_all : (p + 1) * y.coarse_all] = plane[: y.coarse_all]
        rows = s.z_rows - s.z_fine
        is_mid = iota((rows, x.fine), 1) < x.mid_all
        message[s.z_fine :] = jnp.where(is_mid, packed[0, :rows], packed[1, :rows])
    for message, route in zip(messages[nz:], s.z2_routes):
        up = route.up().astype(jnp.int32)
        message[...] = jnp.zeros(message.shape, F32)
        for p in range(z.second):
            plane = coarse[up * (z.coarse_all - z.second) + p]
            message[p * y.coarse_all : (p + 1) * y.coarse_all] = plane[: y.coarse_all]


class Slab:
    def __init__(self, message, mid, coarse):
        self.message, self.mid, self.coarse = message, mid, coarse

    def mid_rows(self, first, count):
        return self.message[self.mid + first : self.mid + first + count]

    def coarse_rows(self, first, count):
        return self.message[self.coarse + first : self.coarse + first + count]

    def rows(self, is_mid, first_mid, first_coarse, count):
        coarse = 0.0 if first_coarse is None else self.coarse_rows(first_coarse, count)
        mid = 0.0 if self.mid is None else self.message[self.mid + first_mid : self.mid + first_mid + count]
        return jnp.where(is_mid, mid, coarse)


def slabs(s, z_messages, z2_messages):
    out = []
    for message in z_messages:
        for p in range(SPAN):
            mid = s.z_fine + p * s.y.mid_all if p < EDGE else None
            out.append(Slab(message, mid, s.z_fine + p * s.y.coarse_all))
    for message in z2_messages:
        out += [Slab(message, None, p * s.y.coarse_all) for p in range(s.z.second)]
    return out


def spread_kernel(s, nz, nz2, _, __, *rest):
    z_messages, z2_messages = rest[:nz], rest[nz : nz + nz2]
    ahead, behind, packed = rest[-3:]
    z, y, x = s.z, s.y, s.x
    planes = slabs(s, z_messages, z2_messages)
    count = s.slab_rows - s.slab_fine
    lane = iota((count, x.fine), 1)
    packed[...] = jnp.zeros(packed.shape, F32)
    for p, plane in enumerate(planes):
        packed[1, p * SPAN : (p + 1) * SPAN] = plane.coarse_rows(0, SPAN)
    for n in range(s.pieces if s.extra else 0):
        first = x.mid_all + n * s.spare
        turned = pltpu.roll(packed[1, s.slab_mid : s.slab_mid + up8(s.extra)], x.fine - s.spare - first, 1)
        packed[2, n * s.extra : (n + 1) * s.extra] = turned[: s.extra]
    coarse = jnp.where(lane < x.fine - s.spare, packed[1, :count], packed[2, :count])
    for message, route in zip((ahead, behind), s.y_routes):
        up = route.up()
        at = 0
        for z_message in z_messages:
            slab = z_message[: s.z_fine].reshape(RADIUS, 2 * RADIUS, x.fine)
            edge = jnp.where(up, slab[:, RADIUS:], slab[:, :RADIUS])
            message[at : at + RADIUS * RADIUS] = edge.reshape(RADIUS * RADIUS, x.fine)
            at += RADIUS * RADIUS
        at = 0
        for plane in planes:
            if plane.mid is not None:
                first, last = plane.mid_rows(0, EDGE), plane.mid_rows(y.mid_all - EDGE, EDGE)
                packed[0, at : at + EDGE] = jnp.where(up, last, first)
                at += EDGE
        message[s.slab_fine :] = jnp.where(lane < x.mid_all, packed[0, :count], coarse)


def pass_kernel(s, nz, far, charges, *outs):
    z, x = s.z, s.x
    rows = RADIUS * s.inner
    for out, route in zip(outs, s.z_routes):
        planes = charges[pl.ds(route.up().astype(jnp.int32) * (z.fine - RADIUS), RADIUS)]
        out[:rows] = planes[:, RADIUS : RADIUS + s.inner].reshape(rows, x.fine)
        out[rows:] = far[...]
    for out in outs[nz:]:
        out[...] = far[...]


def roll_ends(s, plane_rows, count, groups):
    x = s.x
    lane = iota((count, x.fine), 1)
    for g in groups:
        ends = [jnp.zeros(lane.shape, F32)] * 2
        for j in range(min(s.side, s.fine_planes - g * s.side)):
            plane = plane_rows(g * s.side + j)
            here = (lane >= RADIUS * j) & (lane < RADIUS * (j + 1))
            for n, start in enumerate((x.fine - RADIUS, 0)):
                shift = (RADIUS * j - start) % x.fine
                ends[n] = jnp.where(here, pltpu.roll(plane, shift, 1) if shift else plane, ends[n])
        yield g, ends


def early_kernel(s, charges, x_fine, y_own, t_part, last, start):
    z, y, x = s.z, s.y, s.x
    t_part[...] = jnp.zeros(t_part.shape, F32)
    for g in range(0, z.fine, 8):
        a, b = split(contract_x(s, charges[g : g + 8].reshape(8 * y.fine, x.fine), x_fine))
        for p in range(8):
            rows = slice(p * y.fine, (p + 1) * y.fine)
            store_terms(t_part, RADIUS + g + p, None, contract_y(s, y_own, a[rows], b[rows]))
    for g, ends in roll_ends(s, lambda p: charges[p], y.fine, range(s.own_groups)):
        rows = slice(g * y.fine, (g + 1) * y.fine)
        last[rows], start[rows] = ends


def collect_kernel(s, nz, nz2, last, start, own, *rest):
    z_messages, z2_messages = rest[:nz], rest[nz : nz + nz2]
    rest = rest[nz + nz2 :]
    pairs = rest[:4]
    fars = rest[4 : 5 + nz + nz2]
    fine, slab, sums, first, second, raw, rows, near = rest[5 + nz + nz2 :]
    z, y, x = s.z, s.y, s.x
    below = s.y_routes[0].below()
    planes = slabs(s, z_messages, z2_messages)

    def sides(which, start, count):
        a, b = (message[start : start + count] for message in pairs[2 * which : 2 * which + 2])
        return jnp.where(below, a, b), jnp.where(below, b, a)

    parts = [(0, z.fine, 0, 0)] + [(z.fine + n * RADIUS, RADIUS, 1, n * RADIUS * RADIUS) for n in range(nz)]
    for at, count, which, row in parts:
        low, high = sides(which, row, RADIUS * count)
        fine[at : at + count, :RADIUS] = low.reshape(count, RADIUS, x.fine)
        fine[at : at + count, RADIUS:] = high.reshape(count, RADIUS, x.fine)
    sums[...] = jnp.zeros(sums.shape, F32)
    raw[...] = jnp.zeros(raw.shape, F32)
    inner_rows = RADIUS * s.inner
    for n, far in enumerate(fars):
        is_joint = 0 < n <= nz
        if is_joint:
            outer = z_messages[n - 1][: s.z_fine].reshape(RADIUS, 2 * RADIUS, x.fine)
            planes_here = slice((n - 1) * RADIUS, n * RADIUS)
            slab[planes_here, :RADIUS] = outer[:, :RADIUS]
            slab[planes_here, RADIUS : RADIUS + s.inner] = far[:inner_rows].reshape(RADIUS, s.inner, x.fine)
            slab[planes_here, RADIUS + s.inner :] = outer[:, RADIUS:]
        two_away = far[inner_rows:] if is_joint else far[...]
        for g in range(s.far_groups):
            turned = pltpu.roll(two_away, (x.mid_all - g * x.coarse_all) % x.fine, 1)
            for p in range(g * s.far_planes, min((g + 1) * s.far_planes, z.coarse_all)):
                at = p % s.far_planes * y.second
                rows[n, p, : y.second] = turned[at : at + y.second]
    is_mid = iota((y.second, x.fine), 1) < x.mid_all

    lane = iota((up8(s.extra), x.fine), 1)
    for side, got in enumerate(sides(1, s.slab_fine, s.slab_sums)):
        near[side, : s.slab_sums] = got
        if s.extra:
            total = jnp.zeros(lane.shape, F32)
            for n in range(s.pieces):
                begin = x.mid_all + n * s.spare
                piece = near[side, n * s.extra : n * s.extra + up8(s.extra)]
                turned = pltpu.roll(piece, begin + s.spare, 1)
                total = jnp.where(lane >= begin, turned, total)
            near[side, s.slab_mid : s.slab_mid + s.extra] = total[: s.extra]
    is_mid_edge = iota((EDGE, x.fine), 1) < x.mid_all
    is_mid_span = iota((SPAN, x.fine), 1) < x.mid_all

    def rows_of_plane(out, p, body, mids, coarses, far_plane):
        out[p, : y.mid_all] = body
        for base, shift, n in ((s.low, SPAN - EDGE, 0), (s.high, 0, 1)):
            if coarses is not None:
                out[p, base : base + SPAN] = jnp.where(is_mid_span, 0.0, coarses[n])
            if mids is not None:
                at = slice(base + shift, base + shift + EDGE)
                out[p, at] = jnp.where(is_mid_edge, mids[n], out[p, at])
        if far_plane is not None:
            at = slice(s.far, s.far + y.second)
            out[p, at] = jnp.where(is_mid, out[p, at], rows[far_plane][: y.second])

    for p in range(z.mid_all):
        far_plane = (0, p) if p < z.coarse_all else None
        mids = sides(0, s.y_fine + p * EDGE, EDGE)
        coarses = sides(0, s.y_fine + p * SPAN, SPAN) if p < z.coarse_all else None
        rows_of_plane(sums, s.place_of(p), own[p, : y.mid_all], mids, coarses, far_plane)
    is_mid_row = iota((SPAN, x.fine), 1) < x.mid_all
    is_mid_rest = iota((y.mid_all - SPAN, x.fine), 1) < x.mid_all
    slab_far = [(1 + n, p) for n in range(nz) for p in range(SPAN)]
    for n, route in enumerate(s.z2_routes):
        at = jnp.where(route.below(), z.coarse_all - z.second, 0)
        slab_far += [(1 + nz + n, at + p) for p in range(z.second)]
    held = 0
    for p, plane in enumerate(planes):
        body = [plane.rows(is_mid_row, 0, 0, SPAN), plane.rows(is_mid_rest, SPAN, None, y.mid_all - SPAN)]
        mids = None
        if plane.mid is not None:
            mids = sides(1, s.slab_fine + held * EDGE, EDGE)
            held += 1
        coarses = [near[side, p * SPAN : (p + 1) * SPAN] for side in range(2)]
        rows_of_plane(raw, p, jnp.concatenate(body, axis=0), mids, coarses, slab_far[p])
    is_mid = iota((s.sum_rows, x.fine), 1) < x.mid_all

    def number(condition, a, b):
        return jnp.where(condition, a, b)

    for n, route in enumerate(s.z_routes):
        lower, base = route.below(), n * SPAN
        for j in range(RADIUS):
            a = raw[base + number(lower, 0, 3) + j]
            b = raw[base + number(lower, SPAN - 5 - RADIUS, 5) + j]
            sums[s.slab_start + n * RADIUS + j] = jnp.where(is_mid, a, b)
        for i in range(3):
            at = number(lower, 0, s.place_of(z.mid)) + i
            sums[at] = sums[at] + jnp.where(is_mid, raw[base + number(lower, EDGE - 3, 0) + i], 0.0)
        for i in range(5):
            at = number(lower, 0, z.coarse) + i
            sums[at] = sums[at] + jnp.where(is_mid, 0.0, raw[base + number(lower, SPAN - 5, 0) + i])
    for n, route in enumerate(s.z2_routes):
        base = len(s.z_routes) * SPAN + n * z.second
        at = s.slab_start + number(route.below(), RADIUS - z.coarse, RADIUS + z.coarse - 5)
        for p in range(z.second):
            sums[at + p] = sums[at + p] + jnp.where(is_mid, 0.0, raw[base + p])

    up = s.x_routes[0].up()
    half, shift = s.fine_rows // 2, x.fine // 2
    is_first_half = iota((half, x.fine), 1) < shift
    own_ends = roll_ends(s, lambda p: fine[p], 2 * RADIUS, range(s.own_groups))
    slab_rows = [jnp.concatenate([slab[p], fine[z.fine + p]], axis=0) for p in range(nz * RADIUS)]
    slab_ends = roll_ends(s, lambda p: slab_rows[p - z.fine], s.fine_rows, range(s.own_groups, s.fine_groups))
    for g, ends in list(own_ends) + list(slab_ends):
        both = ends
        if g < s.own_groups:
            rows = slice(g * y.fine, (g + 1) * y.fine)
            both = [jnp.concatenate([old[rows], new], axis=0) for old, new in zip((last, start), ends)]
        if s.folded and g == s.fine_groups - 1:
            both = [jnp.where(is_first_half, e[:half], pltpu.roll(e[half:], shift, 1)) for e in both]
        at = slice(g * s.fine_rows, g * s.fine_rows + both[0].shape[0])
        first[at] = jnp.where(up, both[0], both[1])
        second[at] = jnp.where(up, both[1], both[0])
    width = EDGE + SPAN
    row, lane = iota((2 * width, x.fine), 0), iota((2 * width, x.fine), 1)
    is_first = row < width
    goes_up = choose(up, is_first, ~is_first)
    slot = jnp.where(is_first, row, row - width)
    from_mid = jnp.where(goes_up, x.mid_all - EDGE + slot, slot)
    from_coarse = slot - EDGE + jnp.where(goes_up, x.mid_all + x.coarse_all - SPAN, x.mid_all)
    wanted = jnp.where(slot < EDGE, from_mid, from_coarse)
    picked_sums = pick((lane == wanted).astype(BF16), sums[...].reshape(s.sum_planes * s.sum_rows, x.fine))
    spare = s.sum_blocks * 128 - picked_sums.shape[1]
    if spare:
        picked_sums = jnp.concatenate([picked_sums, jnp.zeros((2 * width, spare), F32)], axis=1)
    for n, message in enumerate((first, second)):
        rows = picked_sums[n * width : (n + 1) * width]
        for b in range(s.coarse_blocks):
            at = s.fine_ends + b * width
            message[at : at + width] = rows[:, b * 128 : (b + 1) * 128]
        for b in range(s.coarse_blocks, s.sum_blocks):
            at = s.mid_ends + (b - s.coarse_blocks) * up8(EDGE)
            message[at : at + up8(EDGE)] = rows[: up8(EDGE), b * 128 : (b + 1) * 128]


def band(taps, level, offset, valid):
    at = jnp.where(valid, offset + RADIUS, -1)
    out = [jnp.zeros(at.shape, F32) for _ in range(TERMS)]
    for tap in range(TAPS):
        here = at == tap
        out = [jnp.where(here, taps[level, term, tap], total) for term, total in enumerate(out)]
    return out


def dot(a, b):
    return jnp.dot(a, b, precision=EXACT, preferred_element_type=F32)


def z_columns(s):
    return s.z.fine * RADIUS


def lower_x(x):
    return x.index() > 0


def higher_x(x):
    return x.index() < x.count - 1


def later_kernel(s, taps, ends, table):
    y, x = s.y, s.x
    for level in range(2):
        for term in range(TERMS):
            for tap in range(TAPS):
                table[(level * TERMS + term) * TAPS + tap] = jnp.full((8, x.fine), taps[level, term, tap], F32)
    is_second = iota((8, x.fine), 1) >= x.fine // TERMS
    for tap in range(TAPS):
        table[2 * TERMS * TAPS + tap] = jnp.where(is_second, taps[2, 1, tap], taps[2, 0, tap])

    z, slots, wide = s.z, s.side * s.fine_groups, z_columns(s)
    slot, column = iota((slots, wide), 0), iota((slots, wide), 1)
    where, valid = slot, slot < z.fine
    for n, route in enumerate(s.z_routes):
        lower, i, first = route.below(), z.index(), z.fine + n * RADIUS
        here = (slot >= first) & (slot < first + RADIUS)
        where = jnp.where(here, slot - first + jnp.where(lower, -RADIUS, z.fine), where)
        valid = choose(here, choose(lower, i >= 1, i + 1 < z.count), valid)
    planes = band(taps, 0, where - column // RADIUS, valid)
    r, c = iota((RADIUS, wide), 0), iota((RADIUS, wide), 1) % RADIUS
    cells = (slots, RADIUS, wide)
    for side, (offset, valid) in enumerate(((r - c - RADIUS, lower_x(x)), (r - c + RADIUS, higher_x(x)))):
        columns = band(taps, 0, offset, choose(valid, r >= 0, r < 0))
        for term in range(TERMS):
            joint = jnp.broadcast_to(planes[term][:, None, :], cells) * jnp.broadcast_to(columns[term][None], cells)
            high, low = split(joint.reshape(slots * RADIUS, wide))
            at = 2 * term + side
            ends[at, : slots * RADIUS] = high
            ends[at, slots * RADIUS : 2 * slots * RADIUS] = high
            ends[at, 2 * slots * RADIUS :] = low

def operator_kernel(s, taps, x_fine, x_sums, y_own, y_edge, y_fine, y_mid, y_coarse, widen_x, widen_y):
    y, x = s.y, s.x
    own, edge = x.fine, 64
    shape = (own + edge, x.fine)
    row, lane = iota(shape, 0), iota(shape, 1)
    t = row - own
    lower, higher = x.index() > 0, x.index() < x.count - 1
    is_own = row < own

    def place(half, own_place, own_valid, first, count, low_place, high_place):
        is_low = t < half
        r = jnp.where(is_low, t, t - half) - first
        there = (r >= 0) & (r < count) & (t < 2 * half) & choose(is_low, lower, higher)
        valid = choose(is_own, own_valid, there)
        return jnp.where(is_own, own_place, jnp.where(is_low, low_place + r, high_place + r)), valid

    half = s.edge_sums
    cell, column = iota((own, x.fine), 0), iota((own, x.fine), 1)
    fine = band(taps, 0, cell - column, cell >= 0)
    where, valid = place(half, row - 1, row < x.mid_all, 0, EDGE, 2 - EDGE, x.mid - 1)
    mid = band(taps, 1, where - (lane - 1), valid & (lane < x.mid_all))
    first = x.mid_all
    inside = (row >= first) & (row < first + x.coarse_all)
    where, valid = place(half, row - first - 2, inside, EDGE, SPAN, 3 - SPAN, x.coarse - 2)
    side = x.fine // TERMS
    column = lane % side
    terms = band(taps, 2, where - (column - 2), valid & (column < x.coarse_all))
    coarse = terms[0]
    for term in range(1, TERMS):
        coarse = jnp.where(lane >= term * side, terms[term], coarse)
    a, b = iota((x.fine, x.fine), 0), iota((x.fine, x.fine), 1)
    from_mid = jnp.where((a < x.mid_all) & x.holds_mid(a - 1), weight_of(b - 2 * (a - 1)), 0.0)
    c = a % side
    from_coarse = jnp.where((c < x.coarse_all) & x.holds_coarse(c - 2), weight_of(b - 1 - 2 * (c - 2)), 0.0)
    high, low = split(dot(from_coarse, from_mid))
    widen_x[:own] = high
    widen_x[own : 2 * own] = high
    widen_x[2 * own :] = low
    columns = [(x_fine, 0, 0, fine)]
    columns += [(x_sums, half, 0, [dot(m, from_mid) for m in mid])]
    columns += [(x_sums, half, TERMS * x.fine, [coarse])]
    for out, half, at, terms in columns:
        for term, matrix in enumerate(terms):
            high, low = split(matrix)
            cols = slice(at + term * x.fine, at + (term + 1) * x.fine)
            n = 2 * half
            out[0:own, cols] = high[:own]
            out[own : 2 * own, cols] = high[:own]
            out[2 * own : 3 * own, cols] = low[:own]
            if n:
                out[3 * own :, cols] = jnp.zeros((out.shape[0] - 3 * own, x.fine), BF16)
                out[3 * own : 3 * own + n, cols] = high[own : own + n]
                out[3 * own + n : 3 * own + 2 * n, cols] = high[own : own + n]
                out[3 * own + 128 : 3 * own + 128 + n, cols] = low[own : own + n]

    lower, higher = y.index() > 0, y.index() < y.count - 1
    far_below = s.y2_routes[0].below()
    n = up8(y.mid_all)

    def write(out, size, terms):
        part = iota(terms[0].shape, 1) >= 2 * size
        for term, matrix in enumerate(terms):
            high, low = split(matrix)
            n = matrix.shape[0]
            out[term * n : (term + 1) * n] = jnp.where(part, low.astype(F32), high.astype(F32)).astype(BF16)

    def columns_of(rows, size):
        lane = iota((rows, 3 * size), 1)
        return jnp.where(lane >= 2 * size, lane - 2 * size, jnp.where(lane >= size, lane - size, lane))

    c = columns_of(y.fine, s.fine_rows)
    is_low = (c >= y.fine) & (c < y.fine + RADIUS)
    is_high = c >= y.fine + RADIUS
    where = jnp.where(is_low, c - y.fine - RADIUS, jnp.where(is_high, c - RADIUS, c))
    valid = choose(is_low, lower, choose(is_high, higher, c >= 0))
    write(y_fine, s.fine_rows, band(taps, 0, where - iota(c.shape, 0), valid))
    c = columns_of(y.fine, y.fine)
    write(y_own, y.fine, band(taps, 0, c - iota(c.shape, 0), c >= 0))
    c = columns_of(y.fine, 2 * RADIUS)
    where = jnp.where(c < RADIUS, c - RADIUS, c - RADIUS + y.fine)
    write(y_edge, 2 * RADIUS, band(taps, 0, where - iota(c.shape, 0), choose(c < RADIUS, lower, higher)))

    c = columns_of(n, s.sum_rows)
    r = iota(c.shape, 0)
    is_low = (c >= s.low) & (c < s.low + SPAN)
    is_high = (c >= s.high) & (c < s.high + SPAN)
    is_far = (c >= s.far) & (c < s.far + y.second)
    where = jnp.where(is_low, c - s.low + 2 - SPAN, jnp.where(is_high, c - s.high + y.mid - 1, c - 1))
    valid = choose(is_low, lower, choose(is_high, higher, c < y.mid_all))
    mid = band(taps, 1, where - (r - 1), valid & (r < y.mid_all))
    far = jnp.where(far_below, -2 - y.coarse, 2 * y.coarse - 2)
    where = jnp.where(is_low, c - s.low + 3 - SPAN, jnp.where(is_high, c - s.high + y.coarse - 2, c - 2))
    where = jnp.where(is_far, c - s.far + far, where)
    valid = choose(is_low, lower, choose(is_high, higher, (c < y.coarse_all) | is_far))
    coarse = band(taps, 2, where - (r - 2), valid & (r < y.coarse_all))
    o, k = iota((y.fine, n), 0), iota((y.fine, n), 1)
    from_mid = jnp.where((k < y.mid_all) & y.holds_mid(k - 1), weight_of(o - 2 * (k - 1)), 0.0)
    m = s.coarse_rows
    c = columns_of(n, m)
    k = iota(c.shape, 0)
    from_coarse = jnp.where((c < y.coarse_all) & y.holds_coarse(c - 2), weight_of(k - 1 - 2 * (c - 2)), 0.0)
    write(y_mid, s.sum_rows, [dot(from_mid, matrix) for matrix in mid])
    write(y_coarse, s.sum_rows, [matrix[:m] for matrix in coarse])
    write(widen_y, m, [dot(from_mid, from_coarse)])


def contract_y(s, weights, high, low):
    joined = jnp.concatenate([high, low, high], axis=0)
    result = jnp.dot(weights[...], joined, preferred_element_type=F32)
    n, m = s.y.fine, s.x.fine
    return [result[t * n : (t + 1) * n, t * m : (t + 1) * m] for t in range(TERMS)]


def contract_z(table, level, held, base, count):
    rows = held.shape[2:]
    totals = [None] * count
    for t in range(held.shape[1]):
        for j in range(count + TAPS - 1):
            plane = held[base + j, t].reshape(rows[0] // 8, 8, rows[1])
            for i in range(max(0, j - TAPS + 1), min(count, j + 1)):
                term = table[(level * TERMS + t) * TAPS + j - i][None] * plane
                totals[i] = term if totals[i] is None else totals[i] + term
    return [total.reshape(rows) for total in totals]


def slab_starts(s, below_at, above_at):
    result = []
    for route in s.z_routes:
        lower, i = route.below(), s.z.index()
        valid = choose(lower, i >= 1, i + 1 < s.z.count)
        result.append((jnp.where(lower, below_at, above_at), valid))
    return result


def store_terms(held, at, valid, parts):
    for t, part in enumerate(parts):
        held[at, t] = part if valid is None else jnp.where(valid, part, 0.0)


BLOCK = 4


def fine_places(s):
    places = [(RADIUS + p, None) for p in range(s.z.fine)]
    for start, valid in slab_starts(s, 0, s.z.fine + RADIUS):
        places += [(start + p, valid) for p in range(RADIUS)]
    return places


def contract_x(s, grid, weights):
    high, low = split(grid)
    joined = jnp.concatenate([high, low, high], axis=1)
    return jnp.dot(joined, weights[: 3 * s.x.fine], preferred_element_type=F32)


def own_kernel(s, table, t_part, fine, slab, sums, x_fine, x_sums, y_edge, y_fine, fine_part, sums_part, t_fine):
    z, x = s.z, s.x
    t_fine[...] = t_part[...]
    fine_at = fine_places(s)

    def slab_group(g, count):
        n = s.fine_rows
        planes = jnp.concatenate([slab[g : g + count], fine[z.fine + g : z.fine + g + count]], axis=1)
        a, b = split(contract_x(s, planes.reshape(count * n, x.fine), x_fine))
        for p in range(count):
            rows = slice(p * n, (p + 1) * n)
            store_terms(t_fine, *fine_at[z.fine + g + p], contract_y(s, y_fine, a[rows], b[rows]))

    def fine_group(g, count):
        n = 2 * RADIUS
        a, b = split(contract_x(s, fine[g : g + count].reshape(count * n, x.fine), x_fine))
        for p in range(count):
            rows = slice(p * n, (p + 1) * n)
            at, valid = fine_at[g + p]
            for t, part in enumerate(contract_y(s, y_edge, a[rows], b[rows])):
                t_fine[at, t] = t_fine[at, t] + (part if valid is None else jnp.where(valid, part, 0.0))

    def fine_block(k):
        for i, total in enumerate(contract_z(table, 0, t_fine, k, BLOCK)):
            fine_part[k + i] = total

    def sum_part(g, count):
        n = s.sum_rows
        grid = sums[g : g + count].reshape(count * n, x.fine)
        sums_part[g * n : (g + count) * n] = contract_x(s, grid, x_sums)

    later = []
    done = 0
    for g in range(0, s.fine_planes - z.fine, 8):
        slab_group(g, 8)
    for g in range(0, z.fine, 8):
        fine_group(g, 8)
        while later:
            later.pop(0)()
        if g >= 0:
            ready = g if g + 8 < z.fine else z.fine
            later += [lambda k=k: fine_block(k) for k in range(done, ready, BLOCK)]
            done = max(done, ready)
    starts = list(range(0, s.sum_planes, 8))
    while later or starts:
        if starts:
            sum_part(starts[0], min(8, s.sum_planes - starts[0]))
            starts.pop(0)
        if later:
            later.pop(0)()


def sum_kernel(s, table, fine, sums, first, second, x_sums, ends, y_fine, y_mid, y_coarse, widen_x, widen_y, result, *scratch):
    sums_ends, t_mid, t_coarse, p_mid, p_coarse, narrow, out, left = scratch
    z, y, x = s.z, s.y, s.x
    below = s.x_routes[0].below()
    half = s.edge_sums
    def ends_of(start, rows):
        one, two = first[start : start + rows], second[start : start + rows]
        return jnp.where(below, one, two), jnp.where(below, two, one)

    for b in range(s.sum_blocks):
        if b < s.coarse_blocks:
            pair = ends_of(s.fine_ends + b * half, half)
        else:
            rest = jnp.zeros((half - up8(EDGE), 128), F32)
            pair = ends_of(s.mid_ends + (b - s.coarse_blocks) * up8(EDGE), up8(EDGE))
            pair = [jnp.concatenate([ends, rest], axis=0) for ends in pair]
        rows = jnp.concatenate(pair, axis=0)
        zeros = jnp.zeros((128 - 4 * half, 128), F32)
        sums_ends[b * 128 : (b + 1) * 128] = jnp.concatenate([rows, rows, zeros], axis=0).T

    def along_x(start, rows):
        edge_high, edge_low = split(sums_ends[start : start + rows])
        is_high = iota(edge_high.shape, 1) < 2 * half
        packed = jnp.where(is_high, edge_high.astype(F32), edge_low.astype(F32)).astype(BF16)
        joined = jnp.concatenate([packed, edge_high], axis=1)
        part = jnp.dot(joined, x_sums[3 * x.fine :], preferred_element_type=F32)
        return split(sums[start : start + rows] + part)

    def fine_edges():
        columns = []
        for flip in range(2):
            for g in range(s.fine_groups):
                is_folded = s.folded and g == s.fine_groups - 1
                at = slice(g * s.fine_rows, s.fine_ends if is_folded else (g + 1) * s.fine_rows)
                pair = (first[at], second[at])
                ends_here = jnp.where(below, pair[flip], pair[1 - flip])
                if is_folded:
                    ends_here = jnp.concatenate([ends_here, pltpu.roll(ends_here, x.fine // 2, 1)], axis=0)
                columns.append(ends_here)
        high, low = split(jnp.concatenate(columns, axis=1))
        joined = jnp.concatenate([high, low, high], axis=0)
        high, low = split(jnp.dot(y_fine[...], joined, preferred_element_type=F32))
        width = s.fine_groups * x.fine
        result = []
        for side in range(2):
            total = 0.0
            for t in range(TERMS):
                rows, cols = slice(t * y.fine, (t + 1) * y.fine), slice(side * width, (side + 1) * width)
                a, b = high[rows, cols], low[rows, cols]
                joined = jnp.concatenate([a, b, a], axis=1)
                total = total + jnp.dot(joined, ends[2 * t + side], preferred_element_type=F32)
            result.append(total)
        return result

    t_mid[...] = jnp.zeros(t_mid.shape, F32)
    t_coarse[...] = jnp.zeros(t_coarse.shape, F32)
    mid_at = [(RADIUS + p, None) for p in range(z.mid_all)]
    mid_at, rest_at = mid_at[: z.coarse_all], mid_at[z.coarse_all :]
    coarse_at = [(RADIUS + p, None) for p in range(z.coarse_all)]
    for start, valid in slab_starts(s, 0, z.mid + 3 + RADIUS):
        mid_at += [(start + p, valid) for p in range(RADIUS)]
    mid_at += rest_at
    for start, valid in slab_starts(s, 0, z.coarse + 5 + RADIUS):
        coarse_at += [(start + p, valid) for p in range(RADIUS)]
    coarse_at += [(None, None)] * len(rest_at)
    is_second = iota((s.coarse_rows, x.fine), 1) >= x.fine // TERMS

    def sum_group(g, count):
        n = s.sum_rows
        a, b = along_x(g * n, count * n)
        for p in range(count):
            rows = slice(p * n, (p + 1) * n)
            at, valid = mid_at[g + p]
            cols = slice(0, TERMS * x.fine)
            store_terms(t_mid, at, valid, contract_y(s, y_mid, a[rows, cols], b[rows, cols]))
            at, valid = coarse_at[g + p]
            if at is not None:
                cols = slice(TERMS * x.fine, (TERMS + 1) * x.fine)
                joined = jnp.concatenate([a[rows, cols], b[rows, cols], a[rows, cols]], axis=0)
                both = jnp.dot(y_coarse[...], joined, preferred_element_type=F32)
                m = s.coarse_rows
                store_terms(t_coarse, at, valid, [jnp.where(is_second, both[m:], both[:m])])

    def coarse_block(k):
        count = min(BLOCK, z.coarse_all - k)
        for i, total in enumerate(contract_z(table, 2, t_coarse, k, count)):
            narrow[k + i] = jnp.where(z.holds_coarse(k + i - 2), total, 0.0)

    def widen():
        m = s.coarse_rows
        high, low = split(narrow[...].reshape(z.coarse_all * m, x.fine))
        joined = jnp.concatenate([high, low, high], axis=1)
        high, low = split(jnp.dot(joined, widen_x[...], preferred_element_type=F32))
        for p in range(z.coarse_all):
            rows = slice(p * m, (p + 1) * m)
            joined = jnp.concatenate([high[rows], low[rows], high[rows]], axis=0)
            p_coarse[p] = jnp.dot(widen_y[...], joined, preferred_element_type=F32)

    def mid_block(k):
        count = min(BLOCK, z.mid_all - k)
        for i, total in enumerate(contract_z(table, 1, t_mid, k, count)):
            m = k + i - 1
            for offset, weight in WEIGHTS:
                if (m - offset) % 2 == 0 and 0 <= (m - offset) // 2 + 2 < z.coarse_all:
                    total = total + weight * p_coarse[(m - offset) // 2 + 2]
            p_mid[k + i] = jnp.where(z.holds_mid(m), total, 0.0)

    edges = fine_edges()
    lane = iota((y.fine, x.fine), 1)

    def begin(k):
        block, at = k // s.side, k % s.side * RADIUS
        low, high = (edge[:, block * x.fine : (block + 1) * x.fine] for edge in edges)
        low = pltpu.roll(low, -at % x.fine, 1) if at else low
        turn = (x.fine - RADIUS - at) % x.fine
        high = pltpu.roll(high, turn, 1) if turn else high
        out[k] = fine[k] + jnp.where(lane < RADIUS, low, jnp.where(lane >= x.fine - RADIUS, high, 0.0))

    def finish(k):
        total = out[k]
        for offset, weight in WEIGHTS:
            if (k - offset) % 2 == 0:
                total = total + weight * p_mid[(k - offset) // 2 + 1]
        out[k] = total

    groups = list(range(0, s.sum_planes, 14))
    share = -(-z.fine // len(groups))
    for n, g in enumerate(groups):
        sum_group(g, min(14, s.sum_planes - g))
        for k in range(n * share, min((n + 1) * share, z.fine)):
            begin(k)
    for k in range(0, z.coarse_all, BLOCK):
        coarse_block(k)
    widen()
    done, copies = 0, []
    for k in range(0, z.mid_all, BLOCK):
        mid_block(k)
        ready = z.fine if k + BLOCK >= z.mid_all else 2 * k + 2
        while done < ready:
            finish(done)
            done += 1
            if done % 8 == 0:
                part = pl.ds(done - 8, 8)
                copies.append(pltpu.make_async_copy(out.at[part], result.at[part], left.at[done // 8 - 1]))
                copies[-1].start()
    for copy in copies:
        copy.wait()


def call(kernel, outs, ins, scratch=(), flops=10**7, out_space=pltpu.VMEM):
    specs = [SMEM if a.ndim == 3 and a.shape[-1] == TAPS else VMEM for a in ins]
    size = sum(a.size * a.dtype.itemsize for a in ins) + sum(o.size * o.dtype.itemsize for o in outs)
    return pl.pallas_call(
        kernel,
        out_shape=tuple(outs),
        in_specs=specs,
        out_specs=tuple(pl.BlockSpec(memory_space=out_space) for _ in outs),
        scratch_shapes=list(scratch),
        compiler_params=PARAMS,
        cost_estimate=pl.CostEstimate(flops=flops, bytes_accessed=size, transcendentals=0),
    )(*ins)


def array(*shape, dtype=F32):
    return jax.ShapeDtypeStruct(shape, dtype)


def local(charges, kernel_taps):
    z, y, x = (Cut(name, size) for name, size in zip(("gz", "gy", "gx"), charges.shape))
    s = Sizes(z, y, x)
    n = x.fine
    nz, nz2 = len(s.z_routes), len(s.z2_routes)

    def bound(kernel, *static):
        return lambda *refs: kernel(s, *static, *refs)

    rows = up8(y.mid_all)
    (weights,) = call(bound(narrow_kernel), [array(n, 2 * n, dtype=BF16)], [], flops=10**10)
    held, own, ahead, behind, far, *messages = call(
        bound(restrict_kernel, nz),
        [array(*charges.shape), array(z.mid_all, rows, n)] + [array(s.y_rows, n)] * 2 + [array(s.far_rows, n)] + [array(s.z_rows, n)] * nz + [array(s.z2_rows, n)] * nz2,
        [charges, weights],
        [
            pltpu.VMEM((z.fine, y.fine + 32, n), F32),
            pltpu.VMEM((z.mid_all, rows, n), F32),
            pltpu.VMEM((z.mid_all, up8(y.mid + 24), n), F32),
            pltpu.VMEM((z.mid_all, rows, n), F32),
            pltpu.VMEM((2, max(s.z_rows - s.z_fine, s.y_rows - s.y_fine), n), F32),
            pltpu.VMEM((s.far_groups, s.far_rows, n), F32),
        ],
    )
    z_got = [route(m) for route, m in zip(s.z_routes + s.z2_routes, messages)]
    sides = [s.y_routes[0](ahead), s.y_routes[1](behind)]
    far = s.y2_routes[0](far)
    passed = call(
        bound(pass_kernel, nz),
        [array(RADIUS * s.inner + s.far_rows, n)] * nz + [array(s.far_rows, n)] * nz2,
        [far, held],
        flops=15 * 10**8,
    )
    operators = call(
        bound(operator_kernel),
        [
            array(3 * n, TERMS * n, dtype=BF16),
            array(3 * n + 256, (TERMS + 1) * n, dtype=BF16),
            array(TERMS * y.fine, 3 * y.fine, dtype=BF16),
            array(TERMS * y.fine, 6 * RADIUS, dtype=BF16),
            array(TERMS * y.fine, 3 * s.fine_rows, dtype=BF16),
            array(TERMS * y.fine, 3 * s.sum_rows, dtype=BF16),
            array(TERMS * s.coarse_rows, 3 * s.sum_rows, dtype=BF16),
            array(3 * n, n, dtype=BF16),
            array(y.fine, 3 * s.coarse_rows, dtype=BF16),
        ],
        [kernel_taps],
    )
    later = call(
        bound(later_kernel),
        [array(2 * TERMS, 3 * s.fine_groups * n, z_columns(s), dtype=BF16), array((2 * TERMS + 1) * TAPS, 8, n)],
        [kernel_taps],
    )
    ends, table = later
    ahead, behind = call(
        bound(spread_kernel, nz, nz2),
        [array(s.slab_rows, n), array(s.slab_rows, n)],
        [passed[0], later[1], *z_got],
        [pltpu.VMEM((3, up8(max(s.slab_coarse, s.slab_rows - s.slab_fine)) + 8, n), F32)],
    )
    sides += [s.y_routes[0](ahead), s.y_routes[1](behind)]
    fars = [far] + [route(m) for route, m in zip(s.z_routes + s.z2_routes, passed)]
    x_fine, x_sums, y_own, y_edge, y_fine, y_mid, y_coarse, widen_x, widen_y = operators
    t_part, last, start = call(
        bound(early_kernel),
        [array(z.fine + 2 * RADIUS, TERMS, y.fine, n)] + [array(s.own_groups * y.fine, n)] * 2,
        [held, x_fine, y_own],
    )
    fine, slab, sums, first, second = call(
        bound(collect_kernel, nz, nz2),
        [
            array(s.fine_planes, 2 * RADIUS, n),
            array(nz * RADIUS, y.fine, n),
            array(s.sum_planes, s.sum_rows, n),
            array(s.x_rows, n),
            array(s.x_rows, n),
        ],
        [last, start, own, *z_got, *sides, *fars],
        [
            pltpu.VMEM((s.slab_planes, s.sum_rows, n), F32),
            pltpu.VMEM((1 + nz + nz2, z.coarse_all, 8, n), F32),
            pltpu.VMEM((2, up8(s.slab_coarse) + 8, n), F32),
        ],
    )
    first, second = s.x_routes[0](first), s.x_routes[1](second)
    fine, sums = call(
        bound(own_kernel),
        [array(z.fine, y.fine, n), array(s.sum_planes * s.sum_rows, (TERMS + 1) * n)],
        [table, t_part, fine, slab, sums, x_fine, x_sums, y_edge, y_fine],
        [pltpu.VMEM((z.fine + 2 * RADIUS, TERMS, y.fine, n), F32)],
    )
    (out,) = call(
        bound(sum_kernel),
        [array(z.fine, y.fine, n)],
        [table, fine, sums, first, second, x_sums, ends, y_fine, y_mid, y_coarse, widen_x, widen_y],
        [
            pltpu.VMEM((s.sum_blocks * 128, n), F32),
            pltpu.VMEM((z.mid + 2 * RADIUS + 3, TERMS, y.fine, n), F32),
            pltpu.VMEM((z.coarse + 2 * RADIUS + 5, 1, s.coarse_rows, n), F32),
            pltpu.VMEM((z.mid_all, y.fine, n), F32),
            pltpu.VMEM((z.coarse_all, y.fine, n), F32),
            pltpu.VMEM((z.coarse_all, s.coarse_rows, n), F32),
            pltpu.VMEM((z.fine, y.fine, n), F32),
            pltpu.SemaphoreType.DMA((z.fine // 8,)),
        ],
        out_space=pltpu.HBM,
    )
    return out


def solution(mesh):
    return jax.shard_map(
        local,
        mesh=mesh,
        in_specs=(P("gz", "gy", "gx"), P()),
        out_specs=P("gz", "gy", "gx"),
        check_vma=False,
    )
```

```python
import jax
import jax.numpy as jnp
from jax import lax
from jax.experimental import pallas as pl
from jax.experimental.pallas import tpu as pltpu
from jax.sharding import PartitionSpec as P

RADIUS = 8
TAPS = 17
TERMS = 2
WEIGHTS = ((-3, -0.0625), (-1, 0.5625), (0, 1.0), (1, 0.5625), (3, -0.0625))
EXACT = lax.Precision.HIGHEST
SPAN = RADIUS + 5
EDGE = RADIUS + 3
F32, BF16 = jnp.float32, jnp.bfloat16
PARAMS = pltpu.CompilerParams(vmem_limit_bytes=32 * 1024 * 1024)
VMEM = pl.BlockSpec(memory_space=pltpu.VMEM)
SMEM = pl.BlockSpec(memory_space=pltpu.SMEM)


def up8(n):
    return -(-n // 8) * 8


def iota(shape, dim):
    return lax.broadcasted_iota(jnp.int32, shape, dim)


def weight_of(difference):
    size = jnp.abs(difference)
    out = jnp.where(size == 1, 0.5625, jnp.where(size == 3, -0.0625, 0.0))
    return jnp.where(size == 0, 1.0, out)


def choose(condition, a, b):
    return jnp.where(condition, jnp.where(a, 1, 0), jnp.where(b, 1, 0)) != 0


class Cut:
    def __init__(self, name, length):
        self.name, self.fine = name, length
        self.count = lax.axis_size(name)
        self.mid, self.coarse = length // 2, length // 4
        self.mid_all, self.coarse_all = self.mid + 3, self.coarse + 5
        self.second = max(SPAN - self.coarse, 0)

    def index(self):
        return lax.axis_index(self.name)

    def holds_mid(self, k):
        k = k + self.index() * self.mid
        return (k >= 0) & (k < self.mid * self.count)

    def holds_coarse(self, k):
        k = k + self.index() * self.coarse
        return (k >= 0) & (k < self.coarse * self.count)


class Route:
    def __init__(self, names, pairs, up, below):
        self.names, self.pairs, self.up, self.below = names, pairs, up, below

    def __call__(self, x):
        return lax.ppermute(x, self.names, self.pairs)


def flip(pairs):
    return [(b, a) for a, b in pairs]


def swap(cut, steps):
    pairs = [(i, i + steps) for i in range(cut.count - steps)]

    def up():
        return cut.index() + steps < cut.count

    return [Route(cut.name, pairs + flip(pairs), up, lambda: ~up())]


def both_ways(cut, steps):
    pairs = [(i, i + steps) for i in range(cut.count - steps)]
    yes, no = (lambda: cut.index() >= 0), (lambda: cut.index() < 0)
    return [Route(cut.name, pairs, yes, yes), Route(cut.name, flip(pairs), no, no)]


def folded(cut, beside, names):
    n, m = cut.count, lax.axis_size(beside)

    def place(c, i):
        return c * n + i if names[0] == beside else i * m + c

    pairs = []
    for c in range(0, m, 2):
        cycle = [place(c, i) for i in range(n)] + [place(c + 1, i) for i in reversed(range(n))]
        pairs += list(zip(cycle, cycle[1:] + cycle[:1]))

    def even():
        return lax.axis_index(beside) % 2 == 0

    def odd():
        return lax.axis_index(beside) % 2 == 1

    return [Route(names, pairs, even, even), Route(names, flip(pairs), odd, odd)]


def split(x):
    high = x.astype(BF16)
    return high, (x - high.astype(F32)).astype(BF16)


def pick(selector, x):
    nt = (((1,), (1,)), ((), ()))
    a = x.astype(BF16)
    rest = x - a.astype(F32)
    b = rest.astype(BF16)
    c = (rest - b.astype(F32)).astype(BF16)
    out = lax.dot_general(selector, c, nt, preferred_element_type=F32)
    out = out + lax.dot_general(selector, b, nt, preferred_element_type=F32)
    return out + lax.dot_general(selector, a, nt, preferred_element_type=F32)


class Sizes:
    def place_of(self, p):
        return p if p < self.slab_start else p + self.coarse_planes - self.slab_start

    def __init__(self, z, y, x):
        self.z, self.y, self.x = z, y, x
        self.z_routes = swap(z, 1) if z.count <= 2 else both_ways(z, 1)
        self.z2_routes = [] if z.count <= 2 else swap(z, 2) if z.count <= 4 else both_ways(z, 2)
        self.y_routes = folded(y, x.name, (x.name, y.name))
        self.y2_routes = swap(y, 2)
        self.x_routes = folded(x, z.name, (x.name, z.name))
        self.inner = y.fine - 2 * RADIUS
        self.z_fine = RADIUS * 2 * RADIUS
        self.z_sums = max(EDGE * y.mid_all, SPAN * y.coarse_all)
        self.z_rows = up8(self.z_fine + self.z_sums)
        self.z2_rows = up8(z.second * y.coarse_all)
        self.slab_planes = SPAN * len(self.z_routes) + z.second * len(self.z2_routes)
        self.fine_planes = z.fine + RADIUS * len(self.z_routes)
        self.sum_planes = z.mid_all + RADIUS * len(self.z_routes)
        self.coarse_rows = -(-y.coarse_all // 16) * 16
        self.y_fine = RADIUS * z.fine
        self.y_sums = max(EDGE * z.mid_all, SPAN * z.coarse_all)
        self.y_rows = up8(self.y_fine + self.y_sums)
        self.slab_fine = RADIUS * RADIUS * len(self.z_routes)
        self.slab_mid = EDGE * EDGE * len(self.z_routes)
        self.slab_coarse = SPAN * self.slab_planes
        self.extra = max(self.slab_coarse - self.slab_mid, 0)
        self.spare = x.fine - x.mid_all - x.coarse_all
        self.pieces = -(-x.coarse_all // max(self.spare, 1))
        if self.pieces * self.extra > self.slab_mid:
            self.extra = 0
        self.slab_sums = max(self.slab_mid, self.slab_coarse - self.extra)
        self.slab_rows = up8(self.slab_fine + self.slab_sums)
        self.far_groups = x.fine // x.coarse_all
        self.far_planes = -(-z.coarse_all // self.far_groups)
        self.far_rows = up8(y.second * self.far_planes)
        self.slab_start = z.coarse_all
        self.coarse_planes = z.coarse_all + RADIUS * len(self.z_routes)
        self.fine_rows = y.fine + 2 * RADIUS
        self.far = y.coarse_all
        self.low = y.mid_all
        self.high = self.low + SPAN
        self.sum_rows = -(-(self.high + SPAN) // 16) * 16
        self.edge_sums = EDGE + SPAN
        self.side = x.fine // RADIUS
        self.fine_groups = -(-self.fine_planes // self.side)
        assert z.fine % self.side == 0
        self.own_groups = z.fine // self.side
        self.folded = 0 < self.fine_planes % self.side <= self.side // 2
        self.fine_ends = self.fine_groups * self.fine_rows - (self.fine_rows // 2 if self.folded else 0)
        self.sum_blocks = -(-self.sum_planes * self.sum_rows // 128)
        self.coarse_blocks = -(-self.coarse_planes * self.sum_rows // 128)
        self.mid_ends = self.fine_ends + self.coarse_blocks * self.edge_sums
        self.x_rows = self.mid_ends + (self.sum_blocks - self.coarse_blocks) * up8(EDGE)
        assert x.mid_all + x.coarse_all <= x.fine
        assert self.far + y.second <= self.low and y.second <= 8 and y.coarse_all == SPAN and z.coarse_all == SPAN
        assert z.coarse >= RADIUS and y.coarse >= RADIUS and y.count == 4


def narrow_kernel(s, out):
    x = s.x
    lanes = (x.fine, x.fine)
    cell, lane = iota(lanes, 0), iota(lanes, 1)
    k = lane - 1
    to_mid = jnp.where((lane < x.mid_all) & x.holds_mid(k), weight_of(cell - 2 * k), 0.0)
    c = lane - x.mid_all - 2
    inside = (lane >= x.mid_all) & (lane < x.mid_all + x.coarse_all) & x.holds_coarse(c)
    to_coarse = jnp.where(inside, weight_of(cell - 1 - 2 * c), 0.0)
    narrow = to_mid + jnp.dot(to_mid, to_coarse, precision=EXACT, preferred_element_type=F32)
    out[...] = jnp.concatenate(split(narrow), axis=1)


def restrict_kernel(s, nz, source, narrow, charges, own, ahead, behind, far, *rest):
    messages, (wide, mid, high, coarse, packed, groups) = rest[:-6], rest[-6:]
    z, y, x = s.z, s.y, s.x
    wide[...] = jnp.zeros(wide.shape, F32)
    charges[...] = source[...]
    cells = source[...].reshape(z.fine * y.fine, x.fine)
    top, rest = cells.astype(BF16), cells
    rest = rest - top.astype(F32)
    middle = rest.astype(BF16)
    low = (rest - middle.astype(F32)).astype(BF16)
    weights = narrow[...]
    both = jnp.dot(low, weights, preferred_element_type=F32)
    both = both + jnp.dot(
        jnp.concatenate([top, middle], axis=1), jnp.concatenate([weights, weights], axis=0), preferred_element_type=F32
    )
    reduced = both[:, : x.fine] + both[:, x.fine :]
    wide[:, 8 : 8 + y.fine, :] = reduced.reshape(z.fine, y.fine, x.fine)
    rows = 0.0
    for offset, weight in WEIGHTS:
        rows = rows + weight * wide[:, pl.ds(6 + offset, y.mid_all, stride=2), :]
    keep = y.holds_mid(iota((y.mid_all, x.fine), 0) - 1)
    mid[...] = jnp.zeros(mid.shape, F32)
    coarse[...] = jnp.zeros(coarse.shape, F32)
    high[...] = jnp.zeros(high.shape, F32)
    for p in range(z.mid_all):
        total = 0.0
        for offset, weight in WEIGHTS:
            at = 2 * (p - 1) + offset
            if 0 <= at < z.fine:
                total = total + weight * rows[at]
        total = jnp.where(keep & z.holds_mid(p - 1), total, 0.0)
        mid[p, : y.mid_all] = total
        high[p, 8 : 8 + y.mid_all] = total
    rows = 0.0
    for offset, weight in WEIGHTS:
        rows = rows + weight * high[:, pl.ds(5 + offset, y.coarse_all, stride=2), :]
    keep = y.holds_coarse(iota((y.coarse_all, x.fine), 0) - 2)
    for p in range(z.coarse_all):
        total = 0.0
        for offset, weight in WEIGHTS:
            at = 2 * (p - 2) + offset + 1
            if 0 <= at < z.mid_all:
                total = total + weight * rows[at]
        coarse[p, : y.coarse_all] = jnp.where(keep & z.holds_coarse(p - 2), total, 0.0)
    is_mid = iota(mid.shape[1:], 1) < x.mid_all
    for p in range(z.mid_all):
        own[p] = jnp.where(is_mid, mid[p], coarse[p]) if p < z.coarse_all else jnp.where(is_mid, mid[p], 0.0)
    up = s.y2_routes[0].up()
    count, end = y.second, y.coarse_all
    groups[...] = jnp.zeros(groups.shape, F32)
    for p in range(z.coarse_all):
        g, at = p // s.far_planes, p % s.far_planes * count
        groups[g, at : at + count] = jnp.where(up, own[p, end - count : end], own[p, :count])
    lane = iota(far.shape, 1)
    total = jnp.zeros(far.shape, F32)
    for g in range(s.far_groups):
        first = g * x.coarse_all
        turned = pltpu.roll(groups[g], (first - x.mid_all) % x.fine, 1)
        total = jnp.where((lane >= first) & (lane < first + x.coarse_all), turned, total)
    far[...] = total
    for message, route in zip((ahead, behind), s.y_routes):
        up = route.up()
        edge = jnp.where(up, charges[:, y.fine - RADIUS :, :], charges[:, :RADIUS, :])
        message[: s.y_fine] = edge.reshape(s.y_fine, x.fine)
        packed[...] = jnp.zeros(packed.shape, F32)
        for p in range(z.mid_all):
            packed[0, p * EDGE : (p + 1) * EDGE] = jnp.where(up, mid[p, y.mid_all - EDGE : y.mid_all], mid[p, :EDGE])
        for p in range(z.coarse_all):
            packed[1, p * SPAN : (p + 1) * SPAN] = coarse[p, :SPAN]
        rows = s.y_rows - s.y_fine
        is_mid = iota((rows, x.fine), 1) < x.mid_all
        message[s.y_fine :] = jnp.where(is_mid, packed[0, :rows], packed[1, :rows])
    for message, route in zip(messages, s.z_routes):
        up = route.up().astype(jnp.int32)
        planes = charges[pl.ds(up * (z.fine - RADIUS), RADIUS)]
        outer = jnp.concatenate([planes[:, :RADIUS], planes[:, y.fine - RADIUS :]], axis=1)
        message[: s.z_fine] = outer.reshape(s.z_fine, x.fine)
        packed[...] = jnp.zeros(packed.shape, F32)
        for p in range(EDGE):
            packed[0, p * y.mid_all : (p + 1) * y.mid_all] = mid[up * (z.mid_all - EDGE) + p][: y.mid_all]
        for p in range(SPAN):
            plane = coarse[up * (z.coarse_all - SPAN) + p]
            packed[1, p * y.coarse_all : (p + 1) * y.coarse_all] = plane[: y.coarse_all]
        rows = s.z_rows - s.z_fine
        is_mid = iota((rows, x.fine), 1) < x.mid_all
        message[s.z_fine :] = jnp.where(is_mid, packed[0, :rows], packed[1, :rows])
    for message, route in zip(messages[nz:], s.z2_routes):
        up = route.up().astype(jnp.int32)
        message[...] = jnp.zeros(message.shape, F32)
        for p in range(z.second):
            plane = coarse[up * (z.coarse_all - z.second) + p]
            message[p * y.coarse_all : (p + 1) * y.coarse_all] = plane[: y.coarse_all]


class Slab:
    def __init__(self, message, mid, coarse):
        self.message, self.mid, self.coarse = message, mid, coarse

    def mid_rows(self, first, count):
        return self.message[self.mid + first : self.mid + first + count]

    def coarse_rows(self, first, count):
        return self.message[self.coarse + first : self.coarse + first + count]

    def rows(self, is_mid, first_mid, first_coarse, count):
        coarse = 0.0 if first_coarse is None else self.coarse_rows(first_coarse, count)
        mid = 0.0 if self.mid is None else self.message[self.mid + first_mid : self.mid + first_mid + count]
        return jnp.where(is_mid, mid, coarse)


def slabs(s, z_messages, z2_messages):
    out = []
    for message in z_messages:
        for p in range(SPAN):
            mid = s.z_fine + p * s.y.mid_all if p < EDGE else None
            out.append(Slab(message, mid, s.z_fine + p * s.y.coarse_all))
    for message in z2_messages:
        out += [Slab(message, None, p * s.y.coarse_all) for p in range(s.z.second)]
    return out


def spread_kernel(s, nz, nz2, _, *rest):
    z_messages, z2_messages = rest[:nz], rest[nz : nz + nz2]
    ahead, behind, packed = rest[-3:]
    z, y, x = s.z, s.y, s.x
    planes = slabs(s, z_messages, z2_messages)
    count = s.slab_rows - s.slab_fine
    lane = iota((count, x.fine), 1)
    packed[...] = jnp.zeros(packed.shape, F32)
    for p, plane in enumerate(planes):
        packed[1, p * SPAN : (p + 1) * SPAN] = plane.coarse_rows(0, SPAN)
    for n in range(s.pieces if s.extra else 0):
        first = x.mid_all + n * s.spare
        turned = pltpu.roll(packed[1, s.slab_mid : s.slab_mid + up8(s.extra)], x.fine - s.spare - first, 1)
        packed[2, n * s.extra : (n + 1) * s.extra] = turned[: s.extra]
    coarse = jnp.where(lane < x.fine - s.spare, packed[1, :count], packed[2, :count])
    for message, route in zip((ahead, behind), s.y_routes):
        up = route.up()
        at = 0
        for z_message in z_messages:
            slab = z_message[: s.z_fine].reshape(RADIUS, 2 * RADIUS, x.fine)
            edge = jnp.where(up, slab[:, RADIUS:], slab[:, :RADIUS])
            message[at : at + RADIUS * RADIUS] = edge.reshape(RADIUS * RADIUS, x.fine)
            at += RADIUS * RADIUS
        at = 0
        for plane in planes:
            if plane.mid is not None:
                first, last = plane.mid_rows(0, EDGE), plane.mid_rows(y.mid_all - EDGE, EDGE)
                packed[0, at : at + EDGE] = jnp.where(up, last, first)
                at += EDGE
        message[s.slab_fine :] = jnp.where(lane < x.mid_all, packed[0, :count], coarse)


def pass_kernel(s, nz, far, charges, *outs):
    z, x = s.z, s.x
    rows = RADIUS * s.inner
    for out, route in zip(outs, s.z_routes):
        planes = charges[pl.ds(route.up().astype(jnp.int32) * (z.fine - RADIUS), RADIUS)]
        out[:rows] = planes[:, RADIUS : RADIUS + s.inner].reshape(rows, x.fine)
        out[rows:] = far[...]
    for out in outs[nz:]:
        out[...] = far[...]


def roll_ends(s, plane_rows, count, groups):
    x = s.x
    lane = iota((count, x.fine), 1)
    for g in groups:
        ends = [jnp.zeros(lane.shape, F32)] * 2
        for j in range(min(s.side, s.fine_planes - g * s.side)):
            plane = plane_rows(g * s.side + j)
            here = (lane >= RADIUS * j) & (lane < RADIUS * (j + 1))
            for n, start in enumerate((x.fine - RADIUS, 0)):
                shift = (RADIUS * j - start) % x.fine
                ends[n] = jnp.where(here, pltpu.roll(plane, shift, 1) if shift else plane, ends[n])
        yield g, ends


def early_kernel(s, charges, x_fine, y_own, _, t_part, last, start):
    z, y, x = s.z, s.y, s.x
    t_part[...] = jnp.zeros(t_part.shape, F32)
    for g in range(0, z.fine, 8):
        a, b = split(contract_x(s, charges[g : g + 8].reshape(8 * y.fine, x.fine), x_fine))
        for p in range(8):
            rows = slice(p * y.fine, (p + 1) * y.fine)
            store_terms(t_part, RADIUS + g + p, None, contract_y(s, y_own, a[rows], b[rows]))
    for g, ends in roll_ends(s, lambda p: charges[p], y.fine, range(s.own_groups)):
        rows = slice(g * y.fine, (g + 1) * y.fine)
        last[rows], start[rows] = ends


def collect_kernel(s, nz, nz2, last, start, own, *rest):
    z_messages, z2_messages = rest[:nz], rest[nz : nz + nz2]
    rest = rest[nz + nz2 :]
    pairs = rest[:4]
    fars = rest[4 : 5 + nz + nz2]
    fine, slab, sums, first, second, raw, rows, near = rest[5 + nz + nz2 :]
    z, y, x = s.z, s.y, s.x
    below = s.y_routes[0].below()
    planes = slabs(s, z_messages, z2_messages)

    def sides(which, start, count):
        a, b = (message[start : start + count] for message in pairs[2 * which : 2 * which + 2])
        return jnp.where(below, a, b), jnp.where(below, b, a)

    parts = [(0, z.fine, 0, 0)] + [(z.fine + n * RADIUS, RADIUS, 1, n * RADIUS * RADIUS) for n in range(nz)]
    for at, count, which, row in parts:
        low, high = sides(which, row, RADIUS * count)
        fine[at : at + count, :RADIUS] = low.reshape(count, RADIUS, x.fine)
        fine[at : at + count, RADIUS:] = high.reshape(count, RADIUS, x.fine)
    sums[...] = jnp.zeros(sums.shape, F32)
    raw[...] = jnp.zeros(raw.shape, F32)
    inner_rows = RADIUS * s.inner
    for n, far in enumerate(fars):
        is_joint = 0 < n <= nz
        if is_joint:
            outer = z_messages[n - 1][: s.z_fine].reshape(RADIUS, 2 * RADIUS, x.fine)
            planes_here = slice((n - 1) * RADIUS, n * RADIUS)
            slab[planes_here, :RADIUS] = outer[:, :RADIUS]
            slab[planes_here, RADIUS : RADIUS + s.inner] = far[:inner_rows].reshape(RADIUS, s.inner, x.fine)
            slab[planes_here, RADIUS + s.inner :] = outer[:, RADIUS:]
        two_away = far[inner_rows:] if is_joint else far[...]
        for g in range(s.far_groups):
            turned = pltpu.roll(two_away, (x.mid_all - g * x.coarse_all) % x.fine, 1)
            for p in range(g * s.far_planes, min((g + 1) * s.far_planes, z.coarse_all)):
                at = p % s.far_planes * y.second
                rows[n, p, : y.second] = turned[at : at + y.second]
    is_mid = iota((y.second, x.fine), 1) < x.mid_all

    lane = iota((up8(s.extra), x.fine), 1)
    for side, got in enumerate(sides(1, s.slab_fine, s.slab_sums)):
        near[side, : s.slab_sums] = got
        if s.extra:
            total = jnp.zeros(lane.shape, F32)
            for n in range(s.pieces):
                begin = x.mid_all + n * s.spare
                piece = near[side, n * s.extra : n * s.extra + up8(s.extra)]
                turned = pltpu.roll(piece, begin + s.spare, 1)
                total = jnp.where(lane >= begin, turned, total)
            near[side, s.slab_mid : s.slab_mid + s.extra] = total[: s.extra]
    is_mid_edge = iota((EDGE, x.fine), 1) < x.mid_all
    is_mid_span = iota((SPAN, x.fine), 1) < x.mid_all

    def rows_of_plane(out, p, body, mids, coarses, far_plane):
        out[p, : y.mid_all] = body
        for base, shift, n in ((s.low, SPAN - EDGE, 0), (s.high, 0, 1)):
            if coarses is not None:
                out[p, base : base + SPAN] = jnp.where(is_mid_span, 0.0, coarses[n])
            if mids is not None:
                at = slice(base + shift, base + shift + EDGE)
                out[p, at] = jnp.where(is_mid_edge, mids[n], out[p, at])
        if far_plane is not None:
            at = slice(s.far, s.far + y.second)
            out[p, at] = jnp.where(is_mid, out[p, at], rows[far_plane][: y.second])

    for p in range(z.mid_all):
        far_plane = (0, p) if p < z.coarse_all else None
        mids = sides(0, s.y_fine + p * EDGE, EDGE)
        coarses = sides(0, s.y_fine + p * SPAN, SPAN) if p < z.coarse_all else None
        rows_of_plane(sums, s.place_of(p), own[p, : y.mid_all], mids, coarses, far_plane)
    is_mid_row = iota((SPAN, x.fine), 1) < x.mid_all
    is_mid_rest = iota((y.mid_all - SPAN, x.fine), 1) < x.mid_all
    slab_far = [(1 + n, p) for n in range(nz) for p in range(SPAN)]
    for n, route in enumerate(s.z2_routes):
        at = jnp.where(route.below(), z.coarse_all - z.second, 0)
        slab_far += [(1 + nz + n, at + p) for p in range(z.second)]
    held = 0
    for p, plane in enumerate(planes):
        body = [plane.rows(is_mid_row, 0, 0, SPAN), plane.rows(is_mid_rest, SPAN, None, y.mid_all - SPAN)]
        mids = None
        if plane.mid is not None:
            mids = sides(1, s.slab_fine + held * EDGE, EDGE)
            held += 1
        coarses = [near[side, p * SPAN : (p + 1) * SPAN] for side in range(2)]
        rows_of_plane(raw, p, jnp.concatenate(body, axis=0), mids, coarses, slab_far[p])
    is_mid = iota((s.sum_rows, x.fine), 1) < x.mid_all

    def number(condition, a, b):
        return jnp.where(condition, a, b)

    for n, route in enumerate(s.z_routes):
        lower, base = route.below(), n * SPAN
        for j in range(RADIUS):
            a = raw[base + number(lower, 0, 3) + j]
            b = raw[base + number(lower, SPAN - 5 - RADIUS, 5) + j]
            sums[s.slab_start + n * RADIUS + j] = jnp.where(is_mid, a, b)
        for i in range(3):
            at = number(lower, 0, s.place_of(z.mid)) + i
            sums[at] = sums[at] + jnp.where(is_mid, raw[base + number(lower, EDGE - 3, 0) + i], 0.0)
        for i in range(5):
            at = number(lower, 0, z.coarse) + i
            sums[at] = sums[at] + jnp.where(is_mid, 0.0, raw[base + number(lower, SPAN - 5, 0) + i])
    for n, route in enumerate(s.z2_routes):
        base = len(s.z_routes) * SPAN + n * z.second
        at = s.slab_start + number(route.below(), RADIUS - z.coarse, RADIUS + z.coarse - 5)
        for p in range(z.second):
            sums[at + p] = sums[at + p] + jnp.where(is_mid, 0.0, raw[base + p])

    up = s.x_routes[0].up()
    half, shift = s.fine_rows // 2, x.fine // 2
    is_first_half = iota((half, x.fine), 1) < shift
    own_ends = roll_ends(s, lambda p: fine[p], 2 * RADIUS, range(s.own_groups))
    slab_rows = [jnp.concatenate([slab[p], fine[z.fine + p]], axis=0) for p in range(nz * RADIUS)]
    slab_ends = roll_ends(s, lambda p: slab_rows[p - z.fine], s.fine_rows, range(s.own_groups, s.fine_groups))
    for g, ends in list(own_ends) + list(slab_ends):
        both = ends
        if g < s.own_groups:
            rows = slice(g * y.fine, (g + 1) * y.fine)
            both = [jnp.concatenate([old[rows], new], axis=0) for old, new in zip((last, start), ends)]
        if s.folded and g == s.fine_groups - 1:
            both = [jnp.where(is_first_half, e[:half], pltpu.roll(e[half:], shift, 1)) for e in both]
        at = slice(g * s.fine_rows, g * s.fine_rows + both[0].shape[0])
        first[at] = jnp.where(up, both[0], both[1])
        second[at] = jnp.where(up, both[1], both[0])
    width = EDGE + SPAN
    row, lane = iota((2 * width, x.fine), 0), iota((2 * width, x.fine), 1)
    is_first = row < width
    goes_up = choose(up, is_first, ~is_first)
    slot = jnp.where(is_first, row, row - width)
    from_mid = jnp.where(goes_up, x.mid_all - EDGE + slot, slot)
    from_coarse = slot - EDGE + jnp.where(goes_up, x.mid_all + x.coarse_all - SPAN, x.mid_all)
    wanted = jnp.where(slot < EDGE, from_mid, from_coarse)
    picked_sums = pick((lane == wanted).astype(BF16), sums[...].reshape(s.sum_planes * s.sum_rows, x.fine))
    spare = s.sum_blocks * 128 - picked_sums.shape[1]
    if spare:
        picked_sums = jnp.concatenate([picked_sums, jnp.zeros((2 * width, spare), F32)], axis=1)
    for n, message in enumerate((first, second)):
        rows = picked_sums[n * width : (n + 1) * width]
        for b in range(s.coarse_blocks):
            at = s.fine_ends + b * width
            message[at : at + width] = rows[:, b * 128 : (b + 1) * 128]
        for b in range(s.coarse_blocks, s.sum_blocks):
            at = s.mid_ends + (b - s.coarse_blocks) * up8(EDGE)
            message[at : at + up8(EDGE)] = rows[: up8(EDGE), b * 128 : (b + 1) * 128]


def band(taps, level, offset, valid):
    at = jnp.where(valid, offset + RADIUS, -1)
    out = [jnp.zeros(at.shape, F32) for _ in range(TERMS)]
    for tap in range(TAPS):
        here = at == tap
        out = [jnp.where(here, taps[level, term, tap], total) for term, total in enumerate(out)]
    return out


def dot(a, b):
    return jnp.dot(a, b, precision=EXACT, preferred_element_type=F32)


def z_columns(s):
    return s.z.fine * RADIUS


def lower_x(x):
    return x.index() > 0


def higher_x(x):
    return x.index() < x.count - 1


def later_kernel(s, taps, ends, table):
    y, x = s.y, s.x
    for level in range(2):
        for term in range(TERMS):
            for tap in range(TAPS):
                table[(level * TERMS + term) * TAPS + tap] = jnp.full((8, x.fine), taps[level, term, tap], F32)
    is_second = iota((8, x.fine), 1) >= x.fine // TERMS
    for tap in range(TAPS):
        table[2 * TERMS * TAPS + tap] = jnp.where(is_second, taps[2, 1, tap], taps[2, 0, tap])

    z, slots, wide = s.z, s.side * s.fine_groups, z_columns(s)
    slot, column = iota((slots, wide), 0), iota((slots, wide), 1)
    where, valid = slot, slot < z.fine
    for n, route in enumerate(s.z_routes):
        lower, i, first = route.below(), z.index(), z.fine + n * RADIUS
        here = (slot >= first) & (slot < first + RADIUS)
        where = jnp.where(here, slot - first + jnp.where(lower, -RADIUS, z.fine), where)
        valid = choose(here, choose(lower, i >= 1, i + 1 < z.count), valid)
    planes = band(taps, 0, where - column // RADIUS, valid)
    r, c = iota((RADIUS, wide), 0), iota((RADIUS, wide), 1) % RADIUS
    cells = (slots, RADIUS, wide)
    for side, (offset, valid) in enumerate(((r - c - RADIUS, lower_x(x)), (r - c + RADIUS, higher_x(x)))):
        columns = band(taps, 0, offset, choose(valid, r >= 0, r < 0))
        for term in range(TERMS):
            joint = jnp.broadcast_to(planes[term][:, None, :], cells) * jnp.broadcast_to(columns[term][None], cells)
            high, low = split(joint.reshape(slots * RADIUS, wide))
            at = 2 * term + side
            ends[at, : slots * RADIUS] = high
            ends[at, slots * RADIUS : 2 * slots * RADIUS] = high
            ends[at, 2 * slots * RADIUS :] = low

def operator_kernel(s, taps, x_fine, x_sums, y_own, y_edge, y_fine, y_mid, y_coarse, widen_x, widen_y):
    y, x = s.y, s.x
    own, edge = x.fine, 64
    shape = (own + edge, x.fine)
    row, lane = iota(shape, 0), iota(shape, 1)
    t = row - own
    lower, higher = x.index() > 0, x.index() < x.count - 1
    is_own = row < own

    def place(half, own_place, own_valid, first, count, low_place, high_place):
        is_low = t < half
        r = jnp.where(is_low, t, t - half) - first
        there = (r >= 0) & (r < count) & (t < 2 * half) & choose(is_low, lower, higher)
        valid = choose(is_own, own_valid, there)
        return jnp.where(is_own, own_place, jnp.where(is_low, low_place + r, high_place + r)), valid

    half = s.edge_sums
    cell, column = iota((own, x.fine), 0), iota((own, x.fine), 1)
    fine = band(taps, 0, cell - column, cell >= 0)
    where, valid = place(half, row - 1, row < x.mid_all, 0, EDGE, 2 - EDGE, x.mid - 1)
    mid = band(taps, 1, where - (lane - 1), valid & (lane < x.mid_all))
    first = x.mid_all
    inside = (row >= first) & (row < first + x.coarse_all)
    where, valid = place(half, row - first - 2, inside, EDGE, SPAN, 3 - SPAN, x.coarse - 2)
    side = x.fine // TERMS
    column = lane % side
    terms = band(taps, 2, where - (column - 2), valid & (column < x.coarse_all))
    coarse = terms[0]
    for term in range(1, TERMS):
        coarse = jnp.where(lane >= term * side, terms[term], coarse)
    a, b = iota((x.fine, x.fine), 0), iota((x.fine, x.fine), 1)
    from_mid = jnp.where((a < x.mid_all) & x.holds_mid(a - 1), weight_of(b - 2 * (a - 1)), 0.0)
    c = a % side
    from_coarse = jnp.where((c < x.coarse_all) & x.holds_coarse(c - 2), weight_of(b - 1 - 2 * (c - 2)), 0.0)
    high, low = split(dot(from_coarse, from_mid))
    widen_x[:own] = high
    widen_x[own : 2 * own] = high
    widen_x[2 * own :] = low
    columns = [(x_fine, 0, 0, fine)]
    columns += [(x_sums, half, 0, [dot(m, from_mid) for m in mid])]
    columns += [(x_sums, half, TERMS * x.fine, [coarse])]
    for out, half, at, terms in columns:
        for term, matrix in enumerate(terms):
            high, low = split(matrix)
            cols = slice(at + term * x.fine, at + (term + 1) * x.fine)
            n = 2 * half
            out[0:own, cols] = high[:own]
            out[own : 2 * own, cols] = high[:own]
            out[2 * own : 3 * own, cols] = low[:own]
            if n:
                out[3 * own :, cols] = jnp.zeros((out.shape[0] - 3 * own, x.fine), BF16)
                out[3 * own : 3 * own + n, cols] = high[own : own + n]
                out[3 * own + n : 3 * own + 2 * n, cols] = high[own : own + n]
                out[3 * own + 128 : 3 * own + 128 + n, cols] = low[own : own + n]

    lower, higher = y.index() > 0, y.index() < y.count - 1
    far_below = s.y2_routes[0].below()
    n = up8(y.mid_all)

    def write(out, size, terms):
        part = iota(terms[0].shape, 1) >= 2 * size
        for term, matrix in enumerate(terms):
            high, low = split(matrix)
            n = matrix.shape[0]
            out[term * n : (term + 1) * n] = jnp.where(part, low.astype(F32), high.astype(F32)).astype(BF16)

    def columns_of(rows, size):
        lane = iota((rows, 3 * size), 1)
        return jnp.where(lane >= 2 * size, lane - 2 * size, jnp.where(lane >= size, lane - size, lane))

    c = columns_of(y.fine, s.fine_rows)
    is_low = (c >= y.fine) & (c < y.fine + RADIUS)
    is_high = c >= y.fine + RADIUS
    where = jnp.where(is_low, c - y.fine - RADIUS, jnp.where(is_high, c - RADIUS, c))
    valid = choose(is_low, lower, choose(is_high, higher, c >= 0))
    write(y_fine, s.fine_rows, band(taps, 0, where - iota(c.shape, 0), valid))
    c = columns_of(y.fine, y.fine)
    write(y_own, y.fine, band(taps, 0, c - iota(c.shape, 0), c >= 0))
    c = columns_of(y.fine, 2 * RADIUS)
    where = jnp.where(c < RADIUS, c - RADIUS, c - RADIUS + y.fine)
    write(y_edge, 2 * RADIUS, band(taps, 0, where - iota(c.shape, 0), choose(c < RADIUS, lower, higher)))

    c = columns_of(n, s.sum_rows)
    r = iota(c.shape, 0)
    is_low = (c >= s.low) & (c < s.low + SPAN)
    is_high = (c >= s.high) & (c < s.high + SPAN)
    is_far = (c >= s.far) & (c < s.far + y.second)
    where = jnp.where(is_low, c - s.low + 2 - SPAN, jnp.where(is_high, c - s.high + y.mid - 1, c - 1))
    valid = choose(is_low, lower, choose(is_high, higher, c < y.mid_all))
    mid = band(taps, 1, where - (r - 1), valid & (r < y.mid_all))
    far = jnp.where(far_below, -2 - y.coarse, 2 * y.coarse - 2)
    where = jnp.where(is_low, c - s.low + 3 - SPAN, jnp.where(is_high, c - s.high + y.coarse - 2, c - 2))
    where = jnp.where(is_far, c - s.far + far, where)
    valid = choose(is_low, lower, choose(is_high, higher, (c < y.coarse_all) | is_far))
    coarse = band(taps, 2, where - (r - 2), valid & (r < y.coarse_all))
    o, k = iota((y.fine, n), 0), iota((y.fine, n), 1)
    from_mid = jnp.where((k < y.mid_all) & y.holds_mid(k - 1), weight_of(o - 2 * (k - 1)), 0.0)
    m = s.coarse_rows
    c = columns_of(n, m)
    k = iota(c.shape, 0)
    from_coarse = jnp.where((c < y.coarse_all) & y.holds_coarse(c - 2), weight_of(k - 1 - 2 * (c - 2)), 0.0)
    write(y_mid, s.sum_rows, [dot(from_mid, matrix) for matrix in mid])
    write(y_coarse, s.sum_rows, [matrix[:m] for matrix in coarse])
    write(widen_y, m, [dot(from_mid, from_coarse)])


def contract_y(s, weights, high, low):
    joined = jnp.concatenate([high, low, high], axis=0)
    result = jnp.dot(weights[...], joined, preferred_element_type=F32)
    n, m = s.y.fine, s.x.fine
    return [result[t * n : (t + 1) * n, t * m : (t + 1) * m] for t in range(TERMS)]


def contract_z(table, level, held, base, count):
    rows = held.shape[2:]
    totals = [None] * count
    for t in range(held.shape[1]):
        for j in range(count + TAPS - 1):
            plane = held[base + j, t].reshape(rows[0] // 8, 8, rows[1])
            for i in range(max(0, j - TAPS + 1), min(count, j + 1)):
                term = table[(level * TERMS + t) * TAPS + j - i][None] * plane
                totals[i] = term if totals[i] is None else totals[i] + term
    return [total.reshape(rows) for total in totals]


def slab_starts(s, below_at, above_at):
    result = []
    for route in s.z_routes:
        lower, i = route.below(), s.z.index()
        valid = choose(lower, i >= 1, i + 1 < s.z.count)
        result.append((jnp.where(lower, below_at, above_at), valid))
    return result


def store_terms(held, at, valid, parts):
    for t, part in enumerate(parts):
        held[at, t] = part if valid is None else jnp.where(valid, part, 0.0)


BLOCK = 4


def fine_places(s):
    places = [(RADIUS + p, None) for p in range(s.z.fine)]
    for start, valid in slab_starts(s, 0, s.z.fine + RADIUS):
        places += [(start + p, valid) for p in range(RADIUS)]
    return places


def contract_x(s, grid, weights):
    high, low = split(grid)
    joined = jnp.concatenate([high, low, high], axis=1)
    return jnp.dot(joined, weights[: 3 * s.x.fine], preferred_element_type=F32)


def own_kernel(s, table, t_part, fine, slab, sums, x_fine, x_sums, y_edge, y_fine, fine_part, sums_part, t_fine):
    z, x = s.z, s.x
    t_fine[...] = t_part[...]
    fine_at = fine_places(s)

    def slab_group(g, count):
        n = s.fine_rows
        planes = jnp.concatenate([slab[g : g + count], fine[z.fine + g : z.fine + g + count]], axis=1)
        a, b = split(contract_x(s, planes.reshape(count * n, x.fine), x_fine))
        for p in range(count):
            rows = slice(p * n, (p + 1) * n)
            store_terms(t_fine, *fine_at[z.fine + g + p], contract_y(s, y_fine, a[rows], b[rows]))

    def fine_group(g, count):
        n = 2 * RADIUS
        a, b = split(contract_x(s, fine[g : g + count].reshape(count * n, x.fine), x_fine))
        for p in range(count):
            rows = slice(p * n, (p + 1) * n)
            at, valid = fine_at[g + p]
            for t, part in enumerate(contract_y(s, y_edge, a[rows], b[rows])):
                t_fine[at, t] = t_fine[at, t] + (part if valid is None else jnp.where(valid, part, 0.0))

    def fine_block(k):
        for i, total in enumerate(contract_z(table, 0, t_fine, k, BLOCK)):
            fine_part[k + i] = total

    def sum_part(g, count):
        n = s.sum_rows
        grid = sums[g : g + count].reshape(count * n, x.fine)
        sums_part[g * n : (g + count) * n] = contract_x(s, grid, x_sums)

    later = []
    done = 0
    for g in range(0, s.fine_planes - z.fine, 8):
        slab_group(g, 8)
    for g in range(0, z.fine, 8):
        fine_group(g, 8)
        while later:
            later.pop(0)()
        if g >= 0:
            ready = g if g + 8 < z.fine else z.fine
            later += [lambda k=k: fine_block(k) for k in range(done, ready, BLOCK)]
            done = max(done, ready)
    starts = list(range(0, s.sum_planes, 8))
    while later or starts:
        if starts:
            sum_part(starts[0], min(8, s.sum_planes - starts[0]))
            starts.pop(0)
        if later:
            later.pop(0)()


def sum_kernel(s, table, fine, sums, first, second, x_sums, ends, y_fine, y_mid, y_coarse, widen_x, widen_y, result, *scratch):
    sums_ends, t_mid, t_coarse, p_mid, p_coarse, narrow, out, left = scratch
    z, y, x = s.z, s.y, s.x
    below = s.x_routes[0].below()
    half = s.edge_sums
    def ends_of(start, rows):
        one, two = first[start : start + rows], second[start : start + rows]
        return jnp.where(below, one, two), jnp.where(below, two, one)

    for b in range(s.sum_blocks):
        if b < s.coarse_blocks:
            pair = ends_of(s.fine_ends + b * half, half)
        else:
            rest = jnp.zeros((half - up8(EDGE), 128), F32)
            pair = ends_of(s.mid_ends + (b - s.coarse_blocks) * up8(EDGE), up8(EDGE))
            pair = [jnp.concatenate([ends, rest], axis=0) for ends in pair]
        rows = jnp.concatenate(pair, axis=0)
        zeros = jnp.zeros((128 - 4 * half, 128), F32)
        sums_ends[b * 128 : (b + 1) * 128] = jnp.concatenate([rows, rows, zeros], axis=0).T

    def along_x(start, rows):
        edge_high, edge_low = split(sums_ends[start : start + rows])
        is_high = iota(edge_high.shape, 1) < 2 * half
        packed = jnp.where(is_high, edge_high.astype(F32), edge_low.astype(F32)).astype(BF16)
        joined = jnp.concatenate([packed, edge_high], axis=1)
        part = jnp.dot(joined, x_sums[3 * x.fine :], preferred_element_type=F32)
        return split(sums[start : start + rows] + part)

    def fine_edges():
        columns = []
        for flip in range(2):
            for g in range(s.fine_groups):
                is_folded = s.folded and g == s.fine_groups - 1
                at = slice(g * s.fine_rows, s.fine_ends if is_folded else (g + 1) * s.fine_rows)
                pair = (first[at], second[at])
                ends_here = jnp.where(below, pair[flip], pair[1 - flip])
                if is_folded:
                    ends_here = jnp.concatenate([ends_here, pltpu.roll(ends_here, x.fine // 2, 1)], axis=0)
                columns.append(ends_here)
        high, low = split(jnp.concatenate(columns, axis=1))
        joined = jnp.concatenate([high, low, high], axis=0)
        high, low = split(jnp.dot(y_fine[...], joined, preferred_element_type=F32))
        width = s.fine_groups * x.fine
        result = []
        for side in range(2):
            total = 0.0
            for t in range(TERMS):
                rows, cols = slice(t * y.fine, (t + 1) * y.fine), slice(side * width, (side + 1) * width)
                a, b = high[rows, cols], low[rows, cols]
                joined = jnp.concatenate([a, b, a], axis=1)
                total = total + jnp.dot(joined, ends[2 * t + side], preferred_element_type=F32)
            result.append(total)
        return result

    t_mid[...] = jnp.zeros(t_mid.shape, F32)
    t_coarse[...] = jnp.zeros(t_coarse.shape, F32)
    mid_at = [(RADIUS + p, None) for p in range(z.mid_all)]
    mid_at, rest_at = mid_at[: z.coarse_all], mid_at[z.coarse_all :]
    coarse_at = [(RADIUS + p, None) for p in range(z.coarse_all)]
    for start, valid in slab_starts(s, 0, z.mid + 3 + RADIUS):
        mid_at += [(start + p, valid) for p in range(RADIUS)]
    mid_at += rest_at
    for start, valid in slab_starts(s, 0, z.coarse + 5 + RADIUS):
        coarse_at += [(start + p, valid) for p in range(RADIUS)]
    coarse_at += [(None, None)] * len(rest_at)
    is_second = iota((s.coarse_rows, x.fine), 1) >= x.fine // TERMS

    def sum_group(g, count):
        n = s.sum_rows
        a, b = along_x(g * n, count * n)
        for p in range(count):
            rows = slice(p * n, (p + 1) * n)
            at, valid = mid_at[g + p]
            cols = slice(0, TERMS * x.fine)
            store_terms(t_mid, at, valid, contract_y(s, y_mid, a[rows, cols], b[rows, cols]))
            at, valid = coarse_at[g + p]
            if at is not None:
                cols = slice(TERMS * x.fine, (TERMS + 1) * x.fine)
                joined = jnp.concatenate([a[rows, cols], b[rows, cols], a[rows, cols]], axis=0)
                both = jnp.dot(y_coarse[...], joined, preferred_element_type=F32)
                m = s.coarse_rows
                store_terms(t_coarse, at, valid, [jnp.where(is_second, both[m:], both[:m])])

    def coarse_block(k):
        count = min(BLOCK, z.coarse_all - k)
        for i, total in enumerate(contract_z(table, 2, t_coarse, k, count)):
            narrow[k + i] = jnp.where(z.holds_coarse(k + i - 2), total, 0.0)

    def widen():
        m = s.coarse_rows
        high, low = split(narrow[...].reshape(z.coarse_all * m, x.fine))
        joined = jnp.concatenate([high, low, high], axis=1)
        high, low = split(jnp.dot(joined, widen_x[...], preferred_element_type=F32))
        for p in range(z.coarse_all):
            rows = slice(p * m, (p + 1) * m)
            joined = jnp.concatenate([high[rows], low[rows], high[rows]], axis=0)
            p_coarse[p] = jnp.dot(widen_y[...], joined, preferred_element_type=F32)

    def mid_block(k):
        count = min(BLOCK, z.mid_all - k)
        for i, total in enumerate(contract_z(table, 1, t_mid, k, count)):
            m = k + i - 1
            for offset, weight in WEIGHTS:
                if (m - offset) % 2 == 0 and 0 <= (m - offset) // 2 + 2 < z.coarse_all:
                    total = total + weight * p_coarse[(m - offset) // 2 + 2]
            p_mid[k + i] = jnp.where(z.holds_mid(m), total, 0.0)

    edges = fine_edges()
    lane = iota((y.fine, x.fine), 1)

    def begin(k):
        block, at = k // s.side, k % s.side * RADIUS
        low, high = (edge[:, block * x.fine : (block + 1) * x.fine] for edge in edges)
        low = pltpu.roll(low, -at % x.fine, 1) if at else low
        turn = (x.fine - RADIUS - at) % x.fine
        high = pltpu.roll(high, turn, 1) if turn else high
        out[k] = fine[k] + jnp.where(lane < RADIUS, low, jnp.where(lane >= x.fine - RADIUS, high, 0.0))

    def finish(k):
        total = out[k]
        for offset, weight in WEIGHTS:
            if (k - offset) % 2 == 0:
                total = total + weight * p_mid[(k - offset) // 2 + 1]
        out[k] = total

    groups = list(range(0, s.sum_planes, 14))
    share = -(-z.fine // len(groups))
    for n, g in enumerate(groups):
        sum_group(g, min(14, s.sum_planes - g))
        for k in range(n * share, min((n + 1) * share, z.fine)):
            begin(k)
    for k in range(0, z.coarse_all, BLOCK):
        coarse_block(k)
    widen()
    done, copies = 0, []
    for k in range(0, z.mid_all, BLOCK):
        mid_block(k)
        ready = z.fine if k + BLOCK >= z.mid_all else 2 * k + 2
        while done < ready:
            finish(done)
            done += 1
            if done % 8 == 0:
                part = pl.ds(done - 8, 8)
                copies.append(pltpu.make_async_copy(out.at[part], result.at[part], left.at[done // 8 - 1]))
                copies[-1].start()
    for copy in copies:
        copy.wait()


def call(kernel, outs, ins, scratch=(), flops=10**7, out_space=pltpu.VMEM):
    specs = [SMEM if a.ndim == 3 and a.shape[-1] == TAPS else VMEM for a in ins]
    size = sum(a.size * a.dtype.itemsize for a in ins) + sum(o.size * o.dtype.itemsize for o in outs)
    return pl.pallas_call(
        kernel,
        out_shape=tuple(outs),
        in_specs=specs,
        out_specs=tuple(pl.BlockSpec(memory_space=out_space) for _ in outs),
        scratch_shapes=list(scratch),
        compiler_params=PARAMS,
        cost_estimate=pl.CostEstimate(flops=flops, bytes_accessed=size, transcendentals=0),
    )(*ins)


def array(*shape, dtype=F32):
    return jax.ShapeDtypeStruct(shape, dtype)


def local(charges, kernel_taps):
    z, y, x = (Cut(name, size) for name, size in zip(("gz", "gy", "gx"), charges.shape))
    s = Sizes(z, y, x)
    n = x.fine
    nz, nz2 = len(s.z_routes), len(s.z2_routes)

    def bound(kernel, *static):
        return lambda *refs: kernel(s, *static, *refs)

    rows = up8(y.mid_all)
    (weights,) = call(bound(narrow_kernel), [array(n, 2 * n, dtype=BF16)], [], flops=10**10)
    held, own, ahead, behind, far, *messages = call(
        bound(restrict_kernel, nz),
        [array(*charges.shape), array(z.mid_all, rows, n)] + [array(s.y_rows, n)] * 2 + [array(s.far_rows, n)] + [array(s.z_rows, n)] * nz + [array(s.z2_rows, n)] * nz2,
        [charges, weights],
        [
            pltpu.VMEM((z.fine, y.fine + 32, n), F32),
            pltpu.VMEM((z.mid_all, rows, n), F32),
            pltpu.VMEM((z.mid_all, up8(y.mid + 24), n), F32),
            pltpu.VMEM((z.mid_all, rows, n), F32),
            pltpu.VMEM((2, max(s.z_rows - s.z_fine, s.y_rows - s.y_fine), n), F32),
            pltpu.VMEM((s.far_groups, s.far_rows, n), F32),
        ],
    )
    z_got = [route(m) for route, m in zip(s.z_routes + s.z2_routes, messages)]
    sides = [s.y_routes[0](ahead), s.y_routes[1](behind)]
    far = s.y2_routes[0](far)
    passed = call(
        bound(pass_kernel, nz),
        [array(RADIUS * s.inner + s.far_rows, n)] * nz + [array(s.far_rows, n)] * nz2,
        [far, held],
        flops=15 * 10**8,
    )
    operators = call(
        bound(operator_kernel),
        [
            array(3 * n, TERMS * n, dtype=BF16),
            array(3 * n + 256, (TERMS + 1) * n, dtype=BF16),
            array(TERMS * y.fine, 3 * y.fine, dtype=BF16),
            array(TERMS * y.fine, 6 * RADIUS, dtype=BF16),
            array(TERMS * y.fine, 3 * s.fine_rows, dtype=BF16),
            array(TERMS * y.fine, 3 * s.sum_rows, dtype=BF16),
            array(TERMS * s.coarse_rows, 3 * s.sum_rows, dtype=BF16),
            array(3 * n, n, dtype=BF16),
            array(y.fine, 3 * s.coarse_rows, dtype=BF16),
        ],
        [kernel_taps],
    )
    later = call(
        bound(later_kernel),
        [array(2 * TERMS, 3 * s.fine_groups * n, z_columns(s), dtype=BF16), array((2 * TERMS + 1) * TAPS, 8, n)],
        [kernel_taps],
    )
    ends, table = later
    ahead, behind = call(
        bound(spread_kernel, nz, nz2),
        [array(s.slab_rows, n), array(s.slab_rows, n)],
        [passed[0], *z_got],
        [pltpu.VMEM((3, up8(max(s.slab_coarse, s.slab_rows - s.slab_fine)) + 8, n), F32)],
    )
    sides += [s.y_routes[0](ahead), s.y_routes[1](behind)]
    fars = [far] + [route(m) for route, m in zip(s.z_routes + s.z2_routes, passed)]
    x_fine, x_sums, y_own, y_edge, y_fine, y_mid, y_coarse, widen_x, widen_y = operators
    t_part, last, start = call(
        bound(early_kernel),
        [array(z.fine + 2 * RADIUS, TERMS, y.fine, n)] + [array(s.own_groups * y.fine, n)] * 2,
        [held, x_fine, y_own, table],
    )
    fine, slab, sums, first, second = call(
        bound(collect_kernel, nz, nz2),
        [
            array(s.fine_planes, 2 * RADIUS, n),
            array(nz * RADIUS, y.fine, n),
            array(s.sum_planes, s.sum_rows, n),
            array(s.x_rows, n),
            array(s.x_rows, n),
        ],
        [last, start, own, *z_got, *sides, *fars],
        [
            pltpu.VMEM((s.slab_planes, s.sum_rows, n), F32),
            pltpu.VMEM((1 + nz + nz2, z.coarse_all, 8, n), F32),
            pltpu.VMEM((2, up8(s.slab_coarse) + 8, n), F32),
        ],
    )
    first, second = s.x_routes[0](first), s.x_routes[1](second)
    fine, sums = call(
        bound(own_kernel),
        [array(z.fine, y.fine, n), array(s.sum_planes * s.sum_rows, (TERMS + 1) * n)],
        [table, t_part, fine, slab, sums, x_fine, x_sums, y_edge, y_fine],
        [pltpu.VMEM((z.fine + 2 * RADIUS, TERMS, y.fine, n), F32)],
    )
    (out,) = call(
        bound(sum_kernel),
        [array(z.fine, y.fine, n)],
        [table, fine, sums, first, second, x_sums, ends, y_fine, y_mid, y_coarse, widen_x, widen_y],
        [
            pltpu.VMEM((s.sum_blocks * 128, n), F32),
            pltpu.VMEM((z.mid + 2 * RADIUS + 3, TERMS, y.fine, n), F32),
            pltpu.VMEM((z.coarse + 2 * RADIUS + 5, 1, s.coarse_rows, n), F32),
            pltpu.VMEM((z.mid_all, y.fine, n), F32),
            pltpu.VMEM((z.coarse_all, y.fine, n), F32),
            pltpu.VMEM((z.coarse_all, s.coarse_rows, n), F32),
            pltpu.VMEM((z.fine, y.fine, n), F32),
            pltpu.SemaphoreType.DMA((z.fine // 8,)),
        ],
        out_space=pltpu.HBM,
    )
    return out


def solution(mesh):
    return jax.shard_map(
        local,
        mesh=mesh,
        in_specs=(P("gz", "gy", "gx"), P()),
        out_specs=P("gz", "gy", "gx"),
        check_vma=False,
    )
```

```python
import jax
import jax.numpy as jnp
from jax import lax
from jax.experimental import pallas as pl
from jax.experimental.pallas import tpu as pltpu
from jax.sharding import PartitionSpec as P

RADIUS = 8
TAPS = 17
TERMS = 2
WEIGHTS = ((-3, -0.0625), (-1, 0.5625), (0, 1.0), (1, 0.5625), (3, -0.0625))
EXACT = lax.Precision.HIGHEST
SPAN = RADIUS + 5
EDGE = RADIUS + 3
F32, BF16 = jnp.float32, jnp.bfloat16
PARAMS = pltpu.CompilerParams(vmem_limit_bytes=32 * 1024 * 1024)
VMEM = pl.BlockSpec(memory_space=pltpu.VMEM)
SMEM = pl.BlockSpec(memory_space=pltpu.SMEM)


def up8(n):
    return -(-n // 8) * 8


def iota(shape, dim):
    return lax.broadcasted_iota(jnp.int32, shape, dim)


def weight_of(difference):
    size = jnp.abs(difference)
    out = jnp.where(size == 1, 0.5625, jnp.where(size == 3, -0.0625, 0.0))
    return jnp.where(size == 0, 1.0, out)


def choose(condition, a, b):
    return jnp.where(condition, jnp.where(a, 1, 0), jnp.where(b, 1, 0)) != 0


class Cut:
    def __init__(self, name, length):
        self.name, self.fine = name, length
        self.count = lax.axis_size(name)
        self.mid, self.coarse = length // 2, length // 4
        self.mid_all, self.coarse_all = self.mid + 3, self.coarse + 5
        self.second = max(SPAN - self.coarse, 0)

    def index(self):
        return lax.axis_index(self.name)

    def holds_mid(self, k):
        k = k + self.index() * self.mid
        return (k >= 0) & (k < self.mid * self.count)

    def holds_coarse(self, k):
        k = k + self.index() * self.coarse
        return (k >= 0) & (k < self.coarse * self.count)


class Route:
    def __init__(self, names, pairs, up, below):
        self.names, self.pairs, self.up, self.below = names, pairs, up, below

    def __call__(self, x):
        return lax.ppermute(x, self.names, self.pairs)


def flip(pairs):
    return [(b, a) for a, b in pairs]


def swap(cut, steps):
    pairs = [(i, i + steps) for i in range(cut.count - steps)]

    def up():
        return cut.index() + steps < cut.count

    return [Route(cut.name, pairs + flip(pairs), up, lambda: ~up())]


def both_ways(cut, steps):
    pairs = [(i, i + steps) for i in range(cut.count - steps)]
    yes, no = (lambda: cut.index() >= 0), (lambda: cut.index() < 0)
    return [Route(cut.name, pairs, yes, yes), Route(cut.name, flip(pairs), no, no)]


def folded(cut, beside, names):
    n, m = cut.count, lax.axis_size(beside)

    def place(c, i):
        return c * n + i if names[0] == beside else i * m + c

    pairs = []
    for c in range(0, m, 2):
        cycle = [place(c, i) for i in range(n)] + [place(c + 1, i) for i in reversed(range(n))]
        pairs += list(zip(cycle, cycle[1:] + cycle[:1]))

    def even():
        return lax.axis_index(beside) % 2 == 0

    def odd():
        return lax.axis_index(beside) % 2 == 1

    return [Route(names, pairs, even, even), Route(names, flip(pairs), odd, odd)]


def split(x):
    high = x.astype(BF16)
    return high, (x - high.astype(F32)).astype(BF16)


def pick(selector, x):
    nt = (((1,), (1,)), ((), ()))
    a = x.astype(BF16)
    rest = x - a.astype(F32)
    b = rest.astype(BF16)
    c = (rest - b.astype(F32)).astype(BF16)
    out = lax.dot_general(selector, c, nt, preferred_element_type=F32)
    out = out + lax.dot_general(selector, b, nt, preferred_element_type=F32)
    return out + lax.dot_general(selector, a, nt, preferred_element_type=F32)


class Sizes:
    def place_of(self, p):
        return p if p < self.slab_start else p + self.coarse_planes - self.slab_start

    def __init__(self, z, y, x):
        self.z, self.y, self.x = z, y, x
        self.z_routes = swap(z, 1) if z.count <= 2 else both_ways(z, 1)
        self.z2_routes = [] if z.count <= 2 else swap(z, 2) if z.count <= 4 else both_ways(z, 2)
        self.y_routes = folded(y, x.name, (x.name, y.name))
        self.y2_routes = swap(y, 2)
        self.x_routes = folded(x, z.name, (x.name, z.name))
        self.inner = y.fine - 2 * RADIUS
        self.z_fine = RADIUS * 2 * RADIUS
        self.z_sums = max(EDGE * y.mid_all, SPAN * y.coarse_all)
        self.z_rows = up8(self.z_fine + self.z_sums)
        self.z2_rows = up8(z.second * y.coarse_all)
        self.slab_planes = SPAN * len(self.z_routes) + z.second * len(self.z2_routes)
        self.fine_planes = z.fine + RADIUS * len(self.z_routes)
        self.sum_planes = z.mid_all + RADIUS * len(self.z_routes)
        self.coarse_rows = -(-y.coarse_all // 16) * 16
        self.y_fine = RADIUS * z.fine
        self.y_sums = max(EDGE * z.mid_all, SPAN * z.coarse_all)
        self.y_rows = up8(self.y_fine + self.y_sums)
        self.slab_fine = RADIUS * RADIUS * len(self.z_routes)
        self.slab_mid = EDGE * EDGE * len(self.z_routes)
        self.slab_coarse = SPAN * self.slab_planes
        self.extra = max(self.slab_coarse - self.slab_mid, 0)
        self.spare = x.fine - x.mid_all - x.coarse_all
        self.pieces = -(-x.coarse_all // max(self.spare, 1))
        if self.pieces * self.extra > self.slab_mid:
            self.extra = 0
        self.slab_sums = max(self.slab_mid, self.slab_coarse - self.extra)
        self.slab_rows = up8(self.slab_fine + self.slab_sums)
        self.far_groups = x.fine // x.coarse_all
        self.far_planes = -(-z.coarse_all // self.far_groups)
        self.far_rows = up8(y.second * self.far_planes)
        self.slab_start = z.coarse_all
        self.coarse_planes = z.coarse_all + RADIUS * len(self.z_routes)
        self.fine_rows = y.fine + 2 * RADIUS
        self.far = y.coarse_all
        self.low = y.mid_all
        self.high = self.low + SPAN
        self.sum_rows = -(-(self.high + SPAN) // 16) * 16
        self.edge_sums = EDGE + SPAN
        self.side = x.fine // RADIUS
        self.fine_groups = -(-self.fine_planes // self.side)
        assert z.fine % self.side == 0
        self.own_groups = z.fine // self.side
        self.folded = 0 < self.fine_planes % self.side <= self.side // 2
        self.fine_ends = self.fine_groups * self.fine_rows - (self.fine_rows // 2 if self.folded else 0)
        self.sum_blocks = -(-self.sum_planes * self.sum_rows // 128)
        self.coarse_blocks = -(-self.coarse_planes * self.sum_rows // 128)
        self.mid_ends = self.fine_ends + self.coarse_blocks * self.edge_sums
        self.x_rows = self.mid_ends + (self.sum_blocks - self.coarse_blocks) * up8(EDGE)
        assert x.mid_all + x.coarse_all <= x.fine
        assert self.far + y.second <= self.low and y.second <= 8 and y.coarse_all == SPAN and z.coarse_all == SPAN
        assert z.coarse >= RADIUS and y.coarse >= RADIUS and y.count == 4


def narrow_kernel(s, out):
    x = s.x
    lanes = (x.fine, x.fine)
    cell, lane = iota(lanes, 0), iota(lanes, 1)
    k = lane - 1
    to_mid = jnp.where((lane < x.mid_all) & x.holds_mid(k), weight_of(cell - 2 * k), 0.0)
    c = lane - x.mid_all - 2
    inside = (lane >= x.mid_all) & (lane < x.mid_all + x.coarse_all) & x.holds_coarse(c)
    to_coarse = jnp.where(inside, weight_of(cell - 1 - 2 * c), 0.0)
    narrow = to_mid + jnp.dot(to_mid, to_coarse, precision=EXACT, preferred_element_type=F32)
    out[...] = jnp.concatenate(split(narrow), axis=1)


def restrict_kernel(s, nz, source, narrow, charges, own, ahead, behind, far, *rest):
    messages, (wide, mid, high, coarse, packed, groups) = rest[:-6], rest[-6:]
    z, y, x = s.z, s.y, s.x
    wide[...] = jnp.zeros(wide.shape, F32)
    charges[...] = source[...]
    cells = source[...].reshape(z.fine * y.fine, x.fine)
    top, rest = cells.astype(BF16), cells
    rest = rest - top.astype(F32)
    middle = rest.astype(BF16)
    low = (rest - middle.astype(F32)).astype(BF16)
    weights = narrow[...]
    both = jnp.dot(low, weights, preferred_element_type=F32)
    both = both + jnp.dot(
        jnp.concatenate([top, middle], axis=1), jnp.concatenate([weights, weights], axis=0), preferred_element_type=F32
    )
    reduced = both[:, : x.fine] + both[:, x.fine :]
    wide[:, 8 : 8 + y.fine, :] = reduced.reshape(z.fine, y.fine, x.fine)
    rows = 0.0
    for offset, weight in WEIGHTS:
        rows = rows + weight * wide[:, pl.ds(6 + offset, y.mid_all, stride=2), :]
    keep = y.holds_mid(iota((y.mid_all, x.fine), 0) - 1)
    mid[...] = jnp.zeros(mid.shape, F32)
    coarse[...] = jnp.zeros(coarse.shape, F32)
    high[...] = jnp.zeros(high.shape, F32)
    for p in range(z.mid_all):
        total = 0.0
        for offset, weight in WEIGHTS:
            at = 2 * (p - 1) + offset
            if 0 <= at < z.fine:
                total = total + weight * rows[at]
        total = jnp.where(keep & z.holds_mid(p - 1), total, 0.0)
        mid[p, : y.mid_all] = total
        high[p, 8 : 8 + y.mid_all] = total
    rows = 0.0
    for offset, weight in WEIGHTS:
        rows = rows + weight * high[:, pl.ds(5 + offset, y.coarse_all, stride=2), :]
    keep = y.holds_coarse(iota((y.coarse_all, x.fine), 0) - 2)
    for p in range(z.coarse_all):
        total = 0.0
        for offset, weight in WEIGHTS:
            at = 2 * (p - 2) + offset + 1
            if 0 <= at < z.mid_all:
                total = total + weight * rows[at]
        coarse[p, : y.coarse_all] = jnp.where(keep & z.holds_coarse(p - 2), total, 0.0)
    is_mid = iota(mid.shape[1:], 1) < x.mid_all
    for p in range(z.mid_all):
        own[p] = jnp.where(is_mid, mid[p], coarse[p]) if p < z.coarse_all else jnp.where(is_mid, mid[p], 0.0)
    up = s.y2_routes[0].up()
    count, end = y.second, y.coarse_all
    groups[...] = jnp.zeros(groups.shape, F32)
    for p in range(z.coarse_all):
        g, at = p // s.far_planes, p % s.far_planes * count
        groups[g, at : at + count] = jnp.where(up, own[p, end - count : end], own[p, :count])
    lane = iota(far.shape, 1)
    total = jnp.zeros(far.shape, F32)
    for g in range(s.far_groups):
        first = g * x.coarse_all
        turned = pltpu.roll(groups[g], (first - x.mid_all) % x.fine, 1)
        total = jnp.where((lane >= first) & (lane < first + x.coarse_all), turned, total)
    far[...] = total
    for message, route in zip((ahead, behind), s.y_routes):
        up = route.up()
        edge = jnp.where(up, charges[:, y.fine - RADIUS :, :], charges[:, :RADIUS, :])
        message[: s.y_fine] = edge.reshape(s.y_fine, x.fine)
        packed[...] = jnp.zeros(packed.shape, F32)
        for p in range(z.mid_all):
            packed[0, p * EDGE : (p + 1) * EDGE] = jnp.where(up, mid[p, y.mid_all - EDGE : y.mid_all], mid[p, :EDGE])
        for p in range(z.coarse_all):
            packed[1, p * SPAN : (p + 1) * SPAN] = coarse[p, :SPAN]
        rows = s.y_rows - s.y_fine
        is_mid = iota((rows, x.fine), 1) < x.mid_all
        message[s.y_fine :] = jnp.where(is_mid, packed[0, :rows], packed[1, :rows])
    for message, route in zip(messages, s.z_routes):
        up = route.up().astype(jnp.int32)
        planes = charges[pl.ds(up * (z.fine - RADIUS), RADIUS)]
        outer = jnp.concatenate([planes[:, :RADIUS], planes[:, y.fine - RADIUS :]], axis=1)
        message[: s.z_fine] = outer.reshape(s.z_fine, x.fine)
        packed[...] = jnp.zeros(packed.shape, F32)
        for p in range(EDGE):
            packed[0, p * y.mid_all : (p + 1) * y.mid_all] = mid[up * (z.mid_all - EDGE) + p][: y.mid_all]
        for p in range(SPAN):
            plane = coarse[up * (z.coarse_all - SPAN) + p]
            packed[1, p * y.coarse_all : (p + 1) * y.coarse_all] = plane[: y.coarse_all]
        rows = s.z_rows - s.z_fine
        is_mid = iota((rows, x.fine), 1) < x.mid_all
        message[s.z_fine :] = jnp.where(is_mid, packed[0, :rows], packed[1, :rows])
    for message, route in zip(messages[nz:], s.z2_routes):
        up = route.up().astype(jnp.int32)
        message[...] = jnp.zeros(message.shape, F32)
        for p in range(z.second):
            plane = coarse[up * (z.coarse_all - z.second) + p]
            message[p * y.coarse_all : (p + 1) * y.coarse_all] = plane[: y.coarse_all]


class Slab:
    def __init__(self, message, mid, coarse):
        self.message, self.mid, self.coarse = message, mid, coarse

    def mid_rows(self, first, count):
        return self.message[self.mid + first : self.mid + first + count]

    def coarse_rows(self, first, count):
        return self.message[self.coarse + first : self.coarse + first + count]

    def rows(self, is_mid, first_mid, first_coarse, count):
        coarse = 0.0 if first_coarse is None else self.coarse_rows(first_coarse, count)
        mid = 0.0 if self.mid is None else self.message[self.mid + first_mid : self.mid + first_mid + count]
        return jnp.where(is_mid, mid, coarse)


def slabs(s, z_messages, z2_messages):
    out = []
    for message in z_messages:
        for p in range(SPAN):
            mid = s.z_fine + p * s.y.mid_all if p < EDGE else None
            out.append(Slab(message, mid, s.z_fine + p * s.y.coarse_all))
    for message in z2_messages:
        out += [Slab(message, None, p * s.y.coarse_all) for p in range(s.z.second)]
    return out


def spread_kernel(s, nz, nz2, _, *rest):
    z_messages, z2_messages = rest[:nz], rest[nz : nz + nz2]
    ahead, behind, packed = rest[-3:]
    z, y, x = s.z, s.y, s.x
    planes = slabs(s, z_messages, z2_messages)
    count = s.slab_rows - s.slab_fine
    lane = iota((count, x.fine), 1)
    packed[...] = jnp.zeros(packed.shape, F32)
    for p, plane in enumerate(planes):
        packed[1, p * SPAN : (p + 1) * SPAN] = plane.coarse_rows(0, SPAN)
    for n in range(s.pieces if s.extra else 0):
        first = x.mid_all + n * s.spare
        turned = pltpu.roll(packed[1, s.slab_mid : s.slab_mid + up8(s.extra)], x.fine - s.spare - first, 1)
        packed[2, n * s.extra : (n + 1) * s.extra] = turned[: s.extra]
    coarse = jnp.where(lane < x.fine - s.spare, packed[1, :count], packed[2, :count])
    for message, route in zip((ahead, behind), s.y_routes):
        up = route.up()
        at = 0
        for z_message in z_messages:
            slab = z_message[: s.z_fine].reshape(RADIUS, 2 * RADIUS, x.fine)
            edge = jnp.where(up, slab[:, RADIUS:], slab[:, :RADIUS])
            message[at : at + RADIUS * RADIUS] = edge.reshape(RADIUS * RADIUS, x.fine)
            at += RADIUS * RADIUS
        at = 0
        for plane in planes:
            if plane.mid is not None:
                first, last = plane.mid_rows(0, EDGE), plane.mid_rows(y.mid_all - EDGE, EDGE)
                packed[0, at : at + EDGE] = jnp.where(up, last, first)
                at += EDGE
        message[s.slab_fine :] = jnp.where(lane < x.mid_all, packed[0, :count], coarse)


def pass_kernel(s, nz, far, charges, *outs):
    z, x = s.z, s.x
    rows = RADIUS * s.inner
    for out, route in zip(outs, s.z_routes):
        planes = charges[pl.ds(route.up().astype(jnp.int32) * (z.fine - RADIUS), RADIUS)]
        out[:rows] = planes[:, RADIUS : RADIUS + s.inner].reshape(rows, x.fine)
        out[rows:] = far[...]
    for out in outs[nz:]:
        out[...] = far[...]


def roll_ends(s, plane_rows, count, groups):
    x = s.x
    lane = iota((count, x.fine), 1)
    for g in groups:
        ends = [jnp.zeros(lane.shape, F32)] * 2
        for j in range(min(s.side, s.fine_planes - g * s.side)):
            plane = plane_rows(g * s.side + j)
            here = (lane >= RADIUS * j) & (lane < RADIUS * (j + 1))
            for n, start in enumerate((x.fine - RADIUS, 0)):
                shift = (RADIUS * j - start) % x.fine
                ends[n] = jnp.where(here, pltpu.roll(plane, shift, 1) if shift else plane, ends[n])
        yield g, ends


def early_kernel(s, charges, x_fine, y_own, _, t_part, last, start):
    z, y, x = s.z, s.y, s.x
    clear_ends(t_part, z.fine)
    for g in range(0, z.fine, 8):
        a, b = split(contract_x(s, charges[g : g + 8].reshape(8 * y.fine, x.fine), x_fine))
        for p in range(8):
            rows = slice(p * y.fine, (p + 1) * y.fine)
            store_terms(t_part, RADIUS + g + p, None, contract_y(s, y_own, a[rows], b[rows]))
    for g, ends in roll_ends(s, lambda p: charges[p], y.fine, range(s.own_groups)):
        rows = slice(g * y.fine, (g + 1) * y.fine)
        last[rows], start[rows] = ends


def collect_kernel(s, nz, nz2, last, start, own, *rest):
    z_messages, z2_messages = rest[:nz], rest[nz : nz + nz2]
    rest = rest[nz + nz2 :]
    pairs = rest[:4]
    fars = rest[4 : 5 + nz + nz2]
    fine, slab, sums, first, second, raw, rows, near = rest[5 + nz + nz2 :]
    z, y, x = s.z, s.y, s.x
    below = s.y_routes[0].below()
    planes = slabs(s, z_messages, z2_messages)

    def sides(which, start, count):
        a, b = (message[start : start + count] for message in pairs[2 * which : 2 * which + 2])
        return jnp.where(below, a, b), jnp.where(below, b, a)

    parts = [(0, z.fine, 0, 0)] + [(z.fine + n * RADIUS, RADIUS, 1, n * RADIUS * RADIUS) for n in range(nz)]
    for at, count, which, row in parts:
        low, high = sides(which, row, RADIUS * count)
        fine[at : at + count, :RADIUS] = low.reshape(count, RADIUS, x.fine)
        fine[at : at + count, RADIUS:] = high.reshape(count, RADIUS, x.fine)
    sums[...] = jnp.zeros(sums.shape, F32)
    raw[...] = jnp.zeros(raw.shape, F32)
    inner_rows = RADIUS * s.inner
    for n, far in enumerate(fars):
        is_joint = 0 < n <= nz
        if is_joint:
            outer = z_messages[n - 1][: s.z_fine].reshape(RADIUS, 2 * RADIUS, x.fine)
            planes_here = slice((n - 1) * RADIUS, n * RADIUS)
            slab[planes_here, :RADIUS] = outer[:, :RADIUS]
            slab[planes_here, RADIUS : RADIUS + s.inner] = far[:inner_rows].reshape(RADIUS, s.inner, x.fine)
            slab[planes_here, RADIUS + s.inner :] = outer[:, RADIUS:]
        two_away = far[inner_rows:] if is_joint else far[...]
        for g in range(s.far_groups):
            turned = pltpu.roll(two_away, (x.mid_all - g * x.coarse_all) % x.fine, 1)
            for p in range(g * s.far_planes, min((g + 1) * s.far_planes, z.coarse_all)):
                at = p % s.far_planes * y.second
                rows[n, p, : y.second] = turned[at : at + y.second]
    is_mid = iota((y.second, x.fine), 1) < x.mid_all

    lane = iota((up8(s.extra), x.fine), 1)
    for side, got in enumerate(sides(1, s.slab_fine, s.slab_sums)):
        near[side, : s.slab_sums] = got
        if s.extra:
            total = jnp.zeros(lane.shape, F32)
            for n in range(s.pieces):
                begin = x.mid_all + n * s.spare
                piece = near[side, n * s.extra : n * s.extra + up8(s.extra)]
                turned = pltpu.roll(piece, begin + s.spare, 1)
                total = jnp.where(lane >= begin, turned, total)
            near[side, s.slab_mid : s.slab_mid + s.extra] = total[: s.extra]
    is_mid_edge = iota((EDGE, x.fine), 1) < x.mid_all
    is_mid_span = iota((SPAN, x.fine), 1) < x.mid_all

    def rows_of_plane(out, p, body, mids, coarses, far_plane):
        out[p, : y.mid_all] = body
        for base, shift, n in ((s.low, SPAN - EDGE, 0), (s.high, 0, 1)):
            if coarses is not None:
                out[p, base : base + SPAN] = jnp.where(is_mid_span, 0.0, coarses[n])
            if mids is not None:
                at = slice(base + shift, base + shift + EDGE)
                out[p, at] = jnp.where(is_mid_edge, mids[n], out[p, at])
        if far_plane is not None:
            at = slice(s.far, s.far + y.second)
            out[p, at] = jnp.where(is_mid, out[p, at], rows[far_plane][: y.second])

    for p in range(z.mid_all):
        far_plane = (0, p) if p < z.coarse_all else None
        mids = sides(0, s.y_fine + p * EDGE, EDGE)
        coarses = sides(0, s.y_fine + p * SPAN, SPAN) if p < z.coarse_all else None
        rows_of_plane(sums, s.place_of(p), own[p, : y.mid_all], mids, coarses, far_plane)
    is_mid_row = iota((SPAN, x.fine), 1) < x.mid_all
    is_mid_rest = iota((y.mid_all - SPAN, x.fine), 1) < x.mid_all
    slab_far = [(1 + n, p) for n in range(nz) for p in range(SPAN)]
    for n, route in enumerate(s.z2_routes):
        at = jnp.where(route.below(), z.coarse_all - z.second, 0)
        slab_far += [(1 + nz + n, at + p) for p in range(z.second)]
    held = 0
    for p, plane in enumerate(planes):
        body = [plane.rows(is_mid_row, 0, 0, SPAN), plane.rows(is_mid_rest, SPAN, None, y.mid_all - SPAN)]
        mids = None
        if plane.mid is not None:
            mids = sides(1, s.slab_fine + held * EDGE, EDGE)
            held += 1
        coarses = [near[side, p * SPAN : (p + 1) * SPAN] for side in range(2)]
        rows_of_plane(raw, p, jnp.concatenate(body, axis=0), mids, coarses, slab_far[p])
    is_mid = iota((s.sum_rows, x.fine), 1) < x.mid_all

    def number(condition, a, b):
        return jnp.where(condition, a, b)

    for n, route in enumerate(s.z_routes):
        lower, base = route.below(), n * SPAN
        for j in range(RADIUS):
            a = raw[base + number(lower, 0, 3) + j]
            b = raw[base + number(lower, SPAN - 5 - RADIUS, 5) + j]
            sums[s.slab_start + n * RADIUS + j] = jnp.where(is_mid, a, b)
        for i in range(3):
            at = number(lower, 0, s.place_of(z.mid)) + i
            sums[at] = sums[at] + jnp.where(is_mid, raw[base + number(lower, EDGE - 3, 0) + i], 0.0)
        for i in range(5):
            at = number(lower, 0, z.coarse) + i
            sums[at] = sums[at] + jnp.where(is_mid, 0.0, raw[base + number(lower, SPAN - 5, 0) + i])
    for n, route in enumerate(s.z2_routes):
        base = len(s.z_routes) * SPAN + n * z.second
        at = s.slab_start + number(route.below(), RADIUS - z.coarse, RADIUS + z.coarse - 5)
        for p in range(z.second):
            sums[at + p] = sums[at + p] + jnp.where(is_mid, 0.0, raw[base + p])

    up = s.x_routes[0].up()
    half, shift = s.fine_rows // 2, x.fine // 2
    is_first_half = iota((half, x.fine), 1) < shift
    own_ends = roll_ends(s, lambda p: fine[p], 2 * RADIUS, range(s.own_groups))
    slab_rows = [jnp.concatenate([slab[p], fine[z.fine + p]], axis=0) for p in range(nz * RADIUS)]
    slab_ends = roll_ends(s, lambda p: slab_rows[p - z.fine], s.fine_rows, range(s.own_groups, s.fine_groups))
    for g, ends in list(own_ends) + list(slab_ends):
        both = ends
        if g < s.own_groups:
            rows = slice(g * y.fine, (g + 1) * y.fine)
            both = [jnp.concatenate([old[rows], new], axis=0) for old, new in zip((last, start), ends)]
        if s.folded and g == s.fine_groups - 1:
            both = [jnp.where(is_first_half, e[:half], pltpu.roll(e[half:], shift, 1)) for e in both]
        at = slice(g * s.fine_rows, g * s.fine_rows + both[0].shape[0])
        first[at] = jnp.where(up, both[0], both[1])
        second[at] = jnp.where(up, both[1], both[0])
    width = EDGE + SPAN
    row, lane = iota((2 * width, x.fine), 0), iota((2 * width, x.fine), 1)
    is_first = row < width
    goes_up = choose(up, is_first, ~is_first)
    slot = jnp.where(is_first, row, row - width)
    from_mid = jnp.where(goes_up, x.mid_all - EDGE + slot, slot)
    from_coarse = slot - EDGE + jnp.where(goes_up, x.mid_all + x.coarse_all - SPAN, x.mid_all)
    wanted = jnp.where(slot < EDGE, from_mid, from_coarse)
    picked_sums = pick((lane == wanted).astype(BF16), sums[...].reshape(s.sum_planes * s.sum_rows, x.fine))
    spare = s.sum_blocks * 128 - picked_sums.shape[1]
    if spare:
        picked_sums = jnp.concatenate([picked_sums, jnp.zeros((2 * width, spare), F32)], axis=1)
    for n, message in enumerate((first, second)):
        rows = picked_sums[n * width : (n + 1) * width]
        for b in range(s.coarse_blocks):
            at = s.fine_ends + b * width
            message[at : at + width] = rows[:, b * 128 : (b + 1) * 128]
        for b in range(s.coarse_blocks, s.sum_blocks):
            at = s.mid_ends + (b - s.coarse_blocks) * up8(EDGE)
            message[at : at + up8(EDGE)] = rows[: up8(EDGE), b * 128 : (b + 1) * 128]


def band(taps, level, offset, valid):
    at = jnp.where(valid, offset + RADIUS, -1)
    out = [jnp.zeros(at.shape, F32) for _ in range(TERMS)]
    for tap in range(TAPS):
        here = at == tap
        out = [jnp.where(here, taps[level, term, tap], total) for term, total in enumerate(out)]
    return out


def dot(a, b):
    return jnp.dot(a, b, precision=EXACT, preferred_element_type=F32)


def z_columns(s):
    return s.z.fine * RADIUS


def lower_x(x):
    return x.index() > 0


def higher_x(x):
    return x.index() < x.count - 1


def later_kernel(s, taps, ends, table):
    y, x = s.y, s.x
    for level in range(2):
        for term in range(TERMS):
            for tap in range(TAPS):
                table[(level * TERMS + term) * TAPS + tap] = jnp.full((8, x.fine), taps[level, term, tap], F32)
    is_second = iota((8, x.fine), 1) >= x.fine // TERMS
    for tap in range(TAPS):
        table[2 * TERMS * TAPS + tap] = jnp.where(is_second, taps[2, 1, tap], taps[2, 0, tap])

    z, slots, wide = s.z, s.side * s.fine_groups, z_columns(s)
    slot, column = iota((slots, wide), 0), iota((slots, wide), 1)
    where, valid = slot, slot < z.fine
    for n, route in enumerate(s.z_routes):
        lower, i, first = route.below(), z.index(), z.fine + n * RADIUS
        here = (slot >= first) & (slot < first + RADIUS)
        where = jnp.where(here, slot - first + jnp.where(lower, -RADIUS, z.fine), where)
        valid = choose(here, choose(lower, i >= 1, i + 1 < z.count), valid)
    planes = band(taps, 0, where - column // RADIUS, valid)
    r, c = iota((RADIUS, wide), 0), iota((RADIUS, wide), 1) % RADIUS
    cells = (slots, RADIUS, wide)
    for side, (offset, valid) in enumerate(((r - c - RADIUS, lower_x(x)), (r - c + RADIUS, higher_x(x)))):
        columns = band(taps, 0, offset, choose(valid, r >= 0, r < 0))
        for term in range(TERMS):
            joint = jnp.broadcast_to(planes[term][:, None, :], cells) * jnp.broadcast_to(columns[term][None], cells)
            high, low = split(joint.reshape(slots * RADIUS, wide))
            at = 2 * term + side
            ends[at, : slots * RADIUS] = high
            ends[at, slots * RADIUS : 2 * slots * RADIUS] = high
            ends[at, 2 * slots * RADIUS :] = low

def operator_kernel(s, taps, x_fine, x_sums, y_own, y_edge, y_fine, y_mid, y_coarse, widen_x, widen_y):
    y, x = s.y, s.x
    own, edge = x.fine, 64
    shape = (own + edge, x.fine)
    row, lane = iota(shape, 0), iota(shape, 1)
    t = row - own
    lower, higher = x.index() > 0, x.index() < x.count - 1
    is_own = row < own

    def place(half, own_place, own_valid, first, count, low_place, high_place):
        is_low = t < half
        r = jnp.where(is_low, t, t - half) - first
        there = (r >= 0) & (r < count) & (t < 2 * half) & choose(is_low, lower, higher)
        valid = choose(is_own, own_valid, there)
        return jnp.where(is_own, own_place, jnp.where(is_low, low_place + r, high_place + r)), valid

    half = s.edge_sums
    cell, column = iota((own, x.fine), 0), iota((own, x.fine), 1)
    fine = band(taps, 0, cell - column, cell >= 0)
    where, valid = place(half, row - 1, row < x.mid_all, 0, EDGE, 2 - EDGE, x.mid - 1)
    mid = band(taps, 1, where - (lane - 1), valid & (lane < x.mid_all))
    first = x.mid_all
    inside = (row >= first) & (row < first + x.coarse_all)
    where, valid = place(half, row - first - 2, inside, EDGE, SPAN, 3 - SPAN, x.coarse - 2)
    side = x.fine // TERMS
    column = lane % side
    terms = band(taps, 2, where - (column - 2), valid & (column < x.coarse_all))
    coarse = terms[0]
    for term in range(1, TERMS):
        coarse = jnp.where(lane >= term * side, terms[term], coarse)
    a, b = iota((x.fine, x.fine), 0), iota((x.fine, x.fine), 1)
    from_mid = jnp.where((a < x.mid_all) & x.holds_mid(a - 1), weight_of(b - 2 * (a - 1)), 0.0)
    c = a % side
    from_coarse = jnp.where((c < x.coarse_all) & x.holds_coarse(c - 2), weight_of(b - 1 - 2 * (c - 2)), 0.0)
    high, low = split(dot(from_coarse, from_mid))
    widen_x[:own] = high
    widen_x[own : 2 * own] = high
    widen_x[2 * own :] = low
    columns = [(x_fine, 0, 0, fine)]
    columns += [(x_sums, half, 0, [dot(m, from_mid) for m in mid])]
    columns += [(x_sums, half, TERMS * x.fine, [coarse])]
    for out, half, at, terms in columns:
        for term, matrix in enumerate(terms):
            high, low = split(matrix)
            cols = slice(at + term * x.fine, at + (term + 1) * x.fine)
            n = 2 * half
            out[0:own, cols] = high[:own]
            out[own : 2 * own, cols] = high[:own]
            out[2 * own : 3 * own, cols] = low[:own]
            if n:
                out[3 * own :, cols] = jnp.zeros((out.shape[0] - 3 * own, x.fine), BF16)
                out[3 * own : 3 * own + n, cols] = high[own : own + n]
                out[3 * own + n : 3 * own + 2 * n, cols] = high[own : own + n]
                out[3 * own + 128 : 3 * own + 128 + n, cols] = low[own : own + n]

    lower, higher = y.index() > 0, y.index() < y.count - 1
    far_below = s.y2_routes[0].below()
    n = up8(y.mid_all)

    def write(out, size, terms):
        part = iota(terms[0].shape, 1) >= 2 * size
        for term, matrix in enumerate(terms):
            high, low = split(matrix)
            n = matrix.shape[0]
            out[term * n : (term + 1) * n] = jnp.where(part, low.astype(F32), high.astype(F32)).astype(BF16)

    def columns_of(rows, size):
        lane = iota((rows, 3 * size), 1)
        return jnp.where(lane >= 2 * size, lane - 2 * size, jnp.where(lane >= size, lane - size, lane))

    c = columns_of(y.fine, s.fine_rows)
    is_low = (c >= y.fine) & (c < y.fine + RADIUS)
    is_high = c >= y.fine + RADIUS
    where = jnp.where(is_low, c - y.fine - RADIUS, jnp.where(is_high, c - RADIUS, c))
    valid = choose(is_low, lower, choose(is_high, higher, c >= 0))
    write(y_fine, s.fine_rows, band(taps, 0, where - iota(c.shape, 0), valid))
    c = columns_of(y.fine, y.fine)
    write(y_own, y.fine, band(taps, 0, c - iota(c.shape, 0), c >= 0))
    c = columns_of(y.fine, 2 * RADIUS)
    where = jnp.where(c < RADIUS, c - RADIUS, c - RADIUS + y.fine)
    write(y_edge, 2 * RADIUS, band(taps, 0, where - iota(c.shape, 0), choose(c < RADIUS, lower, higher)))

    c = columns_of(n, s.sum_rows)
    r = iota(c.shape, 0)
    is_low = (c >= s.low) & (c < s.low + SPAN)
    is_high = (c >= s.high) & (c < s.high + SPAN)
    is_far = (c >= s.far) & (c < s.far + y.second)
    where = jnp.where(is_low, c - s.low + 2 - SPAN, jnp.where(is_high, c - s.high + y.mid - 1, c - 1))
    valid = choose(is_low, lower, choose(is_high, higher, c < y.mid_all))
    mid = band(taps, 1, where - (r - 1), valid & (r < y.mid_all))
    far = jnp.where(far_below, -2 - y.coarse, 2 * y.coarse - 2)
    where = jnp.where(is_low, c - s.low + 3 - SPAN, jnp.where(is_high, c - s.high + y.coarse - 2, c - 2))
    where = jnp.where(is_far, c - s.far + far, where)
    valid = choose(is_low, lower, choose(is_high, higher, (c < y.coarse_all) | is_far))
    coarse = band(taps, 2, where - (r - 2), valid & (r < y.coarse_all))
    o, k = iota((y.fine, n), 0), iota((y.fine, n), 1)
    from_mid = jnp.where((k < y.mid_all) & y.holds_mid(k - 1), weight_of(o - 2 * (k - 1)), 0.0)
    m = s.coarse_rows
    c = columns_of(n, m)
    k = iota(c.shape, 0)
    from_coarse = jnp.where((c < y.coarse_all) & y.holds_coarse(c - 2), weight_of(k - 1 - 2 * (c - 2)), 0.0)
    write(y_mid, s.sum_rows, [dot(from_mid, matrix) for matrix in mid])
    write(y_coarse, s.sum_rows, [matrix[:m] for matrix in coarse])
    write(widen_y, m, [dot(from_mid, from_coarse)])


def contract_y(s, weights, high, low):
    joined = jnp.concatenate([high, low, high], axis=0)
    result = jnp.dot(weights[...], joined, preferred_element_type=F32)
    n, m = s.y.fine, s.x.fine
    return [result[t * n : (t + 1) * n, t * m : (t + 1) * m] for t in range(TERMS)]


def contract_z(table, level, held, base, count):
    rows = held.shape[2:]
    totals = [None] * count
    for t in range(held.shape[1]):
        for j in range(count + TAPS - 1):
            plane = held[base + j, t].reshape(rows[0] // 8, 8, rows[1])
            for i in range(max(0, j - TAPS + 1), min(count, j + 1)):
                term = table[(level * TERMS + t) * TAPS + j - i][None] * plane
                totals[i] = term if totals[i] is None else totals[i] + term
    return [total.reshape(rows) for total in totals]


def slab_starts(s, below_at, above_at):
    result = []
    for route in s.z_routes:
        lower, i = route.below(), s.z.index()
        valid = choose(lower, i >= 1, i + 1 < s.z.count)
        result.append((jnp.where(lower, below_at, above_at), valid))
    return result


def store_terms(held, at, valid, parts):
    for t, part in enumerate(parts):
        held[at, t] = part if valid is None else jnp.where(valid, part, 0.0)


BLOCK = 4


def clear_ends(held, own):
    zeros = jnp.zeros((RADIUS,) + held.shape[1:], F32)
    held[:RADIUS] = zeros
    held[RADIUS + own :] = zeros


def fine_places(s):
    places = [(RADIUS + p, None) for p in range(s.z.fine)]
    for start, valid in slab_starts(s, 0, s.z.fine + RADIUS):
        places += [(start + p, valid) for p in range(RADIUS)]
    return places


def contract_x(s, grid, weights):
    high, low = split(grid)
    joined = jnp.concatenate([high, low, high], axis=1)
    return jnp.dot(joined, weights[: 3 * s.x.fine], preferred_element_type=F32)


def own_kernel(s, table, t_part, fine, slab, sums, x_fine, x_sums, y_edge, y_fine, fine_part, sums_part, t_fine):
    z, x = s.z, s.x
    t_fine[...] = t_part[...]
    fine_at = fine_places(s)

    def slab_group(g, count):
        n = s.fine_rows
        planes = jnp.concatenate([slab[g : g + count], fine[z.fine + g : z.fine + g + count]], axis=1)
        a, b = split(contract_x(s, planes.reshape(count * n, x.fine), x_fine))
        for p in range(count):
            rows = slice(p * n, (p + 1) * n)
            store_terms(t_fine, *fine_at[z.fine + g + p], contract_y(s, y_fine, a[rows], b[rows]))

    def fine_group(g, count):
        n = 2 * RADIUS
        a, b = split(contract_x(s, fine[g : g + count].reshape(count * n, x.fine), x_fine))
        for p in range(count):
            rows = slice(p * n, (p + 1) * n)
            at, valid = fine_at[g + p]
            for t, part in enumerate(contract_y(s, y_edge, a[rows], b[rows])):
                t_fine[at, t] = t_fine[at, t] + (part if valid is None else jnp.where(valid, part, 0.0))

    def fine_block(k):
        for i, total in enumerate(contract_z(table, 0, t_fine, k, BLOCK)):
            fine_part[k + i] = total

    def sum_part(g, count):
        n = s.sum_rows
        grid = sums[g : g + count].reshape(count * n, x.fine)
        sums_part[g * n : (g + count) * n] = contract_x(s, grid, x_sums)

    later = []
    done = 0
    for g in range(0, s.fine_planes - z.fine, 8):
        slab_group(g, 8)
    for g in range(0, z.fine, 8):
        fine_group(g, 8)
        while later:
            later.pop(0)()
        if g >= 0:
            ready = g if g + 8 < z.fine else z.fine
            later += [lambda k=k: fine_block(k) for k in range(done, ready, BLOCK)]
            done = max(done, ready)
    starts = list(range(0, s.sum_planes, 8))
    while later or starts:
        if starts:
            sum_part(starts[0], min(8, s.sum_planes - starts[0]))
            starts.pop(0)
        if later:
            later.pop(0)()


def sum_kernel(s, table, fine, sums, first, second, x_sums, ends, y_fine, y_mid, y_coarse, widen_x, widen_y, result, *scratch):
    sums_ends, t_mid, t_coarse, p_mid, p_coarse, narrow, out, left = scratch
    z, y, x = s.z, s.y, s.x
    below = s.x_routes[0].below()
    half = s.edge_sums
    def ends_of(start, rows):
        one, two = first[start : start + rows], second[start : start + rows]
        return jnp.where(below, one, two), jnp.where(below, two, one)

    for b in range(s.sum_blocks):
        if b < s.coarse_blocks:
            pair = ends_of(s.fine_ends + b * half, half)
        else:
            rest = jnp.zeros((half - up8(EDGE), 128), F32)
            pair = ends_of(s.mid_ends + (b - s.coarse_blocks) * up8(EDGE), up8(EDGE))
            pair = [jnp.concatenate([ends, rest], axis=0) for ends in pair]
        rows = jnp.concatenate(pair, axis=0)
        zeros = jnp.zeros((128 - 4 * half, 128), F32)
        sums_ends[b * 128 : (b + 1) * 128] = jnp.concatenate([rows, rows, zeros], axis=0).T

    def along_x(start, rows):
        edge = sums_ends[start : start + rows]
        edge_high = edge.astype(BF16)
        is_high = iota(edge.shape, 1) < 2 * half
        packed = jnp.where(is_high, edge, edge - edge_high.astype(F32)).astype(BF16)
        joined = jnp.concatenate([packed, edge_high], axis=1)
        part = jnp.dot(joined, x_sums[3 * x.fine :], preferred_element_type=F32)
        return split(sums[start : start + rows] + part)

    def fine_edges():
        columns = []
        for flip in range(2):
            for g in range(s.fine_groups):
                is_folded = s.folded and g == s.fine_groups - 1
                at = slice(g * s.fine_rows, s.fine_ends if is_folded else (g + 1) * s.fine_rows)
                pair = (first[at], second[at])
                ends_here = jnp.where(below, pair[flip], pair[1 - flip])
                if is_folded:
                    ends_here = jnp.concatenate([ends_here, pltpu.roll(ends_here, x.fine // 2, 1)], axis=0)
                columns.append(ends_here)
        high, low = split(jnp.concatenate(columns, axis=1))
        joined = jnp.concatenate([high, low, high], axis=0)
        high, low = split(jnp.dot(y_fine[...], joined, preferred_element_type=F32))
        width = s.fine_groups * x.fine
        result = []
        for side in range(2):
            total = 0.0
            for t in range(TERMS):
                rows, cols = slice(t * y.fine, (t + 1) * y.fine), slice(side * width, (side + 1) * width)
                a, b = high[rows, cols], low[rows, cols]
                joined = jnp.concatenate([a, b, a], axis=1)
                total = total + jnp.dot(joined, ends[2 * t + side], preferred_element_type=F32)
            result.append(total)
        return result

    clear_ends(t_mid, z.mid_all)
    clear_ends(t_coarse, z.coarse_all)
    mid_at = [(RADIUS + p, None) for p in range(z.mid_all)]
    mid_at, rest_at = mid_at[: z.coarse_all], mid_at[z.coarse_all :]
    coarse_at = [(RADIUS + p, None) for p in range(z.coarse_all)]
    for start, valid in slab_starts(s, 0, z.mid + 3 + RADIUS):
        mid_at += [(start + p, valid) for p in range(RADIUS)]
    mid_at += rest_at
    for start, valid in slab_starts(s, 0, z.coarse + 5 + RADIUS):
        coarse_at += [(start + p, valid) for p in range(RADIUS)]
    coarse_at += [(None, None)] * len(rest_at)
    is_second = iota((s.coarse_rows, x.fine), 1) >= x.fine // TERMS

    def sum_group(g, count):
        n = s.sum_rows
        a, b = along_x(g * n, count * n)
        for p in range(count):
            rows = slice(p * n, (p + 1) * n)
            at, valid = mid_at[g + p]
            cols = slice(0, TERMS * x.fine)
            store_terms(t_mid, at, valid, contract_y(s, y_mid, a[rows, cols], b[rows, cols]))
            at, valid = coarse_at[g + p]
            if at is not None:
                cols = slice(TERMS * x.fine, (TERMS + 1) * x.fine)
                joined = jnp.concatenate([a[rows, cols], b[rows, cols], a[rows, cols]], axis=0)
                both = jnp.dot(y_coarse[...], joined, preferred_element_type=F32)
                m = s.coarse_rows
                store_terms(t_coarse, at, valid, [jnp.where(is_second, both[m:], both[:m])])

    def coarse_block(k):
        count = min(BLOCK, z.coarse_all - k)
        for i, total in enumerate(contract_z(table, 2, t_coarse, k, count)):
            narrow[k + i] = jnp.where(z.holds_coarse(k + i - 2), total, 0.0)

    def widen():
        m = s.coarse_rows
        high, low = split(narrow[...].reshape(z.coarse_all * m, x.fine))
        joined = jnp.concatenate([high, low, high], axis=1)
        high, low = split(jnp.dot(joined, widen_x[...], preferred_element_type=F32))
        for p in range(z.coarse_all):
            rows = slice(p * m, (p + 1) * m)
            joined = jnp.concatenate([high[rows], low[rows], high[rows]], axis=0)
            p_coarse[p] = jnp.dot(widen_y[...], joined, preferred_element_type=F32)

    def mid_block(k):
        count = min(BLOCK, z.mid_all - k)
        for i, total in enumerate(contract_z(table, 1, t_mid, k, count)):
            m = k + i - 1
            for offset, weight in WEIGHTS:
                if (m - offset) % 2 == 0 and 0 <= (m - offset) // 2 + 2 < z.coarse_all:
                    total = total + weight * p_coarse[(m - offset) // 2 + 2]
            p_mid[k + i] = jnp.where(z.holds_mid(m), total, 0.0)

    edges = fine_edges()
    lane = iota((y.fine, x.fine), 1)

    def begin(k):
        block, at = k // s.side, k % s.side * RADIUS
        low, high = (edge[:, block * x.fine : (block + 1) * x.fine] for edge in edges)
        low = pltpu.roll(low, -at % x.fine, 1) if at else low
        turn = (x.fine - RADIUS - at) % x.fine
        high = pltpu.roll(high, turn, 1) if turn else high
        out[k] = fine[k] + jnp.where(lane < RADIUS, low, jnp.where(lane >= x.fine - RADIUS, high, 0.0))

    def finish(k):
        total = out[k]
        for offset, weight in WEIGHTS:
            if (k - offset) % 2 == 0:
                total = total + weight * p_mid[(k - offset) // 2 + 1]
        out[k] = total

    groups = list(range(0, s.sum_planes, 14))
    share = -(-z.fine // len(groups))
    for n, g in enumerate(groups):
        sum_group(g, min(14, s.sum_planes - g))
        for k in range(n * share, min((n + 1) * share, z.fine)):
            begin(k)
    for k in range(0, z.coarse_all, BLOCK):
        coarse_block(k)
    widen()
    done, copies = 0, []
    for k in range(0, z.mid_all, BLOCK):
        mid_block(k)
        ready = z.fine if k + BLOCK >= z.mid_all else 2 * k + 2
        while done < ready:
            finish(done)
            done += 1
            if done % 8 == 0:
                part = pl.ds(done - 8, 8)
                copies.append(pltpu.make_async_copy(out.at[part], result.at[part], left.at[done // 8 - 1]))
                copies[-1].start()
    for copy in copies:
        copy.wait()


def call(kernel, outs, ins, scratch=(), flops=10**7, out_space=pltpu.VMEM):
    specs = [SMEM if a.ndim == 3 and a.shape[-1] == TAPS else VMEM for a in ins]
    size = sum(a.size * a.dtype.itemsize for a in ins) + sum(o.size * o.dtype.itemsize for o in outs)
    return pl.pallas_call(
        kernel,
        out_shape=tuple(outs),
        in_specs=specs,
        out_specs=tuple(pl.BlockSpec(memory_space=out_space) for _ in outs),
        scratch_shapes=list(scratch),
        compiler_params=PARAMS,
        cost_estimate=pl.CostEstimate(flops=flops, bytes_accessed=size, transcendentals=0),
    )(*ins)


def array(*shape, dtype=F32):
    return jax.ShapeDtypeStruct(shape, dtype)


def local(charges, kernel_taps):
    z, y, x = (Cut(name, size) for name, size in zip(("gz", "gy", "gx"), charges.shape))
    s = Sizes(z, y, x)
    n = x.fine
    nz, nz2 = len(s.z_routes), len(s.z2_routes)

    def bound(kernel, *static):
        return lambda *refs: kernel(s, *static, *refs)

    rows = up8(y.mid_all)
    (weights,) = call(bound(narrow_kernel), [array(n, 2 * n, dtype=BF16)], [], flops=10**10)
    held, own, ahead, behind, far, *messages = call(
        bound(restrict_kernel, nz),
        [array(*charges.shape), array(z.mid_all, rows, n)] + [array(s.y_rows, n)] * 2 + [array(s.far_rows, n)] + [array(s.z_rows, n)] * nz + [array(s.z2_rows, n)] * nz2,
        [charges, weights],
        [
            pltpu.VMEM((z.fine, y.fine + 32, n), F32),
            pltpu.VMEM((z.mid_all, rows, n), F32),
            pltpu.VMEM((z.mid_all, up8(y.mid + 24), n), F32),
            pltpu.VMEM((z.mid_all, rows, n), F32),
            pltpu.VMEM((2, max(s.z_rows - s.z_fine, s.y_rows - s.y_fine), n), F32),
            pltpu.VMEM((s.far_groups, s.far_rows, n), F32),
        ],
    )
    z_got = [route(m) for route, m in zip(s.z_routes + s.z2_routes, messages)]
    sides = [s.y_routes[0](ahead), s.y_routes[1](behind)]
    far = s.y2_routes[0](far)
    passed = call(
        bound(pass_kernel, nz),
        [array(RADIUS * s.inner + s.far_rows, n)] * nz + [array(s.far_rows, n)] * nz2,
        [far, held],
        flops=15 * 10**8,
    )
    operators = call(
        bound(operator_kernel),
        [
            array(3 * n, TERMS * n, dtype=BF16),
            array(3 * n + 256, (TERMS + 1) * n, dtype=BF16),
            array(TERMS * y.fine, 3 * y.fine, dtype=BF16),
            array(TERMS * y.fine, 6 * RADIUS, dtype=BF16),
            array(TERMS * y.fine, 3 * s.fine_rows, dtype=BF16),
            array(TERMS * y.fine, 3 * s.sum_rows, dtype=BF16),
            array(TERMS * s.coarse_rows, 3 * s.sum_rows, dtype=BF16),
            array(3 * n, n, dtype=BF16),
            array(y.fine, 3 * s.coarse_rows, dtype=BF16),
        ],
        [kernel_taps],
    )
    later = call(
        bound(later_kernel),
        [array(2 * TERMS, 3 * s.fine_groups * n, z_columns(s), dtype=BF16), array((2 * TERMS + 1) * TAPS, 8, n)],
        [kernel_taps],
    )
    ends, table = later
    ahead, behind = call(
        bound(spread_kernel, nz, nz2),
        [array(s.slab_rows, n), array(s.slab_rows, n)],
        [passed[0], *z_got],
        [pltpu.VMEM((3, up8(max(s.slab_coarse, s.slab_rows - s.slab_fine)) + 8, n), F32)],
    )
    sides += [s.y_routes[0](ahead), s.y_routes[1](behind)]
    fars = [far] + [route(m) for route, m in zip(s.z_routes + s.z2_routes, passed)]
    x_fine, x_sums, y_own, y_edge, y_fine, y_mid, y_coarse, widen_x, widen_y = operators
    t_part, last, start = call(
        bound(early_kernel),
        [array(z.fine + 2 * RADIUS, TERMS, y.fine, n)] + [array(s.own_groups * y.fine, n)] * 2,
        [held, x_fine, y_own, table],
    )
    fine, slab, sums, first, second = call(
        bound(collect_kernel, nz, nz2),
        [
            array(s.fine_planes, 2 * RADIUS, n),
            array(nz * RADIUS, y.fine, n),
            array(s.sum_planes, s.sum_rows, n),
            array(s.x_rows, n),
            array(s.x_rows, n),
        ],
        [last, start, own, *z_got, *sides, *fars],
        [
            pltpu.VMEM((s.slab_planes, s.sum_rows, n), F32),
            pltpu.VMEM((1 + nz + nz2, z.coarse_all, 8, n), F32),
            pltpu.VMEM((2, up8(s.slab_coarse) + 8, n), F32),
        ],
    )
    first, second = s.x_routes[0](first), s.x_routes[1](second)
    fine, sums = call(
        bound(own_kernel),
        [array(z.fine, y.fine, n), array(s.sum_planes * s.sum_rows, (TERMS + 1) * n)],
        [table, t_part, fine, slab, sums, x_fine, x_sums, y_edge, y_fine],
        [pltpu.VMEM((z.fine + 2 * RADIUS, TERMS, y.fine, n), F32)],
    )
    (out,) = call(
        bound(sum_kernel),
        [array(z.fine, y.fine, n)],
        [table, fine, sums, first, second, x_sums, ends, y_fine, y_mid, y_coarse, widen_x, widen_y],
        [
            pltpu.VMEM((s.sum_blocks * 128, n), F32),
            pltpu.VMEM((z.mid + 2 * RADIUS + 3, TERMS, y.fine, n), F32),
            pltpu.VMEM((z.coarse + 2 * RADIUS + 5, 1, s.coarse_rows, n), F32),
            pltpu.VMEM((z.mid_all, y.fine, n), F32),
            pltpu.VMEM((z.coarse_all, y.fine, n), F32),
            pltpu.VMEM((z.coarse_all, s.coarse_rows, n), F32),
            pltpu.VMEM((z.fine, y.fine, n), F32),
            pltpu.SemaphoreType.DMA((z.fine // 8,)),
        ],
        out_space=pltpu.HBM,
    )
    return out


def solution(mesh):
    return jax.shard_map(
        local,
        mesh=mesh,
        in_specs=(P("gz", "gy", "gx"), P()),
        out_specs=P("gz", "gy", "gx"),
        check_vma=False,
    )
```

```python
import jax
import jax.numpy as jnp
from jax import lax
from jax.experimental import pallas as pl
from jax.experimental.pallas import tpu as pltpu
from jax.sharding import PartitionSpec as P

RADIUS = 8
TAPS = 17
TERMS = 2
WEIGHTS = ((-3, -0.0625), (-1, 0.5625), (0, 1.0), (1, 0.5625), (3, -0.0625))
EXACT = lax.Precision.HIGHEST
SPAN = RADIUS + 5
EDGE = RADIUS + 3
F32, BF16 = jnp.float32, jnp.bfloat16
PARAMS = pltpu.CompilerParams(vmem_limit_bytes=32 * 1024 * 1024)
VMEM = pl.BlockSpec(memory_space=pltpu.VMEM)
SMEM = pl.BlockSpec(memory_space=pltpu.SMEM)


def up8(n):
    return -(-n // 8) * 8


def iota(shape, dim):
    return lax.broadcasted_iota(jnp.int32, shape, dim)


def weight_of(difference):
    size = jnp.abs(difference)
    out = jnp.where(size == 1, 0.5625, jnp.where(size == 3, -0.0625, 0.0))
    return jnp.where(size == 0, 1.0, out)


def choose(condition, a, b):
    return jnp.where(condition, jnp.where(a, 1, 0), jnp.where(b, 1, 0)) != 0


class Cut:
    def __init__(self, name, length):
        self.name, self.fine = name, length
        self.count = lax.axis_size(name)
        self.mid, self.coarse = length // 2, length // 4
        self.mid_all, self.coarse_all = self.mid + 3, self.coarse + 5
        self.second = max(SPAN - self.coarse, 0)

    def index(self):
        return lax.axis_index(self.name)

    def holds_mid(self, k):
        k = k + self.index() * self.mid
        return (k >= 0) & (k < self.mid * self.count)

    def holds_coarse(self, k):
        k = k + self.index() * self.coarse
        return (k >= 0) & (k < self.coarse * self.count)


class Route:
    def __init__(self, names, pairs, up, below):
        self.names, self.pairs, self.up, self.below = names, pairs, up, below

    def __call__(self, x):
        return lax.ppermute(x, self.names, self.pairs)


def flip(pairs):
    return [(b, a) for a, b in pairs]


def swap(cut, steps):
    pairs = [(i, i + steps) for i in range(cut.count - steps)]

    def up():
        return cut.index() + steps < cut.count

    return [Route(cut.name, pairs + flip(pairs), up, lambda: ~up())]


def both_ways(cut, steps):
    pairs = [(i, i + steps) for i in range(cut.count - steps)]
    yes, no = (lambda: cut.index() >= 0), (lambda: cut.index() < 0)
    return [Route(cut.name, pairs, yes, yes), Route(cut.name, flip(pairs), no, no)]


def folded(cut, beside, names):
    n, m = cut.count, lax.axis_size(beside)

    def place(c, i):
        return c * n + i if names[0] == beside else i * m + c

    pairs = []
    for c in range(0, m, 2):
        cycle = [place(c, i) for i in range(n)] + [place(c + 1, i) for i in reversed(range(n))]
        pairs += list(zip(cycle, cycle[1:] + cycle[:1]))

    def even():
        return lax.axis_index(beside) % 2 == 0

    def odd():
        return lax.axis_index(beside) % 2 == 1

    return [Route(names, pairs, even, even), Route(names, flip(pairs), odd, odd)]


def split(x):
    high = x.astype(BF16)
    return high, (x - high.astype(F32)).astype(BF16)


def pick(selector, x):
    nt = (((1,), (1,)), ((), ()))
    a = x.astype(BF16)
    rest = x - a.astype(F32)
    b = rest.astype(BF16)
    c = (rest - b.astype(F32)).astype(BF16)
    out = lax.dot_general(selector, c, nt, preferred_element_type=F32)
    out = out + lax.dot_general(selector, b, nt, preferred_element_type=F32)
    return out + lax.dot_general(selector, a, nt, preferred_element_type=F32)


class Sizes:
    def place_of(self, p):
        return p if p < self.slab_start else p + self.coarse_planes - self.slab_start

    def __init__(self, z, y, x):
        self.z, self.y, self.x = z, y, x
        self.z_routes = swap(z, 1) if z.count <= 2 else both_ways(z, 1)
        self.z2_routes = [] if z.count <= 2 else swap(z, 2) if z.count <= 4 else both_ways(z, 2)
        self.y_routes = folded(y, x.name, (x.name, y.name))
        self.y2_routes = swap(y, 2)
        self.x_routes = folded(x, z.name, (x.name, z.name))
        self.inner = y.fine - 2 * RADIUS
        self.z_fine = RADIUS * 2 * RADIUS
        self.z_sums = max(EDGE * y.mid_all, SPAN * y.coarse_all)
        self.z_rows = up8(self.z_fine + self.z_sums)
        self.z2_rows = up8(z.second * y.coarse_all)
        self.slab_planes = SPAN * len(self.z_routes) + z.second * len(self.z2_routes)
        self.fine_planes = z.fine + RADIUS * len(self.z_routes)
        self.sum_planes = z.mid_all + RADIUS * len(self.z_routes)
        self.coarse_rows = -(-y.coarse_all // 16) * 16
        self.y_fine = RADIUS * z.fine
        self.y_sums = max(EDGE * z.mid_all, SPAN * z.coarse_all)
        self.y_rows = up8(self.y_fine + self.y_sums)
        self.slab_fine = RADIUS * RADIUS * len(self.z_routes)
        self.slab_mid = EDGE * EDGE * len(self.z_routes)
        self.slab_coarse = SPAN * self.slab_planes
        self.extra = max(self.slab_coarse - self.slab_mid, 0)
        self.spare = x.fine - x.mid_all - x.coarse_all
        self.pieces = -(-x.coarse_all // max(self.spare, 1))
        if self.pieces * self.extra > self.slab_mid:
            self.extra = 0
        self.slab_sums = max(self.slab_mid, self.slab_coarse - self.extra)
        self.slab_rows = up8(self.slab_fine + self.slab_sums)
        self.far_groups = x.fine // x.coarse_all
        self.far_planes = -(-z.coarse_all // self.far_groups)
        self.far_rows = up8(y.second * self.far_planes)
        self.slab_start = z.coarse_all
        self.coarse_planes = z.coarse_all + RADIUS * len(self.z_routes)
        self.fine_rows = y.fine + 2 * RADIUS
        self.far = y.coarse_all
        self.low = y.mid_all
        self.high = self.low + SPAN
        self.sum_rows = -(-(self.high + SPAN) // 16) * 16
        self.edge_sums = EDGE + SPAN
        self.side = x.fine // RADIUS
        self.fine_groups = -(-self.fine_planes // self.side)
        assert z.fine % self.side == 0
        self.own_groups = z.fine // self.side
        self.folded = 0 < self.fine_planes % self.side <= self.side // 2
        self.fine_ends = self.fine_groups * self.fine_rows - (self.fine_rows // 2 if self.folded else 0)
        self.sum_blocks = -(-self.sum_planes * self.sum_rows // 128)
        self.coarse_blocks = -(-self.coarse_planes * self.sum_rows // 128)
        self.mid_ends = self.fine_ends + self.coarse_blocks * self.edge_sums
        self.x_rows = self.mid_ends + (self.sum_blocks - self.coarse_blocks) * up8(EDGE)
        assert x.mid_all + x.coarse_all <= x.fine
        assert self.far + y.second <= self.low and y.second <= 8 and y.coarse_all == SPAN and z.coarse_all == SPAN
        assert z.coarse >= RADIUS and y.coarse >= RADIUS and y.count == 4


def narrow_kernel(s, out):
    x = s.x
    lanes = (x.fine, x.fine)
    cell, lane = iota(lanes, 0), iota(lanes, 1)
    k = lane - 1
    to_mid = jnp.where((lane < x.mid_all) & x.holds_mid(k), weight_of(cell - 2 * k), 0.0)
    c = lane - x.mid_all - 2
    inside = (lane >= x.mid_all) & (lane < x.mid_all + x.coarse_all) & x.holds_coarse(c)
    to_coarse = jnp.where(inside, weight_of(cell - 1 - 2 * c), 0.0)
    narrow = to_mid + jnp.dot(to_mid, to_coarse, precision=EXACT, preferred_element_type=F32)
    out[...] = jnp.concatenate(split(narrow), axis=1)


def restrict_kernel(s, nz, source, narrow, charges, own, ahead, behind, far, *rest):
    messages, (wide, mid, high, coarse, packed, groups) = rest[:-6], rest[-6:]
    z, y, x = s.z, s.y, s.x
    wide[:, :8] = jnp.zeros((z.fine, 8, x.fine), F32)
    wide[:, 8 + y.fine :] = jnp.zeros((z.fine, wide.shape[1] - 8 - y.fine, x.fine), F32)
    charges[...] = source[...]
    cells = source[...].reshape(z.fine * y.fine, x.fine)
    top, rest = cells.astype(BF16), cells
    rest = rest - top.astype(F32)
    middle = rest.astype(BF16)
    low = (rest - middle.astype(F32)).astype(BF16)
    weights = narrow[...]
    both = jnp.dot(low, weights, preferred_element_type=F32)
    both = both + jnp.dot(
        jnp.concatenate([top, middle], axis=1), jnp.concatenate([weights, weights], axis=0), preferred_element_type=F32
    )
    reduced = both[:, : x.fine] + both[:, x.fine :]
    wide[:, 8 : 8 + y.fine, :] = reduced.reshape(z.fine, y.fine, x.fine)
    rows = 0.0
    for offset, weight in WEIGHTS:
        rows = rows + weight * wide[:, pl.ds(6 + offset, y.mid_all, stride=2), :]
    keep = y.holds_mid(iota((y.mid_all, x.fine), 0) - 1)
    mid[...] = jnp.zeros(mid.shape, F32)
    coarse[...] = jnp.zeros(coarse.shape, F32)
    high[...] = jnp.zeros(high.shape, F32)
    for p in range(z.mid_all):
        total = 0.0
        for offset, weight in WEIGHTS:
            at = 2 * (p - 1) + offset
            if 0 <= at < z.fine:
                total = total + weight * rows[at]
        total = jnp.where(keep & z.holds_mid(p - 1), total, 0.0)
        mid[p, : y.mid_all] = total
        high[p, 8 : 8 + y.mid_all] = total
    rows = 0.0
    for offset, weight in WEIGHTS:
        rows = rows + weight * high[:, pl.ds(5 + offset, y.coarse_all, stride=2), :]
    keep = y.holds_coarse(iota((y.coarse_all, x.fine), 0) - 2)
    for p in range(z.coarse_all):
        total = 0.0
        for offset, weight in WEIGHTS:
            at = 2 * (p - 2) + offset + 1
            if 0 <= at < z.mid_all:
                total = total + weight * rows[at]
        coarse[p, : y.coarse_all] = jnp.where(keep & z.holds_coarse(p - 2), total, 0.0)
    is_mid = iota(mid.shape[1:], 1) < x.mid_all
    for p in range(z.mid_all):
        own[p] = jnp.where(is_mid, mid[p], coarse[p]) if p < z.coarse_all else jnp.where(is_mid, mid[p], 0.0)
    up = s.y2_routes[0].up()
    count, end = y.second, y.coarse_all
    groups[...] = jnp.zeros(groups.shape, F32)
    for p in range(z.coarse_all):
        g, at = p // s.far_planes, p % s.far_planes * count
        groups[g, at : at + count] = jnp.where(up, own[p, end - count : end], own[p, :count])
    lane = iota(far.shape, 1)
    total = jnp.zeros(far.shape, F32)
    for g in range(s.far_groups):
        first = g * x.coarse_all
        turned = pltpu.roll(groups[g], (first - x.mid_all) % x.fine, 1)
        total = jnp.where((lane >= first) & (lane < first + x.coarse_all), turned, total)
    far[...] = total
    for message, route in zip((ahead, behind), s.y_routes):
        up = route.up()
        edge = jnp.where(up, charges[:, y.fine - RADIUS :, :], charges[:, :RADIUS, :])
        message[: s.y_fine] = edge.reshape(s.y_fine, x.fine)
        packed[...] = jnp.zeros(packed.shape, F32)
        for p in range(z.mid_all):
            packed[0, p * EDGE : (p + 1) * EDGE] = jnp.where(up, mid[p, y.mid_all - EDGE : y.mid_all], mid[p, :EDGE])
        for p in range(z.coarse_all):
            packed[1, p * SPAN : (p + 1) * SPAN] = coarse[p, :SPAN]
        rows = s.y_rows - s.y_fine
        is_mid = iota((rows, x.fine), 1) < x.mid_all
        message[s.y_fine :] = jnp.where(is_mid, packed[0, :rows], packed[1, :rows])
    for message, route in zip(messages, s.z_routes):
        up = route.up().astype(jnp.int32)
        planes = charges[pl.ds(up * (z.fine - RADIUS), RADIUS)]
        outer = jnp.concatenate([planes[:, :RADIUS], planes[:, y.fine - RADIUS :]], axis=1)
        message[: s.z_fine] = outer.reshape(s.z_fine, x.fine)
        packed[...] = jnp.zeros(packed.shape, F32)
        for p in range(EDGE):
            packed[0, p * y.mid_all : (p + 1) * y.mid_all] = mid[up * (z.mid_all - EDGE) + p][: y.mid_all]
        for p in range(SPAN):
            plane = coarse[up * (z.coarse_all - SPAN) + p]
            packed[1, p * y.coarse_all : (p + 1) * y.coarse_all] = plane[: y.coarse_all]
        rows = s.z_rows - s.z_fine
        is_mid = iota((rows, x.fine), 1) < x.mid_all
        message[s.z_fine :] = jnp.where(is_mid, packed[0, :rows], packed[1, :rows])
    for message, route in zip(messages[nz:], s.z2_routes):
        up = route.up().astype(jnp.int32)
        message[...] = jnp.zeros(message.shape, F32)
        for p in range(z.second):
            plane = coarse[up * (z.coarse_all - z.second) + p]
            message[p * y.coarse_all : (p + 1) * y.coarse_all] = plane[: y.coarse_all]


class Slab:
    def __init__(self, message, mid, coarse):
        self.message, self.mid, self.coarse = message, mid, coarse

    def mid_rows(self, first, count):
        return self.message[self.mid + first : self.mid + first + count]

    def coarse_rows(self, first, count):
        return self.message[self.coarse + first : self.coarse + first + count]

    def rows(self, is_mid, first_mid, first_coarse, count):
        coarse = 0.0 if first_coarse is None else self.coarse_rows(first_coarse, count)
        mid = 0.0 if self.mid is None else self.message[self.mid + first_mid : self.mid + first_mid + count]
        return jnp.where(is_mid, mid, coarse)


def slabs(s, z_messages, z2_messages):
    out = []
    for message in z_messages:
        for p in range(SPAN):
            mid = s.z_fine + p * s.y.mid_all if p < EDGE else None
            out.append(Slab(message, mid, s.z_fine + p * s.y.coarse_all))
    for message in z2_messages:
        out += [Slab(message, None, p * s.y.coarse_all) for p in range(s.z.second)]
    return out


def spread_kernel(s, nz, nz2, _, *rest):
    z_messages, z2_messages = rest[:nz], rest[nz : nz + nz2]
    ahead, behind, packed = rest[-3:]
    z, y, x = s.z, s.y, s.x
    planes = slabs(s, z_messages, z2_messages)
    count = s.slab_rows - s.slab_fine
    lane = iota((count, x.fine), 1)
    packed[...] = jnp.zeros(packed.shape, F32)
    for p, plane in enumerate(planes):
        packed[1, p * SPAN : (p + 1) * SPAN] = plane.coarse_rows(0, SPAN)
    for n in range(s.pieces if s.extra else 0):
        first = x.mid_all + n * s.spare
        turned = pltpu.roll(packed[1, s.slab_mid : s.slab_mid + up8(s.extra)], x.fine - s.spare - first, 1)
        packed[2, n * s.extra : (n + 1) * s.extra] = turned[: s.extra]
    coarse = jnp.where(lane < x.fine - s.spare, packed[1, :count], packed[2, :count])
    for message, route in zip((ahead, behind), s.y_routes):
        up = route.up()
        at = 0
        for z_message in z_messages:
            slab = z_message[: s.z_fine].reshape(RADIUS, 2 * RADIUS, x.fine)
            edge = jnp.where(up, slab[:, RADIUS:], slab[:, :RADIUS])
            message[at : at + RADIUS * RADIUS] = edge.reshape(RADIUS * RADIUS, x.fine)
            at += RADIUS * RADIUS
        at = 0
        for plane in planes:
            if plane.mid is not None:
                first, last = plane.mid_rows(0, EDGE), plane.mid_rows(y.mid_all - EDGE, EDGE)
                packed[0, at : at + EDGE] = jnp.where(up, last, first)
                at += EDGE
        message[s.slab_fine :] = jnp.where(lane < x.mid_all, packed[0, :count], coarse)


def pass_kernel(s, nz, far, charges, *outs):
    z, x = s.z, s.x
    rows = RADIUS * s.inner
    for out, route in zip(outs, s.z_routes):
        planes = charges[pl.ds(route.up().astype(jnp.int32) * (z.fine - RADIUS), RADIUS)]
        out[:rows] = planes[:, RADIUS : RADIUS + s.inner].reshape(rows, x.fine)
        out[rows:] = far[...]
    for out in outs[nz:]:
        out[...] = far[...]


def roll_ends(s, plane_rows, count, groups):
    x = s.x
    lane = iota((count, x.fine), 1)
    for g in groups:
        ends = [jnp.zeros(lane.shape, F32)] * 2
        for j in range(min(s.side, s.fine_planes - g * s.side)):
            plane = plane_rows(g * s.side + j)
            here = (lane >= RADIUS * j) & (lane < RADIUS * (j + 1))
            for n, start in enumerate((x.fine - RADIUS, 0)):
                shift = (RADIUS * j - start) % x.fine
                ends[n] = jnp.where(here, pltpu.roll(plane, shift, 1) if shift else plane, ends[n])
        yield g, ends


def early_kernel(s, charges, x_fine, y_own, _, t_part, last, start):
    z, y, x = s.z, s.y, s.x
    t_part[...] = jnp.zeros(t_part.shape, F32)
    for g in range(0, z.fine, 8):
        a, b = split(contract_x(s, charges[g : g + 8].reshape(8 * y.fine, x.fine), x_fine))
        for p in range(8):
            rows = slice(p * y.fine, (p + 1) * y.fine)
            store_terms(t_part, RADIUS + g + p, None, contract_y(s, y_own, a[rows], b[rows]))
    for g, ends in roll_ends(s, lambda p: charges[p], y.fine, range(s.own_groups)):
        rows = slice(g * y.fine, (g + 1) * y.fine)
        last[rows], start[rows] = ends


def collect_kernel(s, nz, nz2, last, start, own, *rest):
    z_messages, z2_messages = rest[:nz], rest[nz : nz + nz2]
    rest = rest[nz + nz2 :]
    pairs = rest[:4]
    fars = rest[4 : 5 + nz + nz2]
    fine, slab, sums, first, second, raw, rows, near = rest[5 + nz + nz2 :]
    z, y, x = s.z, s.y, s.x
    below = s.y_routes[0].below()
    planes = slabs(s, z_messages, z2_messages)

    def sides(which, start, count):
        a, b = (message[start : start + count] for message in pairs[2 * which : 2 * which + 2])
        return jnp.where(below, a, b), jnp.where(below, b, a)

    parts = [(0, z.fine, 0, 0)] + [(z.fine + n * RADIUS, RADIUS, 1, n * RADIUS * RADIUS) for n in range(nz)]
    for at, count, which, row in parts:
        low, high = sides(which, row, RADIUS * count)
        fine[at : at + count, :RADIUS] = low.reshape(count, RADIUS, x.fine)
        fine[at : at + count, RADIUS:] = high.reshape(count, RADIUS, x.fine)
    sums[...] = jnp.zeros(sums.shape, F32)
    raw[...] = jnp.zeros(raw.shape, F32)
    inner_rows = RADIUS * s.inner
    for n, far in enumerate(fars):
        is_joint = 0 < n <= nz
        if is_joint:
            outer = z_messages[n - 1][: s.z_fine].reshape(RADIUS, 2 * RADIUS, x.fine)
            planes_here = slice((n - 1) * RADIUS, n * RADIUS)
            slab[planes_here, :RADIUS] = outer[:, :RADIUS]
            slab[planes_here, RADIUS : RADIUS + s.inner] = far[:inner_rows].reshape(RADIUS, s.inner, x.fine)
            slab[planes_here, RADIUS + s.inner :] = outer[:, RADIUS:]
        two_away = far[inner_rows:] if is_joint else far[...]
        for g in range(s.far_groups):
            turned = pltpu.roll(two_away, (x.mid_all - g * x.coarse_all) % x.fine, 1)
            for p in range(g * s.far_planes, min((g + 1) * s.far_planes, z.coarse_all)):
                at = p % s.far_planes * y.second
                rows[n, p, : y.second] = turned[at : at + y.second]
    is_mid = iota((y.second, x.fine), 1) < x.mid_all

    lane = iota((up8(s.extra), x.fine), 1)
    for side, got in enumerate(sides(1, s.slab_fine, s.slab_sums)):
        near[side, : s.slab_sums] = got
        if s.extra:
            total = jnp.zeros(lane.shape, F32)
            for n in range(s.pieces):
                begin = x.mid_all + n * s.spare
                piece = near[side, n * s.extra : n * s.extra + up8(s.extra)]
                turned = pltpu.roll(piece, begin + s.spare, 1)
                total = jnp.where(lane >= begin, turned, total)
            near[side, s.slab_mid : s.slab_mid + s.extra] = total[: s.extra]
    is_mid_edge = iota((EDGE, x.fine), 1) < x.mid_all
    is_mid_span = iota((SPAN, x.fine), 1) < x.mid_all

    def rows_of_plane(out, p, body, mids, coarses, far_plane):
        out[p, : y.mid_all] = body
        for base, shift, n in ((s.low, SPAN - EDGE, 0), (s.high, 0, 1)):
            if coarses is not None:
                out[p, base : base + SPAN] = jnp.where(is_mid_span, 0.0, coarses[n])
            if mids is not None:
                at = slice(base + shift, base + shift + EDGE)
                out[p, at] = jnp.where(is_mid_edge, mids[n], out[p, at])
        if far_plane is not None:
            at = slice(s.far, s.far + y.second)
            out[p, at] = jnp.where(is_mid, out[p, at], rows[far_plane][: y.second])

    for p in range(z.mid_all):
        far_plane = (0, p) if p < z.coarse_all else None
        mids = sides(0, s.y_fine + p * EDGE, EDGE)
        coarses = sides(0, s.y_fine + p * SPAN, SPAN) if p < z.coarse_all else None
        rows_of_plane(sums, s.place_of(p), own[p, : y.mid_all], mids, coarses, far_plane)
    is_mid_row = iota((SPAN, x.fine), 1) < x.mid_all
    is_mid_rest = iota((y.mid_all - SPAN, x.fine), 1) < x.mid_all
    slab_far = [(1 + n, p) for n in range(nz) for p in range(SPAN)]
    for n, route in enumerate(s.z2_routes):
        at = jnp.where(route.below(), z.coarse_all - z.second, 0)
        slab_far += [(1 + nz + n, at + p) for p in range(z.second)]
    held = 0
    for p, plane in enumerate(planes):
        body = [plane.rows(is_mid_row, 0, 0, SPAN), plane.rows(is_mid_rest, SPAN, None, y.mid_all - SPAN)]
        mids = None
        if plane.mid is not None:
            mids = sides(1, s.slab_fine + held * EDGE, EDGE)
            held += 1
        coarses = [near[side, p * SPAN : (p + 1) * SPAN] for side in range(2)]
        rows_of_plane(raw, p, jnp.concatenate(body, axis=0), mids, coarses, slab_far[p])
    is_mid = iota((s.sum_rows, x.fine), 1) < x.mid_all

    def number(condition, a, b):
        return jnp.where(condition, a, b)

    for n, route in enumerate(s.z_routes):
        lower, base = route.below(), n * SPAN
        for j in range(RADIUS):
            a = raw[base + number(lower, 0, 3) + j]
            b = raw[base + number(lower, SPAN - 5 - RADIUS, 5) + j]
            sums[s.slab_start + n * RADIUS + j] = jnp.where(is_mid, a, b)
        for i in range(3):
            at = number(lower, 0, s.place_of(z.mid)) + i
            sums[at] = sums[at] + jnp.where(is_mid, raw[base + number(lower, EDGE - 3, 0) + i], 0.0)
        for i in range(5):
            at = number(lower, 0, z.coarse) + i
            sums[at] = sums[at] + jnp.where(is_mid, 0.0, raw[base + number(lower, SPAN - 5, 0) + i])
    for n, route in enumerate(s.z2_routes):
        base = len(s.z_routes) * SPAN + n * z.second
        at = s.slab_start + number(route.below(), RADIUS - z.coarse, RADIUS + z.coarse - 5)
        for p in range(z.second):
            sums[at + p] = sums[at + p] + jnp.where(is_mid, 0.0, raw[base + p])

    up = s.x_routes[0].up()
    half, shift = s.fine_rows // 2, x.fine // 2
    is_first_half = iota((half, x.fine), 1) < shift
    own_ends = roll_ends(s, lambda p: fine[p], 2 * RADIUS, range(s.own_groups))
    slab_rows = [jnp.concatenate([slab[p], fine[z.fine + p]], axis=0) for p in range(nz * RADIUS)]
    slab_ends = roll_ends(s, lambda p: slab_rows[p - z.fine], s.fine_rows, range(s.own_groups, s.fine_groups))
    for g, ends in list(own_ends) + list(slab_ends):
        both = ends
        if g < s.own_groups:
            rows = slice(g * y.fine, (g + 1) * y.fine)
            both = [jnp.concatenate([old[rows], new], axis=0) for old, new in zip((last, start), ends)]
        if s.folded and g == s.fine_groups - 1:
            both = [jnp.where(is_first_half, e[:half], pltpu.roll(e[half:], shift, 1)) for e in both]
        at = slice(g * s.fine_rows, g * s.fine_rows + both[0].shape[0])
        first[at] = jnp.where(up, both[0], both[1])
        second[at] = jnp.where(up, both[1], both[0])
    width = EDGE + SPAN
    row, lane = iota((2 * width, x.fine), 0), iota((2 * width, x.fine), 1)
    is_first = row < width
    goes_up = choose(up, is_first, ~is_first)
    slot = jnp.where(is_first, row, row - width)
    from_mid = jnp.where(goes_up, x.mid_all - EDGE + slot, slot)
    from_coarse = slot - EDGE + jnp.where(goes_up, x.mid_all + x.coarse_all - SPAN, x.mid_all)
    wanted = jnp.where(slot < EDGE, from_mid, from_coarse)
    picked_sums = pick((lane == wanted).astype(BF16), sums[...].reshape(s.sum_planes * s.sum_rows, x.fine))
    spare = s.sum_blocks * 128 - picked_sums.shape[1]
    if spare:
        picked_sums = jnp.concatenate([picked_sums, jnp.zeros((2 * width, spare), F32)], axis=1)
    for n, message in enumerate((first, second)):
        rows = picked_sums[n * width : (n + 1) * width]
        for b in range(s.coarse_blocks):
            at = s.fine_ends + b * width
            message[at : at + width] = rows[:, b * 128 : (b + 1) * 128]
        for b in range(s.coarse_blocks, s.sum_blocks):
            at = s.mid_ends + (b - s.coarse_blocks) * up8(EDGE)
            message[at : at + up8(EDGE)] = rows[: up8(EDGE), b * 128 : (b + 1) * 128]


def band(taps, level, offset, valid):
    at = jnp.where(valid, offset + RADIUS, -1)
    out = [jnp.zeros(at.shape, F32) for _ in range(TERMS)]
    for tap in range(TAPS):
        here = at == tap
        out = [jnp.where(here, taps[level, term, tap], total) for term, total in enumerate(out)]
    return out


def dot(a, b):
    return jnp.dot(a, b, precision=EXACT, preferred_element_type=F32)


def z_columns(s):
    return s.z.fine * RADIUS


def lower_x(x):
    return x.index() > 0


def higher_x(x):
    return x.index() < x.count - 1


def later_kernel(s, taps, ends, table):
    y, x = s.y, s.x
    for level in range(2):
        for term in range(TERMS):
            for tap in range(TAPS):
                table[(level * TERMS + term) * TAPS + tap] = jnp.full((8, x.fine), taps[level, term, tap], F32)
    is_second = iota((8, x.fine), 1) >= x.fine // TERMS
    for tap in range(TAPS):
        table[2 * TERMS * TAPS + tap] = jnp.where(is_second, taps[2, 1, tap], taps[2, 0, tap])

    z, slots, wide = s.z, s.side * s.fine_groups, z_columns(s)
    slot, column = iota((slots, wide), 0), iota((slots, wide), 1)
    where, valid = slot, slot < z.fine
    for n, route in enumerate(s.z_routes):
        lower, i, first = route.below(), z.index(), z.fine + n * RADIUS
        here = (slot >= first) & (slot < first + RADIUS)
        where = jnp.where(here, slot - first + jnp.where(lower, -RADIUS, z.fine), where)
        valid = choose(here, choose(lower, i >= 1, i + 1 < z.count), valid)
    planes = band(taps, 0, where - column // RADIUS, valid)
    r, c = iota((RADIUS, wide), 0), iota((RADIUS, wide), 1) % RADIUS
    cells = (slots, RADIUS, wide)
    for side, (offset, valid) in enumerate(((r - c - RADIUS, lower_x(x)), (r - c + RADIUS, higher_x(x)))):
        columns = band(taps, 0, offset, choose(valid, r >= 0, r < 0))
        for term in range(TERMS):
            joint = jnp.broadcast_to(planes[term][:, None, :], cells) * jnp.broadcast_to(columns[term][None], cells)
            high, low = split(joint.reshape(slots * RADIUS, wide))
            at = 2 * term + side
            ends[at, : slots * RADIUS] = high
            ends[at, slots * RADIUS : 2 * slots * RADIUS] = high
            ends[at, 2 * slots * RADIUS :] = low

def operator_kernel(s, taps, x_fine, x_sums, y_own, y_edge, y_fine, y_mid, y_coarse, widen_x, widen_y):
    y, x = s.y, s.x
    own, edge = x.fine, 64
    shape = (own + edge, x.fine)
    row, lane = iota(shape, 0), iota(shape, 1)
    t = row - own
    lower, higher = x.index() > 0, x.index() < x.count - 1
    is_own = row < own

    def place(half, own_place, own_valid, first, count, low_place, high_place):
        is_low = t < half
        r = jnp.where(is_low, t, t - half) - first
        there = (r >= 0) & (r < count) & (t < 2 * half) & choose(is_low, lower, higher)
        valid = choose(is_own, own_valid, there)
        return jnp.where(is_own, own_place, jnp.where(is_low, low_place + r, high_place + r)), valid

    half = s.edge_sums
    cell, column = iota((own, x.fine), 0), iota((own, x.fine), 1)
    fine = band(taps, 0, cell - column, cell >= 0)
    where, valid = place(half, row - 1, row < x.mid_all, 0, EDGE, 2 - EDGE, x.mid - 1)
    mid = band(taps, 1, where - (lane - 1), valid & (lane < x.mid_all))
    first = x.mid_all
    inside = (row >= first) & (row < first + x.coarse_all)
    where, valid = place(half, row - first - 2, inside, EDGE, SPAN, 3 - SPAN, x.coarse - 2)
    side = x.fine // TERMS
    column = lane % side
    terms = band(taps, 2, where - (column - 2), valid & (column < x.coarse_all))
    coarse = terms[0]
    for term in range(1, TERMS):
        coarse = jnp.where(lane >= term * side, terms[term], coarse)
    a, b = iota((x.fine, x.fine), 0), iota((x.fine, x.fine), 1)
    from_mid = jnp.where((a < x.mid_all) & x.holds_mid(a - 1), weight_of(b - 2 * (a - 1)), 0.0)
    c = a % side
    from_coarse = jnp.where((c < x.coarse_all) & x.holds_coarse(c - 2), weight_of(b - 1 - 2 * (c - 2)), 0.0)
    high, low = split(dot(from_coarse, from_mid))
    widen_x[:own] = high
    widen_x[own : 2 * own] = high
    widen_x[2 * own :] = low
    columns = [(x_fine, 0, 0, fine)]
    columns += [(x_sums, half, 0, [dot(m, from_mid) for m in mid])]
    columns += [(x_sums, half, TERMS * x.fine, [coarse])]
    for out, half, at, terms in columns:
        for term, matrix in enumerate(terms):
            high, low = split(matrix)
            cols = slice(at + term * x.fine, at + (term + 1) * x.fine)
            n = 2 * half
            out[0:own, cols] = high[:own]
            out[own : 2 * own, cols] = high[:own]
            out[2 * own : 3 * own, cols] = low[:own]
            if n:
                out[3 * own :, cols] = jnp.zeros((out.shape[0] - 3 * own, x.fine), BF16)
                out[3 * own : 3 * own + n, cols] = high[own : own + n]
                out[3 * own + n : 3 * own + 2 * n, cols] = high[own : own + n]
                out[3 * own + 128 : 3 * own + 128 + n, cols] = low[own : own + n]

    lower, higher = y.index() > 0, y.index() < y.count - 1
    far_below = s.y2_routes[0].below()
    n = up8(y.mid_all)

    def write(out, size, terms):
        part = iota(terms[0].shape, 1) >= 2 * size
        for term, matrix in enumerate(terms):
            high, low = split(matrix)
            n = matrix.shape[0]
            out[term * n : (term + 1) * n] = jnp.where(part, low.astype(F32), high.astype(F32)).astype(BF16)

    def columns_of(rows, size):
        lane = iota((rows, 3 * size), 1)
        return jnp.where(lane >= 2 * size, lane - 2 * size, jnp.where(lane >= size, lane - size, lane))

    c = columns_of(y.fine, s.fine_rows)
    is_low = (c >= y.fine) & (c < y.fine + RADIUS)
    is_high = c >= y.fine + RADIUS
    where = jnp.where(is_low, c - y.fine - RADIUS, jnp.where(is_high, c - RADIUS, c))
    valid = choose(is_low, lower, choose(is_high, higher, c >= 0))
    write(y_fine, s.fine_rows, band(taps, 0, where - iota(c.shape, 0), valid))
    c = columns_of(y.fine, y.fine)
    write(y_own, y.fine, band(taps, 0, c - iota(c.shape, 0), c >= 0))
    c = columns_of(y.fine, 2 * RADIUS)
    where = jnp.where(c < RADIUS, c - RADIUS, c - RADIUS + y.fine)
    write(y_edge, 2 * RADIUS, band(taps, 0, where - iota(c.shape, 0), choose(c < RADIUS, lower, higher)))

    c = columns_of(n, s.sum_rows)
    r = iota(c.shape, 0)
    is_low = (c >= s.low) & (c < s.low + SPAN)
    is_high = (c >= s.high) & (c < s.high + SPAN)
    is_far = (c >= s.far) & (c < s.far + y.second)
    where = jnp.where(is_low, c - s.low + 2 - SPAN, jnp.where(is_high, c - s.high + y.mid - 1, c - 1))
    valid = choose(is_low, lower, choose(is_high, higher, c < y.mid_all))
    mid = band(taps, 1, where - (r - 1), valid & (r < y.mid_all))
    far = jnp.where(far_below, -2 - y.coarse, 2 * y.coarse - 2)
    where = jnp.where(is_low, c - s.low + 3 - SPAN, jnp.where(is_high, c - s.high + y.coarse - 2, c - 2))
    where = jnp.where(is_far, c - s.far + far, where)
    valid = choose(is_low, lower, choose(is_high, higher, (c < y.coarse_all) | is_far))
    coarse = band(taps, 2, where - (r - 2), valid & (r < y.coarse_all))
    o, k = iota((y.fine, n), 0), iota((y.fine, n), 1)
    from_mid = jnp.where((k < y.mid_all) & y.holds_mid(k - 1), weight_of(o - 2 * (k - 1)), 0.0)
    m = s.coarse_rows
    c = columns_of(n, m)
    k = iota(c.shape, 0)
    from_coarse = jnp.where((c < y.coarse_all) & y.holds_coarse(c - 2), weight_of(k - 1 - 2 * (c - 2)), 0.0)
    write(y_mid, s.sum_rows, [dot(from_mid, matrix) for matrix in mid])
    write(y_coarse, s.sum_rows, [matrix[:m] for matrix in coarse])
    write(widen_y, m, [dot(from_mid, from_coarse)])


def contract_y(s, weights, high, low):
    joined = jnp.concatenate([high, low, high], axis=0)
    result = jnp.dot(weights[...], joined, preferred_element_type=F32)
    n, m = s.y.fine, s.x.fine
    return [result[t * n : (t + 1) * n, t * m : (t + 1) * m] for t in range(TERMS)]


def contract_z(table, level, held, base, count):
    rows = held.shape[2:]
    totals = [None] * count
    for t in range(held.shape[1]):
        for j in range(count + TAPS - 1):
            plane = held[base + j, t].reshape(rows[0] // 8, 8, rows[1])
            for i in range(max(0, j - TAPS + 1), min(count, j + 1)):
                term = table[(level * TERMS + t) * TAPS + j - i][None] * plane
                totals[i] = term if totals[i] is None else totals[i] + term
    return [total.reshape(rows) for total in totals]


def slab_starts(s, below_at, above_at):
    result = []
    for route in s.z_routes:
        lower, i = route.below(), s.z.index()
        valid = choose(lower, i >= 1, i + 1 < s.z.count)
        result.append((jnp.where(lower, below_at, above_at), valid))
    return result


def store_terms(held, at, valid, parts):
    for t, part in enumerate(parts):
        held[at, t] = part if valid is None else jnp.where(valid, part, 0.0)


BLOCK = 4


def fine_places(s):
    places = [(RADIUS + p, None) for p in range(s.z.fine)]
    for start, valid in slab_starts(s, 0, s.z.fine + RADIUS):
        places += [(start + p, valid) for p in range(RADIUS)]
    return places


def contract_x(s, grid, weights):
    high, low = split(grid)
    joined = jnp.concatenate([high, low, high], axis=1)
    return jnp.dot(joined, weights[: 3 * s.x.fine], preferred_element_type=F32)


def own_kernel(s, table, t_part, fine, slab, sums, x_fine, x_sums, y_edge, y_fine, fine_part, sums_part, t_fine):
    z, x = s.z, s.x
    t_fine[...] = t_part[...]
    fine_at = fine_places(s)

    def slab_group(g, count):
        n = s.fine_rows
        planes = jnp.concatenate([slab[g : g + count], fine[z.fine + g : z.fine + g + count]], axis=1)
        a, b = split(contract_x(s, planes.reshape(count * n, x.fine), x_fine))
        for p in range(count):
            rows = slice(p * n, (p + 1) * n)
            store_terms(t_fine, *fine_at[z.fine + g + p], contract_y(s, y_fine, a[rows], b[rows]))

    def fine_group(g, count):
        n = 2 * RADIUS
        a, b = split(contract_x(s, fine[g : g + count].reshape(count * n, x.fine), x_fine))
        for p in range(count):
            rows = slice(p * n, (p + 1) * n)
            at, valid = fine_at[g + p]
            for t, part in enumerate(contract_y(s, y_edge, a[rows], b[rows])):
                t_fine[at, t] = t_fine[at, t] + (part if valid is None else jnp.where(valid, part, 0.0))

    def fine_block(k):
        for i, total in enumerate(contract_z(table, 0, t_fine, k, BLOCK)):
            fine_part[k + i] = total

    def sum_part(g, count):
        n = s.sum_rows
        grid = sums[g : g + count].reshape(count * n, x.fine)
        sums_part[g * n : (g + count) * n] = contract_x(s, grid, x_sums)

    later = []
    done = 0
    for g in range(0, s.fine_planes - z.fine, 8):
        slab_group(g, 8)
    for g in range(0, z.fine, 8):
        fine_group(g, 8)
        while later:
            later.pop(0)()
        if g >= 0:
            ready = g if g + 8 < z.fine else z.fine
            later += [lambda k=k: fine_block(k) for k in range(done, ready, BLOCK)]
            done = max(done, ready)
    starts = list(range(0, s.sum_planes, 8))
    while later or starts:
        if starts:
            sum_part(starts[0], min(8, s.sum_planes - starts[0]))
            starts.pop(0)
        if later:
            later.pop(0)()


def sum_kernel(s, table, fine, sums, first, second, x_sums, ends, y_fine, y_mid, y_coarse, widen_x, widen_y, result, *scratch):
    sums_ends, t_mid, t_coarse, p_mid, p_coarse, narrow, out, left = scratch
    z, y, x = s.z, s.y, s.x
    below = s.x_routes[0].below()
    half = s.edge_sums
    def ends_of(start, rows):
        one, two = first[start : start + rows], second[start : start + rows]
        return jnp.where(below, one, two), jnp.where(below, two, one)

    for b in range(s.sum_blocks):
        if b < s.coarse_blocks:
            pair = ends_of(s.fine_ends + b * half, half)
        else:
            rest = jnp.zeros((half - up8(EDGE), 128), F32)
            pair = ends_of(s.mid_ends + (b - s.coarse_blocks) * up8(EDGE), up8(EDGE))
            pair = [jnp.concatenate([ends, rest], axis=0) for ends in pair]
        rows = jnp.concatenate(pair, axis=0)
        zeros = jnp.zeros((128 - 4 * half, 128), F32)
        sums_ends[b * 128 : (b + 1) * 128] = jnp.concatenate([rows, rows, zeros], axis=0).T

    def along_x(start, rows):
        edge_high, edge_low = split(sums_ends[start : start + rows])
        is_high = iota(edge_high.shape, 1) < 2 * half
        packed = jnp.where(is_high, edge_high.astype(F32), edge_low.astype(F32)).astype(BF16)
        joined = jnp.concatenate([packed, edge_high], axis=1)
        part = jnp.dot(joined, x_sums[3 * x.fine :], preferred_element_type=F32)
        return split(sums[start : start + rows] + part)

    def fine_edges():
        columns = []
        for flip in range(2):
            for g in range(s.fine_groups):
                is_folded = s.folded and g == s.fine_groups - 1
                at = slice(g * s.fine_rows, s.fine_ends if is_folded else (g + 1) * s.fine_rows)
                pair = (first[at], second[at])
                ends_here = jnp.where(below, pair[flip], pair[1 - flip])
                if is_folded:
                    ends_here = jnp.concatenate([ends_here, pltpu.roll(ends_here, x.fine // 2, 1)], axis=0)
                columns.append(ends_here)
        high, low = split(jnp.concatenate(columns, axis=1))
        joined = jnp.concatenate([high, low, high], axis=0)
        high, low = split(jnp.dot(y_fine[...], joined, preferred_element_type=F32))
        width = s.fine_groups * x.fine
        result = []
        for side in range(2):
            total = 0.0
            for t in range(TERMS):
                rows, cols = slice(t * y.fine, (t + 1) * y.fine), slice(side * width, (side + 1) * width)
                a, b = high[rows, cols], low[rows, cols]
                joined = jnp.concatenate([a, b, a], axis=1)
                total = total + jnp.dot(joined, ends[2 * t + side], preferred_element_type=F32)
            result.append(total)
        return result

    t_mid[...] = jnp.zeros(t_mid.shape, F32)
    t_coarse[...] = jnp.zeros(t_coarse.shape, F32)
    mid_at = [(RADIUS + p, None) for p in range(z.mid_all)]
    mid_at, rest_at = mid_at[: z.coarse_all], mid_at[z.coarse_all :]
    coarse_at = [(RADIUS + p, None) for p in range(z.coarse_all)]
    for start, valid in slab_starts(s, 0, z.mid + 3 + RADIUS):
        mid_at += [(start + p, valid) for p in range(RADIUS)]
    mid_at += rest_at
    for start, valid in slab_starts(s, 0, z.coarse + 5 + RADIUS):
        coarse_at += [(start + p, valid) for p in range(RADIUS)]
    coarse_at += [(None, None)] * len(rest_at)
    is_second = iota((s.coarse_rows, x.fine), 1) >= x.fine // TERMS

    def sum_group(g, count):
        n = s.sum_rows
        a, b = along_x(g * n, count * n)
        for p in range(count):
            rows = slice(p * n, (p + 1) * n)
            at, valid = mid_at[g + p]
            cols = slice(0, TERMS * x.fine)
            store_terms(t_mid, at, valid, contract_y(s, y_mid, a[rows, cols], b[rows, cols]))
            at, valid = coarse_at[g + p]
            if at is not None:
                cols = slice(TERMS * x.fine, (TERMS + 1) * x.fine)
                joined = jnp.concatenate([a[rows, cols], b[rows, cols], a[rows, cols]], axis=0)
                both = jnp.dot(y_coarse[...], joined, preferred_element_type=F32)
                m = s.coarse_rows
                store_terms(t_coarse, at, valid, [jnp.where(is_second, both[m:], both[:m])])

    def coarse_block(k):
        count = min(BLOCK, z.coarse_all - k)
        for i, total in enumerate(contract_z(table, 2, t_coarse, k, count)):
            narrow[k + i] = jnp.where(z.holds_coarse(k + i - 2), total, 0.0)

    def widen():
        m = s.coarse_rows
        high, low = split(narrow[...].reshape(z.coarse_all * m, x.fine))
        joined = jnp.concatenate([high, low, high], axis=1)
        high, low = split(jnp.dot(joined, widen_x[...], preferred_element_type=F32))
        for p in range(z.coarse_all):
            rows = slice(p * m, (p + 1) * m)
            joined = jnp.concatenate([high[rows], low[rows], high[rows]], axis=0)
            p_coarse[p] = jnp.dot(widen_y[...], joined, preferred_element_type=F32)

    def mid_block(k):
        count = min(BLOCK, z.mid_all - k)
        for i, total in enumerate(contract_z(table, 1, t_mid, k, count)):
            m = k + i - 1
            for offset, weight in WEIGHTS:
                if (m - offset) % 2 == 0 and 0 <= (m - offset) // 2 + 2 < z.coarse_all:
                    total = total + weight * p_coarse[(m - offset) // 2 + 2]
            p_mid[k + i] = jnp.where(z.holds_mid(m), total, 0.0)

    edges = fine_edges()
    lane = iota((y.fine, x.fine), 1)

    def begin(k):
        block, at = k // s.side, k % s.side * RADIUS
        low, high = (edge[:, block * x.fine : (block + 1) * x.fine] for edge in edges)
        low = pltpu.roll(low, -at % x.fine, 1) if at else low
        turn = (x.fine - RADIUS - at) % x.fine
        high = pltpu.roll(high, turn, 1) if turn else high
        out[k] = fine[k] + jnp.where(lane < RADIUS, low, jnp.where(lane >= x.fine - RADIUS, high, 0.0))

    def finish(k):
        total = out[k]
        for offset, weight in WEIGHTS:
            if (k - offset) % 2 == 0:
                total = total + weight * p_mid[(k - offset) // 2 + 1]
        out[k] = total

    groups = list(range(0, s.sum_planes, 14))
    share = -(-z.fine // len(groups))
    for n, g in enumerate(groups):
        sum_group(g, min(14, s.sum_planes - g))
        for k in range(n * share, min((n + 1) * share, z.fine)):
            begin(k)
    for k in range(0, z.coarse_all, BLOCK):
        coarse_block(k)
    widen()
    done, copies = 0, []
    for k in range(0, z.mid_all, BLOCK):
        mid_block(k)
        ready = z.fine if k + BLOCK >= z.mid_all else 2 * k + 2
        while done < ready:
            finish(done)
            done += 1
            if done % 8 == 0:
                part = pl.ds(done - 8, 8)
                copies.append(pltpu.make_async_copy(out.at[part], result.at[part], left.at[done // 8 - 1]))
                copies[-1].start()
    for copy in copies:
        copy.wait()


def call(kernel, outs, ins, scratch=(), flops=10**7, out_space=pltpu.VMEM):
    specs = [SMEM if a.ndim == 3 and a.shape[-1] == TAPS else VMEM for a in ins]
    size = sum(a.size * a.dtype.itemsize for a in ins) + sum(o.size * o.dtype.itemsize for o in outs)
    return pl.pallas_call(
        kernel,
        out_shape=tuple(outs),
        in_specs=specs,
        out_specs=tuple(pl.BlockSpec(memory_space=out_space) for _ in outs),
        scratch_shapes=list(scratch),
        compiler_params=PARAMS,
        cost_estimate=pl.CostEstimate(flops=flops, bytes_accessed=size, transcendentals=0),
    )(*ins)


def array(*shape, dtype=F32):
    return jax.ShapeDtypeStruct(shape, dtype)


def local(charges, kernel_taps):
    z, y, x = (Cut(name, size) for name, size in zip(("gz", "gy", "gx"), charges.shape))
    s = Sizes(z, y, x)
    n = x.fine
    nz, nz2 = len(s.z_routes), len(s.z2_routes)

    def bound(kernel, *static):
        return lambda *refs: kernel(s, *static, *refs)

    rows = up8(y.mid_all)
    (weights,) = call(bound(narrow_kernel), [array(n, 2 * n, dtype=BF16)], [], flops=10**10)
    held, own, ahead, behind, far, *messages = call(
        bound(restrict_kernel, nz),
        [array(*charges.shape), array(z.mid_all, rows, n)] + [array(s.y_rows, n)] * 2 + [array(s.far_rows, n)] + [array(s.z_rows, n)] * nz + [array(s.z2_rows, n)] * nz2,
        [charges, weights],
        [
            pltpu.VMEM((z.fine, y.fine + 32, n), F32),
            pltpu.VMEM((z.mid_all, rows, n), F32),
            pltpu.VMEM((z.mid_all, up8(y.mid + 24), n), F32),
            pltpu.VMEM((z.mid_all, rows, n), F32),
            pltpu.VMEM((2, max(s.z_rows - s.z_fine, s.y_rows - s.y_fine), n), F32),
            pltpu.VMEM((s.far_groups, s.far_rows, n), F32),
        ],
    )
    z_got = [route(m) for route, m in zip(s.z_routes + s.z2_routes, messages)]
    sides = [s.y_routes[0](ahead), s.y_routes[1](behind)]
    far = s.y2_routes[0](far)
    passed = call(
        bound(pass_kernel, nz),
        [array(RADIUS * s.inner + s.far_rows, n)] * nz + [array(s.far_rows, n)] * nz2,
        [far, held],
        flops=15 * 10**8,
    )
    operators = call(
        bound(operator_kernel),
        [
            array(3 * n, TERMS * n, dtype=BF16),
            array(3 * n + 256, (TERMS + 1) * n, dtype=BF16),
            array(TERMS * y.fine, 3 * y.fine, dtype=BF16),
            array(TERMS * y.fine, 6 * RADIUS, dtype=BF16),
            array(TERMS * y.fine, 3 * s.fine_rows, dtype=BF16),
            array(TERMS * y.fine, 3 * s.sum_rows, dtype=BF16),
            array(TERMS * s.coarse_rows, 3 * s.sum_rows, dtype=BF16),
            array(3 * n, n, dtype=BF16),
            array(y.fine, 3 * s.coarse_rows, dtype=BF16),
        ],
        [kernel_taps],
    )
    later = call(
        bound(later_kernel),
        [array(2 * TERMS, 3 * s.fine_groups * n, z_columns(s), dtype=BF16), array((2 * TERMS + 1) * TAPS, 8, n)],
        [kernel_taps],
    )
    ends, table = later
    ahead, behind = call(
        bound(spread_kernel, nz, nz2),
        [array(s.slab_rows, n), array(s.slab_rows, n)],
        [passed[0], *z_got],
        [pltpu.VMEM((3, up8(max(s.slab_coarse, s.slab_rows - s.slab_fine)) + 8, n), F32)],
    )
    sides += [s.y_routes[0](ahead), s.y_routes[1](behind)]
    fars = [far] + [route(m) for route, m in zip(s.z_routes + s.z2_routes, passed)]
    x_fine, x_sums, y_own, y_edge, y_fine, y_mid, y_coarse, widen_x, widen_y = operators
    t_part, last, start = call(
        bound(early_kernel),
        [array(z.fine + 2 * RADIUS, TERMS, y.fine, n)] + [array(s.own_groups * y.fine, n)] * 2,
        [held, x_fine, y_own, table],
    )
    fine, slab, sums, first, second = call(
        bound(collect_kernel, nz, nz2),
        [
            array(s.fine_planes, 2 * RADIUS, n),
            array(nz * RADIUS, y.fine, n),
            array(s.sum_planes, s.sum_rows, n),
            array(s.x_rows, n),
            array(s.x_rows, n),
        ],
        [last, start, own, *z_got, *sides, *fars],
        [
            pltpu.VMEM((s.slab_planes, s.sum_rows, n), F32),
            pltpu.VMEM((1 + nz + nz2, z.coarse_all, 8, n), F32),
            pltpu.VMEM((2, up8(s.slab_coarse) + 8, n), F32),
        ],
    )
    first, second = s.x_routes[0](first), s.x_routes[1](second)
    fine, sums = call(
        bound(own_kernel),
        [array(z.fine, y.fine, n), array(s.sum_planes * s.sum_rows, (TERMS + 1) * n)],
        [table, t_part, fine, slab, sums, x_fine, x_sums, y_edge, y_fine],
        [pltpu.VMEM((z.fine + 2 * RADIUS, TERMS, y.fine, n), F32)],
    )
    (out,) = call(
        bound(sum_kernel),
        [array(z.fine, y.fine, n)],
        [table, fine, sums, first, second, x_sums, ends, y_fine, y_mid, y_coarse, widen_x, widen_y],
        [
            pltpu.VMEM((s.sum_blocks * 128, n), F32),
            pltpu.VMEM((z.mid + 2 * RADIUS + 3, TERMS, y.fine, n), F32),
            pltpu.VMEM((z.coarse + 2 * RADIUS + 5, 1, s.coarse_rows, n), F32),
            pltpu.VMEM((z.mid_all, y.fine, n), F32),
            pltpu.VMEM((z.coarse_all, y.fine, n), F32),
            pltpu.VMEM((z.coarse_all, s.coarse_rows, n), F32),
            pltpu.VMEM((z.fine, y.fine, n), F32),
            pltpu.SemaphoreType.DMA((z.fine // 8,)),
        ],
        out_space=pltpu.HBM,
    )
    return out


def solution(mesh):
    return jax.shard_map(
        local,
        mesh=mesh,
        in_specs=(P("gz", "gy", "gx"), P()),
        out_specs=P("gz", "gy", "gx"),
        check_vma=False,
    )
```
